32 devices in a mesh: outer: 4 (over x, core), inner: 8 (over z, y).
Axes of the slice: x: 2, y: 2, z: 4, core: 2. Of those that a mesh axis runs over, the one named last changes fastest.
Arguments:
- tokens: bfloat16 [12288, 1152], P(('outer', 'inner')), may hold values from -6 to 6
- conditioning: float32 [3, 1152], replicated, may hold values from -6 to 6
- column_sample: int32 [768], P(('outer', 'inner')), may hold values from 0 to 2, as said below
- is_image: int32 [3], replicated, may hold values from 0 to 1, as said below
- output_grad: bfloat16 [12288, 1152], P(('outer', 'inner')), may hold values from -6 to 6
- weights: float32 [23887872], P(('outer', 'inner'))
- first_moment: float32 [23887872], P(('outer', 'inner')), may hold values from -0.0012207031 to 0.0012207031
- second_moment: float32 [23887872], P(('outer', 'inner')), may hold values from 4.1834003e-08 to 1.6733601e-07
- biases: float32 [16128], replicated, may hold values from -0.25 to 0.25
- bias_first: float32 [16128], replicated, may hold values from -0.0012207031 to 0.0012207031
- bias_second: float32 [16128], replicated, may hold values from 4.1834003e-08 to 1.6733601e-07
Outputs:
- block_out: float32 [12288, 1152], P(('outer', 'inner'))
- input_grad: float32 [12288, 1152], P(('outer', 'inner'))
- cond_grad: float32 [3, 1152], replicated
- grad_norm: float32 [], replicated
- new_weights: float32 [23887872], P(('outer', 'inner'))
- first_out: float32 [23887872], P(('outer', 'inner'))
- second_out: float32 [23887872], P(('outer', 'inner'))
- new_biases: float32 [16128], replicated
- bias_first_out: float32 [16128], replicated
- bias_second_out: float32 [16128], replicated
The draws below stay inside these ranges and needn't reach their ends.
Inputs may be any that keep to these rules, and one draw needn't show every extreme that they name: `column_sample`: each group number names exactly 256 columns. `is_image`: exactly max(1, 0) groups are images.
All inputs are finite; a program needn't handle non-finite values.
Results may differ from the reference program's by a relative error of at most 0.012.
The reference program's roundings to bfloat16 on the way count: a program that leaves them out, or rounds other values in their place, can miss the bound.
Values may be sent and summed in bfloat16 or wider, within the bound.
A program may use at most 384 MiB of HBM per device.

```python
import math
import jax
import jax.numpy as jnp
from jax import lax

D = 1152
H = 16
HD = 72
FF = 4608
FRAMES = 16
PATCHES = 256
STEP = 8
COLUMNS = 768
GROUPS = 3
TOKENS = 12288
PARAMS = 23887872
BIAS_COUNT = 16128


def draw_weights(key, part):
    key = jax.random.fold_in(key, 11)
    position = jnp.arange(PARAMS)
    spread = jnp.where(position < 3 * D * D, D ** (-0.5), jnp.where(position < 4 * D * D, FRAMES ** 0.5 * D ** (-0.5), jnp.where(position < 4 * D * D + D * FF, D ** (-0.5), jnp.where(position < 4 * D * D + 2 * D * FF, FF ** (-0.5), D ** (-0.5)))))
    return (jax.random.normal(key, (PARAMS,), jnp.float32) * spread).astype(jnp.float32)


def draw_column_sample(key, part):
    key = jax.random.fold_in(key, 23)
    shuffled = jax.random.permutation(key, COLUMNS).astype(jnp.int32)
    return (shuffled // PATCHES).astype(jnp.int32)


def draw_is_image(key, part):
    key = jax.random.fold_in(key, 37)
    shuffled = jax.random.permutation(key, GROUPS).astype(jnp.int32)
    return (shuffled < max(1, GROUPS // 8)).astype(jnp.int32)


def level_of(own_key, dims, cuts, smallest, top_value):
    factor_of, own = 1.0, jax.random.fold_in(own_key, 6)
    for dim, blocks in cuts:
        steps = jnp.exp(jax.random.uniform(jax.random.fold_in(own, dim), (blocks,), jnp.float32, smallest / len(cuts), top_value / len(cuts)))
        factor_of = factor_of * jnp.repeat(steps, dims[dim] // blocks).reshape([-1 if axis == dim else 1 for axis in range(len(dims))])
    return factor_of


def noise(stream_key, shape, scale, limit, split=(), held_as=jnp.bfloat16):
    loudness = level_of(stream_key, shape, split, -0.22, 0.18) if split else 1.0
    values = jax.random.normal(stream_key, shape, jnp.float32) * scale * loudness
    return jnp.minimum(jnp.maximum(values, -limit), limit).astype(held_as)


def setup_inputs(seed: int = 0) -> dict:
    key_of = jax.random.split(jax.random.key(seed), 12)
    tokens = noise(key_of[0], (TOKENS, D), 1.0, 6.0, ((0, 32),))
    conditioning = noise(key_of[1], (GROUPS, D), 1.0, 6.0, (), jnp.float32)
    column_sample = draw_column_sample(jax.random.fold_in(key_of[11], 71), 0)
    is_image = draw_is_image(jax.random.fold_in(key_of[11], 71), 0)
    output_grad = noise(key_of[4], (TOKENS, D), 1.0, 6.0, ((0, 32),))
    weights = draw_weights(jax.random.fold_in(key_of[11], 71), 0)
    first_moment = noise(key_of[6], (PARAMS,), ((PARAMS + BIAS_COUNT) ** -0.5), 0.0012207031, ((0, 32),), jnp.float32)
    second_moment = jnp.clip(jnp.exp(math.log(1.6733601171381451e-07) - 1.3862944 * jax.random.uniform(key_of[7], (PARAMS,), jnp.float32) ** level_of(key_of[7], (PARAMS,), ((0, 32),), -0.2, 0.2)), 4.183400292845363e-08, 1.6733601171381451e-07)
    biases = noise(key_of[8], (BIAS_COUNT,), 0.04, 0.25, (), jnp.float32)
    bias_first = noise(key_of[9], (BIAS_COUNT,), ((PARAMS + BIAS_COUNT) ** -0.5), 0.0012207031, (), jnp.float32)
    bias_second = jnp.clip(jnp.exp(jax.random.uniform(key_of[10], (BIAS_COUNT,), jnp.float32, math.log(4.183400292845363e-08), math.log(1.6733601171381451e-07))), 4.183400292845363e-08, 1.6733601171381451e-07)
    return dict(tokens=tokens, conditioning=conditioning, column_sample=column_sample, is_image=is_image, output_grad=output_grad, weights=weights, first_moment=first_moment, second_moment=second_moment, biases=biases, bias_first=bias_first, bias_second=bias_second)


NORM_EPS = 1e-06
LEARN_RATE = 0.02
BETA_FIRST = 0.5
BETA_SECOND = 0.55
ADAM_EPS = 1e-08
WEIGHT_DECAY = 0.01
CLIP_NORM = 1.0

@jax.custom_vjp
def low(v):
    return lax.optimization_barrier(v.astype(jnp.bfloat16)).astype(jnp.float32)

@jax.custom_vjp
def low_back(v):
    return v

def low_keep(v):
    return (low(v), None)

def low_pass(kept, grad):
    return (grad,)

def back_keep(v):
    return (v, None)

def back_low(kept, grad):
    return (low(grad),)
low.defvjp(low_keep, low_pass)
low_back.defvjp(back_keep, back_low)

def exact_dot(left_side, right_side):
    return jnp.dot(left_side, right_side, precision=lax.Precision.HIGHEST, preferred_element_type=jnp.float32)

def layer_norm(values):
    centered = values - lax.optimization_barrier(jnp.mean(values, axis=-1, keepdims=True))
    return centered * lax.rsqrt(lax.optimization_barrier(jnp.mean(centered * centered, axis=-1, keepdims=True)) + NORM_EPS)

def unpack_mats(flat):
    shapes = [(D, 3 * D), (D, D), (D, FF), (FF, D), (D, 6 * D)]
    pieces = []
    offset = 0
    for height, breadth in shapes:
        pieces.append(lax.slice_in_dim(flat, offset, offset + height * breadth).reshape(height, breadth))
        offset = offset + height * breadth
    return pieces

def split_bias(vector):
    widths = [D, D, D, FF, D, 6 * D]
    pieces = []
    offset = 0
    for span_width in widths:
        pieces.append(lax.slice_in_dim(vector, offset, offset + span_width))
        offset = offset + span_width
    return pieces

def column_block(block_rows, block_mods, block_video, mats, bias_vals):
    w_qkv, w_proj, w_up, w_down, w_ada = mats
    b_query, b_value, b_proj, b_up, b_down, b_ada = split_bias(bias_vals)
    columns = block_mods.shape[0]
    row_count = columns * FRAMES
    states = block_rows.reshape(columns, FRAMES, D)
    mod_parts = block_mods.reshape(columns, 1, 6, D)
    shift_att, scale_att, gate_att = (mod_parts[:, :, 0], mod_parts[:, :, 1], mod_parts[:, :, 2])
    shift_mlp, scale_mlp, gate_mlp = (mod_parts[:, :, 3], mod_parts[:, :, 4], mod_parts[:, :, 5])
    input_att = low(layer_norm(states) * (1.0 + scale_att) + shift_att).reshape(row_count, D)
    qkv_bias = jnp.concatenate([b_query, jnp.zeros((D,), jnp.float32), b_value])
    projected = low(low_back(exact_dot(input_att, w_qkv) + qkv_bias))
    queries = projected[:, :D].reshape(columns, FRAMES, H, HD)
    key_part = projected[:, D:2 * D].reshape(columns, FRAMES, H, HD)
    value_part = projected[:, 2 * D:].reshape(columns, FRAMES, H, HD)
    scores = jnp.einsum('cqhd,ckhd->chqk', queries, key_part, precision=lax.Precision.HIGHEST) / math.sqrt(HD)
    scores = low_back(scores)
    probabilities = low(jax.nn.softmax(scores, axis=-1))
    attended = jnp.einsum('chqk,ckhd->cqhd', probabilities, value_part, precision=lax.Precision.HIGHEST)
    attended = low(low_back(attended.reshape(row_count, D)))
    branch = low_back(exact_dot(attended, w_proj) + b_proj).reshape(columns, FRAMES, D)
    middle = states + gate_att * branch
    input_mlp = low(layer_norm(middle) * (1.0 + scale_mlp) + shift_mlp).reshape(row_count, D)
    hidden = low_back(exact_dot(input_mlp, w_up) + b_up)
    active = low(jax.nn.gelu(hidden, approximate=True))
    outcome = low_back(exact_dot(active, w_down) + b_down).reshape(columns, FRAMES, D)
    result = middle + gate_mlp * outcome
    is_video = block_video[:, None, None] > 0.5
    return jnp.where(is_video, result, states).reshape(row_count, D)

def adamw(parameter, gradient, first_state, second_state):
    first_new = BETA_FIRST * first_state + (1.0 - BETA_FIRST) * gradient
    second_new = BETA_SECOND * second_state + (1.0 - BETA_SECOND) * gradient * gradient
    first_hat = first_new / (1.0 - BETA_FIRST ** STEP)
    second_hat = second_new / (1.0 - BETA_SECOND ** STEP)
    updated = parameter - LEARN_RATE * (first_hat / (jnp.sqrt(second_hat) + ADAM_EPS) + WEIGHT_DECAY * parameter)
    return (updated, first_new, second_new)

def reference(tokens, conditioning, column_sample, is_image, output_grad, weights, first_moment, second_moment, biases, bias_first, bias_second):
    columns_all = column_sample.shape[0]
    block_cols = math.gcd(columns_all, 256)
    blocks = columns_all // block_cols
    video_group = 1.0 - is_image.astype(jnp.float32)

    def forward(token_vals, cond_vals, weight_vals, bias_vals):
        mats = unpack_mats(low(weight_vals))
        ada_bias = split_bias(bias_vals)[5]
        mods_all = exact_dot(low(jax.nn.silu(cond_vals)), mats[4]) + ada_bias
        mods = jnp.take(mods_all, column_sample, axis=0).reshape(blocks, block_cols, 6 * D)
        video_cols = jnp.take(video_group, column_sample).reshape(blocks, block_cols)
        stacked = token_vals.reshape(blocks, block_cols * FRAMES, D)

        def one_block(operands):
            return column_block(operands[0], operands[1], operands[2], mats, bias_vals)
        outputs = lax.map(jax.checkpoint(one_block), (stacked, mods, video_cols))
        return outputs.reshape(columns_all * FRAMES, D)
    block_out, pullback = jax.vjp(forward, tokens.astype(jnp.float32), conditioning, weights, biases)
    input_grad, cond_grad, weight_grad, bias_grad = pullback(output_grad.astype(jnp.float32))
    grad_norm = jnp.sqrt(jnp.sum(weight_grad * weight_grad) + jnp.sum(bias_grad * bias_grad))
    factor = jnp.minimum(1.0, CLIP_NORM / (grad_norm + 1e-06))
    new_weights, first_out, second_out = adamw(weights, weight_grad * factor, first_moment, second_moment)
    new_biases, bias_first_out, bias_second_out = adamw(biases, bias_grad * factor, bias_first, bias_second)
    return (block_out, input_grad, cond_grad, grad_norm, new_weights, first_out, second_out, new_biases, bias_first_out, bias_second_out)
```

```python
import functools
import math

import jax
import jax.numpy as jnp
from jax import lax
from jax.experimental import pallas as pl
from jax.experimental.pallas import tpu as pltpu
from jax.sharding import PartitionSpec as P

D = 1152
H = 16
HD = 72
FF = 4608
FRAMES = 16
STEP = 8


NORM_EPS = 1e-06
LEARN_RATE = 0.02
BETA_FIRST = 0.5
BETA_SECOND = 0.55
ADAM_EPS = 1e-08
WEIGHT_DECAY = 0.01
CLIP_NORM = 1.0
BLOCK_UNITS = 4 * D + 2 * FF

MESH = pl.DeviceIdType.MESH
UNITS = 648
ROWS = 656
QUART = 160
HALFQ = 80
MAIN = 640
TAIL = 16
DEPTH = (4, 4, 3)
BASE = (0, 4, 8)


def flip(z, d):
    if d == 0:
        return z
    if d == 1:
        return z + 1 - 2 * (z % 2)
    if d == 2:
        return z + 2 - 4 * (z // 2)
    return 3 - z


class Place:
    def __init__(self):
        self.o = lax.axis_index("outer")
        self.i = lax.axis_index("inner")
        self.x, self.c = self.o // 2, self.o % 2
        self.z, self.y = self.i // 2, self.i % 2
        self.xo, self.co, self.yo = 1 - self.x, 1 - self.c, 1 - self.y

    def dev(self, dx=0, dc=0, dz=0, dy=0):
        x = self.xo if dx else self.x
        c = self.co if dc else self.c
        y = self.yo if dy else self.y
        return (x * 2 + c, flip(self.z, dz) * 2 + y)

    def greet(self):
        peers = [
            self.dev(dx=1), self.dev(dc=1), self.dev(dx=1, dc=1), self.dev(dy=1),
            self.dev(dz=1), self.dev(dz=2), self.dev(dz=3),
        ]
        barrier = pltpu.get_barrier_semaphore()
        for peer in peers:
            pl.semaphore_signal(barrier, inc=1, device_id=peer, device_id_type=MESH)
        pl.semaphore_wait(barrier, len(peers))


class Copies:
    def __init__(self, send_sems, recv_sems):
        self.send_sems, self.recv_sems = send_sems, recv_sems
        self.count = 0
        self.sent = []

    def slot(self):
        self.count += 1
        return self.count - 1

    def make(self, slot, src, dst, device):
        return pltpu.make_async_remote_copy(
            src_ref=src, dst_ref=dst, send_sem=self.send_sems.at[slot],
            recv_sem=self.recv_sems.at[slot], device_id=device, device_id_type=MESH,
        )

    def send(self, slot, src, dst, device, cond=None):
        def go():
            self.make(slot, src, dst, device).start()
        if cond is None:
            go()
        else:
            pl.when(cond)(go)
        self.sent.append((slot, src, dst, device, cond))

    def wait_recv(self, slot, dst, device, cond=None):
        def go():
            self.make(slot, dst, dst, device).wait_recv()
        if cond is None:
            go()
        else:
            pl.when(cond)(go)

    def drain(self):
        for slot, src, dst, device, cond in self.sent:
            def go(slot=slot, src=src, dst=dst, device=device):
                self.make(slot, src, dst, device).wait_send()
            if cond is None:
                go()
            else:
                pl.when(cond)(go)
        self.sent = []


def rows16(start):
    return pl.multiple_of(start, 16)


def ok(zb, p):
    return None if DEPTH[p] == 4 else zb < DEPTH[p]


def both(a, b):
    if a is None:
        return b
    if b is None:
        return a
    return jnp.logical_and(a, b)


GATHER_COPIES = 3 * (3 + 3 + 4 * 4 + 8) + 7


def gather_kernel(shard, full, send_sems, recv_sems, local_sems):
    me = Place()
    cp = Copies(send_sems, recv_sems)
    me.greet()

    def part(p, zb, yb, x, c, first=0, n=QUART):
        return full.at[p, zb, yb, pl.ds(rows16(320 * x + QUART * c + first), n)]

    def own_of(p):
        return both(me.o == p, ok(me.z, p))

    quarter = rows16(320 * me.x + QUART * me.c)
    own_tail = pltpu.make_async_copy(
        shard.at[pl.ds(MAIN, TAIL)], full.at[me.o, me.z, me.y, pl.ds(MAIN, TAIL)], local_sems.at[0]
    )
    own_tail.start()

    def local_quarter(p):
        return pltpu.make_async_copy(
            shard.at[pl.ds(quarter, QUART)], part(p, me.z, me.y, me.x, me.c), local_sems.at[1]
        )

    slots = {}

    def s0(p):
        @pl.when(own_of(p))
        def _():
            local_quarter(p).start()
        for dx, dc in ((1, 0), (0, 1), (1, 1)):
            s = slots["s0", p, dx, dc] = cp.slot()
            x = me.xo if dx else me.x
            c = me.co if dc else me.c
            cp.send(
                s, shard.at[pl.ds(rows16(320 * x + QUART * c), QUART)],
                part(p, me.z, me.y, x, c), me.dev(dx=dx, dc=dc), own_of(p),
            )

    def s0_wait(p):
        @pl.when(own_of(p))
        def _():
            local_quarter(p).wait()
        ox, oc = p // 2, p % 2
        for dx, dc in ((1, 0), (0, 1), (1, 1)):
            x = me.xo if dx else me.x
            c = me.co if dc else me.c
            cond = both(jnp.logical_and(x == ox, c == oc), ok(me.z, p))
            cp.wait_recv(
                slots["s0", p, dx, dc], part(p, me.z, me.y, me.x, me.c), me.dev(dx=dx, dc=dc), cond
            )

    def spread(p, d):
        zb = flip(me.z, d)
        mine = part(p, zb, me.y, me.x, me.c)
        s = slots["y1", p, d] = cp.slot()
        cp.send(s, mine, mine, me.dev(dy=1), ok(zb, p))
        s = slots["x1", p, d] = cp.slot()
        cp.send(s, mine, mine, me.dev(dx=1), ok(zb, p))

    def s1(p):
        s0_wait(p)
        mine = part(p, me.z, me.y, me.x, me.c)
        for d in (1, 2, 3):
            s = slots["z", p, d] = cp.slot()
            cp.send(s, mine, mine, me.dev(dz=d), ok(me.z, p))
        spread(p, 0)

    def s2(p):
        for d in (1, 2, 3):
            zb = flip(me.z, d)
            cp.wait_recv(
                slots["z", p, d], part(p, zb, me.y, me.x, me.c), me.dev(dz=d), ok(zb, p)
            )
            spread(p, d)

    def s3(p):
        for d in (0, 1, 2, 3):
            zb = flip(me.z, d)
            cp.wait_recv(
                slots["y1", p, d], part(p, zb, me.yo, me.x, me.c), me.dev(dy=1), ok(zb, p)
            )
            s = slots["x2", p, d] = cp.slot()
            out = part(p, zb, me.yo, me.x, me.c, 0, HALFQ)
            cp.send(s, out, out, me.dev(dx=1), ok(zb, p))
            cp.wait_recv(
                slots["x1", p, d], part(p, zb, me.y, me.xo, me.c), me.dev(dx=1), ok(zb, p)
            )
            s = slots["y2", p, d] = cp.slot()
            out = part(p, zb, me.y, me.xo, me.c, HALFQ, HALFQ)
            cp.send(s, out, out, me.dev(dy=1), ok(zb, p))

    def lane(p, zb, x, c):
        return full.at[p, zb, :, pl.ds(rows16(320 * x + QUART * c), QUART)]

    def s4(p):
        for d in (0, 1, 2, 3):
            zb = flip(me.z, d)
            cp.wait_recv(
                slots["x2", p, d], part(p, zb, me.yo, me.xo, me.c, 0, HALFQ), me.dev(dx=1),
                ok(zb, p),
            )
            cp.wait_recv(
                slots["y2", p, d], part(p, zb, me.yo, me.xo, me.c, HALFQ, HALFQ), me.dev(dy=1),
                ok(zb, p),
            )
            for h in (0, 1):
                s = slots["c", p, d, h] = cp.slot()
                cp.send(s, lane(p, zb, h, me.c), lane(p, zb, h, me.c), me.dev(dc=1), ok(zb, p))

    def s5(p):
        for d in (0, 1, 2, 3):
            zb = flip(me.z, d)
            for h in (0, 1):
                cp.wait_recv(
                    slots["c", p, d, h], lane(p, zb, h, me.co), me.dev(dc=1), ok(zb, p)
                )

    tails = pl.ds(MAIN, TAIL)

    def t1():
        own_tail.wait()
        block = full.at[me.o, me.z, me.y, tails]
        for d in (1, 2, 3):
            s = slots["tz", d] = cp.slot()
            cp.send(s, block, block, me.dev(dz=d))

    def t2():
        for d in (1, 2, 3):
            zb = flip(me.z, d)
            cp.wait_recv(slots["tz", d], full.at[me.o, zb, me.y, tails], me.dev(dz=d))
        s = slots["ty"] = cp.slot()
        block = full.at[me.o, :, me.y, tails]
        cp.send(s, block, block, me.dev(dy=1))

    def t3():
        cp.wait_recv(slots["ty"], full.at[me.o, :, me.yo, tails], me.dev(dy=1))
        s = slots["tx"] = cp.slot()
        block = full.at[me.o, :, :, tails]
        cp.send(s, block, block, me.dev(dx=1))

    def t4():
        cp.wait_recv(slots["tx"], full.at[me.xo * 2 + me.c, :, :, tails], me.dev(dx=1))
        for h in (0, 1):
            s = slots["tc", h] = cp.slot()
            block = full.at[h * 2 + me.c, :, :, tails]
            cp.send(s, block, block, me.dev(dc=1))

    def t5():
        for h in (0, 1):
            cp.wait_recv(slots["tc", h], full.at[h * 2 + me.co, :, :, tails], me.dev(dc=1))

    s0(0); s0(1); s0(2); s1(0); t1(); s2(0); s1(1); s3(0); t2(); s2(1); s1(2); s4(0); t3()
    s3(1); s2(2); s5(0); s4(1); t4(); s3(2); s5(1); s4(2); s5(2); t5()
    cp.drain()


def gather_weights(shard):
    return pl.pallas_call(
        gather_kernel,
        out_shape=jax.ShapeDtypeStruct((4, 4, 2, ROWS, D), jnp.bfloat16),
        in_specs=[pl.BlockSpec(memory_space=pl.ANY)],
        out_specs=pl.BlockSpec(memory_space=pl.ANY),
        scratch_shapes=[
            pltpu.SemaphoreType.DMA((GATHER_COPIES,)),
            pltpu.SemaphoreType.DMA((GATHER_COPIES,)),
            pltpu.SemaphoreType.DMA((2,)),
        ],
        compiler_params=pltpu.CompilerParams(collective_id=0, has_side_effects=True),
        name="gather_weights",
    )(shard)


SCATTER_COPIES = 3 * (4 * 2 + 4 * 4 + 3 + 3) + 8
f32 = jnp.float32


def add_rows(dst, srcs, n, step=16):
    def body(j, carry):
        at = pl.ds(pl.multiple_of(j * step, step), step)
        total = srcs[0][at].astype(f32)
        for src in srcs[1:]:
            total = total + src[at].astype(f32)
        dst[at] = total.astype(dst.dtype)
        return carry

    lax.fori_loop(0, n // step, body, 0)


def scatter_kernel(
    partial, out, own, other, rx2, ry2, rx1, ry1, rz, final, tail, tail_in, tail_z,
    send_sems, recv_sems, local_sems,
):
    me = Place()
    cp = Copies(send_sems, recv_sems)
    me.greet()
    slots = {}
    order = (3, 2, 1, 0)

    def guarded(cond, fn):
        if cond is None:
            fn()
        else:
            pl.when(cond)(fn)

    def load(p, d, h):
        zb = flip(me.z, d)
        return pltpu.make_async_copy(
            partial.at[p, zb, :, pl.ds(rows16(320 * h + QUART * me.c), QUART)],
            own.at[BASE[p] + zb, :, h], local_sems.at[(p * 4 + d) * 2 + h],
        )

    def s0(p):
        for d in order:
            zb = flip(me.z, d)
            for h in (0, 1):
                guarded(ok(zb, p), lambda d=d, h=h: load(p, d, h).start())
                s = slots["c", p, d, h] = cp.slot()
                cp.send(
                    s, partial.at[p, zb, :, pl.ds(rows16(320 * h + QUART * me.co), QUART)],
                    other.at[BASE[p] + zb, :, h], me.dev(dc=1), ok(zb, p),
                )

    def s1(p):
        for d in order:
            zb = flip(me.z, d)
            b = BASE[p] + zb
            for h in (0, 1):
                guarded(ok(zb, p), lambda d=d, h=h: load(p, d, h).wait())
                cp.wait_recv(slots["c", p, d, h], other.at[b, :, h], me.dev(dc=1), ok(zb, p))

            def fold(b=b):
                def body(q, carry):
                    add_rows(own.at[b, q // 2, q % 2], [own.at[b, q // 2, q % 2], other.at[b, q // 2, q % 2]], QUART)
                    return carry
                lax.fori_loop(0, 4, body, 0)
            guarded(ok(zb, p), fold)
            s = slots["x2", p, d] = cp.slot()
            cp.send(s, own.at[b, me.yo, me.xo, pl.ds(0, HALFQ)], rx2.at[b], me.dev(dx=1), ok(zb, p))
            s = slots["y2", p, d] = cp.slot()
            cp.send(s, own.at[b, me.yo, me.xo, pl.ds(HALFQ, HALFQ)], ry2.at[b], me.dev(dy=1), ok(zb, p))

    def s2(p):
        for d in order:
            zb = flip(me.z, d)
            b = BASE[p] + zb
            cp.wait_recv(slots["x2", p, d], rx2.at[b], me.dev(dx=1), ok(zb, p))
            view = own.at[b, me.yo, me.x, pl.ds(0, HALFQ)]
            guarded(ok(zb, p), lambda view=view, b=b: add_rows(view, [view, rx2.at[b]], HALFQ))
            s = slots["y1", p, d] = cp.slot()
            cp.send(s, own.at[b, me.yo, me.x], ry1.at[b], me.dev(dy=1), ok(zb, p))
            cp.wait_recv(slots["y2", p, d], ry2.at[b], me.dev(dy=1), ok(zb, p))
            view = own.at[b, me.y, me.xo, pl.ds(HALFQ, HALFQ)]
            guarded(ok(zb, p), lambda view=view, b=b: add_rows(view, [view, ry2.at[b]], HALFQ))
            s = slots["x1", p, d] = cp.slot()
            cp.send(s, own.at[b, me.y, me.xo], rx1.at[b], me.dev(dx=1), ok(zb, p))

    def s3(p):
        for d in order:
            zb = flip(me.z, d)
            b = BASE[p] + zb
            cp.wait_recv(slots["y1", p, d], ry1.at[b], me.dev(dy=1), ok(zb, p))
            cp.wait_recv(slots["x1", p, d], rx1.at[b], me.dev(dx=1), ok(zb, p))
            view = own.at[b, me.y, me.x]
            guarded(
                ok(zb, p),
                lambda view=view, b=b: add_rows(view, [view, ry1.at[b], rx1.at[b]], QUART),
            )
            if d:
                s = slots["z", p, d] = cp.slot()
                cp.send(s, view, rz.at[p, d - 1], me.dev(dz=d), ok(zb, p))

    def s4(p):
        mine = ok(me.z, p)
        for d in (1, 2, 3):
            cp.wait_recv(slots["z", p, d], rz.at[p, d - 1], me.dev(dz=d), mine)
        view = own.at[BASE[p] + me.z, me.y, me.x]
        guarded(
            mine,
            lambda: add_rows(final.at[p], [view, rz.at[p, 0], rz.at[p, 1], rz.at[p, 2]], QUART),
        )
        ox, oc = p // 2, p % 2
        quarter = out.at[pl.ds(rows16(320 * me.x + QUART * me.c), QUART)]
        for dx, dc in ((1, 0), (0, 1), (1, 1)):
            x = me.xo if dx else me.x
            c = me.co if dc else me.c
            s = slots["f", p, dx, dc] = cp.slot()
            cond = both(jnp.logical_and(x == ox, c == oc), mine)
            cp.send(s, final.at[p], quarter, me.dev(dx=dx, dc=dc), cond)

        @pl.when(both(me.o == p, mine))
        def _():
            pltpu.make_async_copy(final.at[p], quarter, local_sems.at[24]).start()

    def s5(p):
        mine = both(me.o == p, ok(me.z, p))
        for dx, dc in ((1, 0), (0, 1), (1, 1)):
            x = me.xo if dx else me.x
            c = me.co if dc else me.c
            cp.wait_recv(
                slots["f", p, dx, dc], out.at[pl.ds(rows16(320 * x + QUART * c), QUART)],
                me.dev(dx=dx, dc=dc), mine,
            )

        @pl.when(mine)
        def _():
            quarter = out.at[pl.ds(rows16(320 * me.x + QUART * me.c), QUART)]
            pltpu.make_async_copy(final.at[p], quarter, local_sems.at[24]).wait()

    tail_load = pltpu.make_async_copy(
        partial.at[:, :, :, pl.ds(MAIN, TAIL)], tail, local_sems.at[25]
    )
    tail_load.start()

    def tail_add(o, zb, yb, srcs):
        add_rows(tail.at[o, zb, yb], [tail.at[o, zb, yb]] + srcs, TAIL)

    def t1():
        tail_load.wait()
        for h in (0, 1):
            s = slots["tc", h] = cp.slot()
            cp.send(s, tail.at[2 * h + me.co], tail_in.at[h], me.dev(dc=1))

    def t2():
        for h in (0, 1):
            cp.wait_recv(slots["tc", h], tail_in.at[h], me.dev(dc=1))

            def body(q, carry, h=h):
                tail_add(2 * h + me.c, q // 2, q % 2, [tail_in.at[h, q // 2, q % 2]])
                return carry
            lax.fori_loop(0, 8, body, 0)
        s = slots["tx"] = cp.slot()
        cp.send(s, tail.at[me.xo * 2 + me.c], tail_in.at[2], me.dev(dx=1))

    def t3():
        cp.wait_recv(slots["tx"], tail_in.at[2], me.dev(dx=1))

        def body(q, carry):
            tail_add(me.o, q // 2, q % 2, [tail_in.at[2, q // 2, q % 2]])
            return carry
        lax.fori_loop(0, 8, body, 0)
        s = slots["ty"] = cp.slot()
        cp.send(s, tail.at[me.o, :, me.yo], tail_in.at[3, :, 0], me.dev(dy=1))

    def t4():
        cp.wait_recv(slots["ty"], tail_in.at[3, :, 0], me.dev(dy=1))

        def body(q, carry):
            tail_add(me.o, q, me.y, [tail_in.at[3, q, 0]])
            return carry
        lax.fori_loop(0, 4, body, 0)
        for d in (1, 2, 3):
            s = slots["tz", d] = cp.slot()
            cp.send(s, tail.at[me.o, flip(me.z, d), me.y], tail_z.at[d - 1], me.dev(dz=d))

    def t5():
        for d in (1, 2, 3):
            cp.wait_recv(slots["tz", d], tail_z.at[d - 1], me.dev(dz=d))
        tail_add(me.o, me.z, me.y, [tail_z.at[0], tail_z.at[1], tail_z.at[2]])
        copy = pltpu.make_async_copy(
            tail.at[me.o, me.z, me.y], out.at[pl.ds(MAIN, TAIL)], local_sems.at[25]
        )
        copy.start()
        copy.wait()

    s0(2); s0(1); s0(0); s1(2); t1(); s1(1); s2(2); t2(); s1(0); s3(2); s2(1); t3(); s4(2)
    s2(0); s3(1); t4(); s4(1); s3(0); t5(); s4(0); s5(2); s5(1); s5(0)
    cp.drain()


def scatter_grads_kernel(partial):
    bf = jnp.bfloat16
    return pl.pallas_call(
        scatter_kernel,
        out_shape=jax.ShapeDtypeStruct((ROWS, D), bf),
        in_specs=[pl.BlockSpec(memory_space=pl.ANY)],
        out_specs=pl.BlockSpec(memory_space=pl.ANY),
        scratch_shapes=[
            pltpu.VMEM((11, 2, 2, QUART, D), bf),
            pltpu.VMEM((11, 2, 2, QUART, D), bf),
            pltpu.VMEM((11, HALFQ, D), bf),
            pltpu.VMEM((11, HALFQ, D), bf),
            pltpu.VMEM((11, QUART, D), bf),
            pltpu.VMEM((11, QUART, D), bf),
            pltpu.VMEM((3, 3, QUART, D), bf),
            pltpu.VMEM((3, QUART, D), bf),
            pltpu.VMEM((4, 4, 2, TAIL, D), bf),
            pltpu.VMEM((4, 4, 2, TAIL, D), bf),
            pltpu.VMEM((3, TAIL, D), bf),
            pltpu.SemaphoreType.DMA((SCATTER_COPIES,)),
            pltpu.SemaphoreType.DMA((SCATTER_COPIES,)),
            pltpu.SemaphoreType.DMA((26,)),
        ],
        compiler_params=pltpu.CompilerParams(
            collective_id=1, has_side_effects=True, vmem_limit_bytes=60 * 2**20
        ),
        name="scatter_grads",
    )(partial)

def gather_blocks(shard_low, kernels):
    if not kernels:
        whole = lax.all_gather(shard_low, ("outer", "inner"), axis=0, tiled=True)
        return whole[:BLOCK_UNITS]
    padded = jnp.pad(shard_low, ((0, ROWS - UNITS), (0, 0)))
    return gather_weights(padded).reshape(32, ROWS, D)[:22, :UNITS].reshape(-1, D)[:BLOCK_UNITS]


def scatter_blocks(grads, units, kernels):
    axes = ("outer", "inner")
    if not kernels:
        count = lax.axis_size(axes) * units
        padded = jnp.pad(grads, ((0, count - BLOCK_UNITS), (0, 0)))
        return lax.psum_scatter(padded, axes, scatter_dimension=0, tiled=True)
    padded = jnp.pad(grads, ((0, 32 * UNITS - BLOCK_UNITS), (0, 0))).reshape(32, UNITS, D)
    padded = jnp.pad(padded, ((0, 0), (0, ROWS - UNITS), (0, 0))).reshape(4, 4, 2, ROWS, D)
    return scatter_grads_kernel(padded)[:UNITS].astype(jnp.float32)


def unpack_mats(flat):
    shapes = [(D, 3 * D), (D, D), (D, FF), (FF, D)]
    pieces = []
    offset = 0
    for height, breadth in shapes:
        pieces.append(
            lax.slice_in_dim(flat, offset, offset + height * breadth).reshape(height, breadth)
        )
        offset = offset + height * breadth
    return pieces


def split_bias(vector):
    widths = [D, D, D, FF, D, 6 * D]
    pieces = []
    offset = 0
    for span_width in widths:
        pieces.append(lax.slice_in_dim(vector, offset, offset + span_width))
        offset = offset + span_width
    return pieces


def layer_stats(values):
    centered = values - jnp.mean(values, axis=-1, keepdims=True)
    inverse = lax.rsqrt(jnp.mean(centered * centered, axis=-1, keepdims=True) + NORM_EPS)
    return (centered * inverse, inverse)


def norm_back(grad_normed, normed, inverse):
    return inverse * (
        grad_normed
        - jnp.mean(grad_normed, axis=-1, keepdims=True)
        - normed * jnp.mean(grad_normed * normed, axis=-1, keepdims=True)
    )


def plain_dot(left_side, right_side):
    return jnp.dot(left_side, right_side, preferred_element_type=jnp.float32)


def left_dot(left_side, right_side):
    return lax.dot_general(
        left_side, right_side, (((0,), (0,)), ((), ())), preferred_element_type=jnp.float32
    )


def right_dot(left_side, right_side):
    return lax.dot_general(
        left_side, right_side, (((1,), (1,)), ((), ())), preferred_element_type=jnp.float32
    )


def exact(left, right, dims):
    return lax.dot_general(
        left, right, dims, precision=lax.Precision.HIGHEST, preferred_element_type=jnp.float32
    )


def ada_selector(soft_cond, first_unit, units):
    groups = soft_cond.shape[0]
    spread = jnp.repeat(soft_cond.astype(jnp.float32), 6, axis=1)
    spread = jnp.pad(spread, ((0, 0), (units, units)))
    start = jnp.clip(first_unit - BLOCK_UNITS + units, 0, 6 * D + units)
    local = lax.dynamic_slice(spread, (jnp.int32(0), start), (groups, units))
    unit = first_unit - BLOCK_UNITS + jnp.arange(units, dtype=jnp.int32)
    part = (unit[:, None] % 6 == jnp.arange(6, dtype=jnp.int32)[None, :]) & (unit[:, None] >= 0)
    part = part.astype(jnp.float32)
    selector = local.T[:, :, None] * part[:, None, :]
    return selector.reshape(units, groups * 6), part


def adamw(parameter, gradient, first_state, second_state):
    first_new = BETA_FIRST * first_state + (1.0 - BETA_FIRST) * gradient
    second_new = BETA_SECOND * second_state + (1.0 - BETA_SECOND) * gradient * gradient
    first_hat = first_new / (1.0 - BETA_FIRST**STEP)
    second_hat = second_new / (1.0 - BETA_SECOND**STEP)
    updated = parameter - LEARN_RATE * (
        first_hat / (jnp.sqrt(second_hat) + ADAM_EPS) + WEIGHT_DECAY * parameter
    )
    return (updated, first_new, second_new)


def on_device(
    tokens,
    conditioning,
    column_sample,
    is_image,
    output_grad,
    weights,
    first_moment,
    second_moment,
    biases,
    bias_first,
    bias_second,
    kernels,
):
    bf16 = jnp.bfloat16
    highest = lax.Precision.HIGHEST
    columns = column_sample.shape[0]
    groups = conditioning.shape[0]
    row_count = columns * FRAMES
    score_scale = 1.0 / math.sqrt(HD)
    units = weights.shape[0] // D
    axes = ("outer", "inner")
    first_unit = lax.axis_index(axes).astype(jnp.int32) * units
    shard = weights.reshape(units, D)
    shard_low = shard.astype(bf16)
    w_qkv, w_proj, w_up, w_down = unpack_mats(gather_blocks(shard_low, kernels).reshape(-1))
    b_query, b_value, b_proj, b_up, b_down, b_ada = split_bias(biases)
    soft_cond = jax.nn.silu(conditioning).astype(bf16)
    selector, ada_part = ada_selector(soft_cond, first_unit, units)
    mods_all = left_dot(selector.astype(bf16), shard_low)
    mods_all = lax.psum(mods_all, axes).reshape(groups, 6 * D) + b_ada
    mods = jnp.take(mods_all, column_sample, axis=0)
    video_cols = jnp.take(1.0 - is_image.astype(jnp.float32), column_sample)
    mod_parts = mods.reshape(columns, 1, 6, D)
    shift_att, scale_att, gate_att = (mod_parts[:, :, 0], mod_parts[:, :, 1], mod_parts[:, :, 2])
    shift_mlp, scale_mlp, gate_mlp = (mod_parts[:, :, 3], mod_parts[:, :, 4], mod_parts[:, :, 5])
    states = tokens.astype(jnp.float32).reshape(columns, FRAMES, D)
    normed_att, inverse_att = layer_stats(states)
    input_att = (normed_att * (1.0 + scale_att) + shift_att).astype(bf16).reshape(row_count, D)
    qkv_bias = jnp.concatenate([b_query, jnp.zeros((D,), jnp.float32), b_value])
    projected = (plain_dot(input_att, w_qkv) + qkv_bias).astype(bf16)
    queries = projected[:, :D].reshape(columns, FRAMES, H, HD)
    key_part = projected[:, D : 2 * D].reshape(columns, FRAMES, H, HD)
    value_part = projected[:, 2 * D :].reshape(columns, FRAMES, H, HD)
    scores = (
        jnp.einsum("cqhd,ckhd->chqk", queries, key_part, preferred_element_type=jnp.float32)
        * score_scale
    )
    probabilities = jax.nn.softmax(scores, axis=-1)
    prob_low = probabilities.astype(bf16)
    attended = jnp.einsum(
        "chqk,ckhd->cqhd", prob_low, value_part, preferred_element_type=jnp.float32
    )
    attended = attended.reshape(row_count, D).astype(bf16)
    branch = (plain_dot(attended, w_proj) + b_proj).reshape(columns, FRAMES, D)
    middle = states + gate_att * branch
    normed_mlp, inverse_mlp = layer_stats(middle)
    input_mlp = (normed_mlp * (1.0 + scale_mlp) + shift_mlp).astype(bf16).reshape(row_count, D)
    hidden = plain_dot(input_mlp, w_up) + b_up
    gelu_out, gelu_back = jax.vjp(lambda pre_act: jax.nn.gelu(pre_act, approximate=True), hidden)
    active = gelu_out.astype(bf16)
    outcome = (plain_dot(active, w_down) + b_down).reshape(columns, FRAMES, D)
    result = middle + gate_mlp * outcome
    is_video = video_cols[:, None, None] > 0.5
    block_out = jnp.where(is_video, result, states).reshape(row_count, D)
    upstream = output_grad.astype(jnp.float32).reshape(columns, FRAMES, D)
    grad_block = jnp.where(is_video, upstream, 0.0)
    grad_gate_mlp = jnp.sum(grad_block * outcome, axis=1)
    grad_outcome = (grad_block * gate_mlp).astype(bf16).reshape(row_count, D)
    grad_w_down = left_dot(active, grad_outcome)
    grad_b_down = jnp.sum(grad_outcome.astype(jnp.float32), axis=0)
    grad_active = right_dot(grad_outcome, w_down)
    grad_hidden = gelu_back(grad_active)[0].astype(bf16)
    grad_w_up = left_dot(input_mlp, grad_hidden)
    grad_b_up = jnp.sum(grad_hidden.astype(jnp.float32), axis=0)
    grad_input_mlp = right_dot(grad_hidden, w_up).reshape(columns, FRAMES, D)
    grad_shift_mlp = jnp.sum(grad_input_mlp, axis=1)
    grad_scale_mlp = jnp.sum(grad_input_mlp * normed_mlp, axis=1)
    grad_middle = grad_block + norm_back(
        grad_input_mlp * (1.0 + scale_mlp), normed_mlp, inverse_mlp
    )
    grad_gate_att = jnp.sum(grad_middle * branch, axis=1)
    grad_branch = (grad_middle * gate_att).astype(bf16).reshape(row_count, D)
    grad_w_proj = left_dot(attended, grad_branch)
    grad_b_proj = jnp.sum(grad_branch.astype(jnp.float32), axis=0)
    grad_attended = right_dot(grad_branch, w_proj).astype(bf16).reshape(columns, FRAMES, H, HD)
    grad_probs = jnp.einsum(
        "cqhd,ckhd->chqk", grad_attended, value_part, preferred_element_type=jnp.float32
    )
    grad_values = jnp.einsum(
        "chqk,cqhd->ckhd", prob_low, grad_attended, preferred_element_type=jnp.float32
    )
    grad_scores = probabilities * (
        grad_probs - jnp.sum(grad_probs * probabilities, axis=-1, keepdims=True)
    )
    grad_scores = grad_scores.astype(bf16)
    grad_queries = (
        jnp.einsum("chqk,ckhd->cqhd", grad_scores, key_part, preferred_element_type=jnp.float32)
        * score_scale
    )
    grad_keys = (
        jnp.einsum("chqk,cqhd->ckhd", grad_scores, queries, preferred_element_type=jnp.float32)
        * score_scale
    )
    grad_projected = jnp.concatenate(
        [
            grad_queries.reshape(row_count, D),
            grad_keys.reshape(row_count, D),
            grad_values.reshape(row_count, D),
        ],
        axis=1,
    ).astype(bf16)
    grad_w_qkv = left_dot(input_att, grad_projected)
    grad_qkv_sums = jnp.sum(grad_projected.astype(jnp.float32), axis=0)
    grad_b_query = grad_qkv_sums[:D]
    grad_b_value = grad_qkv_sums[2 * D :]
    grad_input_att = right_dot(grad_projected, w_qkv).reshape(columns, FRAMES, D)
    grad_shift_att = jnp.sum(grad_input_att, axis=1)
    grad_scale_att = jnp.sum(grad_input_att * normed_att, axis=1)
    grad_states = grad_middle + norm_back(
        grad_input_att * (1.0 + scale_att), normed_att, inverse_att
    )
    input_grad = jnp.where(is_video, grad_states, upstream).reshape(row_count, D)
    grad_mods = jnp.stack(
        [
            grad_shift_att,
            grad_scale_att,
            grad_gate_att,
            grad_shift_mlp,
            grad_scale_mlp,
            grad_gate_mlp,
        ],
        axis=1,
    )
    grad_mods = grad_mods.reshape(columns, 6 * D)
    membership = (column_sample[:, None] == jnp.arange(groups, dtype=jnp.int32)[None, :]).astype(
        jnp.float32
    )
    mods_local = lax.dot_general(
        membership,
        grad_mods,
        (((0,), (0,)), ((), ())),
        precision=highest,
        preferred_element_type=jnp.float32,
    )
    block_grads = [
        grad.astype(bf16 if kernels else jnp.float32).reshape(-1, D)
        for grad in (grad_w_qkv, grad_w_proj, grad_w_up, grad_w_down)
    ]
    bias_head = jnp.concatenate([grad_b_query, grad_b_value, grad_b_proj, grad_b_up, grad_b_down])
    bias_head, grad_mods_all = lax.psum((bias_head, mods_local), axes)
    first_sum = jnp.concatenate([bias_head, jnp.sum(grad_mods_all, axis=0)])
    block_shard = scatter_blocks(jnp.concatenate(block_grads), units, kernels)
    mods_parts = grad_mods_all.reshape(groups * 6, D)
    ada_shard = exact(selector, mods_parts, (((1,), (0,)), ((), ())))
    unit = first_unit + jnp.arange(units, dtype=jnp.int32)
    grad_units = jnp.where(unit[:, None] >= BLOCK_UNITS, ada_shard, block_shard)
    products = exact(shard_low.astype(jnp.float32), mods_parts, (((1,), (1,)), ((), ())))
    products = jnp.sum(products.reshape(units, groups, 6) * ada_part[:, None, :], axis=2)
    spread = jnp.zeros((groups, 6 * D + 2 * units), jnp.float32)
    start = jnp.clip(first_unit - BLOCK_UNITS + units, 0, 6 * D + units)
    spread = lax.dynamic_update_slice(spread, products.T, (jnp.int32(0), start))
    grad_soft = jnp.sum(spread[:, units : units + 6 * D].reshape(groups, D, 6), axis=2)
    square_sum, grad_soft = lax.psum((jnp.sum(grad_units * grad_units), grad_soft), axes)
    silu_out, silu_back = jax.vjp(jax.nn.silu, conditioning)
    second_sum = silu_back(grad_soft)[0]
    grad_shard = grad_units.reshape(-1)
    grad_norm = jnp.sqrt(square_sum + jnp.sum(first_sum * first_sum))
    factor = jnp.minimum(1.0, CLIP_NORM / (grad_norm + 1e-06))
    new_weights, first_out, second_out = adamw(
        weights, grad_shard * factor, first_moment, second_moment
    )
    new_biases, bias_first_out, bias_second_out = adamw(
        biases, first_sum * factor, bias_first, bias_second
    )
    return (
        block_out,
        input_grad,
        second_sum,
        grad_norm,
        new_weights,
        first_out,
        second_out,
        new_biases,
        bias_first_out,
        bias_second_out,
    )


def solution(mesh):
    in_specs = (
        P(("outer", "inner"), None),
        P(),
        P(("outer", "inner")),
        P(),
        P(("outer", "inner"), None),
        P(("outer", "inner")),
        P(("outer", "inner")),
        P(("outer", "inner")),
        P(),
        P(),
        P(),
    )
    out_specs = (
        P(("outer", "inner"), None),
        P(("outer", "inner"), None),
        P(),
        P(),
        P(("outer", "inner")),
        P(("outer", "inner")),
        P(("outer", "inner")),
        P(),
        P(),
        P(),
    )
    kernels = dict(mesh.shape) == {"outer": 4, "inner": 8}
    return jax.shard_map(
        functools.partial(on_device, kernels=kernels), mesh=mesh, in_specs=in_specs, out_specs=out_specs, check_vma=False
    )
```

```python
import functools
import math

import jax
import jax.numpy as jnp
from jax import lax
from jax.experimental import pallas as pl
from jax.experimental.pallas import tpu as pltpu
from jax.sharding import PartitionSpec as P

D = 1152
H = 16
HD = 72
FF = 4608
FRAMES = 16
STEP = 8


NORM_EPS = 1e-06
LEARN_RATE = 0.02
BETA_FIRST = 0.5
BETA_SECOND = 0.55
ADAM_EPS = 1e-08
WEIGHT_DECAY = 0.01
CLIP_NORM = 1.0
BLOCK_UNITS = 4 * D + 2 * FF


MESH = pl.DeviceIdType.MESH
UNITS = 648
GROUPS8 = 81
QUART = 20
HALFQ = 10
MAIN = 80
TAIL = 1
DEPTH = (4, 4, 3)
BASE = (0, 4, 8)


def flip(z, d):
    if d == 0:
        return z
    if d == 1:
        return z + 1 - 2 * (z % 2)
    if d == 2:
        return z + 2 - 4 * (z // 2)
    return 3 - z


class Place:
    def __init__(self):
        self.o = lax.axis_index("outer")
        self.i = lax.axis_index("inner")
        self.x, self.c = self.o // 2, self.o % 2
        self.z, self.y = self.i // 2, self.i % 2
        self.xo, self.co, self.yo = 1 - self.x, 1 - self.c, 1 - self.y

    def dev(self, dx=0, dc=0, dz=0, dy=0):
        x = self.xo if dx else self.x
        c = self.co if dc else self.c
        y = self.yo if dy else self.y
        return (x * 2 + c, flip(self.z, dz) * 2 + y)

    def greet(self):
        peers = [
            self.dev(dx=1), self.dev(dc=1), self.dev(dx=1, dc=1), self.dev(dy=1),
            self.dev(dz=1), self.dev(dz=2), self.dev(dz=3),
        ]
        barrier = pltpu.get_barrier_semaphore()
        for peer in peers:
            pl.semaphore_signal(barrier, inc=1, device_id=peer, device_id_type=MESH)
        pl.semaphore_wait(barrier, len(peers))


class Copies:
    def __init__(self, send_sems, recv_sems):
        self.send_sems, self.recv_sems = send_sems, recv_sems
        self.count = 0
        self.sent = []

    def slot(self):
        self.count += 1
        return self.count - 1

    def make(self, slot, src, dst, device):
        return pltpu.make_async_remote_copy(
            src_ref=src, dst_ref=dst, send_sem=self.send_sems.at[slot],
            recv_sem=self.recv_sems.at[slot], device_id=device, device_id_type=MESH,
        )

    def send(self, slot, src, dst, device, cond=None):
        def go():
            self.make(slot, src, dst, device).start()
        if cond is None:
            go()
        else:
            pl.when(cond)(go)
        self.sent.append((slot, src, dst, device, cond))

    def wait_recv(self, slot, dst, device, cond=None):
        def go():
            self.make(slot, dst, dst, device).wait_recv()
        if cond is None:
            go()
        else:
            pl.when(cond)(go)

    def drain(self):
        for slot, src, dst, device, cond in self.sent:
            def go(slot=slot, src=src, dst=dst, device=device):
                self.make(slot, src, dst, device).wait_send()
            if cond is None:
                go()
            else:
                pl.when(cond)(go)
        self.sent = []


def ok(zb, p):
    return None if DEPTH[p] == 4 else zb < DEPTH[p]


def both(a, b):
    if a is None:
        return b
    if b is None:
        return a
    return jnp.logical_and(a, b)


GATHER_COPIES = 3 * (3 + 3 + 4 * 4 + 8) + 7


def gather_kernel(shard, full, send_sems, recv_sems, local_sems):
    me = Place()
    cp = Copies(send_sems, recv_sems)
    me.greet()

    def part(p, zb, yb, x, c, first=0, n=QUART):
        return full.at[p, zb, yb, pl.ds((2 * QUART * x + QUART * c + first), n)]

    def own_of(p):
        return both(me.o == p, ok(me.z, p))

    quarter = (2 * QUART * me.x + QUART * me.c)
    own_tail = pltpu.make_async_copy(
        shard.at[pl.ds(MAIN, TAIL)], full.at[me.o, me.z, me.y, pl.ds(MAIN, TAIL)], local_sems.at[0]
    )
    own_tail.start()

    def local_quarter(p):
        return pltpu.make_async_copy(
            shard.at[pl.ds(quarter, QUART)], part(p, me.z, me.y, me.x, me.c), local_sems.at[1]
        )

    slots = {}

    def s0(p):
        @pl.when(own_of(p))
        def _():
            local_quarter(p).start()
        for dx, dc in ((1, 0), (0, 1), (1, 1)):
            s = slots["s0", p, dx, dc] = cp.slot()
            x = me.xo if dx else me.x
            c = me.co if dc else me.c
            cp.send(
                s, shard.at[pl.ds((2 * QUART * x + QUART * c), QUART)],
                part(p, me.z, me.y, x, c), me.dev(dx=dx, dc=dc), own_of(p),
            )

    def s0_wait(p):
        @pl.when(own_of(p))
        def _():
            local_quarter(p).wait()
        ox, oc = p // 2, p % 2
        for dx, dc in ((1, 0), (0, 1), (1, 1)):
            x = me.xo if dx else me.x
            c = me.co if dc else me.c
            cond = both(jnp.logical_and(x == ox, c == oc), ok(me.z, p))
            cp.wait_recv(
                slots["s0", p, dx, dc], part(p, me.z, me.y, me.x, me.c), me.dev(dx=dx, dc=dc), cond
            )

    def spread(p, d):
        zb = flip(me.z, d)
        mine = part(p, zb, me.y, me.x, me.c)
        s = slots["y1", p, d] = cp.slot()
        cp.send(s, mine, mine, me.dev(dy=1), ok(zb, p))
        s = slots["x1", p, d] = cp.slot()
        cp.send(s, mine, mine, me.dev(dx=1), ok(zb, p))

    def s1(p):
        s0_wait(p)
        mine = part(p, me.z, me.y, me.x, me.c)
        for d in (1, 2, 3):
            s = slots["z", p, d] = cp.slot()
            cp.send(s, mine, mine, me.dev(dz=d), ok(me.z, p))
        spread(p, 0)

    def s2(p):
        for d in (1, 2, 3):
            zb = flip(me.z, d)
            cp.wait_recv(
                slots["z", p, d], part(p, zb, me.y, me.x, me.c), me.dev(dz=d), ok(zb, p)
            )
            spread(p, d)

    def s3(p):
        for d in (0, 1, 2, 3):
            zb = flip(me.z, d)
            cp.wait_recv(
                slots["y1", p, d], part(p, zb, me.yo, me.x, me.c), me.dev(dy=1), ok(zb, p)
            )
            s = slots["x2", p, d] = cp.slot()
            out = part(p, zb, me.yo, me.x, me.c, 0, HALFQ)
            cp.send(s, out, out, me.dev(dx=1), ok(zb, p))
            cp.wait_recv(
                slots["x1", p, d], part(p, zb, me.y, me.xo, me.c), me.dev(dx=1), ok(zb, p)
            )
            s = slots["y2", p, d] = cp.slot()
            out = part(p, zb, me.y, me.xo, me.c, HALFQ, HALFQ)
            cp.send(s, out, out, me.dev(dy=1), ok(zb, p))

    def lane(p, zb, x, c):
        return full.at[p, zb, :, pl.ds((2 * QUART * x + QUART * c), QUART)]

    def s4(p):
        for d in (0, 1, 2, 3):
            zb = flip(me.z, d)
            cp.wait_recv(
                slots["x2", p, d], part(p, zb, me.yo, me.xo, me.c, 0, HALFQ), me.dev(dx=1),
                ok(zb, p),
            )
            cp.wait_recv(
                slots["y2", p, d], part(p, zb, me.yo, me.xo, me.c, HALFQ, HALFQ), me.dev(dy=1),
                ok(zb, p),
            )
            for h in (0, 1):
                s = slots["c", p, d, h] = cp.slot()
                cp.send(s, lane(p, zb, h, me.c), lane(p, zb, h, me.c), me.dev(dc=1), ok(zb, p))

    def s5(p):
        for d in (0, 1, 2, 3):
            zb = flip(me.z, d)
            for h in (0, 1):
                cp.wait_recv(
                    slots["c", p, d, h], lane(p, zb, h, me.co), me.dev(dc=1), ok(zb, p)
                )

    tails = pl.ds(MAIN, TAIL)

    def t1():
        own_tail.wait()
        block = full.at[me.o, me.z, me.y, tails]
        for d in (1, 2, 3):
            s = slots["tz", d] = cp.slot()
            cp.send(s, block, block, me.dev(dz=d))

    def t2():
        for d in (1, 2, 3):
            zb = flip(me.z, d)
            cp.wait_recv(slots["tz", d], full.at[me.o, zb, me.y, tails], me.dev(dz=d))
        s = slots["ty"] = cp.slot()
        block = full.at[me.o, :, me.y, tails]
        cp.send(s, block, block, me.dev(dy=1))

    def t3():
        cp.wait_recv(slots["ty"], full.at[me.o, :, me.yo, tails], me.dev(dy=1))
        s = slots["tx"] = cp.slot()
        block = full.at[me.o, :, :, tails]
        cp.send(s, block, block, me.dev(dx=1))

    def t4():
        cp.wait_recv(slots["tx"], full.at[me.xo * 2 + me.c, :, :, tails], me.dev(dx=1))
        for h in (0, 1):
            s = slots["tc", h] = cp.slot()
            block = full.at[h * 2 + me.c, :, :, tails]
            cp.send(s, block, block, me.dev(dc=1))

    def t5():
        for h in (0, 1):
            cp.wait_recv(slots["tc", h], full.at[h * 2 + me.co, :, :, tails], me.dev(dc=1))

    s0(0); s0(1); s0(2); s1(0); t1(); s2(0); s1(1); s3(0); t2(); s2(1); s1(2); s4(0); t3()
    s3(1); s2(2); s5(0); s4(1); t4(); s3(2); s5(1); s4(2); s5(2); t5()
    cp.drain()


def gather_weights(shard):
    return pl.pallas_call(
        gather_kernel,
        out_shape=jax.ShapeDtypeStruct((4, 4, 2, GROUPS8, 8, D), jnp.bfloat16),
        in_specs=[pl.BlockSpec(memory_space=pl.ANY)],
        out_specs=pl.BlockSpec(memory_space=pl.ANY),
        scratch_shapes=[
            pltpu.SemaphoreType.DMA((GATHER_COPIES,)),
            pltpu.SemaphoreType.DMA((GATHER_COPIES,)),
            pltpu.SemaphoreType.DMA((2,)),
        ],
        compiler_params=pltpu.CompilerParams(collective_id=0, has_side_effects=True),
        name="gather_weights",
    )(shard)


SCATTER_COPIES = 3 * (4 * 2 + 4 * 4 + 3 + 3) + 8
f32 = jnp.float32


def add_rows(dst, srcs, n):
    step = 2 if n % 2 == 0 else 1

    def body(j, carry):
        at = pl.ds(j * step, step)
        total = srcs[0][at].astype(f32)
        for src in srcs[1:]:
            total = total + src[at].astype(f32)
        dst[at] = total.astype(dst.dtype)
        return carry

    lax.fori_loop(0, n // step, body, 0)


def scatter_kernel(
    partial, out, own, other, rx2, ry2, rx1, ry1, rz, final, tail, tail_in, tail_z,
    send_sems, recv_sems, local_sems,
):
    me = Place()
    cp = Copies(send_sems, recv_sems)
    me.greet()
    slots = {}
    order = (3, 2, 1, 0)

    def guarded(cond, fn):
        if cond is None:
            fn()
        else:
            pl.when(cond)(fn)

    def load(p, d, h):
        zb = flip(me.z, d)
        return pltpu.make_async_copy(
            partial.at[p, zb, :, pl.ds((2 * QUART * h + QUART * me.c), QUART)],
            own.at[BASE[p] + zb, :, h], local_sems.at[(p * 4 + d) * 2 + h],
        )

    def s0(p):
        for d in order:
            zb = flip(me.z, d)
            for h in (0, 1):
                guarded(ok(zb, p), lambda d=d, h=h: load(p, d, h).start())
                s = slots["c", p, d, h] = cp.slot()
                cp.send(
                    s, partial.at[p, zb, :, pl.ds((2 * QUART * h + QUART * me.co), QUART)],
                    other.at[BASE[p] + zb, :, h], me.dev(dc=1), ok(zb, p),
                )

    def s1(p):
        for d in order:
            zb = flip(me.z, d)
            b = BASE[p] + zb
            for h in (0, 1):
                guarded(ok(zb, p), lambda d=d, h=h: load(p, d, h).wait())
                cp.wait_recv(slots["c", p, d, h], other.at[b, :, h], me.dev(dc=1), ok(zb, p))

            def fold(b=b):
                def body(q, carry):
                    add_rows(own.at[b, q // 2, q % 2], [own.at[b, q // 2, q % 2], other.at[b, q // 2, q % 2]], QUART)
                    return carry
                lax.fori_loop(0, 4, body, 0)
            guarded(ok(zb, p), fold)
            s = slots["x2", p, d] = cp.slot()
            cp.send(s, own.at[b, me.yo, me.xo, pl.ds(0, HALFQ)], rx2.at[b], me.dev(dx=1), ok(zb, p))
            s = slots["y2", p, d] = cp.slot()
            cp.send(s, own.at[b, me.yo, me.xo, pl.ds(HALFQ, HALFQ)], ry2.at[b], me.dev(dy=1), ok(zb, p))

    def s2(p):
        for d in order:
            zb = flip(me.z, d)
            b = BASE[p] + zb
            cp.wait_recv(slots["x2", p, d], rx2.at[b], me.dev(dx=1), ok(zb, p))
            view = own.at[b, me.yo, me.x, pl.ds(0, HALFQ)]
            guarded(ok(zb, p), lambda view=view, b=b: add_rows(view, [view, rx2.at[b]], HALFQ))
            s = slots["y1", p, d] = cp.slot()
            cp.send(s, own.at[b, me.yo, me.x], ry1.at[b], me.dev(dy=1), ok(zb, p))
            cp.wait_recv(slots["y2", p, d], ry2.at[b], me.dev(dy=1), ok(zb, p))
            view = own.at[b, me.y, me.xo, pl.ds(HALFQ, HALFQ)]
            guarded(ok(zb, p), lambda view=view, b=b: add_rows(view, [view, ry2.at[b]], HALFQ))
            s = slots["x1", p, d] = cp.slot()
            cp.send(s, own.at[b, me.y, me.xo], rx1.at[b], me.dev(dx=1), ok(zb, p))

    def s3(p):
        for d in order:
            zb = flip(me.z, d)
            b = BASE[p] + zb
            cp.wait_recv(slots["y1", p, d], ry1.at[b], me.dev(dy=1), ok(zb, p))
            cp.wait_recv(slots["x1", p, d], rx1.at[b], me.dev(dx=1), ok(zb, p))
            view = own.at[b, me.y, me.x]
            guarded(
                ok(zb, p),
                lambda view=view, b=b: add_rows(view, [view, ry1.at[b], rx1.at[b]], QUART),
            )
            if d:
                s = slots["z", p, d] = cp.slot()
                cp.send(s, view, rz.at[p, d - 1], me.dev(dz=d), ok(zb, p))

    def s4(p):
        mine = ok(me.z, p)
        for d in (1, 2, 3):
            cp.wait_recv(slots["z", p, d], rz.at[p, d - 1], me.dev(dz=d), mine)
        view = own.at[BASE[p] + me.z, me.y, me.x]
        guarded(
            mine,
            lambda: add_rows(final.at[p], [view, rz.at[p, 0], rz.at[p, 1], rz.at[p, 2]], QUART),
        )
        ox, oc = p // 2, p % 2
        quarter = out.at[pl.ds((2 * QUART * me.x + QUART * me.c), QUART)]
        for dx, dc in ((1, 0), (0, 1), (1, 1)):
            x = me.xo if dx else me.x
            c = me.co if dc else me.c
            s = slots["f", p, dx, dc] = cp.slot()
            cond = both(jnp.logical_and(x == ox, c == oc), mine)
            cp.send(s, final.at[p], quarter, me.dev(dx=dx, dc=dc), cond)

        @pl.when(both(me.o == p, mine))
        def _():
            pltpu.make_async_copy(final.at[p], quarter, local_sems.at[24]).start()

    def s5(p):
        mine = both(me.o == p, ok(me.z, p))
        for dx, dc in ((1, 0), (0, 1), (1, 1)):
            x = me.xo if dx else me.x
            c = me.co if dc else me.c
            cp.wait_recv(
                slots["f", p, dx, dc], out.at[pl.ds((2 * QUART * x + QUART * c), QUART)],
                me.dev(dx=dx, dc=dc), mine,
            )

        @pl.when(mine)
        def _():
            quarter = out.at[pl.ds((2 * QUART * me.x + QUART * me.c), QUART)]
            pltpu.make_async_copy(final.at[p], quarter, local_sems.at[24]).wait()

    tail_load = pltpu.make_async_copy(
        partial.at[:, :, :, pl.ds(MAIN, TAIL)], tail, local_sems.at[25]
    )
    tail_load.start()

    def tail_add(o, zb, yb, srcs):
        add_rows(tail.at[o, zb, yb], [tail.at[o, zb, yb]] + srcs, TAIL)

    def t1():
        tail_load.wait()
        for h in (0, 1):
            s = slots["tc", h] = cp.slot()
            cp.send(s, tail.at[2 * h + me.co], tail_in.at[h], me.dev(dc=1))

    def t2():
        for h in (0, 1):
            cp.wait_recv(slots["tc", h], tail_in.at[h], me.dev(dc=1))

            def body(q, carry, h=h):
                tail_add(2 * h + me.c, q // 2, q % 2, [tail_in.at[h, q // 2, q % 2]])
                return carry
            lax.fori_loop(0, 8, body, 0)
        s = slots["tx"] = cp.slot()
        cp.send(s, tail.at[me.xo * 2 + me.c], tail_in.at[2], me.dev(dx=1))

    def t3():
        cp.wait_recv(slots["tx"], tail_in.at[2], me.dev(dx=1))

        def body(q, carry):
            tail_add(me.o, q // 2, q % 2, [tail_in.at[2, q // 2, q % 2]])
            return carry
        lax.fori_loop(0, 8, body, 0)
        s = slots["ty"] = cp.slot()
        cp.send(s, tail.at[me.o, :, me.yo], tail_in.at[3, :, 0], me.dev(dy=1))

    def t4():
        cp.wait_recv(slots["ty"], tail_in.at[3, :, 0], me.dev(dy=1))

        def body(q, carry):
            tail_add(me.o, q, me.y, [tail_in.at[3, q, 0]])
            return carry
        lax.fori_loop(0, 4, body, 0)
        for d in (1, 2, 3):
            s = slots["tz", d] = cp.slot()
            cp.send(s, tail.at[me.o, flip(me.z, d), me.y], tail_z.at[d - 1], me.dev(dz=d))

    def t5():
        for d in (1, 2, 3):
            cp.wait_recv(slots["tz", d], tail_z.at[d - 1], me.dev(dz=d))
        tail_add(me.o, me.z, me.y, [tail_z.at[0], tail_z.at[1], tail_z.at[2]])
        copy = pltpu.make_async_copy(
            tail.at[me.o, me.z, me.y], out.at[pl.ds(MAIN, TAIL)], local_sems.at[25]
        )
        copy.start()
        copy.wait()

    s0(2); s0(1); s0(0); s1(2); t1(); s1(1); s2(2); t2(); s1(0); s3(2); s2(1); t3(); s4(2)
    s2(0); s3(1); t4(); s4(1); s3(0); t5(); s4(0); s5(2); s5(1); s5(0)
    cp.drain()


def scatter_grads_kernel(partial):
    bf = jnp.bfloat16
    return pl.pallas_call(
        scatter_kernel,
        out_shape=jax.ShapeDtypeStruct((GROUPS8, 8, D), bf),
        in_specs=[pl.BlockSpec(memory_space=pl.ANY)],
        out_specs=pl.BlockSpec(memory_space=pl.ANY),
        scratch_shapes=[
            pltpu.VMEM((11, 2, 2, QUART, 8, D), bf),
            pltpu.VMEM((11, 2, 2, QUART, 8, D), bf),
            pltpu.VMEM((11, HALFQ, 8, D), bf),
            pltpu.VMEM((11, HALFQ, 8, D), bf),
            pltpu.VMEM((11, QUART, 8, D), bf),
            pltpu.VMEM((11, QUART, 8, D), bf),
            pltpu.VMEM((3, 3, QUART, 8, D), bf),
            pltpu.VMEM((3, QUART, 8, D), bf),
            pltpu.VMEM((4, 4, 2, TAIL, 8, D), bf),
            pltpu.VMEM((4, 4, 2, TAIL, 8, D), bf),
            pltpu.VMEM((3, TAIL, 8, D), bf),
            pltpu.SemaphoreType.DMA((SCATTER_COPIES,)),
            pltpu.SemaphoreType.DMA((SCATTER_COPIES,)),
            pltpu.SemaphoreType.DMA((26,)),
        ],
        compiler_params=pltpu.CompilerParams(
            collective_id=1, has_side_effects=True, vmem_limit_bytes=60 * 2**20
        ),
        name="scatter_grads",
    )(partial)


bf16 = jnp.bfloat16
MATS = D // 8
AT_PROJ = 3 * MATS
AT_UP = 4 * MATS
AT_DOWN = 8 * MATS
ROOT = math.sqrt(2.0 / math.pi)
CUBIC = 0.044715


def nn_dot(left, right):
    return lax.dot_general(left, right, (((1,), (0,)), ((), ())), preferred_element_type=f32)


def nt_dot(left, right):
    return lax.dot_general(left, right, (((1,), (1,)), ((), ())), preferred_element_type=f32)


def tn_dot(left, right):
    return lax.dot_general(left, right, (((0,), (0,)), ((), ())), preferred_element_type=f32)


def square(ref):
    return ref[...].reshape(D, D)


def norm_rows(values):
    centered = values - jnp.mean(values, axis=-1, keepdims=True)
    inverse = lax.rsqrt(jnp.mean(centered * centered, axis=-1, keepdims=True) + NORM_EPS)
    return centered * inverse, inverse


def norm_rows_back(grad, normed, inverse):
    return inverse * (
        grad
        - jnp.mean(grad, axis=-1, keepdims=True)
        - normed * jnp.mean(grad * normed, axis=-1, keepdims=True)
    )


def frames_of(c):
    return pl.ds(pl.multiple_of(c * FRAMES, FRAMES), FRAMES)


def over_columns(count, body):
    def step(c, carry):
        body(c, frames_of(c), pl.ds(c, 1))
        return carry

    lax.fori_loop(0, count, step, 0)


def split_rows(src, spread, put, ways, step):
    units = src.shape[0] * 8
    rows = units // ways
    for q in range(9):
        lanes = slice(128 * q, 128 * q + 128)
        spread[q, pl.ds(0, units)] = src[:, :, lanes].astype(f32).reshape(units, 128)
        for w in range(ways):
            part = spread[q, pl.ds(w, rows, stride=ways), :]
            put(w, lanes, part.reshape(rows // 8, 8, 128).astype(bf16))


def head_window(h):
    first = min(HD * h // 128, 7) * 128
    lane = lax.broadcasted_iota(jnp.int32, (1, 256), 1) + first
    mask = jnp.logical_and(lane >= HD * h, lane < HD * h + HD)
    return slice(first, first + 256), jnp.where(mask, 1.0, 0.0).astype(bf16)


def same_column():
    row = lax.broadcasted_iota(jnp.int32, (128, 128), 0)
    col = lax.broadcasted_iota(jnp.int32, (128, 128), 1)
    return lax.shift_right_logical(row, 4) == lax.shift_right_logical(col, 4)


SCORE_SCALE = 1.0 / math.sqrt(HD)


def head_probabilities(masked_queries, keys, inside):
    scores = jnp.where(inside, nt_dot(masked_queries, keys) * SCORE_SCALE, -1e30)
    grown = jnp.exp(scores - jnp.max(scores, axis=-1, keepdims=True))
    return grown / jnp.sum(grown, axis=-1, keepdims=True)


def forward_kernel(
    weights, tokens, upstream, mods, b_qkv, b_proj, b_up, b_down,
    block_out, natural, input_att, proj, attended, branch, input_mlp, active, slope, grad_out,
    grad_gate, held, stage, spread, acc, hid, copy_sems,
):
    columns = mods.shape[1]

    def fetch(first, groups, slot):
        return pltpu.make_async_copy(
            weights.at[pl.ds(first, groups)], stage.at[slot, pl.ds(0, groups)], copy_sems.at[slot]
        )

    def whole(mat, slot):
        return pltpu.make_async_copy(
            weights.at[pl.ds(mat * MATS, MATS)], held.at[slot], copy_sems.at[2 + slot]
        )

    def save(mat, slot):
        return pltpu.make_async_copy(held.at[slot], natural.at[mat], copy_sems.at[10 + mat])

    def unweave(first, ways, slot0, blocks=9):
        groups = 16 * ways
        fetch(first, groups, 0).start()

        def step(j, carry):
            slot = lax.rem(j, 2)
            fetch(first + j * groups, groups, slot).wait()

            @pl.when(j + 1 < blocks)
            def _():
                fetch(first + (j + 1) * groups, groups, 1 - slot).start()

            def put(w, lanes, block):
                held[slot0 + w, pl.ds(j * 16, 16), :, lanes] = block

            split_rows(stage.at[slot, pl.ds(0, groups)], spread, put, ways, None)
            return carry

        lax.fori_loop(0, blocks, step, 0)

    whole(3, 3).start()

    def first_norm(c, rows, at):
        normed, _ = norm_rows(tokens[rows].astype(f32))
        input_att[rows] = (normed * (1.0 + mods[1, at]) + mods[0, at]).astype(bf16)

    over_columns(columns, first_norm)
    unweave(0, 3, 0)
    for p in range(3):
        save(p, p).start()

    def project(p, carry):
        proj[p] = (nn_dot(input_att[...], square(held.at[p])) + b_qkv[pl.ds(p, 1)]).astype(bf16)
        return carry

    lax.fori_loop(0, 3, project, 0)

    inside = same_column()

    def attend(g, carry):
        rows = pl.ds(pl.multiple_of(g * 128, 128), 128)
        acc[pl.ds(0, 128)] = jnp.zeros((128, D), f32)
        for h in range(H):
            window, mask = head_window(h)
            probs = head_probabilities(proj[0, rows, window] * mask, proj[1, rows, window], inside)
            acc[pl.ds(0, 128), window] += nn_dot(probs.astype(bf16), proj[2, rows, window] * mask)
        attended[rows] = acc[pl.ds(0, 128)].astype(bf16)
        return carry

    lax.fori_loop(0, columns * FRAMES // 128, attend, 0)
    whole(3, 3).wait()
    branch[...] = nn_dot(attended[...], square(held.at[3])) + b_proj[...]
    for p in range(3):
        save(p, p).wait()
    for b in range(4):
        whole(8 + b, b).start()

    def second_norm(c, rows, at):
        middle = tokens[rows].astype(f32) + mods[2, at] * branch[rows]
        normed, _ = norm_rows(middle)
        input_mlp[rows] = (normed * (1.0 + mods[4, at]) + mods[3, at]).astype(bf16)

    over_columns(columns, second_norm)
    unweave(AT_UP, 4, 4)
    for b in range(4):
        save(3 + b, 4 + b).start()

    def raise_(b, carry):
        hid[...] = nn_dot(input_mlp[...], square(held.at[4 + b])) + b_up[pl.ds(b, 1)]

        def gelu(c, rows, at):
            v = hid[rows]
            sq = v * v
            t = jnp.tanh(ROOT * (v + CUBIC * sq * v))
            half = 0.5 * (1.0 + t)
            active[b, rows] = (v * half).astype(bf16)
            slope[b, rows] = half + (0.5 * ROOT) * v * (1.0 - t * t) * (1.0 + 3.0 * CUBIC * sq)

        over_columns(columns, gelu)
        return carry

    lax.fori_loop(0, 4, raise_, 0)
    acc[...] = jnp.broadcast_to(b_down[...], acc.shape)
    for b in range(4):
        whole(8 + b, b).wait()

    def lower(b, carry):
        acc[...] += nn_dot(active[b], square(held.at[b]))
        return carry

    lax.fori_loop(0, 4, lower, 0)

    def last(c, rows, at):
        x = tokens[rows].astype(f32)
        middle = x + mods[2, at] * branch[rows]
        video = mods[6, at] > 0.5
        outcome = acc[rows]
        block_out[rows] = jnp.where(video, middle + mods[5, at] * outcome, x)
        grad_block = jnp.where(video, upstream[rows].astype(f32), 0.0)
        grad_gate[at] = jnp.sum(grad_block * outcome, axis=0, keepdims=True)
        grad_out[rows] = (grad_block * mods[5, at]).astype(bf16)

    over_columns(columns, last)
    for b in range(4):
        save(3 + b, 4 + b).wait()


def forward(weights, tokens, upstream, mods, b_qkv, b_proj, b_up, b_down):
    rows = tokens.shape[0]
    columns = mods.shape[1]
    vmem = pl.BlockSpec(memory_space=pltpu.VMEM)
    hbm = pl.BlockSpec(memory_space=pl.ANY)
    shape = jax.ShapeDtypeStruct
    return pl.pallas_call(
        forward_kernel,
        out_shape=[
            shape((rows, D), f32),
            shape((7, MATS, 8, D), bf16),
            shape((rows, D), bf16),
            shape((3, rows, D), bf16),
            shape((rows, D), bf16),
            shape((rows, D), f32),
            shape((rows, D), bf16),
            shape((4, rows, D), bf16),
            shape((4, rows, D), f32),
            shape((rows, D), bf16),
            shape((columns, D), f32),
        ],
        in_specs=[hbm] + [vmem] * 7,
        out_specs=[vmem, hbm] + [vmem] * 9,
        scratch_shapes=[
            pltpu.VMEM((8, MATS, 8, D), bf16),
            pltpu.VMEM((2, 64, 8, D), bf16),
            pltpu.VMEM((9, 512, 128), f32),
            pltpu.VMEM((rows, D), f32),
            pltpu.VMEM((rows, D), f32),
            pltpu.SemaphoreType.DMA((17,)),
        ],
        compiler_params=pltpu.CompilerParams(vmem_limit_bytes=60 * 2**20),
        name="block_forward",
    )(weights, tokens, upstream, mods, b_qkv, b_proj, b_up, b_down)


def backward_kernel(
    weights, natural, tokens, upstream, mods, input_att, proj, attended, branch, input_mlp, active,
    slope, grad_out,
    grads, input_grad, grad_mods, bias_sums,
    held, woven, spread, flat, grad_hidden, middle_grad, grad_branch, grad_att, grad_proj, acc,
    copy_sems,
):
    columns = mods.shape[1]

    def fetch(source, first, slot):
        return pltpu.make_async_copy(source.at[first], held.at[slot], copy_sems.at[slot])

    def flat_mat(first, slot):
        return pltpu.make_async_copy(
            weights.at[pl.ds(first, MATS)], held.at[slot], copy_sems.at[slot]
        )

    def store_flat(first, slot):
        return pltpu.make_async_copy(
            flat.at[slot], grads.at[pl.ds(first, MATS)], copy_sems.at[2 + slot]
        )

    bias_sums[...] = jnp.zeros_like(bias_sums)

    def add_bias(row, values):
        bias_sums[pl.ds(row, 1)] += jnp.sum(values.astype(f32), axis=0, keepdims=True)

    flat_mat(AT_DOWN, 0).start()

    def down(b, carry):
        slot = lax.rem(b, 2)
        flat_mat(AT_DOWN + b * MATS, slot).wait()

        @pl.when(b < 3)
        def _():
            flat_mat(AT_DOWN + (b + 1) * MATS, 1 - slot).start()

        acc[...] = nt_dot(grad_out[...], square(held.at[slot]))

        def through(c, rows, at):
            grad = (acc[rows] * slope[b, rows]).astype(bf16)
            grad_hidden[b, rows] = grad
            add_bias(5 + b, grad)

        over_columns(columns, through)

        @pl.when(b >= 2)
        def _():
            store_flat(AT_DOWN + (b - 2) * MATS, slot).wait()

        flat[slot] = tn_dot(active[b], grad_out[...]).reshape(MATS, 8, D).astype(bf16)
        store_flat(AT_DOWN + b * MATS, slot).start()
        return carry

    lax.fori_loop(0, 4, down, 0)
    fetch(natural, 3, 0).start()

    def down_bias(c, rows, at):
        add_bias(4, grad_out[rows])

    over_columns(columns, down_bias)

    def weave(first, ways, left, right_of):
        groups = 48 * ways

        def store(k):
            return pltpu.make_async_copy(
                woven.at[pl.ds(0, groups)], grads.at[pl.ds(first + k * groups, groups)],
                copy_sems.at[4],
            )

        for k in range(3):
            for w in range(ways):
                part = tn_dot(left[:, 384 * k : 384 * k + 384], right_of(w))
                for q in range(9):
                    spread[q, pl.ds(w, 384, stride=ways), :] = part[:, 128 * q : 128 * q + 128]
            if k:
                store(k - 1).wait()

            def pack(j, carry):
                for q in range(9):
                    block = spread[q, pl.ds(pl.multiple_of(j * 128, 128), 128), :]
                    woven[pl.ds(j * 16, 16), :, 128 * q : 128 * q + 128] = block.reshape(
                        16, 8, 128
                    ).astype(bf16)
                return carry

            lax.fori_loop(0, groups // 16, pack, 0)
            store(k).start()
        return lambda: store(2).wait()

    up_done = weave(AT_UP, 4, input_mlp, lambda w: grad_hidden[w])
    acc[...] = jnp.zeros_like(acc)

    def up(b, carry):
        slot = lax.rem(b, 2)
        fetch(natural, 3 + b, slot).wait()

        @pl.when(b < 3)
        def _():
            fetch(natural, 4 + b, 1 - slot).start()

        acc[...] += nt_dot(grad_hidden[b], square(held.at[slot]))
        return carry

    lax.fori_loop(0, 4, up, 0)
    flat_mat(AT_PROJ, 0).start()

    def second_norm_back(c, rows, at):
        br = branch[rows]
        gate = mods[2, at]
        normed, inverse = norm_rows(tokens[rows].astype(f32) + gate * br)
        grad = acc[rows]
        grad_mods[3, at] = jnp.sum(grad, axis=0, keepdims=True)
        grad_mods[4, at] = jnp.sum(grad * normed, axis=0, keepdims=True)
        grad_block = jnp.where(mods[6, at] > 0.5, upstream[rows].astype(f32), 0.0)
        grad_middle = grad_block + norm_rows_back(grad * (1.0 + mods[4, at]), normed, inverse)
        middle_grad[rows] = grad_middle
        grad_mods[2, at] = jnp.sum(grad_middle * br, axis=0, keepdims=True)
        grad = (grad_middle * gate).astype(bf16)
        grad_branch[rows] = grad
        add_bias(3, grad)

    over_columns(columns, second_norm_back)
    store_flat(AT_DOWN + 2 * MATS, 0).wait()
    store_flat(AT_DOWN + 3 * MATS, 1).wait()
    flat[0] = tn_dot(attended[...], grad_branch[...]).reshape(MATS, 8, D).astype(bf16)
    store_flat(AT_PROJ, 0).start()
    flat_mat(AT_PROJ, 0).wait()
    grad_att[...] = nt_dot(grad_branch[...], square(held.at[0])).astype(bf16)
    fetch(natural, 0, 0).start()
    inside = same_column()
    top = pl.ds(0, 128)

    def attend_back(g, carry):
        rows = pl.ds(pl.multiple_of(g * 128, 128), 128)
        for p in range(3):
            acc[pl.ds(p * 128, 128)] = jnp.zeros((128, D), f32)
        for h in range(H):
            window, mask = head_window(h)
            queries = proj[0, rows, window] * mask
            keys = proj[1, rows, window]
            grad = grad_att[rows, window] * mask
            probs = head_probabilities(queries, keys, inside)
            grad_probs = nt_dot(grad, proj[2, rows, window])
            mean = jnp.sum(grad_probs * probs, axis=-1, keepdims=True)
            grad_scores = (probs * (grad_probs - mean)).astype(bf16)
            acc[pl.ds(0, 128), window] += nn_dot(grad_scores, keys * mask)
            acc[pl.ds(128, 128), window] += tn_dot(grad_scores, queries)
            acc[pl.ds(256, 128), window] += tn_dot(probs.astype(bf16), grad)
        for p in range(3):
            scale = SCORE_SCALE if p < 2 else 1.0
            grad = (acc[pl.ds(p * 128, 128)] * scale).astype(bf16)
            grad_proj[p, rows] = grad
            add_bias(p, grad)
        return carry

    lax.fori_loop(0, columns * FRAMES // 128, attend_back, 0)
    up_done()
    qkv_done = weave(0, 3, input_att, lambda w: grad_proj[w])
    acc[...] = jnp.zeros_like(acc)

    def qkv(p, carry):
        slot = lax.rem(p, 2)
        fetch(natural, p, slot).wait()

        @pl.when(p < 2)
        def _():
            fetch(natural, p + 1, 1 - slot).start()

        acc[...] += nt_dot(grad_proj[p], square(held.at[slot]))
        return carry

    lax.fori_loop(0, 3, qkv, 0)

    def first_norm_back(c, rows, at):
        normed, inverse = norm_rows(tokens[rows].astype(f32))
        grad = acc[rows]
        grad_mods[0, at] = jnp.sum(grad, axis=0, keepdims=True)
        grad_mods[1, at] = jnp.sum(grad * normed, axis=0, keepdims=True)
        grad_states = middle_grad[rows] + norm_rows_back(
            grad * (1.0 + mods[1, at]), normed, inverse
        )
        up_rows = upstream[rows].astype(f32)
        input_grad[rows] = jnp.where(mods[6, at] > 0.5, grad_states, up_rows)

    over_columns(columns, first_norm_back)
    store_flat(AT_PROJ, 0).wait()
    qkv_done()


def backward(weights, natural, *operands):
    tokens, mods = operands[0], operands[2]
    rows = tokens.shape[0]
    columns = mods.shape[1]
    vmem = pl.BlockSpec(memory_space=pltpu.VMEM)
    hbm = pl.BlockSpec(memory_space=pl.ANY)
    shape = jax.ShapeDtypeStruct
    return pl.pallas_call(
        backward_kernel,
        out_shape=[
            shape((32 * UNITS // 8, 8, D), bf16),
            shape((rows, D), f32),
            shape((5, columns, D), f32),
            shape((16, D), f32),
        ],
        in_specs=[hbm, hbm] + [vmem] * len(operands),
        out_specs=[hbm] + [vmem] * 3,
        scratch_shapes=[
            pltpu.VMEM((2, MATS, 8, D), bf16),
            pltpu.VMEM((192, 8, D), bf16),
            pltpu.VMEM((9, 1536, 128), f32),
            pltpu.VMEM((2, MATS, 8, D), bf16),
            pltpu.VMEM((4, rows, D), bf16),
            pltpu.VMEM((rows, D), f32),
            pltpu.VMEM((rows, D), bf16),
            pltpu.VMEM((rows, D), bf16),
            pltpu.VMEM((3, rows, D), bf16),
            pltpu.VMEM((rows, D), f32),
            pltpu.SemaphoreType.DMA((5,)),
        ],
        compiler_params=pltpu.CompilerParams(vmem_limit_bytes=62 * 2**20),
        name="block_backward",
    )(weights, natural, *operands)


def gather_blocks(shard_low, kernels):
    if not kernels:
        whole = lax.all_gather(shard_low, ("outer", "inner"), axis=0, tiled=True)
        return whole.reshape(-1, 8, D)
    return gather_weights(shard_low.reshape(GROUPS8, 8, D)).reshape(-1, 8, D)


def scatter_blocks(grads, units, kernels):
    axes = ("outer", "inner")
    if not kernels:
        whole = grads.reshape(-1, D)[: lax.axis_size(axes) * units].astype(f32)
        return lax.psum_scatter(whole, axes, scatter_dimension=0, tiled=True)
    summed = scatter_grads_kernel(grads.reshape(4, 4, 2, GROUPS8, 8, D))
    return summed.reshape(UNITS, D).astype(f32)


def split_bias(vector):
    widths = [D, D, D, FF, D, 6 * D]
    pieces = []
    offset = 0
    for span_width in widths:
        pieces.append(lax.slice_in_dim(vector, offset, offset + span_width))
        offset = offset + span_width
    return pieces


def exact(left, right, dims):
    return lax.dot_general(
        left, right, dims, precision=lax.Precision.HIGHEST, preferred_element_type=jnp.float32
    )


def ada_selector(soft_cond, first_unit, units):
    groups = soft_cond.shape[0]
    spread = jnp.repeat(soft_cond.astype(jnp.float32), 6, axis=1)
    spread = jnp.pad(spread, ((0, 0), (units, units)))
    start = jnp.clip(first_unit - BLOCK_UNITS + units, 0, 6 * D + units)
    local = lax.dynamic_slice(spread, (jnp.int32(0), start), (groups, units))
    unit = first_unit - BLOCK_UNITS + jnp.arange(units, dtype=jnp.int32)
    part = (unit[:, None] % 6 == jnp.arange(6, dtype=jnp.int32)[None, :]) & (unit[:, None] >= 0)
    part = part.astype(jnp.float32)
    selector = local.T[:, :, None] * part[:, None, :]
    return selector.reshape(units, groups * 6), part


def adamw(parameter, gradient, first_state, second_state):
    first_new = BETA_FIRST * first_state + (1.0 - BETA_FIRST) * gradient
    second_new = BETA_SECOND * second_state + (1.0 - BETA_SECOND) * gradient * gradient
    first_hat = first_new / (1.0 - BETA_FIRST**STEP)
    second_hat = second_new / (1.0 - BETA_SECOND**STEP)
    updated = parameter - LEARN_RATE * (
        first_hat / (jnp.sqrt(second_hat) + ADAM_EPS) + WEIGHT_DECAY * parameter
    )
    return (updated, first_new, second_new)


def on_device(
    tokens,
    conditioning,
    column_sample,
    is_image,
    output_grad,
    weights,
    first_moment,
    second_moment,
    biases,
    bias_first,
    bias_second,
    kernels,
):
    columns = column_sample.shape[0]
    groups = conditioning.shape[0]
    units = weights.shape[0] // D
    axes = ("outer", "inner")
    first_unit = lax.axis_index(axes).astype(jnp.int32) * units
    shard = weights.reshape(units, D)
    shard_low = shard.astype(bf16)
    flat = gather_blocks(shard_low, kernels)
    b_query, b_value, b_proj, b_up, b_down, b_ada = split_bias(biases)
    soft_cond = jax.nn.silu(conditioning).astype(bf16)
    selector, ada_part = ada_selector(soft_cond, first_unit, units)
    mods_all = tn_dot(selector.astype(bf16), shard_low)
    mods_all = lax.psum(mods_all, axes).reshape(groups, 6 * D) + b_ada
    video = jnp.broadcast_to(1.0 - is_image.astype(f32)[:, None], (groups, D))
    table = jnp.concatenate([mods_all, video], axis=1)
    membership = (column_sample[:, None] == jnp.arange(groups, dtype=jnp.int32)[None, :]).astype(
        f32
    )
    mods = jnp.take(table, column_sample, axis=0).reshape(columns, 7, D).transpose(1, 0, 2)
    b_qkv = jnp.stack([b_query, jnp.zeros((D,), f32), b_value])
    (
        block_out, natural, input_att, proj, attended, branch, input_mlp, active, slope, grad_out,
        grad_gate,
    ) = forward(
        flat, tokens, output_grad, mods, b_qkv, b_proj[None], b_up.reshape(4, D), b_down[None]
    )
    grads, input_grad, grad_mods, bias_sums = backward(
        flat, natural, tokens, output_grad, mods, input_att, proj, attended, branch, input_mlp,
        active, slope, grad_out,
    )
    grad_mods = jnp.concatenate([grad_mods, grad_gate[None]])
    mods_local = exact(membership, grad_mods, (((0,), (1,)), ((), ()))).reshape(groups, 6 * D)
    bias_head = jnp.concatenate([bias_sums[:1], bias_sums[2:4], bias_sums[5:9], bias_sums[4:5]])
    bias_head, grad_mods_all = lax.psum((bias_head.reshape(-1), mods_local), axes)
    first_sum = jnp.concatenate([bias_head, jnp.sum(grad_mods_all, axis=0)])
    block_shard = scatter_blocks(grads, units, kernels)
    mods_parts = grad_mods_all.reshape(groups * 6, D)
    ada_shard = exact(selector, mods_parts, (((1,), (0,)), ((), ())))
    unit = first_unit + jnp.arange(units, dtype=jnp.int32)
    grad_units = jnp.where(unit[:, None] >= BLOCK_UNITS, ada_shard, block_shard)
    products = exact(shard_low.astype(jnp.float32), mods_parts, (((1,), (1,)), ((), ())))
    products = jnp.sum(products.reshape(units, groups, 6) * ada_part[:, None, :], axis=2)
    spread = jnp.zeros((groups, 6 * D + 2 * units), jnp.float32)
    start = jnp.clip(first_unit - BLOCK_UNITS + units, 0, 6 * D + units)
    spread = lax.dynamic_update_slice(spread, products.T, (jnp.int32(0), start))
    grad_soft = jnp.sum(spread[:, units : units + 6 * D].reshape(groups, D, 6), axis=2)
    square_sum, grad_soft = lax.psum((jnp.sum(grad_units * grad_units), grad_soft), axes)
    silu_out, silu_back = jax.vjp(jax.nn.silu, conditioning)
    second_sum = silu_back(grad_soft)[0]
    grad_shard = grad_units.reshape(-1)
    grad_norm = jnp.sqrt(square_sum + jnp.sum(first_sum * first_sum))
    factor = jnp.minimum(1.0, CLIP_NORM / (grad_norm + 1e-06))
    new_weights, first_out, second_out = adamw(
        weights, grad_shard * factor, first_moment, second_moment
    )
    new_biases, bias_first_out, bias_second_out = adamw(
        biases, first_sum * factor, bias_first, bias_second
    )
    return (
        block_out,
        input_grad,
        second_sum,
        grad_norm,
        new_weights,
        first_out,
        second_out,
        new_biases,
        bias_first_out,
        bias_second_out,
    )


def solution(mesh):
    in_specs = (
        P(("outer", "inner"), None),
        P(),
        P(("outer", "inner")),
        P(),
        P(("outer", "inner"), None),
        P(("outer", "inner")),
        P(("outer", "inner")),
        P(("outer", "inner")),
        P(),
        P(),
        P(),
    )
    out_specs = (
        P(("outer", "inner"), None),
        P(("outer", "inner"), None),
        P(),
        P(),
        P(("outer", "inner")),
        P(("outer", "inner")),
        P(("outer", "inner")),
        P(),
        P(),
        P(),
    )
    kernels = dict(mesh.shape) == {"outer": 4, "inner": 8}
    return jax.shard_map(
        functools.partial(on_device, kernels=kernels), mesh=mesh, in_specs=in_specs, out_specs=out_specs, check_vma=False
    )
```

```python
import functools
import math

import jax
import jax.numpy as jnp
from jax import lax
from jax.experimental import pallas as pl
from jax.experimental.pallas import tpu as pltpu
from jax.sharding import PartitionSpec as P

D = 1152
H = 16
HD = 72
FF = 4608
FRAMES = 16
STEP = 8


NORM_EPS = 1e-06
LEARN_RATE = 0.02
BETA_FIRST = 0.5
BETA_SECOND = 0.55
ADAM_EPS = 1e-08
WEIGHT_DECAY = 0.01
CLIP_NORM = 1.0
BLOCK_UNITS = 4 * D + 2 * FF


MESH = pl.DeviceIdType.MESH
UNITS = 648
GROUPS8 = 81
QUART = 20
HALFQ = 10
MAIN = 80
TAIL = 1
DEPTH = (4, 4, 3)
BASE = (0, 4, 8)


def flip(z, d):
    if d == 0:
        return z
    if d == 1:
        return z + 1 - 2 * (z % 2)
    if d == 2:
        return z + 2 - 4 * (z // 2)
    return 3 - z


class Place:
    def __init__(self):
        self.o = lax.axis_index("outer")
        self.i = lax.axis_index("inner")
        self.x, self.c = self.o // 2, self.o % 2
        self.z, self.y = self.i // 2, self.i % 2
        self.xo, self.co, self.yo = 1 - self.x, 1 - self.c, 1 - self.y

    def dev(self, dx=0, dc=0, dz=0, dy=0):
        x = self.xo if dx else self.x
        c = self.co if dc else self.c
        y = self.yo if dy else self.y
        return (x * 2 + c, flip(self.z, dz) * 2 + y)

    def greet(self):
        peers = [
            self.dev(dx=1), self.dev(dc=1), self.dev(dx=1, dc=1), self.dev(dy=1),
            self.dev(dz=1), self.dev(dz=2), self.dev(dz=3),
        ]
        barrier = pltpu.get_barrier_semaphore()
        for peer in peers:
            pl.semaphore_signal(barrier, inc=1, device_id=peer, device_id_type=MESH)
        pl.semaphore_wait(barrier, len(peers))


class Copies:
    def __init__(self, send_sems, recv_sems):
        self.send_sems, self.recv_sems = send_sems, recv_sems
        self.count = 0
        self.sent = []

    def slot(self):
        self.count += 1
        return self.count - 1

    def make(self, slot, src, dst, device):
        return pltpu.make_async_remote_copy(
            src_ref=src, dst_ref=dst, send_sem=self.send_sems.at[slot],
            recv_sem=self.recv_sems.at[slot], device_id=device, device_id_type=MESH,
        )

    def send(self, slot, src, dst, device, cond=None):
        def go():
            self.make(slot, src, dst, device).start()
        if cond is None:
            go()
        else:
            pl.when(cond)(go)
        self.sent.append((slot, src, dst, device, cond))

    def wait_recv(self, slot, dst, device, cond=None):
        def go():
            self.make(slot, dst, dst, device).wait_recv()
        if cond is None:
            go()
        else:
            pl.when(cond)(go)

    def drain(self):
        for slot, src, dst, device, cond in self.sent:
            def go(slot=slot, src=src, dst=dst, device=device):
                self.make(slot, src, dst, device).wait_send()
            if cond is None:
                go()
            else:
                pl.when(cond)(go)
        self.sent = []


def ok(zb, p):
    return None if DEPTH[p] == 4 else zb < DEPTH[p]


def both(a, b):
    if a is None:
        return b
    if b is None:
        return a
    return jnp.logical_and(a, b)


GATHER_COPIES = 3 * (3 + 3 + 4 * 4 + 8) + 7


def gather_stages(me, cp, shard, full, local_sems):
    def part(p, zb, yb, x, c, first=0, n=QUART):
        return full.at[p, zb, yb, pl.ds((2 * QUART * x + QUART * c + first), n)]

    def own_of(p):
        return both(me.o == p, ok(me.z, p))

    quarter = (2 * QUART * me.x + QUART * me.c)
    own_tail = pltpu.make_async_copy(
        shard.at[pl.ds(MAIN, TAIL)], full.at[me.o, me.z, me.y, pl.ds(MAIN, TAIL)], local_sems.at[0]
    )
    own_tail.start()

    def local_quarter(p):
        return pltpu.make_async_copy(
            shard.at[pl.ds(quarter, QUART)], part(p, me.z, me.y, me.x, me.c), local_sems.at[1]
        )

    slots = {}

    def s0(p):
        @pl.when(own_of(p))
        def _():
            local_quarter(p).start()
        for dx, dc in ((1, 0), (0, 1), (1, 1)):
            s = slots["s0", p, dx, dc] = cp.slot()
            x = me.xo if dx else me.x
            c = me.co if dc else me.c
            cp.send(
                s, shard.at[pl.ds((2 * QUART * x + QUART * c), QUART)],
                part(p, me.z, me.y, x, c), me.dev(dx=dx, dc=dc), own_of(p),
            )

    def s0_wait(p):
        @pl.when(own_of(p))
        def _():
            local_quarter(p).wait()
        ox, oc = p // 2, p % 2
        for dx, dc in ((1, 0), (0, 1), (1, 1)):
            x = me.xo if dx else me.x
            c = me.co if dc else me.c
            cond = both(jnp.logical_and(x == ox, c == oc), ok(me.z, p))
            cp.wait_recv(
                slots["s0", p, dx, dc], part(p, me.z, me.y, me.x, me.c), me.dev(dx=dx, dc=dc), cond
            )

    def spread(p, d):
        zb = flip(me.z, d)
        mine = part(p, zb, me.y, me.x, me.c)
        s = slots["y1", p, d] = cp.slot()
        cp.send(s, mine, mine, me.dev(dy=1), ok(zb, p))
        s = slots["x1", p, d] = cp.slot()
        cp.send(s, mine, mine, me.dev(dx=1), ok(zb, p))

    def s1(p):
        s0_wait(p)
        mine = part(p, me.z, me.y, me.x, me.c)
        for d in (1, 2, 3):
            s = slots["z", p, d] = cp.slot()
            cp.send(s, mine, mine, me.dev(dz=d), ok(me.z, p))
        spread(p, 0)

    def s2(p):
        for d in (1, 2, 3):
            zb = flip(me.z, d)
            cp.wait_recv(
                slots["z", p, d], part(p, zb, me.y, me.x, me.c), me.dev(dz=d), ok(zb, p)
            )
            spread(p, d)

    def s3(p):
        for d in (0, 1, 2, 3):
            zb = flip(me.z, d)
            cp.wait_recv(
                slots["y1", p, d], part(p, zb, me.yo, me.x, me.c), me.dev(dy=1), ok(zb, p)
            )
            s = slots["x2", p, d] = cp.slot()
            out = part(p, zb, me.yo, me.x, me.c, 0, HALFQ)
            cp.send(s, out, out, me.dev(dx=1), ok(zb, p))
            cp.wait_recv(
                slots["x1", p, d], part(p, zb, me.y, me.xo, me.c), me.dev(dx=1), ok(zb, p)
            )
            s = slots["y2", p, d] = cp.slot()
            out = part(p, zb, me.y, me.xo, me.c, HALFQ, HALFQ)
            cp.send(s, out, out, me.dev(dy=1), ok(zb, p))

    def lane(p, zb, x, c):
        return full.at[p, zb, :, pl.ds((2 * QUART * x + QUART * c), QUART)]

    def s4(p):
        for d in (0, 1, 2, 3):
            zb = flip(me.z, d)
            cp.wait_recv(
                slots["x2", p, d], part(p, zb, me.yo, me.xo, me.c, 0, HALFQ), me.dev(dx=1),
                ok(zb, p),
            )
            cp.wait_recv(
                slots["y2", p, d], part(p, zb, me.yo, me.xo, me.c, HALFQ, HALFQ), me.dev(dy=1),
                ok(zb, p),
            )
            for h in (0, 1):
                s = slots["c", p, d, h] = cp.slot()
                cp.send(s, lane(p, zb, h, me.c), lane(p, zb, h, me.c), me.dev(dc=1), ok(zb, p))

    def s5(p):
        for d in (0, 1, 2, 3):
            zb = flip(me.z, d)
            for h in (0, 1):
                cp.wait_recv(
                    slots["c", p, d, h], lane(p, zb, h, me.co), me.dev(dc=1), ok(zb, p)
                )

    tails = pl.ds(MAIN, TAIL)

    def t1():
        own_tail.wait()
        block = full.at[me.o, me.z, me.y, tails]
        for d in (1, 2, 3):
            s = slots["tz", d] = cp.slot()
            cp.send(s, block, block, me.dev(dz=d))

    def t2():
        for d in (1, 2, 3):
            zb = flip(me.z, d)
            cp.wait_recv(slots["tz", d], full.at[me.o, zb, me.y, tails], me.dev(dz=d))
        s = slots["ty"] = cp.slot()
        block = full.at[me.o, :, me.y, tails]
        cp.send(s, block, block, me.dev(dy=1))

    def t3():
        cp.wait_recv(slots["ty"], full.at[me.o, :, me.yo, tails], me.dev(dy=1))
        s = slots["tx"] = cp.slot()
        block = full.at[me.o, :, :, tails]
        cp.send(s, block, block, me.dev(dx=1))

    def t4():
        cp.wait_recv(slots["tx"], full.at[me.xo * 2 + me.c, :, :, tails], me.dev(dx=1))
        for h in (0, 1):
            s = slots["tc", h] = cp.slot()
            block = full.at[h * 2 + me.c, :, :, tails]
            cp.send(s, block, block, me.dev(dc=1))

    def t5():
        for h in (0, 1):
            cp.wait_recv(slots["tc", h], full.at[h * 2 + me.co, :, :, tails], me.dev(dc=1))

    return dict(s0=s0, s1=s1, s2=s2, s3=s3, s4=s4, s5=s5, t1=t1, t2=t2, t3=t3, t4=t4, t5=t5)


SCATTER_COPIES = 3 * (4 * 2 + 4 * 4 + 3 + 3) + 8
f32 = jnp.float32


def add_rows(dst, srcs, n):
    step = 2 if n % 2 == 0 else 1

    def body(j, carry):
        at = pl.ds(j * step, step)
        total = srcs[0][at].astype(f32)
        for src in srcs[1:]:
            total = total + src[at].astype(f32)
        dst[at] = total.astype(dst.dtype)
        return carry

    lax.fori_loop(0, n // step, body, 0)


def scatter_kernel(
    partial, out, own, other, rx2, ry2, rx1, ry1, rz, final, tail, tail_in, tail_z,
    send_sems, recv_sems, local_sems,
):
    me = Place()
    cp = Copies(send_sems, recv_sems)
    me.greet()
    slots = {}
    order = (3, 2, 1, 0)

    def guarded(cond, fn):
        if cond is None:
            fn()
        else:
            pl.when(cond)(fn)

    def load(p, d, h):
        zb = flip(me.z, d)
        return pltpu.make_async_copy(
            partial.at[p, zb, :, pl.ds((2 * QUART * h + QUART * me.c), QUART)],
            own.at[BASE[p] + zb, :, h], local_sems.at[(p * 4 + d) * 2 + h],
        )

    def s0(p):
        for d in order:
            zb = flip(me.z, d)
            for h in (0, 1):
                guarded(ok(zb, p), lambda d=d, h=h: load(p, d, h).start())
                s = slots["c", p, d, h] = cp.slot()
                cp.send(
                    s, partial.at[p, zb, :, pl.ds((2 * QUART * h + QUART * me.co), QUART)],
                    other.at[BASE[p] + zb, :, h], me.dev(dc=1), ok(zb, p),
                )

    def s1(p):
        for d in order:
            zb = flip(me.z, d)
            b = BASE[p] + zb
            for h in (0, 1):
                guarded(ok(zb, p), lambda d=d, h=h: load(p, d, h).wait())
                cp.wait_recv(slots["c", p, d, h], other.at[b, :, h], me.dev(dc=1), ok(zb, p))

            def fold(b=b):
                def body(q, carry):
                    add_rows(own.at[b, q // 2, q % 2], [own.at[b, q // 2, q % 2], other.at[b, q // 2, q % 2]], QUART)
                    return carry
                lax.fori_loop(0, 4, body, 0)
            guarded(ok(zb, p), fold)
            s = slots["x2", p, d] = cp.slot()
            cp.send(s, own.at[b, me.yo, me.xo, pl.ds(0, HALFQ)], rx2.at[b], me.dev(dx=1), ok(zb, p))
            s = slots["y2", p, d] = cp.slot()
            cp.send(s, own.at[b, me.yo, me.xo, pl.ds(HALFQ, HALFQ)], ry2.at[b], me.dev(dy=1), ok(zb, p))

    def s2(p):
        for d in order:
            zb = flip(me.z, d)
            b = BASE[p] + zb
            cp.wait_recv(slots["x2", p, d], rx2.at[b], me.dev(dx=1), ok(zb, p))
            view = own.at[b, me.yo, me.x, pl.ds(0, HALFQ)]
            guarded(ok(zb, p), lambda view=view, b=b: add_rows(view, [view, rx2.at[b]], HALFQ))
            s = slots["y1", p, d] = cp.slot()
            cp.send(s, own.at[b, me.yo, me.x], ry1.at[b], me.dev(dy=1), ok(zb, p))
            cp.wait_recv(slots["y2", p, d], ry2.at[b], me.dev(dy=1), ok(zb, p))
            view = own.at[b, me.y, me.xo, pl.ds(HALFQ, HALFQ)]
            guarded(ok(zb, p), lambda view=view, b=b: add_rows(view, [view, ry2.at[b]], HALFQ))
            s = slots["x1", p, d] = cp.slot()
            cp.send(s, own.at[b, me.y, me.xo], rx1.at[b], me.dev(dx=1), ok(zb, p))

    def s3(p):
        for d in order:
            zb = flip(me.z, d)
            b = BASE[p] + zb
            cp.wait_recv(slots["y1", p, d], ry1.at[b], me.dev(dy=1), ok(zb, p))
            cp.wait_recv(slots["x1", p, d], rx1.at[b], me.dev(dx=1), ok(zb, p))
            view = own.at[b, me.y, me.x]
            guarded(
                ok(zb, p),
                lambda view=view, b=b: add_rows(view, [view, ry1.at[b], rx1.at[b]], QUART),
            )
            if d:
                s = slots["z", p, d] = cp.slot()
                cp.send(s, view, rz.at[p, d - 1], me.dev(dz=d), ok(zb, p))

    def s4(p):
        mine = ok(me.z, p)
        for d in (1, 2, 3):
            cp.wait_recv(slots["z", p, d], rz.at[p, d - 1], me.dev(dz=d), mine)
        view = own.at[BASE[p] + me.z, me.y, me.x]
        guarded(
            mine,
            lambda: add_rows(final.at[p], [view, rz.at[p, 0], rz.at[p, 1], rz.at[p, 2]], QUART),
        )
        ox, oc = p // 2, p % 2
        quarter = out.at[pl.ds((2 * QUART * me.x + QUART * me.c), QUART)]
        for dx, dc in ((1, 0), (0, 1), (1, 1)):
            x = me.xo if dx else me.x
            c = me.co if dc else me.c
            s = slots["f", p, dx, dc] = cp.slot()
            cond = both(jnp.logical_and(x == ox, c == oc), mine)
            cp.send(s, final.at[p], quarter, me.dev(dx=dx, dc=dc), cond)

        @pl.when(both(me.o == p, mine))
        def _():
            pltpu.make_async_copy(final.at[p], quarter, local_sems.at[24]).start()

    def s5(p):
        mine = both(me.o == p, ok(me.z, p))
        for dx, dc in ((1, 0), (0, 1), (1, 1)):
            x = me.xo if dx else me.x
            c = me.co if dc else me.c
            cp.wait_recv(
                slots["f", p, dx, dc], out.at[pl.ds((2 * QUART * x + QUART * c), QUART)],
                me.dev(dx=dx, dc=dc), mine,
            )

        @pl.when(mine)
        def _():
            quarter = out.at[pl.ds((2 * QUART * me.x + QUART * me.c), QUART)]
            pltpu.make_async_copy(final.at[p], quarter, local_sems.at[24]).wait()

    tail_load = pltpu.make_async_copy(
        partial.at[:, :, :, pl.ds(MAIN, TAIL)], tail, local_sems.at[25]
    )
    tail_load.start()

    def tail_add(o, zb, yb, srcs):
        add_rows(tail.at[o, zb, yb], [tail.at[o, zb, yb]] + srcs, TAIL)

    def t1():
        tail_load.wait()
        for h in (0, 1):
            s = slots["tc", h] = cp.slot()
            cp.send(s, tail.at[2 * h + me.co], tail_in.at[h], me.dev(dc=1))

    def t2():
        for h in (0, 1):
            cp.wait_recv(slots["tc", h], tail_in.at[h], me.dev(dc=1))

            def body(q, carry, h=h):
                tail_add(2 * h + me.c, q // 2, q % 2, [tail_in.at[h, q // 2, q % 2]])
                return carry
            lax.fori_loop(0, 8, body, 0)
        s = slots["tx"] = cp.slot()
        cp.send(s, tail.at[me.xo * 2 + me.c], tail_in.at[2], me.dev(dx=1))

    def t3():
        cp.wait_recv(slots["tx"], tail_in.at[2], me.dev(dx=1))

        def body(q, carry):
            tail_add(me.o, q // 2, q % 2, [tail_in.at[2, q // 2, q % 2]])
            return carry
        lax.fori_loop(0, 8, body, 0)
        s = slots["ty"] = cp.slot()
        cp.send(s, tail.at[me.o, :, me.yo], tail_in.at[3, :, 0], me.dev(dy=1))

    def t4():
        cp.wait_recv(slots["ty"], tail_in.at[3, :, 0], me.dev(dy=1))

        def body(q, carry):
            tail_add(me.o, q, me.y, [tail_in.at[3, q, 0]])
            return carry
        lax.fori_loop(0, 4, body, 0)
        for d in (1, 2, 3):
            s = slots["tz", d] = cp.slot()
            cp.send(s, tail.at[me.o, flip(me.z, d), me.y], tail_z.at[d - 1], me.dev(dz=d))

    def t5():
        for d in (1, 2, 3):
            cp.wait_recv(slots["tz", d], tail_z.at[d - 1], me.dev(dz=d))
        tail_add(me.o, me.z, me.y, [tail_z.at[0], tail_z.at[1], tail_z.at[2]])
        copy = pltpu.make_async_copy(
            tail.at[me.o, me.z, me.y], out.at[pl.ds(MAIN, TAIL)], local_sems.at[25]
        )
        copy.start()
        copy.wait()

    s0(2); s0(1); s0(0); s1(2); t1(); s1(1); s2(2); t2(); s1(0); s3(2); s2(1); t3(); s4(2)
    s2(0); s3(1); t4(); s4(1); s3(0); t5(); s4(0); s5(2); s5(1); s5(0)
    cp.drain()


def scatter_grads_kernel(partial):
    bf = jnp.bfloat16
    return pl.pallas_call(
        scatter_kernel,
        out_shape=jax.ShapeDtypeStruct((GROUPS8, 8, D), bf),
        in_specs=[pl.BlockSpec(memory_space=pl.ANY)],
        out_specs=pl.BlockSpec(memory_space=pl.ANY),
        scratch_shapes=[
            pltpu.VMEM((11, 2, 2, QUART, 8, D), bf),
            pltpu.VMEM((11, 2, 2, QUART, 8, D), bf),
            pltpu.VMEM((11, HALFQ, 8, D), bf),
            pltpu.VMEM((11, HALFQ, 8, D), bf),
            pltpu.VMEM((11, QUART, 8, D), bf),
            pltpu.VMEM((11, QUART, 8, D), bf),
            pltpu.VMEM((3, 3, QUART, 8, D), bf),
            pltpu.VMEM((3, QUART, 8, D), bf),
            pltpu.VMEM((4, 4, 2, TAIL, 8, D), bf),
            pltpu.VMEM((4, 4, 2, TAIL, 8, D), bf),
            pltpu.VMEM((3, TAIL, 8, D), bf),
            pltpu.SemaphoreType.DMA((SCATTER_COPIES,)),
            pltpu.SemaphoreType.DMA((SCATTER_COPIES,)),
            pltpu.SemaphoreType.DMA((26,)),
        ],
        compiler_params=pltpu.CompilerParams(
            collective_id=1, has_side_effects=True, vmem_limit_bytes=60 * 2**20
        ),
        name="scatter_grads",
    )(partial)


bf16 = jnp.bfloat16
MATS = D // 8
AT_PROJ = 3 * MATS
AT_UP = 4 * MATS
AT_DOWN = 8 * MATS
ROOT = math.sqrt(2.0 / math.pi)
CUBIC = 0.044715


def nn_dot(left, right):
    return lax.dot_general(left, right, (((1,), (0,)), ((), ())), preferred_element_type=f32)


def nt_dot(left, right):
    return lax.dot_general(left, right, (((1,), (1,)), ((), ())), preferred_element_type=f32)


def tn_dot(left, right):
    return lax.dot_general(left, right, (((0,), (0,)), ((), ())), preferred_element_type=f32)


def square(ref):
    return ref[...].reshape(D, D)


def norm_rows(values):
    centered = values - jnp.mean(values, axis=-1, keepdims=True)
    inverse = lax.rsqrt(jnp.mean(centered * centered, axis=-1, keepdims=True) + NORM_EPS)
    return centered * inverse, inverse


def norm_rows_back(grad, normed, inverse):
    return inverse * (
        grad
        - jnp.mean(grad, axis=-1, keepdims=True)
        - normed * jnp.mean(grad * normed, axis=-1, keepdims=True)
    )


def frames_of(c):
    return pl.ds(pl.multiple_of(c * FRAMES, FRAMES), FRAMES)


def over_columns(count, body):
    def step(c, carry):
        body(c, frames_of(c), pl.ds(c, 1))
        return carry

    lax.fori_loop(0, count, step, 0)


def split_rows(src, spread, put, ways):
    units = src.shape[0] * 8
    rows = units // ways
    for q in range(9):
        lanes = slice(128 * q, 128 * q + 128)
        spread[q, pl.ds(0, units)] = src[:, :, lanes].astype(f32).reshape(units, 128)
        for w in range(ways):
            part = spread[q, pl.ds(w, rows, stride=ways), :]
            put(w, lanes, part.reshape(rows // 8, 8, 128).astype(bf16))


def head_window(h):
    first = min(HD * h // 128, 7) * 128
    lane = lax.broadcasted_iota(jnp.int32, (1, 256), 1) + first
    mask = jnp.logical_and(lane >= HD * h, lane < HD * h + HD)
    return slice(first, first + 256), jnp.where(mask, 1.0, 0.0).astype(bf16)


def same_column():
    row = lax.broadcasted_iota(jnp.int32, (128, 128), 0)
    col = lax.broadcasted_iota(jnp.int32, (128, 128), 1)
    return lax.shift_right_logical(row, 4) == lax.shift_right_logical(col, 4)


SCORE_SCALE = 1.0 / math.sqrt(HD)


def head_probabilities(masked_queries, keys, inside):
    scores = jnp.where(inside, nt_dot(masked_queries, keys) * SCORE_SCALE, -1e30)
    grown = jnp.exp(scores - jnp.max(scores, axis=-1, keepdims=True))
    return grown / jnp.sum(grown, axis=-1, keepdims=True)


SUM_COPIES = 6
SUM_SLOTS = 10


def sum_stages(me, cp, mine, buf):
    slots = {}

    def send(name, src, dst, device):
        slots[name] = cp.slot()
        cp.send(slots[name], src, dst, device)

    def m1():
        send("c", mine, buf.at[0], me.dev(dc=1))

    def m2():
        cp.wait_recv(slots["c"], buf.at[0], me.dev(dc=1))
        buf[1] = mine[...] + buf[0]
        send("x", buf.at[1], buf.at[2], me.dev(dx=1))

    def m3():
        cp.wait_recv(slots["x"], buf.at[2], me.dev(dx=1))
        buf[3] = buf[1] + buf[2]
        send("y", buf.at[3], buf.at[4], me.dev(dy=1))

    def m4():
        cp.wait_recv(slots["y"], buf.at[4], me.dev(dy=1))
        buf[5] = buf[3] + buf[4]
        buf[6 + me.z] = buf[5]
        for d in (1, 2, 3):
            send(d, buf.at[5], buf.at[6 + me.z], me.dev(dz=d))

    def total():
        for d in (1, 2, 3):
            cp.wait_recv(slots[d], buf.at[6 + flip(me.z, d)], me.dev(dz=d))
        return (buf[6] + buf[7]) + (buf[8] + buf[9])

    return m1, m2, m3, m4, total


def forward_body(
    weights, tokens, upstream, mods, b_qkv, b_proj, b_up, b_down,
    block_out, natural, input_att, proj_out, attended, branch, input_mlp, active_out, slope_out,
    grad_out, grad_gate, held, stage, spread, acc, hid, proj, active, slope, copy_sems, ready,
):
    columns = mods.shape[1]

    def fetch(first, groups, slot):
        return pltpu.make_async_copy(
            weights.at[pl.ds(first, groups)], stage.at[slot, pl.ds(0, groups)], copy_sems.at[slot]
        )

    def whole(mat, slot):
        return pltpu.make_async_copy(
            weights.at[pl.ds(mat * MATS, MATS)], held.at[slot], copy_sems.at[2 + slot]
        )

    def save(mat, slot):
        return pltpu.make_async_copy(held.at[slot], natural.at[mat], copy_sems.at[10 + mat])

    def keep(src, dst, n):
        return pltpu.make_async_copy(src, dst, copy_sems.at[17 + n])

    def unweave(first, ways, slot0, blocks=9):
        groups = 16 * ways
        fetch(first, groups, 0).start()

        def step(j, carry):
            slot = lax.rem(j, 2)
            fetch(first + j * groups, groups, slot).wait()

            @pl.when(j + 1 < blocks)
            def _():
                fetch(first + (j + 1) * groups, groups, 1 - slot).start()

            def put(w, lanes, block):
                held[slot0 + w, pl.ds(j * 16, 16), :, lanes] = block

            split_rows(stage.at[slot, pl.ds(0, groups)], spread, put, ways)
            return carry

        lax.fori_loop(0, blocks, step, 0)

    def first_norm(c, rows, at):
        normed, _ = norm_rows(tokens[rows].astype(f32))
        input_att[rows] = (normed * (1.0 + mods[1, at]) + mods[0, at]).astype(bf16)

    over_columns(columns, first_norm)
    ready("qkv")
    whole(3, 3).start()
    unweave(0, 3, 0)
    for p in range(3):
        save(p, p).start()

    def project(p, carry):
        proj[p] = (nn_dot(input_att[...], square(held.at[p])) + b_qkv[pl.ds(p, 1)]).astype(bf16)
        return carry

    lax.fori_loop(0, 3, project, 0)
    keep(proj, proj_out, 0).start()

    inside = same_column()

    def attend(g, carry):
        rows = pl.ds(pl.multiple_of(g * 128, 128), 128)
        acc[pl.ds(0, 128)] = jnp.zeros((128, D), f32)
        for h in range(H):
            window, mask = head_window(h)
            probs = head_probabilities(proj[0, rows, window] * mask, proj[1, rows, window], inside)
            acc[pl.ds(0, 128), window] += nn_dot(probs.astype(bf16), proj[2, rows, window] * mask)
        attended[rows] = acc[pl.ds(0, 128)].astype(bf16)
        return carry

    lax.fori_loop(0, columns * FRAMES // 128, attend, 0)
    ready("proj")
    whole(3, 3).wait()
    branch[...] = nn_dot(attended[...], square(held.at[3])) + b_proj[...]
    for p in range(3):
        save(p, p).wait()

    def second_norm(c, rows, at):
        middle = tokens[rows].astype(f32) + mods[2, at] * branch[rows]
        normed, _ = norm_rows(middle)
        input_mlp[rows] = (normed * (1.0 + mods[4, at]) + mods[3, at]).astype(bf16)

    over_columns(columns, second_norm)
    ready("up")
    unweave(AT_UP, 4, 4)
    for b in range(4):
        save(3 + b, 4 + b).start()

    def raise_(b, carry):
        hid[...] = nn_dot(input_mlp[...], square(held.at[4 + b])) + b_up[pl.ds(b, 1)]

        def gelu(c, rows, at):
            v = hid[rows]
            sq = v * v
            t = jnp.tanh(ROOT * (v + CUBIC * sq * v))
            half = 0.5 * (1.0 + t)
            active[b, rows] = (v * half).astype(bf16)
            slope[b, rows] = half + (0.5 * ROOT) * v * (1.0 - t * t) * (1.0 + 3.0 * CUBIC * sq)

        over_columns(columns, gelu)
        return carry

    lax.fori_loop(0, 4, raise_, 0)
    keep(active, active_out, 1).start()
    keep(slope, slope_out, 2).start()
    acc[...] = jnp.broadcast_to(b_down[...], acc.shape)
    ready("down")
    for b in range(4):
        whole(8 + b, b).start()
    for b in range(4):
        whole(8 + b, b).wait()
        acc[...] += nn_dot(active[b], square(held.at[b]))

    def last(c, rows, at):
        x = tokens[rows].astype(f32)
        middle = x + mods[2, at] * branch[rows]
        video = mods[6, at] > 0.5
        outcome = acc[rows]
        block_out[rows] = jnp.where(video, middle + mods[5, at] * outcome, x)
        grad_block = jnp.where(video, upstream[rows].astype(f32), 0.0)
        grad_gate[at] = jnp.sum(grad_block * outcome, axis=0, keepdims=True)
        grad_out[rows] = (grad_block * mods[5, at]).astype(bf16)

    over_columns(columns, last)
    for b in range(4):
        save(3 + b, 4 + b).wait()
    keep(proj, proj_out, 0).wait()
    keep(active, active_out, 1).wait()
    keep(slope, slope_out, 2).wait()


def forward_kernel(*refs):
    forward_body(*refs, lambda name: None)


def gather_forward_kernel(
    shard, partial, chosen, base, tokens, upstream, b_qkv, b_proj, b_up, b_down,
    full, mods, *refs,
):
    refs, (sums, send_sems, recv_sems, local_sems) = refs[:-4], refs[-4:]
    me = Place()
    cp = Copies(send_sems, recv_sems)
    st = gather_stages(me, cp, shard, full, local_sems)
    s0, s1, s2, s3, s4, s5 = (st["s%d" % n] for n in range(6))
    t1, t2, t3, t4, t5 = (st["t%d" % n] for n in range(1, 6))
    m1, m2, m3, m4, total = sum_stages(me, cp, partial, sums)
    me.greet()
    m1()
    s0(0)
    m2()
    s0(1)
    s1(0)
    m3()
    s0(2)
    t1()
    s2(0)
    m4()
    t2()
    s1(1)
    s3(0)
    t3()
    s2(1)
    t4()
    s1(2)
    table = exact(chosen[...], total(), (((1,), (0,)), ((), ()))) + base[...]
    columns = mods.shape[1]
    for n in range(7):
        mods[n] = table[n * columns : (n + 1) * columns]

    def ready(name):
        if name == "qkv":
            s4(0)
            s3(1)
            t5()
            s2(2)
            s5(0)
        if name == "proj":
            s4(1)
        if name == "up":
            s3(2)
            s5(1)
        if name == "down":
            s4(2)
            s5(2)

    forward_body(
        full.reshape(4 * 4 * 2 * GROUPS8, 8, D), tokens, upstream, mods, b_qkv, b_proj, b_up,
        b_down, *refs, ready,
    )
    cp.drain()


def forward_shapes(rows, columns):
    shape = jax.ShapeDtypeStruct
    return [
        shape((rows, D), f32),
        shape((7, MATS, 8, D), bf16),
        shape((rows, D), bf16),
        shape((3, rows, D), bf16),
        shape((rows, D), bf16),
        shape((rows, D), f32),
        shape((rows, D), bf16),
        shape((4, rows, D), bf16),
        shape((4, rows, D), f32),
        shape((rows, D), bf16),
        shape((columns, D), f32),
    ]


VMEM_SPEC = pl.BlockSpec(memory_space=pltpu.VMEM)
HBM_SPEC = pl.BlockSpec(memory_space=pl.ANY)
FORWARD_SPECS = [
    VMEM_SPEC, HBM_SPEC, VMEM_SPEC, HBM_SPEC, VMEM_SPEC, VMEM_SPEC, VMEM_SPEC, HBM_SPEC, HBM_SPEC,
    VMEM_SPEC, VMEM_SPEC,
]


def forward_scratch(rows):
    return [
        pltpu.VMEM((8, MATS, 8, D), bf16),
        pltpu.VMEM((2, 64, 8, D), bf16),
        pltpu.VMEM((9, 512, 128), f32),
        pltpu.VMEM((rows, D), f32),
        pltpu.VMEM((rows, D), f32),
        pltpu.VMEM((3, rows, D), bf16),
        pltpu.VMEM((4, rows, D), bf16),
        pltpu.VMEM((4, rows, D), f32),
        pltpu.SemaphoreType.DMA((20,)),
    ]


def forward(weights, tokens, upstream, mods, b_qkv, b_proj, b_up, b_down):
    rows = tokens.shape[0]
    return pl.pallas_call(
        forward_kernel,
        out_shape=forward_shapes(rows, mods.shape[1]),
        in_specs=[HBM_SPEC] + [VMEM_SPEC] * 7,
        out_specs=FORWARD_SPECS,
        scratch_shapes=forward_scratch(rows),
        compiler_params=pltpu.CompilerParams(vmem_limit_bytes=60 * 2**20),
        name="block_forward",
    )(weights, tokens, upstream, mods, b_qkv, b_proj, b_up, b_down)


def gather_forward(shard, partial, chosen, base, tokens, upstream, b_qkv, b_proj, b_up, b_down):
    rows = tokens.shape[0]
    columns = rows // FRAMES
    copies = GATHER_COPIES + SUM_COPIES
    return pl.pallas_call(
        gather_forward_kernel,
        out_shape=[
            jax.ShapeDtypeStruct((4, 4, 2, GROUPS8, 8, D), bf16),
            jax.ShapeDtypeStruct((7, columns, D), f32),
        ]
        + forward_shapes(rows, columns),
        in_specs=[HBM_SPEC] + [VMEM_SPEC] * 9,
        out_specs=[HBM_SPEC, VMEM_SPEC] + FORWARD_SPECS,
        scratch_shapes=forward_scratch(rows)
        + [
            pltpu.VMEM((SUM_SLOTS, *partial.shape), f32),
            pltpu.SemaphoreType.DMA((copies,)),
            pltpu.SemaphoreType.DMA((copies,)),
            pltpu.SemaphoreType.DMA((2,)),
        ],
        compiler_params=pltpu.CompilerParams(
            collective_id=0, has_side_effects=True, vmem_limit_bytes=62 * 2**20
        ),
        name="gather_forward",
    )(shard, partial, chosen, base, tokens, upstream, b_qkv, b_proj, b_up, b_down)


def backward_kernel(
    weights, natural, tokens, upstream, mods, input_att, proj, attended, branch, input_mlp, active,
    slope, grad_out,
    grads, input_grad, grad_mods, bias_sums,
    held, woven, spread, flat, grad_hidden, middle_grad, grad_branch, grad_att, grad_proj, acc,
    copy_sems,
):
    columns = mods.shape[1]

    def fetch(source, first, slot):
        return pltpu.make_async_copy(source.at[first], held.at[slot], copy_sems.at[slot])

    def flat_mat(first, slot):
        return pltpu.make_async_copy(
            weights.at[pl.ds(first, MATS)], held.at[slot], copy_sems.at[slot]
        )

    def store_flat(first, slot):
        return pltpu.make_async_copy(
            flat.at[slot], grads.at[pl.ds(first, MATS)], copy_sems.at[2 + slot]
        )

    bias_sums[...] = jnp.zeros_like(bias_sums)

    def add_bias(row, values):
        bias_sums[pl.ds(row, 1)] += jnp.sum(values.astype(f32), axis=0, keepdims=True)

    flat_mat(AT_DOWN, 0).start()

    def down(b, carry):
        slot = lax.rem(b, 2)
        flat_mat(AT_DOWN + b * MATS, slot).wait()

        @pl.when(b < 3)
        def _():
            flat_mat(AT_DOWN + (b + 1) * MATS, 1 - slot).start()

        acc[...] = nt_dot(grad_out[...], square(held.at[slot]))

        def through(c, rows, at):
            grad = (acc[rows] * slope[b, rows]).astype(bf16)
            grad_hidden[b, rows] = grad
            add_bias(5 + b, grad)

        over_columns(columns, through)

        @pl.when(b >= 2)
        def _():
            store_flat(AT_DOWN + (b - 2) * MATS, slot).wait()

        flat[slot] = tn_dot(active[b], grad_out[...]).reshape(MATS, 8, D).astype(bf16)
        store_flat(AT_DOWN + b * MATS, slot).start()
        return carry

    lax.fori_loop(0, 4, down, 0)
    fetch(natural, 3, 0).start()

    def down_bias(c, rows, at):
        add_bias(4, grad_out[rows])

    over_columns(columns, down_bias)

    def weave(first, ways, left, right_of):
        groups = 48 * ways

        def store(k):
            return pltpu.make_async_copy(
                woven.at[pl.ds(0, groups)], grads.at[pl.ds(first + k * groups, groups)],
                copy_sems.at[4],
            )

        for k in range(3):
            for w in range(ways):
                part = tn_dot(left[:, 384 * k : 384 * k + 384], right_of(w))
                for q in range(9):
                    spread[q, pl.ds(w, 384, stride=ways), :] = part[:, 128 * q : 128 * q + 128]
            if k:
                store(k - 1).wait()

            def pack(j, carry):
                for q in range(9):
                    block = spread[q, pl.ds(pl.multiple_of(j * 128, 128), 128), :]
                    woven[pl.ds(j * 16, 16), :, 128 * q : 128 * q + 128] = block.reshape(
                        16, 8, 128
                    ).astype(bf16)
                return carry

            lax.fori_loop(0, groups // 16, pack, 0)
            store(k).start()
        return lambda: store(2).wait()

    up_done = weave(AT_UP, 4, input_mlp, lambda w: grad_hidden[w])
    acc[...] = jnp.zeros_like(acc)

    def up(b, carry):
        slot = lax.rem(b, 2)
        fetch(natural, 3 + b, slot).wait()

        @pl.when(b < 3)
        def _():
            fetch(natural, 4 + b, 1 - slot).start()

        acc[...] += nt_dot(grad_hidden[b], square(held.at[slot]))
        return carry

    lax.fori_loop(0, 4, up, 0)
    flat_mat(AT_PROJ, 0).start()

    def second_norm_back(c, rows, at):
        br = branch[rows]
        gate = mods[2, at]
        normed, inverse = norm_rows(tokens[rows].astype(f32) + gate * br)
        grad = acc[rows]
        grad_mods[3, at] = jnp.sum(grad, axis=0, keepdims=True)
        grad_mods[4, at] = jnp.sum(grad * normed, axis=0, keepdims=True)
        grad_block = jnp.where(mods[6, at] > 0.5, upstream[rows].astype(f32), 0.0)
        grad_middle = grad_block + norm_rows_back(grad * (1.0 + mods[4, at]), normed, inverse)
        middle_grad[rows] = grad_middle
        grad_mods[2, at] = jnp.sum(grad_middle * br, axis=0, keepdims=True)
        grad = (grad_middle * gate).astype(bf16)
        grad_branch[rows] = grad
        add_bias(3, grad)

    over_columns(columns, second_norm_back)
    store_flat(AT_DOWN + 2 * MATS, 0).wait()
    store_flat(AT_DOWN + 3 * MATS, 1).wait()
    flat[0] = tn_dot(attended[...], grad_branch[...]).reshape(MATS, 8, D).astype(bf16)
    store_flat(AT_PROJ, 0).start()
    flat_mat(AT_PROJ, 0).wait()
    grad_att[...] = nt_dot(grad_branch[...], square(held.at[0])).astype(bf16)
    fetch(natural, 0, 0).start()
    inside = same_column()
    top = pl.ds(0, 128)

    def attend_back(g, carry):
        rows = pl.ds(pl.multiple_of(g * 128, 128), 128)
        for p in range(3):
            acc[pl.ds(p * 128, 128)] = jnp.zeros((128, D), f32)
        for h in range(H):
            window, mask = head_window(h)
            queries = proj[0, rows, window] * mask
            keys = proj[1, rows, window]
            grad = grad_att[rows, window] * mask
            probs = head_probabilities(queries, keys, inside)
            grad_probs = nt_dot(grad, proj[2, rows, window])
            mean = jnp.sum(grad_probs * probs, axis=-1, keepdims=True)
            grad_scores = (probs * (grad_probs - mean)).astype(bf16)
            acc[pl.ds(0, 128), window] += nn_dot(grad_scores, keys * mask)
            acc[pl.ds(128, 128), window] += tn_dot(grad_scores, queries)
            acc[pl.ds(256, 128), window] += tn_dot(probs.astype(bf16), grad)
        for p in range(3):
            scale = SCORE_SCALE if p < 2 else 1.0
            grad = (acc[pl.ds(p * 128, 128)] * scale).astype(bf16)
            grad_proj[p, rows] = grad
            add_bias(p, grad)
        return carry

    lax.fori_loop(0, columns * FRAMES // 128, attend_back, 0)
    up_done()
    qkv_done = weave(0, 3, input_att, lambda w: grad_proj[w])
    acc[...] = jnp.zeros_like(acc)

    def qkv(p, carry):
        slot = lax.rem(p, 2)
        fetch(natural, p, slot).wait()

        @pl.when(p < 2)
        def _():
            fetch(natural, p + 1, 1 - slot).start()

        acc[...] += nt_dot(grad_proj[p], square(held.at[slot]))
        return carry

    lax.fori_loop(0, 3, qkv, 0)

    def first_norm_back(c, rows, at):
        normed, inverse = norm_rows(tokens[rows].astype(f32))
        grad = acc[rows]
        grad_mods[0, at] = jnp.sum(grad, axis=0, keepdims=True)
        grad_mods[1, at] = jnp.sum(grad * normed, axis=0, keepdims=True)
        grad_states = middle_grad[rows] + norm_rows_back(
            grad * (1.0 + mods[1, at]), normed, inverse
        )
        up_rows = upstream[rows].astype(f32)
        input_grad[rows] = jnp.where(mods[6, at] > 0.5, grad_states, up_rows)

    over_columns(columns, first_norm_back)
    store_flat(AT_PROJ, 0).wait()
    qkv_done()


def backward(weights, natural, *operands):
    tokens, mods = operands[0], operands[2]
    rows = tokens.shape[0]
    columns = mods.shape[1]
    vmem = pl.BlockSpec(memory_space=pltpu.VMEM)
    hbm = pl.BlockSpec(memory_space=pl.ANY)
    shape = jax.ShapeDtypeStruct
    return pl.pallas_call(
        backward_kernel,
        out_shape=[
            shape((32 * UNITS // 8, 8, D), bf16),
            shape((rows, D), f32),
            shape((5, columns, D), f32),
            shape((16, D), f32),
        ],
        in_specs=[hbm, hbm] + [vmem] * len(operands),
        out_specs=[hbm] + [vmem] * 3,
        scratch_shapes=[
            pltpu.VMEM((2, MATS, 8, D), bf16),
            pltpu.VMEM((192, 8, D), bf16),
            pltpu.VMEM((9, 1536, 128), f32),
            pltpu.VMEM((2, MATS, 8, D), bf16),
            pltpu.VMEM((4, rows, D), bf16),
            pltpu.VMEM((rows, D), f32),
            pltpu.VMEM((rows, D), bf16),
            pltpu.VMEM((rows, D), bf16),
            pltpu.VMEM((3, rows, D), bf16),
            pltpu.VMEM((rows, D), f32),
            pltpu.SemaphoreType.DMA((5,)),
        ],
        compiler_params=pltpu.CompilerParams(vmem_limit_bytes=62 * 2**20),
        name="block_backward",
    )(weights, natural, *operands)


def gather_blocks(shard_low):
    whole = lax.all_gather(shard_low, ("outer", "inner"), axis=0, tiled=True)
    return whole.reshape(-1, 8, D)


def scatter_blocks(grads, units, kernels):
    axes = ("outer", "inner")
    if not kernels:
        whole = grads.reshape(-1, D)[: lax.axis_size(axes) * units].astype(f32)
        return lax.psum_scatter(whole, axes, scatter_dimension=0, tiled=True)
    summed = scatter_grads_kernel(grads.reshape(4, 4, 2, GROUPS8, 8, D))
    return summed.reshape(UNITS, D).astype(f32)


def split_bias(vector):
    widths = [D, D, D, FF, D, 6 * D]
    pieces = []
    offset = 0
    for span_width in widths:
        pieces.append(lax.slice_in_dim(vector, offset, offset + span_width))
        offset = offset + span_width
    return pieces


def exact(left, right, dims):
    return lax.dot_general(
        left, right, dims, precision=lax.Precision.HIGHEST, preferred_element_type=jnp.float32
    )


def ada_selector(soft_cond, first_unit, units):
    groups = soft_cond.shape[0]
    spread = jnp.repeat(soft_cond.astype(jnp.float32), 6, axis=1)
    spread = jnp.pad(spread, ((0, 0), (units, units)))
    start = jnp.clip(first_unit - BLOCK_UNITS + units, 0, 6 * D + units)
    local = lax.dynamic_slice(spread, (jnp.int32(0), start), (groups, units))
    unit = first_unit - BLOCK_UNITS + jnp.arange(units, dtype=jnp.int32)
    part = (unit[:, None] % 6 == jnp.arange(6, dtype=jnp.int32)[None, :]) & (unit[:, None] >= 0)
    part = part.astype(jnp.float32)
    selector = local.T[:, :, None] * part[:, None, :]
    return selector.reshape(units, groups * 6), part


def adamw(parameter, gradient, first_state, second_state):
    first_new = BETA_FIRST * first_state + (1.0 - BETA_FIRST) * gradient
    second_new = BETA_SECOND * second_state + (1.0 - BETA_SECOND) * gradient * gradient
    first_hat = first_new / (1.0 - BETA_FIRST**STEP)
    second_hat = second_new / (1.0 - BETA_SECOND**STEP)
    updated = parameter - LEARN_RATE * (
        first_hat / (jnp.sqrt(second_hat) + ADAM_EPS) + WEIGHT_DECAY * parameter
    )
    return (updated, first_new, second_new)


def on_device(
    tokens,
    conditioning,
    column_sample,
    is_image,
    output_grad,
    weights,
    first_moment,
    second_moment,
    biases,
    bias_first,
    bias_second,
    kernels,
):
    columns = column_sample.shape[0]
    groups = conditioning.shape[0]
    units = weights.shape[0] // D
    axes = ("outer", "inner")
    first_unit = lax.axis_index(axes).astype(jnp.int32) * units
    shard = weights.reshape(units, D)
    shard_low = shard.astype(bf16)
    b_query, b_value, b_proj, b_up, b_down, b_ada = split_bias(biases)
    soft_cond = jax.nn.silu(conditioning).astype(bf16)
    selector, ada_part = ada_selector(soft_cond, first_unit, units)
    mods_part = tn_dot(selector.astype(bf16), shard_low)
    membership = (column_sample[:, None] == jnp.arange(groups, dtype=jnp.int32)[None, :]).astype(
        f32
    )
    video_cols = exact(membership, 1.0 - is_image.astype(f32)[:, None], (((1,), (0,)), ((), ())))
    b_qkv = jnp.stack([b_query, jnp.zeros((D,), f32), b_value])
    bias_args = (b_qkv, b_proj[None], b_up.reshape(4, D), b_down[None])
    video_plane = jnp.broadcast_to(video_cols, (columns, D))
    if kernels:
        eye = jnp.eye(6, dtype=f32)
        chosen = membership[None, :, :, None] * eye[:, None, None, :]
        chosen = jnp.pad(chosen.reshape(6 * columns, groups * 6), ((0, columns), (0, 0)))
        base = jnp.repeat(b_ada.reshape(6, D), columns, axis=0)
        base = jnp.concatenate([base, video_plane])
        flat, mods, *saved = gather_forward(
            shard_low.reshape(GROUPS8, 8, D), mods_part, chosen, base, tokens, output_grad,
            *bias_args,
        )
        flat = flat.reshape(-1, 8, D)
    else:
        flat = gather_blocks(shard_low)
        mods_all = lax.psum(mods_part, axes).reshape(groups, 6 * D) + b_ada
        mods = jnp.take(mods_all, column_sample, axis=0).reshape(columns, 6, D).transpose(1, 0, 2)
        mods = jnp.concatenate([mods, video_plane[None]])
        saved = forward(flat, tokens, output_grad, mods, *bias_args)
    (
        block_out, natural, input_att, proj, attended, branch, input_mlp, active, slope, grad_out,
        grad_gate,
    ) = saved
    grads, input_grad, grad_mods, bias_sums = backward(
        flat, natural, tokens, output_grad, mods, input_att, proj, attended, branch, input_mlp,
        active, slope, grad_out,
    )
    grad_mods = jnp.concatenate([grad_mods, grad_gate[None]])
    mods_local = exact(membership, grad_mods, (((0,), (1,)), ((), ()))).reshape(groups, 6 * D)
    bias_head = jnp.concatenate([bias_sums[:1], bias_sums[2:4], bias_sums[5:9], bias_sums[4:5]])
    bias_head, grad_mods_all = lax.psum((bias_head.reshape(-1), mods_local), axes)
    first_sum = jnp.concatenate([bias_head, jnp.sum(grad_mods_all, axis=0)])
    block_shard = scatter_blocks(grads, units, kernels)
    mods_parts = grad_mods_all.reshape(groups * 6, D)
    ada_shard = exact(selector, mods_parts, (((1,), (0,)), ((), ())))
    unit = first_unit + jnp.arange(units, dtype=jnp.int32)
    grad_units = jnp.where(unit[:, None] >= BLOCK_UNITS, ada_shard, block_shard)
    products = exact(shard_low.astype(jnp.float32), mods_parts, (((1,), (1,)), ((), ())))
    products = jnp.sum(products.reshape(units, groups, 6) * ada_part[:, None, :], axis=2)
    spread = jnp.zeros((groups, 6 * D + 2 * units), jnp.float32)
    start = jnp.clip(first_unit - BLOCK_UNITS + units, 0, 6 * D + units)
    spread = lax.dynamic_update_slice(spread, products.T, (jnp.int32(0), start))
    grad_soft = jnp.sum(spread[:, units : units + 6 * D].reshape(groups, D, 6), axis=2)
    square_sum, grad_soft = lax.psum((jnp.sum(grad_units * grad_units), grad_soft), axes)
    silu_out, silu_back = jax.vjp(jax.nn.silu, conditioning)
    second_sum = silu_back(grad_soft)[0]
    grad_shard = grad_units.reshape(-1)
    grad_norm = jnp.sqrt(square_sum + jnp.sum(first_sum * first_sum))
    factor = jnp.minimum(1.0, CLIP_NORM / (grad_norm + 1e-06))
    new_weights, first_out, second_out = adamw(
        weights, grad_shard * factor, first_moment, second_moment
    )
    new_biases, bias_first_out, bias_second_out = adamw(
        biases, first_sum * factor, bias_first, bias_second
    )
    return (
        block_out,
        input_grad,
        second_sum,
        grad_norm,
        new_weights,
        first_out,
        second_out,
        new_biases,
        bias_first_out,
        bias_second_out,
    )


def solution(mesh):
    in_specs = (
        P(("outer", "inner"), None),
        P(),
        P(("outer", "inner")),
        P(),
        P(("outer", "inner"), None),
        P(("outer", "inner")),
        P(("outer", "inner")),
        P(("outer", "inner")),
        P(),
        P(),
        P(),
    )
    out_specs = (
        P(("outer", "inner"), None),
        P(("outer", "inner"), None),
        P(),
        P(),
        P(("outer", "inner")),
        P(("outer", "inner")),
        P(("outer", "inner")),
        P(),
        P(),
        P(),
    )
    kernels = dict(mesh.shape) == {"outer": 4, "inner": 8}
    return jax.shard_map(
        functools.partial(on_device, kernels=kernels), mesh=mesh, in_specs=in_specs, out_specs=out_specs, check_vma=False
    )
```

```python
import functools
import math

import jax
import jax.numpy as jnp
from jax import lax
from jax.experimental import pallas as pl
from jax.experimental.pallas import tpu as pltpu
from jax.sharding import PartitionSpec as P

D = 1152
H = 16
HD = 72
FF = 4608
FRAMES = 16
STEP = 8


NORM_EPS = 1e-06
LEARN_RATE = 0.02
BETA_FIRST = 0.5
BETA_SECOND = 0.55
ADAM_EPS = 1e-08
WEIGHT_DECAY = 0.01
CLIP_NORM = 1.0
BLOCK_UNITS = 4 * D + 2 * FF


MESH = pl.DeviceIdType.MESH
UNITS = 648
GROUPS8 = 81
QUART = 20
FIRST = 8
SECOND = QUART - FIRST
MAIN = 80
TAIL = 1
DEPTH = (4, 4, 3)
BASE = (0, 4, 8)


def flip(z, d):
    if d == 0:
        return z
    if d == 1:
        return z + 1 - 2 * (z % 2)
    if d == 2:
        return z + 2 - 4 * (z // 2)
    return 3 - z


class Place:
    def __init__(self):
        self.o = lax.axis_index("outer")
        self.i = lax.axis_index("inner")
        self.x, self.c = self.o // 2, self.o % 2
        self.z, self.y = self.i // 2, self.i % 2
        self.xo, self.co, self.yo = 1 - self.x, 1 - self.c, 1 - self.y

    def dev(self, dx=0, dc=0, dz=0, dy=0):
        x = self.xo if dx else self.x
        c = self.co if dc else self.c
        y = self.yo if dy else self.y
        return (x * 2 + c, flip(self.z, dz) * 2 + y)

    def greet(self):
        peers = [
            self.dev(dx=1), self.dev(dc=1), self.dev(dx=1, dc=1), self.dev(dy=1),
            self.dev(dz=1), self.dev(dz=2), self.dev(dz=3),
        ]
        barrier = pltpu.get_barrier_semaphore()
        for peer in peers:
            pl.semaphore_signal(barrier, inc=1, device_id=peer, device_id_type=MESH)
        pl.semaphore_wait(barrier, len(peers))


class Copies:
    def __init__(self, send_sems, recv_sems):
        self.send_sems, self.recv_sems = send_sems, recv_sems
        self.count = 0
        self.sent = []

    def slot(self):
        self.count += 1
        return self.count - 1

    def make(self, slot, src, dst, device):
        return pltpu.make_async_remote_copy(
            src_ref=src, dst_ref=dst, send_sem=self.send_sems.at[slot],
            recv_sem=self.recv_sems.at[slot], device_id=device, device_id_type=MESH,
        )

    def send(self, slot, src, dst, device, cond=None):
        def go():
            self.make(slot, src, dst, device).start()
        if cond is None:
            go()
        else:
            pl.when(cond)(go)
        self.sent.append((slot, src, dst, device, cond))

    def wait_recv(self, slot, dst, device, cond=None):
        def go():
            self.make(slot, dst, dst, device).wait_recv()
        if cond is None:
            go()
        else:
            pl.when(cond)(go)

    def wait_send(self, wanted):
        for entry in self.sent:
            if entry[0] == wanted:
                slot, src, dst, device, cond = entry

                def go():
                    self.make(slot, src, dst, device).wait_send()
                if cond is None:
                    go()
                else:
                    pl.when(cond)(go)
        self.sent = [entry for entry in self.sent if entry[0] != wanted]

    def drain(self):
        for slot, src, dst, device, cond in self.sent:
            def go(slot=slot, src=src, dst=dst, device=device):
                self.make(slot, src, dst, device).wait_send()
            if cond is None:
                go()
            else:
                pl.when(cond)(go)
        self.sent = []


def ok(zb, p):
    return None if DEPTH[p] == 4 else zb < DEPTH[p]


def both(a, b):
    if a is None:
        return b
    if b is None:
        return a
    return jnp.logical_and(a, b)


GATHER_COPIES = 3 * (3 + 3 + 4 * 4 + 8) + 7


def gather_stages(me, cp, shard, full, local_sems):
    def part(p, zb, yb, x, c, first=0, n=QUART):
        return full.at[p, zb, yb, pl.ds((2 * QUART * x + QUART * c + first), n)]

    def own_of(p):
        return both(me.o == p, ok(me.z, p))

    quarter = (2 * QUART * me.x + QUART * me.c)
    own_tail = pltpu.make_async_copy(
        shard.at[pl.ds(MAIN, TAIL)], full.at[me.o, me.z, me.y, pl.ds(MAIN, TAIL)], local_sems.at[0]
    )
    own_tail.start()

    def local_quarter(p):
        return pltpu.make_async_copy(
            shard.at[pl.ds(quarter, QUART)], part(p, me.z, me.y, me.x, me.c), local_sems.at[1]
        )

    slots = {}

    def s0(p):
        @pl.when(own_of(p))
        def _():
            local_quarter(p).start()
        for dx, dc in ((1, 0), (0, 1), (1, 1)):
            s = slots["s0", p, dx, dc] = cp.slot()
            x = me.xo if dx else me.x
            c = me.co if dc else me.c
            cp.send(
                s, shard.at[pl.ds((2 * QUART * x + QUART * c), QUART)],
                part(p, me.z, me.y, x, c), me.dev(dx=dx, dc=dc), own_of(p),
            )

    def s0_wait(p):
        @pl.when(own_of(p))
        def _():
            local_quarter(p).wait()
        ox, oc = p // 2, p % 2
        for dx, dc in ((1, 0), (0, 1), (1, 1)):
            x = me.xo if dx else me.x
            c = me.co if dc else me.c
            cond = both(jnp.logical_and(x == ox, c == oc), ok(me.z, p))
            cp.wait_recv(
                slots["s0", p, dx, dc], part(p, me.z, me.y, me.x, me.c), me.dev(dx=dx, dc=dc), cond
            )

    def spread(p, d):
        zb = flip(me.z, d)
        mine = part(p, zb, me.y, me.x, me.c)
        s = slots["y1", p, d] = cp.slot()
        cp.send(s, mine, mine, me.dev(dy=1), ok(zb, p))
        s = slots["x1", p, d] = cp.slot()
        cp.send(s, mine, mine, me.dev(dx=1), ok(zb, p))

    def s1(p):
        s0_wait(p)
        mine = part(p, me.z, me.y, me.x, me.c)
        for d in (1, 2, 3):
            s = slots["z", p, d] = cp.slot()
            cp.send(s, mine, mine, me.dev(dz=d), ok(me.z, p))
        spread(p, 0)

    def s2(p):
        for d in (1, 2, 3):
            zb = flip(me.z, d)
            cp.wait_recv(
                slots["z", p, d], part(p, zb, me.y, me.x, me.c), me.dev(dz=d), ok(zb, p)
            )
            spread(p, d)

    def s3(p):
        for d in (0, 1, 2, 3):
            zb = flip(me.z, d)
            cp.wait_recv(
                slots["y1", p, d], part(p, zb, me.yo, me.x, me.c), me.dev(dy=1), ok(zb, p)
            )
            s = slots["x2", p, d] = cp.slot()
            out = part(p, zb, me.yo, me.x, me.c, 0, FIRST)
            cp.send(s, out, out, me.dev(dx=1), ok(zb, p))
            cp.wait_recv(
                slots["x1", p, d], part(p, zb, me.y, me.xo, me.c), me.dev(dx=1), ok(zb, p)
            )
            s = slots["y2", p, d] = cp.slot()
            out = part(p, zb, me.y, me.xo, me.c, FIRST, SECOND)
            cp.send(s, out, out, me.dev(dy=1), ok(zb, p))

    def lane(p, zb, x, c):
        return full.at[p, zb, :, pl.ds((2 * QUART * x + QUART * c), QUART)]

    def s4(p):
        for d in (0, 1, 2, 3):
            zb = flip(me.z, d)
            cp.wait_recv(
                slots["x2", p, d], part(p, zb, me.yo, me.xo, me.c, 0, FIRST), me.dev(dx=1),
                ok(zb, p),
            )
            cp.wait_recv(
                slots["y2", p, d], part(p, zb, me.yo, me.xo, me.c, FIRST, SECOND), me.dev(dy=1),
                ok(zb, p),
            )
            for h in (0, 1):
                s = slots["c", p, d, h] = cp.slot()
                cp.send(s, lane(p, zb, h, me.c), lane(p, zb, h, me.c), me.dev(dc=1), ok(zb, p))

    def s5(p):
        for d in (0, 1, 2, 3):
            zb = flip(me.z, d)
            for h in (0, 1):
                cp.wait_recv(
                    slots["c", p, d, h], lane(p, zb, h, me.co), me.dev(dc=1), ok(zb, p)
                )

    tails = pl.ds(MAIN, TAIL)

    def t1():
        own_tail.wait()
        block = full.at[me.o, me.z, me.y, tails]
        for d in (1, 2, 3):
            s = slots["tz", d] = cp.slot()
            cp.send(s, block, block, me.dev(dz=d))

    def t2():
        for d in (1, 2, 3):
            zb = flip(me.z, d)
            cp.wait_recv(slots["tz", d], full.at[me.o, zb, me.y, tails], me.dev(dz=d))
        s = slots["ty"] = cp.slot()
        block = full.at[me.o, :, me.y, tails]
        cp.send(s, block, block, me.dev(dy=1))

    def t3():
        cp.wait_recv(slots["ty"], full.at[me.o, :, me.yo, tails], me.dev(dy=1))
        s = slots["tx"] = cp.slot()
        block = full.at[me.o, :, :, tails]
        cp.send(s, block, block, me.dev(dx=1))

    def t4():
        cp.wait_recv(slots["tx"], full.at[me.xo * 2 + me.c, :, :, tails], me.dev(dx=1))
        for h in (0, 1):
            s = slots["tc", h] = cp.slot()
            block = full.at[h * 2 + me.c, :, :, tails]
            cp.send(s, block, block, me.dev(dc=1))

    def t5():
        for h in (0, 1):
            cp.wait_recv(slots["tc", h], full.at[h * 2 + me.co, :, :, tails], me.dev(dc=1))

    return dict(s0=s0, s1=s1, s2=s2, s3=s3, s4=s4, s5=s5, t1=t1, t2=t2, t3=t3, t4=t4, t5=t5)


SCATTER_COPIES = 3 * (4 * 2 + 4 * 4 + 3 + 3) + 8
RING = 6
ORDER = (3, 2, 1, 0)
f32 = jnp.float32


def guarded(cond, fn):
    if cond is None:
        fn()
    else:
        pl.when(cond)(fn)


def add_rows(dst, srcs, n):
    step = 2 if n % 2 == 0 else 1

    def body(j, carry):
        at = pl.ds(j * step, step)
        total = srcs[0][at].astype(f32)
        for src in srcs[1:]:
            total = total + src[at].astype(f32)
        dst[at] = total.astype(dst.dtype)
        return carry

    lax.fori_loop(0, n // step, body, 0)


def scatter_stages(
    me, cp, partial, out, other, own, stage, rx2, ry2, rx1, ry1, rz, final, tail, tail_in, tail_z,
    local_sems, credit,
):
    slots = {}

    def block(k):
        p, d = 2 - k // 4, ORDER[k % 4]
        zb = flip(me.z, d)
        return p, d, zb, ok(zb, p), k % RING

    def exchange(p):
        for d in ORDER:
            zb = flip(me.z, d)
            for h in (0, 1):
                s = slots["c", p, d, h] = cp.slot()
                view = pl.ds(2 * QUART * h + QUART * me.co, QUART)
                cp.send(
                    s, partial.at[p, zb, :, view], other.at[p, zb, :, h], me.dev(dc=1), ok(zb, p)
                )

    def loads(k):
        p, d, zb, cond, slot = block(k)
        copies = []
        for h in (0, 1):
            view = pl.ds(2 * QUART * h + QUART * me.c, QUART)
            copies.append(
                pltpu.make_async_copy(
                    partial.at[p, zb, :, view], own.at[slot, :, h], local_sems.at[h]
                )
            )
            copies.append(
                pltpu.make_async_copy(other.at[p, zb, :, h], stage.at[h], local_sems.at[2 + h])
            )
        return copies

    def prefetch(k):
        p, d, zb, cond, slot = block(k)
        if k >= RING:
            old = block(k - RING)
            for name in ("x2", "y2", "x1", "y1", "z"):
                if (name, old[0], old[1]) in slots:
                    cp.wait_send(slots[name, old[0], old[1]])
        for h in (0, 1):
            cp.wait_recv(slots["c", p, d, h], other.at[p, zb, :, h], me.dev(dc=1), cond)

        def go():
            for copy in loads(k):
                copy.start()

        guarded(cond, go)

    def fold(k):
        p, d, zb, cond, slot = block(k)

        def go():
            for copy in loads(k):
                copy.wait()

            def body(q, carry):
                y, h = q // 2, q % 2
                add_rows(own.at[slot, y, h], [own.at[slot, y, h], stage.at[h, y]], QUART)
                return carry

            lax.fori_loop(0, 4, body, 0)

        guarded(cond, go)
        if k >= RING:
            pl.semaphore_wait(credit.at[0], 1)
            pl.semaphore_wait(credit.at[1], 1)
        far = own.at[slot, me.yo, me.xo]
        s = slots["x2", p, d] = cp.slot()
        cp.send(s, far.at[pl.ds(0, FIRST)], rx2.at[slot], me.dev(dx=1), cond)
        s = slots["y2", p, d] = cp.slot()
        cp.send(s, far.at[pl.ds(FIRST, SECOND)], ry2.at[slot], me.dev(dy=1), cond)

    def second(k):
        p, d, zb, cond, slot = block(k)
        cp.wait_recv(slots["x2", p, d], rx2.at[slot], me.dev(dx=1), cond)
        view = own.at[slot, me.yo, me.x, pl.ds(0, FIRST)]
        guarded(cond, lambda: add_rows(view, [view, rx2.at[slot]], FIRST))
        s = slots["y1", p, d] = cp.slot()
        cp.send(s, own.at[slot, me.yo, me.x], ry1.at[slot], me.dev(dy=1), cond)
        cp.wait_recv(slots["y2", p, d], ry2.at[slot], me.dev(dy=1), cond)
        view2 = own.at[slot, me.y, me.xo, pl.ds(FIRST, SECOND)]
        guarded(cond, lambda: add_rows(view2, [view2, ry2.at[slot]], SECOND))
        s = slots["x1", p, d] = cp.slot()
        cp.send(s, own.at[slot, me.y, me.xo], rx1.at[slot], me.dev(dx=1), cond)

    def third(k):
        p, d, zb, cond, slot = block(k)
        cp.wait_recv(slots["y1", p, d], ry1.at[slot], me.dev(dy=1), cond)
        cp.wait_recv(slots["x1", p, d], rx1.at[slot], me.dev(dx=1), cond)
        view = own.at[slot, me.y, me.x]
        guarded(cond, lambda: add_rows(view, [view, ry1.at[slot], rx1.at[slot]], QUART))
        if k + RING < 12:
            pl.semaphore_signal(
                credit.at[0], inc=1, device_id=me.dev(dx=1), device_id_type=MESH
            )
            pl.semaphore_signal(
                credit.at[1], inc=1, device_id=me.dev(dy=1), device_id_type=MESH
            )
        if d:
            s = slots["z", p, d] = cp.slot()
            cp.send(s, view, rz.at[p, d - 1], me.dev(dz=d), cond)

    def quarter(x, c):
        return out.at[pl.ds(2 * QUART * x + QUART * c, QUART)]

    def settle(p):
        mine = ok(me.z, p)
        for d in (1, 2, 3):
            cp.wait_recv(slots["z", p, d], rz.at[p, d - 1], me.dev(dz=d), mine)
        view = own.at[(4 * (2 - p) + 3) % RING, me.y, me.x]
        guarded(
            mine,
            lambda: add_rows(final.at[p], [view, rz.at[p, 0], rz.at[p, 1], rz.at[p, 2]], QUART),
        )
        ox, oc = p // 2, p % 2
        for dx, dc in ((1, 0), (0, 1), (1, 1)):
            x = me.xo if dx else me.x
            c = me.co if dc else me.c
            s = slots["f", p, dx, dc] = cp.slot()
            cond = both(jnp.logical_and(x == ox, c == oc), mine)
            cp.send(s, final.at[p], quarter(me.x, me.c), me.dev(dx=dx, dc=dc), cond)

        @pl.when(both(me.o == p, mine))
        def _():
            pltpu.make_async_copy(final.at[p], quarter(me.x, me.c), local_sems.at[4]).start()

    def finish(p):
        mine = both(me.o == p, ok(me.z, p))
        for dx, dc in ((1, 0), (0, 1), (1, 1)):
            x = me.xo if dx else me.x
            c = me.co if dc else me.c
            cp.wait_recv(slots["f", p, dx, dc], quarter(x, c), me.dev(dx=dx, dc=dc), mine)

        @pl.when(mine)
        def _():
            pltpu.make_async_copy(final.at[p], quarter(me.x, me.c), local_sems.at[4]).wait()

    def tail_load():
        return pltpu.make_async_copy(
            partial.at[:, :, :, pl.ds(MAIN, TAIL)], tail, local_sems.at[5]
        )

    def tail_add(o, zb, yb, srcs):
        add_rows(tail.at[o, zb, yb], [tail.at[o, zb, yb]] + srcs, TAIL)

    def t0():
        tail_load().start()

    def t1():
        tail_load().wait()
        for h in (0, 1):
            s = slots["tc", h] = cp.slot()
            cp.send(s, tail.at[2 * h + me.co], tail_in.at[h], me.dev(dc=1))

    def t2():
        for h in (0, 1):
            cp.wait_recv(slots["tc", h], tail_in.at[h], me.dev(dc=1))

            def body(q, carry):
                tail_add(2 * h + me.c, q // 2, q % 2, [tail_in.at[h, q // 2, q % 2]])
                return carry
            lax.fori_loop(0, 8, body, 0)
        s = slots["tx"] = cp.slot()
        cp.send(s, tail.at[me.xo * 2 + me.c], tail_in.at[2], me.dev(dx=1))

    def t3():
        cp.wait_recv(slots["tx"], tail_in.at[2], me.dev(dx=1))

        def body(q, carry):
            tail_add(me.o, q // 2, q % 2, [tail_in.at[2, q // 2, q % 2]])
            return carry
        lax.fori_loop(0, 8, body, 0)
        s = slots["ty"] = cp.slot()
        cp.send(s, tail.at[me.o, :, me.yo], tail_in.at[3, :, 0], me.dev(dy=1))

    def t4():
        cp.wait_recv(slots["ty"], tail_in.at[3, :, 0], me.dev(dy=1))

        def body(q, carry):
            tail_add(me.o, q, me.y, [tail_in.at[3, q, 0]])
            return carry
        lax.fori_loop(0, 4, body, 0)
        for d in (1, 2, 3):
            s = slots["tz", d] = cp.slot()
            cp.send(s, tail.at[me.o, flip(me.z, d), me.y], tail_z.at[d - 1], me.dev(dz=d))

    def t5():
        for d in (1, 2, 3):
            cp.wait_recv(slots["tz", d], tail_z.at[d - 1], me.dev(dz=d))
        tail_add(me.o, me.z, me.y, [tail_z.at[0], tail_z.at[1], tail_z.at[2]])
        copy = pltpu.make_async_copy(
            tail.at[me.o, me.z, me.y], out.at[pl.ds(MAIN, TAIL)], local_sems.at[5]
        )
        copy.start()
        copy.wait()

    return dict(
        exchange=exchange, prefetch=prefetch, fold=fold, second=second, third=third,
        settle=settle, finish=finish, tails=(t0, t1, t2, t3, t4, t5),
    )


def scatter_scratch():
    bf = jnp.bfloat16
    return [
        pltpu.VMEM((RING, 2, 2, QUART, 8, D), bf),
        pltpu.VMEM((2, 2, QUART, 8, D), bf),
        pltpu.VMEM((RING, FIRST, 8, D), bf),
        pltpu.VMEM((RING, SECOND, 8, D), bf),
        pltpu.VMEM((RING, QUART, 8, D), bf),
        pltpu.VMEM((RING, QUART, 8, D), bf),
        pltpu.VMEM((3, 3, QUART, 8, D), bf),
        pltpu.VMEM((3, QUART, 8, D), bf),
        pltpu.VMEM((4, 4, 2, TAIL, 8, D), bf),
        pltpu.VMEM((4, 4, 2, TAIL, 8, D), bf),
        pltpu.VMEM((3, TAIL, 8, D), bf),
        pltpu.SemaphoreType.DMA((6,)),
        pltpu.SemaphoreType.REGULAR((2,)),
    ]


bf16 = jnp.bfloat16
MATS = D // 8
AT_PROJ = 3 * MATS
AT_UP = 4 * MATS
AT_DOWN = 8 * MATS
ROOT = math.sqrt(2.0 / math.pi)
CUBIC = 0.044715


def nn_dot(left, right):
    return lax.dot_general(left, right, (((1,), (0,)), ((), ())), preferred_element_type=f32)


def nt_dot(left, right):
    return lax.dot_general(left, right, (((1,), (1,)), ((), ())), preferred_element_type=f32)


def tn_dot(left, right):
    return lax.dot_general(left, right, (((0,), (0,)), ((), ())), preferred_element_type=f32)


def square(ref):
    return ref[...].reshape(D, D)


def norm_rows(values):
    centered = values - jnp.mean(values, axis=-1, keepdims=True)
    inverse = lax.rsqrt(jnp.mean(centered * centered, axis=-1, keepdims=True) + NORM_EPS)
    return centered * inverse, inverse


def norm_rows_back(grad, normed, inverse):
    return inverse * (
        grad
        - jnp.mean(grad, axis=-1, keepdims=True)
        - normed * jnp.mean(grad * normed, axis=-1, keepdims=True)
    )


def frames_of(c):
    return pl.ds(pl.multiple_of(c * FRAMES, FRAMES), FRAMES)


def over_columns(count, body):
    def step(c, carry):
        body(c, frames_of(c), pl.ds(c, 1))
        return carry

    lax.fori_loop(0, count, step, 0)


def split_rows(src, spread, put, ways):
    units = src.shape[0] * 8
    rows = units // ways
    for q in range(9):
        lanes = slice(128 * q, 128 * q + 128)
        spread[q, pl.ds(0, units)] = src[:, :, lanes].astype(f32).reshape(units, 128)
        for w in range(ways):
            part = spread[q, pl.ds(w, rows, stride=ways), :]
            put(w, lanes, part.reshape(rows // 8, 8, 128).astype(bf16))


def head_window(h):
    first = min(HD * h // 128, 7) * 128
    lane = lax.broadcasted_iota(jnp.int32, (1, 256), 1) + first
    mask = jnp.logical_and(lane >= HD * h, lane < HD * h + HD)
    return slice(first, first + 256), jnp.where(mask, 1.0, 0.0).astype(bf16)


def same_column():
    row = lax.broadcasted_iota(jnp.int32, (128, 128), 0)
    col = lax.broadcasted_iota(jnp.int32, (128, 128), 1)
    return lax.shift_right_logical(row, 4) == lax.shift_right_logical(col, 4)


SCORE_SCALE = 1.0 / math.sqrt(HD)


def head_probabilities(masked_queries, keys, inside):
    scores = jnp.where(inside, nt_dot(masked_queries, keys) * SCORE_SCALE, -1e30)
    grown = jnp.exp(scores - jnp.max(scores, axis=-1, keepdims=True))
    return grown / jnp.sum(grown, axis=-1, keepdims=True)


SUM_COPIES = 6
SUM_SLOTS = 10


def sum_stages(me, cp, mine, buf):
    slots = {}

    def send(name, src, dst, device):
        slots[name] = cp.slot()
        cp.send(slots[name], src, dst, device)

    def m1():
        send("c", mine, buf.at[0], me.dev(dc=1))

    def m2():
        cp.wait_recv(slots["c"], buf.at[0], me.dev(dc=1))
        buf[1] = mine[...] + buf[0]
        send("x", buf.at[1], buf.at[2], me.dev(dx=1))

    def m3():
        cp.wait_recv(slots["x"], buf.at[2], me.dev(dx=1))
        buf[3] = buf[1] + buf[2]
        send("y", buf.at[3], buf.at[4], me.dev(dy=1))

    def m4():
        cp.wait_recv(slots["y"], buf.at[4], me.dev(dy=1))
        buf[5] = buf[3] + buf[4]
        buf[6 + me.z] = buf[5]
        for d in (1, 2, 3):
            send(d, buf.at[5], buf.at[6 + me.z], me.dev(dz=d))

    def total():
        for d in (1, 2, 3):
            cp.wait_recv(slots[d], buf.at[6 + flip(me.z, d)], me.dev(dz=d))
        return (buf[6] + buf[7]) + (buf[8] + buf[9])

    return m1, m2, m3, m4, total


def forward_body(
    weights, tokens, upstream, mods, b_qkv, b_proj, b_up, b_down,
    block_out, natural, input_att, proj_out, attended, branch, input_mlp, active_out, slope_out,
    grad_out, grad_gate, held, stage, spread, acc, hid, proj, active, slope, copy_sems, ready,
):
    columns = mods.shape[1]

    def fetch(first, groups, slot):
        return pltpu.make_async_copy(
            weights.at[pl.ds(first, groups)], stage.at[slot, pl.ds(0, groups)], copy_sems.at[slot]
        )

    def whole(mat, slot):
        return pltpu.make_async_copy(
            weights.at[pl.ds(mat * MATS, MATS)], held.at[slot], copy_sems.at[2 + slot]
        )

    def save(mat, slot):
        return pltpu.make_async_copy(held.at[slot], natural.at[mat], copy_sems.at[10 + mat])

    def keep(src, dst, n):
        return pltpu.make_async_copy(src, dst, copy_sems.at[17 + n])

    def unweave(first, ways, slot0, blocks=9):
        groups = 16 * ways
        fetch(first, groups, 0).start()

        def step(j, carry):
            slot = lax.rem(j, 2)
            fetch(first + j * groups, groups, slot).wait()

            @pl.when(j + 1 < blocks)
            def _():
                fetch(first + (j + 1) * groups, groups, 1 - slot).start()

            def put(w, lanes, block):
                held[slot0 + w, pl.ds(j * 16, 16), :, lanes] = block

            split_rows(stage.at[slot, pl.ds(0, groups)], spread, put, ways)
            return carry

        lax.fori_loop(0, blocks, step, 0)

    def first_norm(c, rows, at):
        normed, _ = norm_rows(tokens[rows].astype(f32))
        input_att[rows] = (normed * (1.0 + mods[1, at]) + mods[0, at]).astype(bf16)

    over_columns(columns, first_norm)
    ready("qkv")
    whole(3, 3).start()
    unweave(0, 3, 0)
    for p in range(3):
        save(p, p).start()

    def project(p, carry):
        proj[p] = (nn_dot(input_att[...], square(held.at[p])) + b_qkv[pl.ds(p, 1)]).astype(bf16)
        return carry

    lax.fori_loop(0, 3, project, 0)
    keep(proj, proj_out, 0).start()

    inside = same_column()

    def attend(g, carry):
        rows = pl.ds(pl.multiple_of(g * 128, 128), 128)
        acc[pl.ds(0, 128)] = jnp.zeros((128, D), f32)
        for h in range(H):
            window, mask = head_window(h)
            probs = head_probabilities(proj[0, rows, window] * mask, proj[1, rows, window], inside)
            acc[pl.ds(0, 128), window] += nn_dot(probs.astype(bf16), proj[2, rows, window] * mask)
        attended[rows] = acc[pl.ds(0, 128)].astype(bf16)
        return carry

    lax.fori_loop(0, columns * FRAMES // 128, attend, 0)
    ready("proj")
    whole(3, 3).wait()
    branch[...] = nn_dot(attended[...], square(held.at[3])) + b_proj[...]
    for p in range(3):
        save(p, p).wait()

    def second_norm(c, rows, at):
        middle = tokens[rows].astype(f32) + mods[2, at] * branch[rows]
        normed, _ = norm_rows(middle)
        input_mlp[rows] = (normed * (1.0 + mods[4, at]) + mods[3, at]).astype(bf16)

    over_columns(columns, second_norm)
    ready("up")
    unweave(AT_UP, 4, 4)
    for b in range(4):
        save(3 + b, 4 + b).start()

    def raise_(b, carry):
        hid[...] = nn_dot(input_mlp[...], square(held.at[4 + b])) + b_up[pl.ds(b, 1)]

        def gelu(c, rows, at):
            v = hid[rows]
            sq = v * v
            t = jnp.tanh(ROOT * (v + CUBIC * sq * v))
            half = 0.5 * (1.0 + t)
            active[b, rows] = (v * half).astype(bf16)
            rise = half + (0.5 * ROOT) * v * (1.0 - t * t) * (1.0 + 3.0 * CUBIC * sq)
            for q in range(9):
                slope[b, q, rows] = rise[:, 128 * q : 128 * q + 128]

        over_columns(columns, gelu)
        return carry

    lax.fori_loop(0, 4, raise_, 0)
    keep(active, active_out, 1).start()
    keep(slope, slope_out, 2).start()
    acc[...] = jnp.broadcast_to(b_down[...], acc.shape)
    ready("down")
    for b in range(4):
        whole(8 + b, b).start()
    for b in range(4):
        whole(8 + b, b).wait()
        acc[...] += nn_dot(active[b], square(held.at[b]))

    def last(c, rows, at):
        x = tokens[rows].astype(f32)
        middle = x + mods[2, at] * branch[rows]
        video = mods[6, at] > 0.5
        outcome = acc[rows]
        block_out[rows] = jnp.where(video, middle + mods[5, at] * outcome, x)
        grad_block = jnp.where(video, upstream[rows].astype(f32), 0.0)
        grad_gate[at] = jnp.sum(grad_block * outcome, axis=0, keepdims=True)
        grad_out[rows] = (grad_block * mods[5, at]).astype(bf16)

    over_columns(columns, last)
    for b in range(4):
        save(3 + b, 4 + b).wait()
    keep(proj, proj_out, 0).wait()
    keep(active, active_out, 1).wait()
    keep(slope, slope_out, 2).wait()


def forward_kernel(*refs):
    forward_body(*refs, lambda name: None)


def gather_forward_kernel(
    shard, partial, chosen, base, tokens, upstream, b_qkv, b_proj, b_up, b_down,
    full, mods, *refs,
):
    refs, (sums, send_sems, recv_sems, local_sems) = refs[:-4], refs[-4:]
    me = Place()
    cp = Copies(send_sems, recv_sems)
    st = gather_stages(me, cp, shard, full, local_sems)
    s0, s1, s2, s3, s4, s5 = (st["s%d" % n] for n in range(6))
    t1, t2, t3, t4, t5 = (st["t%d" % n] for n in range(1, 6))
    m1, m2, m3, m4, total = sum_stages(me, cp, partial, sums)
    me.greet()
    m1()
    s0(0)
    m2()
    s0(1)
    s1(0)
    m3()
    s0(2)
    t1()
    s2(0)
    m4()
    t2()
    s1(1)
    s3(0)
    t3()
    s2(1)
    t4()
    s1(2)
    table = exact(chosen[...], total(), (((1,), (0,)), ((), ()))) + base[...]
    columns = mods.shape[1]
    for n in range(7):
        mods[n] = table[n * columns : (n + 1) * columns]

    def ready(name):
        if name == "qkv":
            s4(0)
            s3(1)
            t5()
            s2(2)
            s5(0)
        if name == "proj":
            s4(1)
        if name == "up":
            s3(2)
            s5(1)
        if name == "down":
            s4(2)
            s5(2)

    forward_body(
        full.reshape(4 * 4 * 2 * GROUPS8, 8, D), tokens, upstream, mods, b_qkv, b_proj, b_up,
        b_down, *refs, ready,
    )
    cp.drain()


def forward_shapes(rows, columns):
    shape = jax.ShapeDtypeStruct
    return [
        shape((rows, D), f32),
        shape((7, MATS, 8, D), bf16),
        shape((rows, D), bf16),
        shape((3, rows, D), bf16),
        shape((rows, D), bf16),
        shape((rows, D), f32),
        shape((rows, D), bf16),
        shape((4, rows, D), bf16),
        shape((4, 9, rows, 128), f32),
        shape((rows, D), bf16),
        shape((columns, D), f32),
    ]


VMEM_SPEC = pl.BlockSpec(memory_space=pltpu.VMEM)
HBM_SPEC = pl.BlockSpec(memory_space=pl.ANY)
FORWARD_SPECS = [
    VMEM_SPEC, HBM_SPEC, VMEM_SPEC, HBM_SPEC, VMEM_SPEC, VMEM_SPEC, VMEM_SPEC, HBM_SPEC, HBM_SPEC,
    VMEM_SPEC, VMEM_SPEC,
]


def forward_scratch(rows):
    return [
        pltpu.VMEM((8, MATS, 8, D), bf16),
        pltpu.VMEM((2, 64, 8, D), bf16),
        pltpu.VMEM((9, 512, 128), f32),
        pltpu.VMEM((rows, D), f32),
        pltpu.VMEM((rows, D), f32),
        pltpu.VMEM((3, rows, D), bf16),
        pltpu.VMEM((4, rows, D), bf16),
        pltpu.VMEM((4, 9, rows, 128), f32),
        pltpu.SemaphoreType.DMA((20,)),
    ]


def forward(weights, tokens, upstream, mods, b_qkv, b_proj, b_up, b_down):
    rows = tokens.shape[0]
    return pl.pallas_call(
        forward_kernel,
        out_shape=forward_shapes(rows, mods.shape[1]),
        in_specs=[HBM_SPEC] + [VMEM_SPEC] * 7,
        out_specs=FORWARD_SPECS,
        scratch_shapes=forward_scratch(rows),
        compiler_params=pltpu.CompilerParams(vmem_limit_bytes=60 * 2**20),
        name="block_forward",
    )(weights, tokens, upstream, mods, b_qkv, b_proj, b_up, b_down)


def gather_forward(shard, partial, chosen, base, tokens, upstream, b_qkv, b_proj, b_up, b_down):
    rows = tokens.shape[0]
    columns = rows // FRAMES
    copies = GATHER_COPIES + SUM_COPIES
    return pl.pallas_call(
        gather_forward_kernel,
        out_shape=[
            jax.ShapeDtypeStruct((4, 4, 2, GROUPS8, 8, D), bf16),
            jax.ShapeDtypeStruct((7, columns, D), f32),
        ]
        + forward_shapes(rows, columns),
        in_specs=[HBM_SPEC] + [VMEM_SPEC] * 9,
        out_specs=[HBM_SPEC, VMEM_SPEC] + FORWARD_SPECS,
        scratch_shapes=forward_scratch(rows)
        + [
            pltpu.VMEM((SUM_SLOTS, *partial.shape), f32),
            pltpu.SemaphoreType.DMA((copies,)),
            pltpu.SemaphoreType.DMA((copies,)),
            pltpu.SemaphoreType.DMA((2,)),
        ],
        compiler_params=pltpu.CompilerParams(
            collective_id=0, has_side_effects=True, vmem_limit_bytes=62 * 2**20
        ),
        name="gather_forward",
    )(shard, partial, chosen, base, tokens, upstream, b_qkv, b_proj, b_up, b_down)


UP_RUNS = ((0, 256), (256, 256), (512, 256), (768, 256), (1024, 128))
QKV_RUNS = ((0, 384), (384, 384), (768, 384))


def backward_body(
    weights, natural, active, slope, tokens, upstream, mods, input_att, proj, attended, branch,
    input_mlp, grad_out,
    grads, input_grad, grad_mods, bias_sums,
    held, woven, spread, acts, grad_hidden, grad_branch, grad_att, acc, copy_sems, tick,
):
    columns = mods.shape[1]
    row_count = columns * FRAMES

    def fetch(first, slot):
        return pltpu.make_async_copy(natural.at[first], held.at[slot], copy_sems.at[slot])

    def flat_mat(first, slot):
        return pltpu.make_async_copy(
            weights.at[pl.ds(first, MATS)], held.at[slot], copy_sems.at[slot]
        )

    def stream(b, slot):
        at = pl.ds(pl.multiple_of(slot * row_count, row_count), row_count)
        return (
            flat_mat(AT_DOWN + b * MATS, slot),
            pltpu.make_async_copy(active.at[b], acts.at[slot], copy_sems.at[2 + slot]),
            pltpu.make_async_copy(slope.at[b], spread.at[:, at], copy_sems.at[4 + slot]),
        )

    def store(first, offset, groups, n):
        return pltpu.make_async_copy(
            woven.at[pl.ds(offset, groups)], grads.at[pl.ds(first, groups)], copy_sems.at[6 + n]
        )

    bias_sums[...] = jnp.zeros_like(bias_sums)

    def add_bias(row, values):
        bias_sums[pl.ds(row, 1)] += jnp.sum(values.astype(f32), axis=0, keepdims=True)

    def outer(first, left, right, pending):
        for r in range(3):
            part = tn_dot(left[:, 384 * r : 384 * r + 384], right[...])
            if pending is not None:
                pending(r)
            woven[pl.ds(48 * r, 48)] = part.reshape(48, 8, D).astype(bf16)
            store(first + 48 * r, 48 * r, 48, r).start()

    for copy in stream(0, 0):
        copy.start()

    def down(b, carry):
        slot = lax.rem(b, 2)
        for copy in stream(b, slot):
            copy.wait()

        @pl.when(b < 3)
        def _():
            for copy in stream(b + 1, 1 - slot):
                copy.start()

        acc[...] = nt_dot(grad_out[...], square(held.at[slot]))

        def through(c, rows, at):
            there = pl.ds(pl.multiple_of(slot * row_count + c * FRAMES, FRAMES), FRAMES)
            rise = jnp.concatenate([spread[q, there] for q in range(9)], axis=1)
            grad = (acc[rows] * rise).astype(bf16)
            grad_hidden[b, rows] = grad
            add_bias(5 + b, grad)

        over_columns(columns, through)
        first = AT_DOWN + b * MATS

        def pending(r):
            @pl.when(b > 0)
            def _():
                store(first - MATS + 48 * r, 48 * r, 48, r).wait()

        outer(first, acts.at[slot], grad_out, pending)
        return carry

    lax.fori_loop(0, 4, down, 0)
    fetch(3, 0).start()

    def down_bias(c, rows, at):
        add_bias(4, grad_out[rows])

    over_columns(columns, down_bias)
    for r in range(3):
        store(AT_DOWN + 3 * MATS + 48 * r, 48 * r, 48, r).wait()
    tick("down")

    def weave(first, ways, left, right, runs, name):
        before = None
        for k, (start, count) in enumerate(runs):
            for w in range(ways):
                part = tn_dot(left[:, start : start + count], right[w])
                for q in range(9):
                    spread[q, pl.ds(w, count, stride=ways), :] = part[:, 128 * q : 128 * q + 128]
            if before is not None:
                before.wait()

            def pack(j, carry):
                for q in range(9):
                    lines = spread[q, pl.ds(pl.multiple_of(j * 128, 128), 128), :]
                    woven[pl.ds(j * 16, 16), :, 128 * q : 128 * q + 128] = lines.reshape(
                        16, 8, 128
                    ).astype(bf16)
                return carry

            groups = count * ways // 8
            lax.fori_loop(0, groups // 16, pack, 0)
            before = store(first + start * ways // 8, 0, groups, 0)
            before.start()
            tick(name, k)
        before.wait()

    weave(AT_UP, 4, input_mlp, grad_hidden, UP_RUNS, "up run")
    tick("up")
    acc[...] = jnp.zeros_like(acc)
    for b in range(4):
        fetch(3 + b, b % 2).wait()
        if b < 3:
            fetch(4 + b, 1 - b % 2).start()
        acc[...] += nt_dot(grad_hidden[b], square(held.at[b % 2]))
        tick("up input", b)
    flat_mat(AT_PROJ, 0).start()

    def second_norm_back(c, rows, at):
        br = branch[rows]
        gate = mods[2, at]
        normed, inverse = norm_rows(tokens[rows].astype(f32) + gate * br)
        grad = acc[rows]
        grad_mods[3, at] = jnp.sum(grad, axis=0, keepdims=True)
        grad_mods[4, at] = jnp.sum(grad * normed, axis=0, keepdims=True)
        grad_block = jnp.where(mods[6, at] > 0.5, upstream[rows].astype(f32), 0.0)
        grad_middle = grad_block + norm_rows_back(grad * (1.0 + mods[4, at]), normed, inverse)
        input_grad[rows] = grad_middle
        grad_mods[2, at] = jnp.sum(grad_middle * br, axis=0, keepdims=True)
        grad = (grad_middle * gate).astype(bf16)
        grad_branch[rows] = grad
        add_bias(3, grad)

    over_columns(columns, second_norm_back)
    tick("norm")
    outer(AT_PROJ, attended, grad_branch, None)
    flat_mat(AT_PROJ, 0).wait()
    grad_att[...] = nt_dot(grad_branch[...], square(held.at[0])).astype(bf16)
    fetch(0, 0).start()
    for r in range(3):
        store(AT_PROJ + 48 * r, 48 * r, 48, r).wait()
    tick("proj")
    inside = same_column()

    def attend_back(g, carry):
        rows = pl.ds(pl.multiple_of(g * 128, 128), 128)
        for p in range(3):
            acc[pl.ds(p * 128, 128)] = jnp.zeros((128, D), f32)
        for h in range(H):
            window, mask = head_window(h)
            queries = proj[0, rows, window] * mask
            keys = proj[1, rows, window]
            grad = grad_att[rows, window] * mask
            probs = head_probabilities(queries, keys, inside)
            grad_probs = nt_dot(grad, proj[2, rows, window])
            mean = jnp.sum(grad_probs * probs, axis=-1, keepdims=True)
            grad_scores = (probs * (grad_probs - mean)).astype(bf16)
            acc[pl.ds(0, 128), window] += nn_dot(grad_scores, keys * mask)
            acc[pl.ds(128, 128), window] += tn_dot(grad_scores, queries)
            acc[pl.ds(256, 128), window] += tn_dot(probs.astype(bf16), grad)
        for p in range(3):
            scale = SCORE_SCALE if p < 2 else 1.0
            grad = (acc[pl.ds(p * 128, 128)] * scale).astype(bf16)
            grad_hidden[p, rows] = grad
            add_bias(p, grad)
        return carry

    for g in range(row_count // 128):
        lax.fori_loop(g, g + 1, attend_back, 0)
        tick("attend", g)
    weave(0, 3, input_att, grad_hidden, QKV_RUNS, "qkv run")
    tick("qkv")
    acc[...] = jnp.zeros_like(acc)
    for p in range(3):
        fetch(p, p % 2).wait()
        if p < 2:
            fetch(p + 1, 1 - p % 2).start()
        acc[...] += nt_dot(grad_hidden[p], square(held.at[p % 2]))
        tick("qkv input", p)

    def first_norm_back(c, rows, at):
        normed, inverse = norm_rows(tokens[rows].astype(f32))
        grad = acc[rows]
        grad_mods[0, at] = jnp.sum(grad, axis=0, keepdims=True)
        grad_mods[1, at] = jnp.sum(grad * normed, axis=0, keepdims=True)
        grad_states = input_grad[rows] + norm_rows_back(
            grad * (1.0 + mods[1, at]), normed, inverse
        )
        up_rows = upstream[rows].astype(f32)
        input_grad[rows] = jnp.where(mods[6, at] > 0.5, grad_states, up_rows)

    over_columns(columns, first_norm_back)
    tick("end")


def backward_kernel(*refs):
    backward_body(*refs, lambda name, step=0: None)


def backward_scatter_kernel(*refs):
    (
        weights, natural, active, slope, tokens, upstream, mods, input_att, proj, attended, branch,
        input_mlp, grad_out, grad_gate, member,
        out, grads, other, input_grad, total_small,
        grad_mods, bias_sums, held, woven, spread, acts, grad_hidden, grad_branch, grad_att, acc, copy_sems,
        own, stage, rx2, ry2, rx1, ry1, rz, final, tail, tail_in, tail_z, local_sems, credit,
        small, sums, send_sems, recv_sems,
    ) = refs
    me = Place()
    cp = Copies(send_sems, recv_sems)
    me.greet()
    st = scatter_stages(
        me, cp, grads, out, other, own, stage, rx2, ry2, rx1, ry1, rz, final, tail, tail_in,
        tail_z, local_sems, credit,
    )
    t0, t1, t2, t3, t4, t5 = st["tails"]
    m1, m2, m3, m4, total = sum_stages(me, cp, small, sums)
    groups = member.shape[0]

    def move(t):
        if t < 12:
            st["fold"](t)
            if t % 4 != 3:
                st["prefetch"](t + 1)
        if 0 <= t - 1 < 12:
            st["second"](t - 1)
        if 0 <= t - 2 < 12:
            st["third"](t - 2)

    def tick(name, step=0):
        if name == "down":
            st["exchange"](2)
            st["prefetch"](0)
        elif name == "up run" and step in (0, 2, 4):
            move(step // 2)
        elif name == "up":
            st["exchange"](1)
        elif name == "up input" and step == 1:
            move(3)
            st["prefetch"](4)
        elif name == "norm":
            move(4)
        elif name == "attend":
            move(5 + step)
            if step == 1:
                st["settle"](2)
        elif name == "qkv":
            st["exchange"](0)
            st["prefetch"](8)
            t0()
        elif name == "qkv input" and step == 0:
            move(8)
            t1()
        elif name == "qkv input" and step == 2:
            t2()
        elif name == "end":
            for n in range(6):
                plane = grad_mods[n] if n < 5 else grad_gate[...]
                small[pl.ds(n * groups, groups)] = exact(
                    member[...], plane, (((1,), (0,)), ((), ()))
                )
            small[pl.ds(6 * groups, 9)] = bias_sums[pl.ds(0, 9)]
            small[pl.ds(6 * groups + 9, small.shape[0] - 6 * groups - 9)] = jnp.zeros(
                (small.shape[0] - 6 * groups - 9, D), f32
            )
            m1()
            move(9)
            t3()
            m2()
            move(10)
            t4()
            m3()
            st["settle"](1)
            move(11)
            t5()
            m4()
            move(12)
            total_small[...] = total()
            move(13)
            st["settle"](0)
            for p in (2, 1, 0):
                st["finish"](p)
            cp.drain()

    backward_body(
        weights, natural, active, slope, tokens, upstream, mods, input_att, proj, attended, branch,
        input_mlp, grad_out,
        grads.reshape(4 * 4 * 2 * GROUPS8, 8, D), input_grad, grad_mods, bias_sums,
        held, woven, spread, acts, grad_hidden, grad_branch, grad_att, acc, copy_sems,
        tick,
    )


def backward_shapes(rows, columns):
    shape = jax.ShapeDtypeStruct
    return [
        shape((rows, D), f32),
        shape((5, columns, D), f32),
        shape((16, D), f32),
    ]


def backward_scratch(rows):
    return [
        pltpu.VMEM((2, MATS, 8, D), bf16),
        pltpu.VMEM((MATS, 8, D), bf16),
        pltpu.VMEM((9, D, 128), f32),
        pltpu.VMEM((2, rows, D), bf16),
        pltpu.VMEM((4, rows, D), bf16),
        pltpu.VMEM((rows, D), bf16),
        pltpu.VMEM((rows, D), bf16),
        pltpu.VMEM((rows, D), f32),
        pltpu.SemaphoreType.DMA((9,)),
    ]


def backward(*operands):
    rows, columns = operands[4].shape[0], operands[6].shape[1]
    return pl.pallas_call(
        backward_kernel,
        out_shape=[jax.ShapeDtypeStruct((32 * UNITS // 8, 8, D), bf16)]
        + backward_shapes(rows, columns),
        in_specs=[HBM_SPEC] * 4 + [VMEM_SPEC] * 9,
        out_specs=[HBM_SPEC] + [VMEM_SPEC] * 3,
        scratch_shapes=backward_scratch(rows),
        compiler_params=pltpu.CompilerParams(vmem_limit_bytes=62 * 2**20),
        name="block_backward",
    )(*operands)


def backward_scatter(operands, grad_gate, member):
    rows, columns = operands[4].shape[0], operands[6].shape[1]
    small = small_rows(member.shape[0])
    copies = SCATTER_COPIES + SUM_COPIES
    shape = jax.ShapeDtypeStruct
    input_grad, grad_mods, bias_sums = backward_shapes(rows, columns)
    return pl.pallas_call(
        backward_scatter_kernel,
        out_shape=[
            shape((GROUPS8, 8, D), bf16),
            shape((4, 4, 2, GROUPS8, 8, D), bf16),
            shape((3, 4, 2, 2, QUART, 8, D), bf16),
            input_grad,
            shape((small, D), f32),
        ],
        in_specs=[HBM_SPEC] * 4 + [VMEM_SPEC] * 11,
        out_specs=[HBM_SPEC] * 3 + [VMEM_SPEC] * 2,
        scratch_shapes=[
            pltpu.VMEM(grad_mods.shape, f32),
            pltpu.VMEM(bias_sums.shape, f32),
        ]
        + backward_scratch(rows)
        + scatter_scratch()
        + [
            pltpu.VMEM((small, D), f32),
            pltpu.VMEM((SUM_SLOTS, small, D), f32),
            pltpu.SemaphoreType.DMA((copies,)),
            pltpu.SemaphoreType.DMA((copies,)),
        ],
        compiler_params=pltpu.CompilerParams(
            collective_id=1, has_side_effects=True, vmem_limit_bytes=63 * 2**20
        ),
        name="backward_scatter",
    )(*operands, grad_gate, member)


def small_rows(groups):
    return -(-(6 * groups + 9) // 8) * 8


def sum_kernel(mine, out, sums, send_sems, recv_sems):
    me = Place()
    cp = Copies(send_sems, recv_sems)
    me.greet()
    m1, m2, m3, m4, total = sum_stages(me, cp, mine, sums)
    m1()
    m2()
    m3()
    m4()
    out[...] = total()
    cp.drain()


def sum_everywhere(values):
    return pl.pallas_call(
        sum_kernel,
        out_shape=jax.ShapeDtypeStruct(values.shape, f32),
        in_specs=[VMEM_SPEC],
        out_specs=VMEM_SPEC,
        scratch_shapes=[
            pltpu.VMEM((SUM_SLOTS, *values.shape), f32),
            pltpu.SemaphoreType.DMA((SUM_COPIES,)),
            pltpu.SemaphoreType.DMA((SUM_COPIES,)),
        ],
        compiler_params=pltpu.CompilerParams(collective_id=2, has_side_effects=True),
        name="sum_everywhere",
    )(values)


def gather_blocks(shard_low):
    whole = lax.all_gather(shard_low, ("outer", "inner"), axis=0, tiled=True)
    return whole.reshape(-1, 8, D)


def scatter_blocks(grads, units):
    axes = ("outer", "inner")
    whole = grads.reshape(-1, D)[: lax.axis_size(axes) * units].astype(f32)
    return lax.psum_scatter(whole, axes, scatter_dimension=0, tiled=True)


def split_bias(vector):
    widths = [D, D, D, FF, D, 6 * D]
    pieces = []
    offset = 0
    for span_width in widths:
        pieces.append(lax.slice_in_dim(vector, offset, offset + span_width))
        offset = offset + span_width
    return pieces


def exact(left, right, dims):
    return lax.dot_general(
        left, right, dims, precision=lax.Precision.HIGHEST, preferred_element_type=jnp.float32
    )


def ada_selector(soft_cond, first_unit, units):
    groups = soft_cond.shape[0]
    spread = jnp.repeat(soft_cond.astype(jnp.float32), 6, axis=1)
    spread = jnp.pad(spread, ((0, 0), (units, units)))
    start = jnp.clip(first_unit - BLOCK_UNITS + units, 0, 6 * D + units)
    local = lax.dynamic_slice(spread, (jnp.int32(0), start), (groups, units))
    unit = first_unit - BLOCK_UNITS + jnp.arange(units, dtype=jnp.int32)
    part = (unit[:, None] % 6 == jnp.arange(6, dtype=jnp.int32)[None, :]) & (unit[:, None] >= 0)
    part = part.astype(jnp.float32)
    selector = local.T[:, :, None] * part[:, None, :]
    return selector.reshape(units, groups * 6), part


def adamw(parameter, gradient, first_state, second_state):
    first_new = BETA_FIRST * first_state + (1.0 - BETA_FIRST) * gradient
    second_new = BETA_SECOND * second_state + (1.0 - BETA_SECOND) * gradient * gradient
    first_hat = first_new / (1.0 - BETA_FIRST**STEP)
    second_hat = second_new / (1.0 - BETA_SECOND**STEP)
    updated = parameter - LEARN_RATE * (
        first_hat / (jnp.sqrt(second_hat) + ADAM_EPS) + WEIGHT_DECAY * parameter
    )
    return (updated, first_new, second_new)


def on_device(
    tokens,
    conditioning,
    column_sample,
    is_image,
    output_grad,
    weights,
    first_moment,
    second_moment,
    biases,
    bias_first,
    bias_second,
    kernels,
):
    columns = column_sample.shape[0]
    groups = conditioning.shape[0]
    units = weights.shape[0] // D
    axes = ("outer", "inner")
    first_unit = lax.axis_index(axes).astype(jnp.int32) * units
    shard = weights.reshape(units, D)
    shard_low = shard.astype(bf16)
    b_query, b_value, b_proj, b_up, b_down, b_ada = split_bias(biases)
    soft_cond = jax.nn.silu(conditioning).astype(bf16)
    selector, ada_part = ada_selector(soft_cond, first_unit, units)
    mods_part = tn_dot(selector.astype(bf16), shard_low)
    membership = (column_sample[:, None] == jnp.arange(groups, dtype=jnp.int32)[None, :]).astype(
        f32
    )
    video_cols = exact(membership, 1.0 - is_image.astype(f32)[:, None], (((1,), (0,)), ((), ())))
    b_qkv = jnp.stack([b_query, jnp.zeros((D,), f32), b_value])
    bias_args = (b_qkv, b_proj[None], b_up.reshape(4, D), b_down[None])
    video_plane = jnp.broadcast_to(video_cols, (columns, D))
    if kernels:
        eye = jnp.eye(6, dtype=f32)
        chosen = membership[None, :, :, None] * eye[:, None, None, :]
        chosen = jnp.pad(chosen.reshape(6 * columns, groups * 6), ((0, columns), (0, 0)))
        base = jnp.repeat(b_ada.reshape(6, D), columns, axis=0)
        base = jnp.concatenate([base, video_plane])
        flat, mods, *saved = gather_forward(
            shard_low.reshape(GROUPS8, 8, D), mods_part, chosen, base, tokens, output_grad,
            *bias_args,
        )
        flat = flat.reshape(-1, 8, D)
    else:
        flat = gather_blocks(shard_low)
        mods_all = lax.psum(mods_part, axes).reshape(groups, 6 * D) + b_ada
        mods = jnp.take(mods_all, column_sample, axis=0).reshape(columns, 6, D).transpose(1, 0, 2)
        mods = jnp.concatenate([mods, video_plane[None]])
        saved = forward(flat, tokens, output_grad, mods, *bias_args)
    (
        block_out, natural, input_att, proj, attended, branch, input_mlp, active, slope, grad_out,
        grad_gate,
    ) = saved
    operands = (
        flat, natural, active, slope, tokens, output_grad, mods, input_att, proj, attended, branch,
        input_mlp, grad_out,
    )
    if kernels:
        shard_sum, _, _, input_grad, small = backward_scatter(operands, grad_gate, membership.T)
        block_shard = shard_sum.reshape(units, D).astype(f32)
        grad_mods_all = small[: 6 * groups].reshape(6, groups, D)
        bias_sums = small[6 * groups : 6 * groups + 9]
    else:
        grads, input_grad, grad_mods, bias_sums = backward(*operands)
        grad_mods = jnp.concatenate([grad_mods, grad_gate[None]])
        mods_local = exact(membership, grad_mods, (((0,), (1,)), ((), ())))
        bias_sums, grad_mods_all = lax.psum((bias_sums, mods_local.transpose(1, 0, 2)), axes)
        block_shard = scatter_blocks(grads, units)
    grad_mods_all = grad_mods_all.transpose(1, 0, 2).reshape(groups, 6 * D)
    bias_head = jnp.concatenate([bias_sums[:1], bias_sums[2:4], bias_sums[5:9], bias_sums[4:5]])
    first_sum = jnp.concatenate([bias_head.reshape(-1), jnp.sum(grad_mods_all, axis=0)])
    mods_parts = grad_mods_all.reshape(groups * 6, D)
    ada_shard = exact(selector, mods_parts, (((1,), (0,)), ((), ())))
    unit = first_unit + jnp.arange(units, dtype=jnp.int32)
    grad_units = jnp.where(unit[:, None] >= BLOCK_UNITS, ada_shard, block_shard)
    products = exact(shard_low.astype(jnp.float32), mods_parts, (((1,), (1,)), ((), ())))
    products = jnp.sum(products.reshape(units, groups, 6) * ada_part[:, None, :], axis=2)
    spread = jnp.zeros((groups, 6 * D + 2 * units), jnp.float32)
    start = jnp.clip(first_unit - BLOCK_UNITS + units, 0, 6 * D + units)
    spread = lax.dynamic_update_slice(spread, products.T, (jnp.int32(0), start))
    grad_soft = jnp.sum(spread[:, units : units + 6 * D].reshape(groups, D, 6), axis=2)
    square_sum = jnp.sum(grad_units * grad_units)
    if kernels:
        rows = jnp.concatenate([grad_soft, jnp.full((8 - groups % 8, D), square_sum / D, f32)])
        rows = sum_everywhere(rows)
        grad_soft, square_sum = rows[:groups], jnp.sum(rows[groups])
    else:
        square_sum, grad_soft = lax.psum((square_sum, grad_soft), axes)
    silu_out, silu_back = jax.vjp(jax.nn.silu, conditioning)
    second_sum = silu_back(grad_soft)[0]
    grad_shard = grad_units.reshape(-1)
    grad_norm = jnp.sqrt(square_sum + jnp.sum(first_sum * first_sum))
    factor = jnp.minimum(1.0, CLIP_NORM / (grad_norm + 1e-06))
    new_weights, first_out, second_out = adamw(
        weights, grad_shard * factor, first_moment, second_moment
    )
    new_biases, bias_first_out, bias_second_out = adamw(
        biases, first_sum * factor, bias_first, bias_second
    )
    return (
        block_out,
        input_grad,
        second_sum,
        grad_norm,
        new_weights,
        first_out,
        second_out,
        new_biases,
        bias_first_out,
        bias_second_out,
    )


def solution(mesh):
    in_specs = (
        P(("outer", "inner"), None),
        P(),
        P(("outer", "inner")),
        P(),
        P(("outer", "inner"), None),
        P(("outer", "inner")),
        P(("outer", "inner")),
        P(("outer", "inner")),
        P(),
        P(),
        P(),
    )
    out_specs = (
        P(("outer", "inner"), None),
        P(("outer", "inner"), None),
        P(),
        P(),
        P(("outer", "inner")),
        P(("outer", "inner")),
        P(("outer", "inner")),
        P(),
        P(),
        P(),
    )
    kernels = dict(mesh.shape) == {"outer": 4, "inner": 8}
    return jax.shard_map(
        functools.partial(on_device, kernels=kernels), mesh=mesh, in_specs=in_specs, out_specs=out_specs, check_vma=False
    )
```

```python
import functools
import math

import jax
import jax.numpy as jnp
from jax import lax
from jax.experimental import pallas as pl
from jax.experimental.pallas import tpu as pltpu
from jax.sharding import PartitionSpec as P

D = 1152
H = 16
HD = 72
FF = 4608
FRAMES = 16
STEP = 8


NORM_EPS = 1e-06
LEARN_RATE = 0.02
BETA_FIRST = 0.5
BETA_SECOND = 0.55
ADAM_EPS = 1e-08
WEIGHT_DECAY = 0.01
CLIP_NORM = 1.0
BLOCK_UNITS = 4 * D + 2 * FF


MESH = pl.DeviceIdType.MESH
UNITS = 648
GROUPS8 = 81
QUART = 20
FIRST = 8
SECOND = QUART - FIRST
MAIN = 80
TAIL = 1
DEPTH = (4, 4, 3)
BASE = (0, 4, 8)


def flip(z, d):
    if d == 0:
        return z
    if d == 1:
        return z + 1 - 2 * (z % 2)
    if d == 2:
        return z + 2 - 4 * (z // 2)
    return 3 - z


class Place:
    def __init__(self):
        self.o = lax.axis_index("outer")
        self.i = lax.axis_index("inner")
        self.x, self.c = self.o // 2, self.o % 2
        self.z, self.y = self.i // 2, self.i % 2
        self.xo, self.co, self.yo = 1 - self.x, 1 - self.c, 1 - self.y

    def dev(self, dx=0, dc=0, dz=0, dy=0):
        x = self.xo if dx else self.x
        c = self.co if dc else self.c
        y = self.yo if dy else self.y
        return (x * 2 + c, flip(self.z, dz) * 2 + y)

    def greet(self):
        peers = [
            self.dev(dx=1), self.dev(dc=1), self.dev(dx=1, dc=1), self.dev(dy=1),
            self.dev(dz=1), self.dev(dz=2), self.dev(dz=3),
        ]
        barrier = pltpu.get_barrier_semaphore()
        for peer in peers:
            pl.semaphore_signal(barrier, inc=1, device_id=peer, device_id_type=MESH)
        pl.semaphore_wait(barrier, len(peers))


class Copies:
    def __init__(self, send_sems, recv_sems):
        self.send_sems, self.recv_sems = send_sems, recv_sems
        self.count = 0
        self.sent = []

    def slot(self):
        self.count += 1
        return self.count - 1

    def make(self, slot, src, dst, device):
        return pltpu.make_async_remote_copy(
            src_ref=src, dst_ref=dst, send_sem=self.send_sems.at[slot],
            recv_sem=self.recv_sems.at[slot], device_id=device, device_id_type=MESH,
        )

    def send(self, slot, src, dst, device, cond=None):
        def go():
            self.make(slot, src, dst, device).start()
        if cond is None:
            go()
        else:
            pl.when(cond)(go)
        self.sent.append((slot, src, dst, device, cond))

    def wait_recv(self, slot, dst, device, cond=None):
        def go():
            self.make(slot, dst, dst, device).wait_recv()
        if cond is None:
            go()
        else:
            pl.when(cond)(go)

    def wait_send(self, wanted):
        for entry in self.sent:
            if entry[0] == wanted:
                slot, src, dst, device, cond = entry

                def go():
                    self.make(slot, src, dst, device).wait_send()
                if cond is None:
                    go()
                else:
                    pl.when(cond)(go)
        self.sent = [entry for entry in self.sent if entry[0] != wanted]

    def drain(self):
        for slot, src, dst, device, cond in self.sent:
            def go(slot=slot, src=src, dst=dst, device=device):
                self.make(slot, src, dst, device).wait_send()
            if cond is None:
                go()
            else:
                pl.when(cond)(go)
        self.sent = []


def ok(zb, p):
    return None if DEPTH[p] == 4 else zb < DEPTH[p]


def both(a, b):
    if a is None:
        return b
    if b is None:
        return a
    return jnp.logical_and(a, b)


GATHER_COPIES = 3 * (3 + 5 + 4 * 4 + 8) + 7


def gather_stages(me, cp, shard, full, local_sems):
    def part(p, zb, yb, x, c, first=0, n=QUART):
        return full.at[p, zb, yb, pl.ds((2 * QUART * x + QUART * c + first), n)]

    def own_of(p):
        return both(me.o == p, ok(me.z, p))

    quarter = (2 * QUART * me.x + QUART * me.c)
    own_tail = pltpu.make_async_copy(
        shard.at[pl.ds(MAIN, TAIL)], full.at[me.o, me.z, me.y, pl.ds(MAIN, TAIL)], local_sems.at[0]
    )
    own_tail.start()

    def local_quarter(p):
        return pltpu.make_async_copy(
            shard.at[pl.ds(quarter, QUART)], part(p, me.z, me.y, me.x, me.c), local_sems.at[1]
        )

    slots = {}

    def s0(p):
        @pl.when(own_of(p))
        def _():
            local_quarter(p).start()
        for dx, dc in ((1, 0), (0, 1), (1, 1)):
            s = slots["s0", p, dx, dc] = cp.slot()
            x = me.xo if dx else me.x
            c = me.co if dc else me.c
            cp.send(
                s, shard.at[pl.ds((2 * QUART * x + QUART * c), QUART)],
                part(p, me.z, me.y, x, c), me.dev(dx=dx, dc=dc), own_of(p),
            )

    def s0_wait(p):
        @pl.when(own_of(p))
        def _():
            local_quarter(p).wait()
        ox, oc = p // 2, p % 2
        for dx, dc in ((1, 0), (0, 1), (1, 1)):
            x = me.xo if dx else me.x
            c = me.co if dc else me.c
            cond = both(jnp.logical_and(x == ox, c == oc), ok(me.z, p))
            cp.wait_recv(
                slots["s0", p, dx, dc], part(p, me.z, me.y, me.x, me.c), me.dev(dx=dx, dc=dc), cond
            )

    def spread(p, d):
        zb = place(d)
        mine = part(p, zb, me.y, me.x, me.c)
        s = slots["y1", p, d] = cp.slot()
        cp.send(s, mine, mine, me.dev(dy=1), ok(zb, p))
        s = slots["x1", p, d] = cp.slot()
        cp.send(s, mine, mine, me.dev(dx=1), ok(zb, p))

    def place(e):
        return (me.z, flip(me.z, 1), 2 - me.z // 2, 3 - 3 * (me.z // 2))[e]

    inner = (me.z + 1) // 2 == 1
    outer = jnp.logical_not(inner)

    def pass_on(p, zb, name, device, cond):
        view = part(p, zb, me.y, me.x, me.c)
        s = slots[name, p] = cp.slot()
        cp.send(s, view, view, device, both(cond, ok(zb, p)))

    def arrive(p, e, name, device, cond):
        zb = place(e)
        view = part(p, zb, me.y, me.x, me.c)
        cp.wait_recv(slots[name, p], view, device, both(cond, ok(zb, p)))

    def s1(p):
        s0_wait(p)
        pass_on(p, me.z, "own to 1", me.dev(dz=1), None)
        pass_on(p, me.z, "own to 3", me.dev(dz=3), inner)
        spread(p, 0)

    def s2(p):
        arrive(p, 1, "own to 1", me.dev(dz=1), None)
        pass_on(p, place(1), "1 to 3", me.dev(dz=3), inner)
        spread(p, 1)
        arrive(p, 2, "own to 3", me.dev(dz=3), inner)
        pass_on(p, place(2), "near to 1", me.dev(dz=1), inner)
        arrive(p, 2, "near to 1", me.dev(dz=1), outer)
        spread(p, 2)
        arrive(p, 3, "1 to 3", me.dev(dz=3), inner)
        pass_on(p, place(3), "far to 1", me.dev(dz=1), inner)
        arrive(p, 3, "far to 1", me.dev(dz=1), outer)
        spread(p, 3)

    def s3(p, entries=(0, 1, 2, 3)):
        for d in entries:
            zb = place(d)
            cp.wait_recv(
                slots["y1", p, d], part(p, zb, me.yo, me.x, me.c), me.dev(dy=1), ok(zb, p)
            )
            s = slots["x2", p, d] = cp.slot()
            out = part(p, zb, me.yo, me.x, me.c, 0, FIRST)
            cp.send(s, out, out, me.dev(dx=1), ok(zb, p))
            cp.wait_recv(
                slots["x1", p, d], part(p, zb, me.y, me.xo, me.c), me.dev(dx=1), ok(zb, p)
            )
            s = slots["y2", p, d] = cp.slot()
            out = part(p, zb, me.y, me.xo, me.c, FIRST, SECOND)
            cp.send(s, out, out, me.dev(dy=1), ok(zb, p))

    def lane(p, zb, x, c):
        return full.at[p, zb, :, pl.ds((2 * QUART * x + QUART * c), QUART)]

    def s4(p):
        for d in (0, 1, 2, 3):
            zb = place(d)
            cp.wait_recv(
                slots["x2", p, d], part(p, zb, me.yo, me.xo, me.c, 0, FIRST), me.dev(dx=1),
                ok(zb, p),
            )
            cp.wait_recv(
                slots["y2", p, d], part(p, zb, me.yo, me.xo, me.c, FIRST, SECOND), me.dev(dy=1),
                ok(zb, p),
            )
            for h in (0, 1):
                s = slots["c", p, d, h] = cp.slot()
                cp.send(s, lane(p, zb, h, me.c), lane(p, zb, h, me.c), me.dev(dc=1), ok(zb, p))

    def s5(p):
        for d in (0, 1, 2, 3):
            zb = place(d)
            for h in (0, 1):
                cp.wait_recv(
                    slots["c", p, d, h], lane(p, zb, h, me.co), me.dev(dc=1), ok(zb, p)
                )

    tails = pl.ds(MAIN, TAIL)

    def t1():
        own_tail.wait()
        block = full.at[me.o, me.z, me.y, tails]
        for d in (1, 2, 3):
            s = slots["tz", d] = cp.slot()
            cp.send(s, block, block, me.dev(dz=d))

    def t2():
        for d in (1, 2, 3):
            zb = flip(me.z, d)
            cp.wait_recv(slots["tz", d], full.at[me.o, zb, me.y, tails], me.dev(dz=d))
        s = slots["ty"] = cp.slot()
        block = full.at[me.o, :, me.y, tails]
        cp.send(s, block, block, me.dev(dy=1))

    def t3():
        cp.wait_recv(slots["ty"], full.at[me.o, :, me.yo, tails], me.dev(dy=1))
        s = slots["tx"] = cp.slot()
        block = full.at[me.o, :, :, tails]
        cp.send(s, block, block, me.dev(dx=1))

    def t4():
        cp.wait_recv(slots["tx"], full.at[me.xo * 2 + me.c, :, :, tails], me.dev(dx=1))
        for h in (0, 1):
            s = slots["tc", h] = cp.slot()
            block = full.at[h * 2 + me.c, :, :, tails]
            cp.send(s, block, block, me.dev(dc=1))

    def t5():
        for h in (0, 1):
            cp.wait_recv(slots["tc", h], full.at[h * 2 + me.co, :, :, tails], me.dev(dc=1))

    return dict(s0=s0, s1=s1, s2=s2, s3=s3, s4=s4, s5=s5, t1=t1, t2=t2, t3=t3, t4=t4, t5=t5)


SCATTER_COPIES = 3 * (4 * 2 + 4 * 4 + 3 + 3) + 8
RING = 6
ORDER = (3, 2, 1, 0)
f32 = jnp.float32


def guarded(cond, fn):
    if cond is None:
        fn()
    else:
        pl.when(cond)(fn)


def add_rows(dst, srcs, n):
    step = 2 if n % 2 == 0 else 1

    def body(j, carry):
        at = pl.ds(j * step, step)
        total = srcs[0][at].astype(f32)
        for src in srcs[1:]:
            total = total + src[at].astype(f32)
        dst[at] = total.astype(dst.dtype)
        return carry

    lax.fori_loop(0, n // step, body, 0)


def scatter_stages(
    me, cp, partial, out, other, own, stage, rx2, ry2, rx1, ry1, rz, final, tail, tail_in, tail_z,
    local_sems, credit,
):
    slots = {}

    def block(k):
        p, d = 2 - k // 4, ORDER[k % 4]
        zb = flip(me.z, d)
        return p, d, zb, ok(zb, p), k % RING

    def exchange(p):
        for d in ORDER:
            zb = flip(me.z, d)
            for h in (0, 1):
                s = slots["c", p, d, h] = cp.slot()
                view = pl.ds(2 * QUART * h + QUART * me.co, QUART)
                cp.send(
                    s, partial.at[p, zb, :, view], other.at[p, zb, :, h], me.dev(dc=1), ok(zb, p)
                )

    def loads(k):
        p, d, zb, cond, slot = block(k)
        copies = []
        for h in (0, 1):
            view = pl.ds(2 * QUART * h + QUART * me.c, QUART)
            copies.append(
                pltpu.make_async_copy(
                    partial.at[p, zb, :, view], own.at[slot, :, h], local_sems.at[h]
                )
            )
            copies.append(
                pltpu.make_async_copy(other.at[p, zb, :, h], stage.at[h], local_sems.at[2 + h])
            )
        return copies

    def prefetch(k):
        p, d, zb, cond, slot = block(k)
        if k >= RING:
            old = block(k - RING)
            for name in ("x2", "y2", "x1", "y1", "z"):
                if (name, old[0], old[1]) in slots:
                    cp.wait_send(slots[name, old[0], old[1]])
        for h in (0, 1):
            cp.wait_recv(slots["c", p, d, h], other.at[p, zb, :, h], me.dev(dc=1), cond)

        def go():
            for copy in loads(k):
                copy.start()

        guarded(cond, go)

    def fold(k):
        p, d, zb, cond, slot = block(k)

        def go():
            for copy in loads(k):
                copy.wait()

            def body(q, carry):
                y, h = q // 2, q % 2
                add_rows(own.at[slot, y, h], [own.at[slot, y, h], stage.at[h, y]], QUART)
                return carry

            lax.fori_loop(0, 4, body, 0)

        guarded(cond, go)
        if k >= RING:
            pl.semaphore_wait(credit.at[0], 1)
            pl.semaphore_wait(credit.at[1], 1)
        far = own.at[slot, me.yo, me.xo]
        s = slots["x2", p, d] = cp.slot()
        cp.send(s, far.at[pl.ds(0, FIRST)], rx2.at[slot], me.dev(dx=1), cond)
        s = slots["y2", p, d] = cp.slot()
        cp.send(s, far.at[pl.ds(FIRST, SECOND)], ry2.at[slot], me.dev(dy=1), cond)

    def second(k):
        p, d, zb, cond, slot = block(k)
        cp.wait_recv(slots["x2", p, d], rx2.at[slot], me.dev(dx=1), cond)
        view = own.at[slot, me.yo, me.x, pl.ds(0, FIRST)]
        guarded(cond, lambda: add_rows(view, [view, rx2.at[slot]], FIRST))
        s = slots["y1", p, d] = cp.slot()
        cp.send(s, own.at[slot, me.yo, me.x], ry1.at[slot], me.dev(dy=1), cond)
        cp.wait_recv(slots["y2", p, d], ry2.at[slot], me.dev(dy=1), cond)
        view2 = own.at[slot, me.y, me.xo, pl.ds(FIRST, SECOND)]
        guarded(cond, lambda: add_rows(view2, [view2, ry2.at[slot]], SECOND))
        s = slots["x1", p, d] = cp.slot()
        cp.send(s, own.at[slot, me.y, me.xo], rx1.at[slot], me.dev(dx=1), cond)

    def third(k):
        p, d, zb, cond, slot = block(k)
        cp.wait_recv(slots["y1", p, d], ry1.at[slot], me.dev(dy=1), cond)
        cp.wait_recv(slots["x1", p, d], rx1.at[slot], me.dev(dx=1), cond)
        view = own.at[slot, me.y, me.x]
        guarded(cond, lambda: add_rows(view, [view, ry1.at[slot], rx1.at[slot]], QUART))
        if k + RING < 12:
            pl.semaphore_signal(
                credit.at[0], inc=1, device_id=me.dev(dx=1), device_id_type=MESH
            )
            pl.semaphore_signal(
                credit.at[1], inc=1, device_id=me.dev(dy=1), device_id_type=MESH
            )
        if d:
            s = slots["z", p, d] = cp.slot()
            cp.send(s, view, rz.at[p, d - 1], me.dev(dz=d), cond)

    def quarter(x, c):
        return out.at[pl.ds(2 * QUART * x + QUART * c, QUART)]

    def settle(p):
        mine = ok(me.z, p)
        for d in (1, 2, 3):
            cp.wait_recv(slots["z", p, d], rz.at[p, d - 1], me.dev(dz=d), mine)
        view = own.at[(4 * (2 - p) + 3) % RING, me.y, me.x]
        guarded(
            mine,
            lambda: add_rows(final.at[p], [view, rz.at[p, 0], rz.at[p, 1], rz.at[p, 2]], QUART),
        )
        ox, oc = p // 2, p % 2
        for dx, dc in ((1, 0), (0, 1), (1, 1)):
            x = me.xo if dx else me.x
            c = me.co if dc else me.c
            s = slots["f", p, dx, dc] = cp.slot()
            cond = both(jnp.logical_and(x == ox, c == oc), mine)
            cp.send(s, final.at[p], quarter(me.x, me.c), me.dev(dx=dx, dc=dc), cond)

        @pl.when(both(me.o == p, mine))
        def _():
            pltpu.make_async_copy(final.at[p], quarter(me.x, me.c), local_sems.at[4]).start()

    def finish(p):
        mine = both(me.o == p, ok(me.z, p))
        for dx, dc in ((1, 0), (0, 1), (1, 1)):
            x = me.xo if dx else me.x
            c = me.co if dc else me.c
            cp.wait_recv(slots["f", p, dx, dc], quarter(x, c), me.dev(dx=dx, dc=dc), mine)

        @pl.when(mine)
        def _():
            pltpu.make_async_copy(final.at[p], quarter(me.x, me.c), local_sems.at[4]).wait()

    def tail_load():
        return pltpu.make_async_copy(
            partial.at[:, :, :, pl.ds(MAIN, TAIL)], tail, local_sems.at[5]
        )

    def tail_add(o, zb, yb, srcs):
        add_rows(tail.at[o, zb, yb], [tail.at[o, zb, yb]] + srcs, TAIL)

    def t0():
        tail_load().start()

    def t1():
        tail_load().wait()
        for h in (0, 1):
            s = slots["tc", h] = cp.slot()
            cp.send(s, tail.at[2 * h + me.co], tail_in.at[h], me.dev(dc=1))

    def t2():
        for h in (0, 1):
            cp.wait_recv(slots["tc", h], tail_in.at[h], me.dev(dc=1))

            def body(q, carry):
                tail_add(2 * h + me.c, q // 2, q % 2, [tail_in.at[h, q // 2, q % 2]])
                return carry
            lax.fori_loop(0, 8, body, 0)
        s = slots["tx"] = cp.slot()
        cp.send(s, tail.at[me.xo * 2 + me.c], tail_in.at[2], me.dev(dx=1))

    def t3():
        cp.wait_recv(slots["tx"], tail_in.at[2], me.dev(dx=1))

        def body(q, carry):
            tail_add(me.o, q // 2, q % 2, [tail_in.at[2, q // 2, q % 2]])
            return carry
        lax.fori_loop(0, 8, body, 0)
        s = slots["ty"] = cp.slot()
        cp.send(s, tail.at[me.o, :, me.yo], tail_in.at[3, :, 0], me.dev(dy=1))

    def t4():
        cp.wait_recv(slots["ty"], tail_in.at[3, :, 0], me.dev(dy=1))

        def body(q, carry):
            tail_add(me.o, q, me.y, [tail_in.at[3, q, 0]])
            return carry
        lax.fori_loop(0, 4, body, 0)
        for d in (1, 2, 3):
            s = slots["tz", d] = cp.slot()
            cp.send(s, tail.at[me.o, flip(me.z, d), me.y], tail_z.at[d - 1], me.dev(dz=d))

    def t5():
        for d in (1, 2, 3):
            cp.wait_recv(slots["tz", d], tail_z.at[d - 1], me.dev(dz=d))
        tail_add(me.o, me.z, me.y, [tail_z.at[0], tail_z.at[1], tail_z.at[2]])
        copy = pltpu.make_async_copy(
            tail.at[me.o, me.z, me.y], out.at[pl.ds(MAIN, TAIL)], local_sems.at[5]
        )
        copy.start()
        copy.wait()

    return dict(
        exchange=exchange, prefetch=prefetch, fold=fold, second=second, third=third,
        settle=settle, finish=finish, tails=(t0, t1, t2, t3, t4, t5),
    )


def scatter_scratch():
    bf = jnp.bfloat16
    return [
        pltpu.VMEM((RING, 2, 2, QUART, 8, D), bf),
        pltpu.VMEM((2, 2, QUART, 8, D), bf),
        pltpu.VMEM((RING, FIRST, 8, D), bf),
        pltpu.VMEM((RING, SECOND, 8, D), bf),
        pltpu.VMEM((RING, QUART, 8, D), bf),
        pltpu.VMEM((RING, QUART, 8, D), bf),
        pltpu.VMEM((3, 3, QUART, 8, D), bf),
        pltpu.VMEM((3, QUART, 8, D), bf),
        pltpu.VMEM((4, 4, 2, TAIL, 8, D), bf),
        pltpu.VMEM((4, 4, 2, TAIL, 8, D), bf),
        pltpu.VMEM((3, TAIL, 8, D), bf),
        pltpu.SemaphoreType.DMA((6,)),
        pltpu.SemaphoreType.REGULAR((2,)),
    ]


bf16 = jnp.bfloat16
MATS = D // 8
AT_PROJ = 3 * MATS
AT_UP = 4 * MATS
AT_DOWN = 8 * MATS
ROOT = math.sqrt(2.0 / math.pi)
CUBIC = 0.044715


def nn_dot(left, right):
    return lax.dot_general(left, right, (((1,), (0,)), ((), ())), preferred_element_type=f32)


def nt_dot(left, right):
    return lax.dot_general(left, right, (((1,), (1,)), ((), ())), preferred_element_type=f32)


def tn_dot(left, right):
    return lax.dot_general(left, right, (((0,), (0,)), ((), ())), preferred_element_type=f32)


def square(ref):
    return ref[...].reshape(D, D)


def norm_rows(values):
    centered = values - jnp.mean(values, axis=-1, keepdims=True)
    inverse = lax.rsqrt(jnp.mean(centered * centered, axis=-1, keepdims=True) + NORM_EPS)
    return centered * inverse, inverse


def norm_rows_back(grad, normed, inverse):
    return inverse * (
        grad
        - jnp.mean(grad, axis=-1, keepdims=True)
        - normed * jnp.mean(grad * normed, axis=-1, keepdims=True)
    )


def frames_of(c):
    return pl.ds(pl.multiple_of(c * FRAMES, FRAMES), FRAMES)


def over_columns(count, body):
    def step(c, carry):
        body(c, frames_of(c), pl.ds(c, 1))
        return carry

    lax.fori_loop(0, count, step, 0)


def split_rows(src, spread, put, ways):
    units = src.shape[0] * 8
    rows = units // ways
    for q in range(9):
        lanes = slice(128 * q, 128 * q + 128)
        spread[q, pl.ds(0, units)] = src[:, :, lanes].astype(f32).reshape(units, 128)
        for w in range(ways):
            part = spread[q, pl.ds(w, rows, stride=ways), :]
            put(w, lanes, part.reshape(rows // 8, 8, 128).astype(bf16))


def head_window(h):
    first = min(HD * h // 128, 7) * 128
    lane = lax.broadcasted_iota(jnp.int32, (1, 256), 1) + first
    mask = jnp.logical_and(lane >= HD * h, lane < HD * h + HD)
    return slice(first, first + 256), jnp.where(mask, 1.0, 0.0).astype(bf16)


def same_column():
    row = lax.broadcasted_iota(jnp.int32, (128, 128), 0)
    col = lax.broadcasted_iota(jnp.int32, (128, 128), 1)
    return lax.shift_right_logical(row, 4) == lax.shift_right_logical(col, 4)


SCORE_SCALE = 1.0 / math.sqrt(HD)


def head_probabilities(masked_queries, keys, inside):
    scores = jnp.where(inside, nt_dot(masked_queries, keys) * SCORE_SCALE, -1e30)
    grown = jnp.exp(scores - jnp.max(scores, axis=-1, keepdims=True))
    return grown / jnp.sum(grown, axis=-1, keepdims=True)


SUM_COPIES = 6
SUM_SLOTS = 10


def sum_stages(me, cp, mine, buf):
    slots = {}

    def send(name, src, dst, device):
        slots[name] = cp.slot()
        cp.send(slots[name], src, dst, device)

    def m1():
        send("c", mine, buf.at[0], me.dev(dc=1))

    def m2():
        cp.wait_recv(slots["c"], buf.at[0], me.dev(dc=1))
        buf[1] = mine[...] + buf[0]
        send("x", buf.at[1], buf.at[2], me.dev(dx=1))

    def m3():
        cp.wait_recv(slots["x"], buf.at[2], me.dev(dx=1))
        buf[3] = buf[1] + buf[2]
        send("y", buf.at[3], buf.at[4], me.dev(dy=1))

    def m4():
        cp.wait_recv(slots["y"], buf.at[4], me.dev(dy=1))
        buf[5] = buf[3] + buf[4]
        buf[6 + me.z] = buf[5]
        for d in (1, 2, 3):
            send(d, buf.at[5], buf.at[6 + me.z], me.dev(dz=d))

    def total():
        for d in (1, 2, 3):
            cp.wait_recv(slots[d], buf.at[6 + flip(me.z, d)], me.dev(dz=d))
        return (buf[6] + buf[7]) + (buf[8] + buf[9])

    return m1, m2, m3, m4, total


def forward_body(
    weights, tokens, upstream, mods, b_qkv, b_proj, b_up, b_down,
    block_out, natural, input_att, proj_out, attended, branch, input_mlp, active_out, slope_out,
    grad_out, grad_gate, grads, held, stage, spread, acc, hid, proj, active, slope, woven,
    copy_sems, ready,
):
    columns = mods.shape[1]

    def fetch(first, groups, slot):
        return pltpu.make_async_copy(
            weights.at[pl.ds(first, groups)], stage.at[slot, pl.ds(0, groups)], copy_sems.at[slot]
        )

    def whole(mat, slot):
        return pltpu.make_async_copy(
            weights.at[pl.ds(mat * MATS, MATS)], held.at[slot], copy_sems.at[2 + slot]
        )

    def save(mat, slot):
        return pltpu.make_async_copy(held.at[slot], natural.at[mat], copy_sems.at[10 + mat])

    def keep(src, dst, n):
        return pltpu.make_async_copy(src, dst, copy_sems.at[17 + n])

    def unweave(first, ways, slot0, blocks=9):
        groups = 16 * ways
        fetch(first, groups, 0).start()

        def step(j, carry):
            slot = lax.rem(j, 2)
            fetch(first + j * groups, groups, slot).wait()

            @pl.when(j + 1 < blocks)
            def _():
                fetch(first + (j + 1) * groups, groups, 1 - slot).start()

            def put(w, lanes, block):
                held[slot0 + w, pl.ds(j * 16, 16), :, lanes] = block

            split_rows(stage.at[slot, pl.ds(0, groups)], spread, put, ways)
            return carry

        lax.fori_loop(0, blocks, step, 0)

    def first_norm(c, rows, at):
        normed, _ = norm_rows(tokens[rows].astype(f32))
        input_att[rows] = (normed * (1.0 + mods[1, at]) + mods[0, at]).astype(bf16)

    over_columns(columns, first_norm)
    ready("qkv")
    whole(3, 3).start()
    unweave(0, 3, 0)
    for p in range(3):
        save(p, p).start()

    for p in range(3):
        proj[p] = (nn_dot(input_att[...], square(held.at[p])) + b_qkv[pl.ds(p, 1)]).astype(bf16)
        ready("project", p)
    keep(proj, proj_out, 0).start()

    inside = same_column()

    def attend(g, carry):
        rows = pl.ds(pl.multiple_of(g * 128, 128), 128)
        acc[pl.ds(0, 128)] = jnp.zeros((128, D), f32)
        for h in range(H):
            window, mask = head_window(h)
            probs = head_probabilities(proj[0, rows, window] * mask, proj[1, rows, window], inside)
            acc[pl.ds(0, 128), window] += nn_dot(probs.astype(bf16), proj[2, rows, window] * mask)
        attended[rows] = acc[pl.ds(0, 128)].astype(bf16)
        return carry

    for g in range(columns * FRAMES // 128):
        lax.fori_loop(g, g + 1, attend, 0)
        ready("attend", g)
    ready("proj")
    whole(3, 3).wait()
    branch[...] = nn_dot(attended[...], square(held.at[3])) + b_proj[...]
    for p in range(3):
        save(p, p).wait()

    def second_norm(c, rows, at):
        middle = tokens[rows].astype(f32) + mods[2, at] * branch[rows]
        normed, _ = norm_rows(middle)
        input_mlp[rows] = (normed * (1.0 + mods[4, at]) + mods[3, at]).astype(bf16)
        grad_block = jnp.where(mods[6, at] > 0.5, upstream[rows].astype(f32), 0.0)
        grad_out[rows] = (grad_block * mods[5, at]).astype(bf16)

    over_columns(columns, second_norm)
    ready("up")
    unweave(AT_UP, 4, 4)
    for b in range(4):
        save(3 + b, 4 + b).start()

    def raise_(b, carry):
        hid[...] = nn_dot(input_mlp[...], square(held.at[4 + b])) + b_up[pl.ds(b, 1)]

        def gelu(c, rows, at):
            v = hid[rows]
            sq = v * v
            t = jnp.tanh(ROOT * (v + CUBIC * sq * v))
            half = 0.5 * (1.0 + t)
            active[b, rows] = (v * half).astype(bf16)
            rise = half + (0.5 * ROOT) * v * (1.0 - t * t) * (1.0 + 3.0 * CUBIC * sq)
            for q in range(9):
                slope[b, q, rows] = rise[:, 128 * q : 128 * q + 128]

        over_columns(columns, gelu)
        return carry

    for b in range(4):
        lax.fori_loop(b, b + 1, raise_, 0)
        ready("raise", b)
    keep(active, active_out, 1).start()
    keep(slope, slope_out, 2).start()
    whole(8, 0).start()

    def stash(b, r):
        return pltpu.make_async_copy(
            woven.at[pl.ds(48 * r, 48)], grads.at[pl.ds(AT_DOWN + b * MATS + 48 * r, 48)],
            copy_sems.at[20 + r],
        )

    for b in range(4):
        for r in range(3):
            part = tn_dot(active[b, :, 384 * r : 384 * r + 384], grad_out[...])
            if b:
                stash(b - 1, r).wait()
            woven[pl.ds(48 * r, 48)] = part.reshape(48, 8, D).astype(bf16)
            stash(b, r).start()
        ready("outer", b)
    acc[...] = jnp.broadcast_to(b_down[...], acc.shape)
    whole(8, 0).wait()
    acc[...] += nn_dot(active[0], square(held.at[0]))
    ready("down")
    for b in range(1, 4):
        whole(8 + b, b).start()
    for b in range(1, 4):
        whole(8 + b, b).wait()
        acc[...] += nn_dot(active[b], square(held.at[b]))

    def last(c, rows, at):
        x = tokens[rows].astype(f32)
        middle = x + mods[2, at] * branch[rows]
        video = mods[6, at] > 0.5
        outcome = acc[rows]
        block_out[rows] = jnp.where(video, middle + mods[5, at] * outcome, x)
        grad_block = jnp.where(video, upstream[rows].astype(f32), 0.0)
        grad_gate[at] = jnp.sum(grad_block * outcome, axis=0, keepdims=True)

    over_columns(columns, last)
    for b in range(4):
        save(3 + b, 4 + b).wait()
    keep(proj, proj_out, 0).wait()
    keep(active, active_out, 1).wait()
    keep(slope, slope_out, 2).wait()
    for r in range(3):
        stash(3, r).wait()


def forward_kernel(*refs):
    forward_body(*refs, lambda name, step=0: None)


def gather_forward_kernel(
    flat_shard, selector, chosen, base, tokens, upstream, b_qkv, b_proj, b_up, b_down,
    full, mods, shard, *refs,
):
    refs, (partial, sums, send_sems, recv_sems, local_sems) = refs[:-5], refs[-5:]
    lines = refs[-3].reshape(4 * 9 * tokens.shape[0], 128)
    arrival = pltpu.make_async_copy(
        flat_shard, lines.at[pl.ds(0, 9 * UNITS)], local_sems.at[1]
    )
    arrival.start()
    arrival.wait()

    def regroup(j, carry):
        for q in range(9):
            part = lines[pl.ds(72 * j + q, 8, stride=9), :]
            shard[j, :, 128 * q : 128 * q + 128] = part.astype(bf16)
        return carry

    lax.fori_loop(0, GROUPS8, regroup, 0)
    partial[...] = nn_dot(selector[...], shard[...].reshape(UNITS, D))
    me = Place()
    cp = Copies(send_sems, recv_sems)
    st = gather_stages(me, cp, shard, full, local_sems)
    s0, s1, s2, s3, s4, s5 = (st["s%d" % n] for n in range(6))
    t1, t2, t3, t4, t5 = (st["t%d" % n] for n in range(1, 6))
    m1, m2, m3, m4, total = sum_stages(me, cp, partial, sums)
    me.greet()
    m1()
    s0(0)
    s0(1)
    s0(2)
    m2()
    s1(0)
    s1(1)
    m3()
    t1()
    s2(0)
    m4()
    t2()
    s1(2)
    s3(0)
    t3()
    s2(1)
    t4()
    table = exact(chosen[...], total(), (((1,), (0,)), ((), ()))) + base[...]
    columns = mods.shape[1]
    for n in range(7):
        mods[n] = table[n * columns : (n + 1) * columns]

    def ready(name, step=0):
        if name == "qkv":
            s4(0)
            t5()
            s5(0)
        elif name == "project":
            s3(1, (step,))
        elif name == "attend":
            if step == 0:
                s3(1, (3,))
            elif step == 1:
                s2(2)
            else:
                s4(1)
        elif name == "up":
            s5(1)
        elif name == "raise":
            s3(2, (step,))
        elif name == "down":
            s4(2)
            s5(2)

    forward_body(
        full.reshape(4 * 4 * 2 * GROUPS8, 8, D), tokens, upstream, mods, b_qkv, b_proj, b_up,
        b_down, *refs, ready,
    )
    cp.drain()


def forward_shapes(rows, columns):
    shape = jax.ShapeDtypeStruct
    return [
        shape((rows, D), f32),
        shape((7, MATS, 8, D), bf16),
        shape((rows, D), bf16),
        shape((3, rows, D), bf16),
        shape((rows, D), bf16),
        shape((rows, D), f32),
        shape((rows, D), bf16),
        shape((4, rows, D), bf16),
        shape((4, 9, rows, 128), f32),
        shape((rows, D), bf16),
        shape((columns, D), f32),
        shape((32 * UNITS // 8, 8, D), bf16),
    ]


VMEM_SPEC = pl.BlockSpec(memory_space=pltpu.VMEM)
HBM_SPEC = pl.BlockSpec(memory_space=pl.ANY)
FORWARD_SPECS = [
    VMEM_SPEC, HBM_SPEC, VMEM_SPEC, HBM_SPEC, VMEM_SPEC, VMEM_SPEC, VMEM_SPEC, HBM_SPEC, HBM_SPEC,
    VMEM_SPEC, VMEM_SPEC, HBM_SPEC,
]


def forward_scratch(rows):
    return [
        pltpu.VMEM((8, MATS, 8, D), bf16),
        pltpu.VMEM((2, 64, 8, D), bf16),
        pltpu.VMEM((9, 512, 128), f32),
        pltpu.VMEM((rows, D), f32),
        pltpu.VMEM((rows, D), f32),
        pltpu.VMEM((3, rows, D), bf16),
        pltpu.VMEM((4, rows, D), bf16),
        pltpu.VMEM((4, 9, rows, 128), f32),
        pltpu.VMEM((MATS, 8, D), bf16),
        pltpu.SemaphoreType.DMA((23,)),
    ]


def forward(weights, tokens, upstream, mods, b_qkv, b_proj, b_up, b_down):
    rows = tokens.shape[0]
    return pl.pallas_call(
        forward_kernel,
        out_shape=forward_shapes(rows, mods.shape[1]),
        in_specs=[HBM_SPEC] + [VMEM_SPEC] * 7,
        out_specs=FORWARD_SPECS,
        scratch_shapes=forward_scratch(rows),
        compiler_params=pltpu.CompilerParams(vmem_limit_bytes=62 * 2**20),
        name="block_forward",
    )(weights, tokens, upstream, mods, b_qkv, b_proj, b_up, b_down)


def gather_forward(
    flat_shard, selector, chosen, base, tokens, upstream, b_qkv, b_proj, b_up, b_down
):
    rows = tokens.shape[0]
    columns = rows // FRAMES
    copies = GATHER_COPIES + SUM_COPIES
    return pl.pallas_call(
        gather_forward_kernel,
        out_shape=[
            jax.ShapeDtypeStruct((4, 4, 2, GROUPS8, 8, D), bf16),
            jax.ShapeDtypeStruct((7, columns, D), f32),
            jax.ShapeDtypeStruct((GROUPS8, 8, D), bf16),
        ]
        + forward_shapes(rows, columns),
        in_specs=[HBM_SPEC] + [VMEM_SPEC] * 9,
        out_specs=[HBM_SPEC, VMEM_SPEC, VMEM_SPEC] + FORWARD_SPECS,
        scratch_shapes=forward_scratch(rows)
        + [
            pltpu.VMEM((selector.shape[0], D), f32),
            pltpu.VMEM((SUM_SLOTS, selector.shape[0], D), f32),
            pltpu.SemaphoreType.DMA((copies,)),
            pltpu.SemaphoreType.DMA((copies,)),
            pltpu.SemaphoreType.DMA((2,)),
        ],
        compiler_params=pltpu.CompilerParams(
            collective_id=0, has_side_effects=True, vmem_limit_bytes=63 * 2**20
        ),
        name="gather_forward",
    )(flat_shard, selector, chosen, base, tokens, upstream, b_qkv, b_proj, b_up, b_down)


UP_RUNS = ((0, 256), (256, 256), (512, 256), (768, 256), (1024, 128))
QKV_RUNS = ((0, 384), (384, 384), (768, 384))


def backward_body(
    weights, natural, slope, tokens, upstream, mods, input_att, proj, attended, branch,
    input_mlp, grad_out,
    grads, input_grad, grad_mods, bias_sums,
    held, woven, spread, grad_hidden, grad_branch, grad_att, acc, copy_sems, tick,
):
    columns = mods.shape[1]
    row_count = columns * FRAMES

    def fetch(first, slot):
        return pltpu.make_async_copy(natural.at[first], held.at[slot], copy_sems.at[slot])

    def flat_mat(first, slot):
        return pltpu.make_async_copy(
            weights.at[pl.ds(first, MATS)], held.at[slot], copy_sems.at[slot]
        )

    def stream(b, slot):
        at = pl.ds(pl.multiple_of(slot * row_count, row_count), row_count)
        return (
            flat_mat(AT_DOWN + b * MATS, slot),
            pltpu.make_async_copy(slope.at[b], spread.at[:, at], copy_sems.at[4 + slot]),
        )

    def store(first, offset, groups, n):
        return pltpu.make_async_copy(
            woven.at[pl.ds(offset, groups)], grads.at[pl.ds(first, groups)], copy_sems.at[6 + n]
        )

    bias_sums[...] = jnp.zeros_like(bias_sums)

    def add_bias(row, values):
        bias_sums[pl.ds(row, 1)] += jnp.sum(values.astype(f32), axis=0, keepdims=True)

    def outer(first, left, right):
        for r in range(3):
            part = tn_dot(left[:, 384 * r : 384 * r + 384], right[...])
            woven[pl.ds(48 * r, 48)] = part.reshape(48, 8, D).astype(bf16)
            store(first + 48 * r, 48 * r, 48, r).start()

    for copy in stream(0, 0):
        copy.start()

    def down(b, carry):
        slot = lax.rem(b, 2)
        for copy in stream(b, slot):
            copy.wait()

        @pl.when(b < 3)
        def _():
            for copy in stream(b + 1, 1 - slot):
                copy.start()

        acc[...] = nt_dot(grad_out[...], square(held.at[slot]))

        def through(c, rows, at):
            there = pl.ds(pl.multiple_of(slot * row_count + c * FRAMES, FRAMES), FRAMES)
            rise = jnp.concatenate([spread[q, there] for q in range(9)], axis=1)
            grad = (acc[rows] * rise).astype(bf16)
            grad_hidden[b, rows] = grad
            add_bias(5 + b, grad)

        over_columns(columns, through)
        return carry

    tick("begin")
    for b in range(4):
        lax.fori_loop(b, b + 1, down, 0)
        tick("down", b)
    fetch(3, 0).start()

    def down_bias(c, rows, at):
        add_bias(4, grad_out[rows])

    over_columns(columns, down_bias)

    def weave(first, ways, left, right, runs, name):
        before = None
        for k, (start, count) in enumerate(runs):
            for w in range(ways):
                part = tn_dot(left[:, start : start + count], right[w])
                for q in range(9):
                    spread[q, pl.ds(w, count, stride=ways), :] = part[:, 128 * q : 128 * q + 128]
            if before is not None:
                before.wait()

            def pack(j, carry):
                for q in range(9):
                    lines = spread[q, pl.ds(pl.multiple_of(j * 128, 128), 128), :]
                    woven[pl.ds(j * 16, 16), :, 128 * q : 128 * q + 128] = lines.reshape(
                        16, 8, 128
                    ).astype(bf16)
                return carry

            groups = count * ways // 8
            lax.fori_loop(0, groups // 16, pack, 0)
            before = store(first + start * ways // 8, 0, groups, 0)
            before.start()
            tick(name, k)
        before.wait()

    weave(AT_UP, 4, input_mlp, grad_hidden, UP_RUNS, "up run")
    tick("up")
    acc[...] = jnp.zeros_like(acc)
    for b in range(4):
        fetch(3 + b, b % 2).wait()
        if b < 3:
            fetch(4 + b, 1 - b % 2).start()
        acc[...] += nt_dot(grad_hidden[b], square(held.at[b % 2]))
        tick("up input", b)
    flat_mat(AT_PROJ, 0).start()

    def second_norm_back(c, rows, at):
        br = branch[rows]
        gate = mods[2, at]
        normed, inverse = norm_rows(tokens[rows].astype(f32) + gate * br)
        grad = acc[rows]
        grad_mods[3, at] = jnp.sum(grad, axis=0, keepdims=True)
        grad_mods[4, at] = jnp.sum(grad * normed, axis=0, keepdims=True)
        grad_block = jnp.where(mods[6, at] > 0.5, upstream[rows].astype(f32), 0.0)
        grad_middle = grad_block + norm_rows_back(grad * (1.0 + mods[4, at]), normed, inverse)
        input_grad[rows] = grad_middle
        grad_mods[2, at] = jnp.sum(grad_middle * br, axis=0, keepdims=True)
        grad = (grad_middle * gate).astype(bf16)
        grad_branch[rows] = grad
        add_bias(3, grad)

    over_columns(columns, second_norm_back)
    tick("norm")
    outer(AT_PROJ, attended, grad_branch)
    flat_mat(AT_PROJ, 0).wait()
    grad_att[...] = nt_dot(grad_branch[...], square(held.at[0])).astype(bf16)
    fetch(0, 0).start()
    for r in range(3):
        store(AT_PROJ + 48 * r, 48 * r, 48, r).wait()
    tick("proj")
    inside = same_column()

    def attend_back(g, carry):
        rows = pl.ds(pl.multiple_of(g * 128, 128), 128)
        for p in range(3):
            acc[pl.ds(p * 128, 128)] = jnp.zeros((128, D), f32)
        for h in range(H):
            window, mask = head_window(h)
            queries = proj[0, rows, window] * mask
            keys = proj[1, rows, window]
            grad = grad_att[rows, window] * mask
            probs = head_probabilities(queries, keys, inside)
            grad_probs = nt_dot(grad, proj[2, rows, window])
            mean = jnp.sum(grad_probs * probs, axis=-1, keepdims=True)
            grad_scores = (probs * (grad_probs - mean)).astype(bf16)
            acc[pl.ds(0, 128), window] += nn_dot(grad_scores, keys * mask)
            acc[pl.ds(128, 128), window] += tn_dot(grad_scores, queries)
            acc[pl.ds(256, 128), window] += tn_dot(probs.astype(bf16), grad)
        for p in range(3):
            scale = SCORE_SCALE if p < 2 else 1.0
            grad = (acc[pl.ds(p * 128, 128)] * scale).astype(bf16)
            grad_hidden[p, rows] = grad
            add_bias(p, grad)
        return carry

    for g in range(row_count // 128):
        lax.fori_loop(g, g + 1, attend_back, 0)
        tick("attend", g)
    weave(0, 3, input_att, grad_hidden, QKV_RUNS, "qkv run")
    tick("qkv")
    acc[...] = jnp.zeros_like(acc)
    for p in range(3):
        fetch(p, p % 2).wait()
        if p < 2:
            fetch(p + 1, 1 - p % 2).start()
        acc[...] += nt_dot(grad_hidden[p], square(held.at[p % 2]))
        tick("qkv input", p)

    def first_norm_back(c, rows, at):
        normed, inverse = norm_rows(tokens[rows].astype(f32))
        grad = acc[rows]
        grad_mods[0, at] = jnp.sum(grad, axis=0, keepdims=True)
        grad_mods[1, at] = jnp.sum(grad * normed, axis=0, keepdims=True)
        grad_states = input_grad[rows] + norm_rows_back(
            grad * (1.0 + mods[1, at]), normed, inverse
        )
        up_rows = upstream[rows].astype(f32)
        input_grad[rows] = jnp.where(mods[6, at] > 0.5, grad_states, up_rows)

    over_columns(columns, first_norm_back)
    tick("end")


def backward_kernel(given, *refs):
    backward_body(*refs, lambda name, step=0: None)


def backward_scatter_kernel(*refs):
    (
        given, weights, natural, slope, tokens, upstream, mods, input_att, proj, attended, branch,
        input_mlp, grad_out, grad_gate, member,
        out, grads, other, input_grad, total_small,
        grad_mods, bias_sums, held, woven, spread, grad_hidden, grad_branch, grad_att, acc, copy_sems,
        own, stage, rx2, ry2, rx1, ry1, rz, final, tail, tail_in, tail_z, local_sems, credit,
        small, sums, send_sems, recv_sems,
    ) = refs
    me = Place()
    cp = Copies(send_sems, recv_sems)
    me.greet()
    st = scatter_stages(
        me, cp, grads, out, other, own, stage, rx2, ry2, rx1, ry1, rz, final, tail, tail_in,
        tail_z, local_sems, credit,
    )
    t0, t1, t2, t3, t4, t5 = st["tails"]
    m1, m2, m3, m4, total = sum_stages(me, cp, small, sums)
    groups = member.shape[0]

    def move(t):
        if t < 12:
            st["fold"](t)
            if t % 4 != 3:
                st["prefetch"](t + 1)
        if 0 <= t - 1 < 12:
            st["second"](t - 1)
        if 0 <= t - 2 < 12:
            st["third"](t - 2)

    def tick(name, step=0):
        if name == "begin":
            st["exchange"](2)
            st["prefetch"](0)
        elif name == "down" and step % 2 == 1:
            move(step // 2)
        elif name == "up run" and step in (1, 4):
            move(2 + step // 4)
        elif name == "up":
            st["exchange"](1)
            st["prefetch"](4)
        elif name == "up input" and step == 1:
            move(4)
        elif name == "norm":
            move(5)
        elif name == "proj":
            st["settle"](2)
        elif name == "attend" and step < 2:
            move(6 + step)
        elif name == "qkv":
            st["exchange"](0)
            st["prefetch"](8)
            t0()
        elif name == "qkv input" and step == 0:
            move(8)
            t1()
        elif name == "qkv input" and step == 2:
            t2()
        elif name == "end":
            for n in range(6):
                plane = grad_mods[n] if n < 5 else grad_gate[...]
                small[pl.ds(n * groups, groups)] = exact(
                    member[...], plane, (((1,), (0,)), ((), ()))
                )
            small[pl.ds(6 * groups, 9)] = bias_sums[pl.ds(0, 9)]
            small[pl.ds(6 * groups + 9, small.shape[0] - 6 * groups - 9)] = jnp.zeros(
                (small.shape[0] - 6 * groups - 9, D), f32
            )
            m1()
            move(9)
            t3()
            m2()
            move(10)
            t4()
            m3()
            st["settle"](1)
            move(11)
            t5()
            m4()
            move(12)
            total_small[...] = total()
            move(13)
            st["settle"](0)
            for p in (2, 1, 0):
                st["finish"](p)
            cp.drain()

    backward_body(
        weights, natural, slope, tokens, upstream, mods, input_att, proj, attended, branch,
        input_mlp, grad_out,
        grads.reshape(4 * 4 * 2 * GROUPS8, 8, D), input_grad, grad_mods, bias_sums,
        held, woven, spread, grad_hidden, grad_branch, grad_att, acc, copy_sems,
        tick,
    )


def backward_shapes(rows, columns):
    shape = jax.ShapeDtypeStruct
    return [
        shape((rows, D), f32),
        shape((5, columns, D), f32),
        shape((16, D), f32),
    ]


def backward_scratch(rows):
    return [
        pltpu.VMEM((2, MATS, 8, D), bf16),
        pltpu.VMEM((MATS, 8, D), bf16),
        pltpu.VMEM((9, D, 128), f32),
        pltpu.VMEM((4, rows, D), bf16),
        pltpu.VMEM((rows, D), bf16),
        pltpu.VMEM((rows, D), bf16),
        pltpu.VMEM((rows, D), f32),
        pltpu.SemaphoreType.DMA((9,)),
    ]


def backward(*operands):
    rows, columns = operands[4].shape[0], operands[6].shape[1]
    return pl.pallas_call(
        backward_kernel,
        out_shape=[jax.ShapeDtypeStruct((32 * UNITS // 8, 8, D), bf16)]
        + backward_shapes(rows, columns),
        in_specs=[HBM_SPEC] * 4 + [VMEM_SPEC] * 9,
        out_specs=[HBM_SPEC] + [VMEM_SPEC] * 3,
        input_output_aliases={0: 0},
        scratch_shapes=backward_scratch(rows),
        compiler_params=pltpu.CompilerParams(vmem_limit_bytes=62 * 2**20),
        name="block_backward",
    )(*operands)


def backward_scatter(operands, grad_gate, member):
    rows, columns = operands[4].shape[0], operands[6].shape[1]
    small = small_rows(member.shape[0])
    copies = SCATTER_COPIES + SUM_COPIES
    shape = jax.ShapeDtypeStruct
    input_grad, grad_mods, bias_sums = backward_shapes(rows, columns)
    return pl.pallas_call(
        backward_scatter_kernel,
        out_shape=[
            shape((GROUPS8, 8, D), bf16),
            shape((4, 4, 2, GROUPS8, 8, D), bf16),
            shape((3, 4, 2, 2, QUART, 8, D), bf16),
            input_grad,
            shape((small, D), f32),
        ],
        in_specs=[HBM_SPEC] * 4 + [VMEM_SPEC] * 11,
        out_specs=[HBM_SPEC] * 3 + [VMEM_SPEC] * 2,
        input_output_aliases={0: 1},
        scratch_shapes=[
            pltpu.VMEM(grad_mods.shape, f32),
            pltpu.VMEM(bias_sums.shape, f32),
        ]
        + backward_scratch(rows)
        + scatter_scratch()
        + [
            pltpu.VMEM((small, D), f32),
            pltpu.VMEM((SUM_SLOTS, small, D), f32),
            pltpu.SemaphoreType.DMA((copies,)),
            pltpu.SemaphoreType.DMA((copies,)),
        ],
        compiler_params=pltpu.CompilerParams(
            collective_id=1, has_side_effects=True, vmem_limit_bytes=63 * 2**20
        ),
        name="backward_scatter",
    )(*operands, grad_gate, member)


def small_rows(groups):
    return -(-(6 * groups + 9) // 8) * 8


def adamw_rows(value, grad, first, second):
    first_new = BETA_FIRST * first + (1.0 - BETA_FIRST) * grad
    second_new = BETA_SECOND * second + (1.0 - BETA_SECOND) * grad * grad
    first_hat = first_new / (1.0 - BETA_FIRST**STEP)
    second_hat = second_new / (1.0 - BETA_SECOND**STEP)
    step = first_hat / (jnp.sqrt(second_hat) + ADAM_EPS) + WEIGHT_DECAY * value
    return value - LEARN_RATE * step, first_new, second_new


def finish_kernel(
    shard_sum, low, small, selector, parts_t, row_of, in_ada, cond, weights, first, second, biases,
    bias_first, bias_second,
    cond_grad, norm_out, new_weights, first_out, second_out, new_biases, bias_first_out,
    bias_second_out,
    ada, flat, bias_flat, mine, sums, send_sems, recv_sems,
):
    groups = cond.shape[0]
    me = Place()
    cp = Copies(send_sems, recv_sems)
    me.greet()
    m1, m2, m3, m4, total = sum_stages(me, cp, mine, sums)
    dims = (((1,), (0,)), ((), ()))
    parts = small[pl.ds(0, 6 * groups)]
    mine[...] = jnp.zeros_like(mine)
    products = exact(parts, low[...].reshape(UNITS, D).astype(f32), (((1,), (1,)), ((), ())))
    products = products * parts_t[...]
    folded = products[:groups]
    for n in range(1, 6):
        folded = folded + products[n * groups : (n + 1) * groups]
    lane = lax.broadcasted_iota(jnp.int32, (UNITS, 128), 1)
    for q in range(9):
        hit = jnp.where(row_of[...] == lane + 128 * q, 1.0, 0.0)
        mine[pl.ds(0, groups), 128 * q : 128 * q + 128] = exact(folded, hit, dims)
    ada[...] = exact(selector[...], parts, dims)

    def spread_group(j, square):
        rows = pl.ds(pl.multiple_of(j * 8, 8), 8)
        grad = jnp.where(in_ada[rows] > 0.5, ada[rows], shard_sum[j].astype(f32))
        for q in range(9):
            flat[pl.ds(72 * j + q, 8, stride=9), :] = grad[:, 128 * q : 128 * q + 128]
        return square + grad * grad

    square = lax.fori_loop(0, GROUPS8, spread_group, jnp.zeros((8, D), f32))
    mine[pl.ds(groups, 1)] = jnp.sum(square, axis=0, keepdims=True)
    m1()
    bias_rows = [small[pl.ds(6 * groups + n, 1)] for n in (0, 2, 3, 5, 6, 7, 8, 4)]
    for n in range(6):
        bias_rows.append(jnp.sum(small[pl.ds(n * groups, groups)], axis=0, keepdims=True))
    for t, line in enumerate(bias_rows):
        for q in range(9):
            bias_flat[pl.ds(9 * t + q, 1)] = line[:, 128 * q : 128 * q + 128]
    bias_square = jnp.sum(bias_flat[...] * bias_flat[...], axis=0, keepdims=True)
    bias_square = jnp.sum(bias_square, axis=1, keepdims=True)
    m2()
    m3()
    m4()
    summed = total()
    norm = jnp.sqrt(jnp.sum(summed[groups : groups + 1], axis=1, keepdims=True) + bias_square)
    factor = jnp.minimum(1.0, CLIP_NORM / (norm + 1e-06))
    norm_out[...] = norm
    c = cond[...]
    gate = 1.0 / (1.0 + jnp.exp(-c))
    cond_grad[...] = summed[:groups] * (gate * (1.0 + c * (1.0 - gate)))
    new_biases[...], bias_first_out[...], bias_second_out[...] = adamw_rows(
        biases[...], bias_flat[...] * factor, bias_first[...], bias_second[...]
    )

    def update(j, carry):
        at = pl.ds(pl.multiple_of(j * 72, 8), 72)
        new_weights[at], first_out[at], second_out[at] = adamw_rows(
            weights[at], flat[at] * factor, first[at], second[at]
        )
        return carry

    lax.fori_loop(0, GROUPS8, update, 0)
    cp.drain()


def finish(*operands):
    cond, weights, biases = operands[7], operands[8], operands[11]
    shape = jax.ShapeDtypeStruct
    like = [shape(weights.shape, f32)] * 3 + [shape(biases.shape, f32)] * 3
    payload = 8 * (cond.shape[0] // 8 + 1)
    return pl.pallas_call(
        finish_kernel,
        out_shape=[shape(cond.shape, f32), shape((1, 1), f32)] + like,
        in_specs=[VMEM_SPEC] * len(operands),
        out_specs=[VMEM_SPEC] * 8,
        scratch_shapes=[
            pltpu.VMEM((UNITS, D), f32),
            pltpu.VMEM(weights.shape, f32),
            pltpu.VMEM(biases.shape, f32),
            pltpu.VMEM((payload, D), f32),
            pltpu.VMEM((SUM_SLOTS, payload, D), f32),
            pltpu.SemaphoreType.DMA((SUM_COPIES,)),
            pltpu.SemaphoreType.DMA((SUM_COPIES,)),
        ],
        compiler_params=pltpu.CompilerParams(
            collective_id=2, has_side_effects=True, vmem_limit_bytes=60 * 2**20
        ),
        name="finish",
    )(*operands)


def gather_blocks(shard_low):
    whole = lax.all_gather(shard_low, ("outer", "inner"), axis=0, tiled=True)
    return whole.reshape(-1, 8, D)


def scatter_blocks(grads, units):
    axes = ("outer", "inner")
    whole = grads.reshape(-1, D)[: lax.axis_size(axes) * units].astype(f32)
    return lax.psum_scatter(whole, axes, scatter_dimension=0, tiled=True)


def split_bias(vector):
    widths = [D, D, D, FF, D, 6 * D]
    pieces = []
    offset = 0
    for span_width in widths:
        pieces.append(lax.slice_in_dim(vector, offset, offset + span_width))
        offset = offset + span_width
    return pieces


def exact(left, right, dims):
    return lax.dot_general(
        left, right, dims, precision=lax.Precision.HIGHEST, preferred_element_type=jnp.float32
    )


def ada_selector(soft_cond, first_unit, units):
    groups = soft_cond.shape[0]
    spread = jnp.repeat(soft_cond.astype(jnp.float32), 6, axis=1)
    spread = jnp.pad(spread, ((0, 0), (units, units)))
    start = jnp.clip(first_unit - BLOCK_UNITS + units, 0, 6 * D + units)
    local = lax.dynamic_slice(spread, (jnp.int32(0), start), (groups, units))
    unit = first_unit - BLOCK_UNITS + jnp.arange(units, dtype=jnp.int32)
    part = (unit[:, None] % 6 == jnp.arange(6, dtype=jnp.int32)[None, :]) & (unit[:, None] >= 0)
    part = part.astype(jnp.float32)
    selector = local.T[:, :, None] * part[:, None, :]
    return selector.reshape(units, groups * 6), part


def adamw(parameter, gradient, first_state, second_state):
    first_new = BETA_FIRST * first_state + (1.0 - BETA_FIRST) * gradient
    second_new = BETA_SECOND * second_state + (1.0 - BETA_SECOND) * gradient * gradient
    first_hat = first_new / (1.0 - BETA_FIRST**STEP)
    second_hat = second_new / (1.0 - BETA_SECOND**STEP)
    updated = parameter - LEARN_RATE * (
        first_hat / (jnp.sqrt(second_hat) + ADAM_EPS) + WEIGHT_DECAY * parameter
    )
    return (updated, first_new, second_new)


def with_kernels(
    tokens, conditioning, output_grad, state, bias_state, first_unit, selector, ada_part,
    membership, video_plane, b_ada, bias_args,
):
    columns, groups = membership.shape
    units = UNITS
    eye = jnp.eye(6, dtype=f32)
    chosen = membership[None, :, None, :] * eye[:, None, :, None]
    chosen = jnp.pad(chosen.reshape(6 * columns, 6 * groups), ((0, columns), (0, 0)))
    base = jnp.repeat(b_ada.reshape(6, D), columns, axis=0)
    base = jnp.concatenate([base, video_plane])
    by_part = selector.reshape(units, groups, 6).transpose(0, 2, 1).reshape(units, 6 * groups)
    state = [part.reshape(9 * units, 128) for part in state]
    (
        flat, mods, shard_low, block_out, natural, input_att, proj, attended, branch, input_mlp, _,
        slope, grad_out, grad_gate, grads,
    ) = gather_forward(
        state[0], by_part.T.astype(bf16), chosen, base, tokens, output_grad, *bias_args
    )
    flat = flat.reshape(-1, 8, D)
    shard_sum, _, _, input_grad, small = backward_scatter(
        (
            grads.reshape(4, 4, 2, GROUPS8, 8, D), flat, natural, slope, tokens, output_grad, mods,
            input_att, proj, attended, branch, input_mlp, grad_out,
        ),
        grad_gate, membership.T,
    )
    unit = first_unit - BLOCK_UNITS + jnp.arange(units, dtype=jnp.int32)
    row_of = jnp.where(unit >= 0, unit // 6, -1)[:, None]
    parts_t = jnp.repeat(ada_part.T, groups, axis=0)
    in_ada = (unit >= 0).astype(f32)[:, None]
    cond_grad, norm, *updated = finish(
        shard_sum, shard_low, small, by_part, parts_t, row_of, in_ada, conditioning, *state,
        *[part.reshape(-1, 128) for part in bias_state],
    )
    return (block_out, input_grad, cond_grad, norm[0, 0], *[part.reshape(-1) for part in updated])


def on_device(
    tokens,
    conditioning,
    column_sample,
    is_image,
    output_grad,
    weights,
    first_moment,
    second_moment,
    biases,
    bias_first,
    bias_second,
    kernels,
):
    columns = column_sample.shape[0]
    groups = conditioning.shape[0]
    units = weights.shape[0] // D
    axes = ("outer", "inner")
    first_unit = lax.axis_index(axes).astype(jnp.int32) * units
    b_query, b_value, b_proj, b_up, b_down, b_ada = split_bias(biases)
    soft_cond = jax.nn.silu(conditioning).astype(bf16)
    selector, ada_part = ada_selector(soft_cond, first_unit, units)
    membership = (column_sample[:, None] == jnp.arange(groups, dtype=jnp.int32)[None, :]).astype(
        f32
    )
    video_cols = exact(membership, 1.0 - is_image.astype(f32)[:, None], (((1,), (0,)), ((), ())))
    b_qkv = jnp.stack([b_query, jnp.zeros((D,), f32), b_value])
    bias_args = (b_qkv, b_proj[None], b_up.reshape(4, D), b_down[None])
    video_plane = jnp.broadcast_to(video_cols, (columns, D))
    if kernels:
        return with_kernels(
            tokens, conditioning, output_grad, (weights, first_moment, second_moment),
            (biases, bias_first, bias_second), first_unit, selector, ada_part, membership,
            video_plane, b_ada, bias_args,
        )
    shard_low = weights.reshape(units, D).astype(bf16)
    flat = gather_blocks(shard_low)
    mods_all = lax.psum(tn_dot(selector.astype(bf16), shard_low), axes)
    mods_all = mods_all.reshape(groups, 6 * D) + b_ada
    mods = jnp.take(mods_all, column_sample, axis=0).reshape(columns, 6, D).transpose(1, 0, 2)
    mods = jnp.concatenate([mods, video_plane[None]])
    (
        block_out, natural, input_att, proj, attended, branch, input_mlp, _, slope, grad_out,
        grad_gate, grads,
    ) = forward(flat, tokens, output_grad, mods, *bias_args)
    grads, input_grad, grad_mods, bias_sums = backward(
        grads, flat, natural, slope, tokens, output_grad, mods, input_att, proj, attended, branch,
        input_mlp, grad_out,
    )
    grad_mods = jnp.concatenate([grad_mods, grad_gate[None]])
    mods_local = exact(membership, grad_mods, (((0,), (1,)), ((), ())))
    bias_sums, grad_mods_all = lax.psum((bias_sums, mods_local.transpose(1, 0, 2)), axes)
    block_shard = scatter_blocks(grads, units)
    grad_mods_all = grad_mods_all.transpose(1, 0, 2).reshape(groups, 6 * D)
    bias_head = jnp.concatenate([bias_sums[:1], bias_sums[2:4], bias_sums[5:9], bias_sums[4:5]])
    first_sum = jnp.concatenate([bias_head.reshape(-1), jnp.sum(grad_mods_all, axis=0)])
    mods_parts = grad_mods_all.reshape(groups * 6, D)
    ada_shard = exact(selector, mods_parts, (((1,), (0,)), ((), ())))
    unit = first_unit + jnp.arange(units, dtype=jnp.int32)
    grad_units = jnp.where(unit[:, None] >= BLOCK_UNITS, ada_shard, block_shard)
    products = exact(shard_low.astype(jnp.float32), mods_parts, (((1,), (1,)), ((), ())))
    products = jnp.sum(products.reshape(units, groups, 6) * ada_part[:, None, :], axis=2)
    spread = jnp.zeros((groups, 6 * D + 2 * units), jnp.float32)
    start = jnp.clip(first_unit - BLOCK_UNITS + units, 0, 6 * D + units)
    spread = lax.dynamic_update_slice(spread, products.T, (jnp.int32(0), start))
    grad_soft = jnp.sum(spread[:, units : units + 6 * D].reshape(groups, D, 6), axis=2)
    square_sum = jnp.sum(grad_units * grad_units)
    square_sum, grad_soft = lax.psum((square_sum, grad_soft), axes)
    silu_out, silu_back = jax.vjp(jax.nn.silu, conditioning)
    second_sum = silu_back(grad_soft)[0]
    grad_shard = grad_units.reshape(-1)
    grad_norm = jnp.sqrt(square_sum + jnp.sum(first_sum * first_sum))
    factor = jnp.minimum(1.0, CLIP_NORM / (grad_norm + 1e-06))
    new_weights, first_out, second_out = adamw(
        weights, grad_shard * factor, first_moment, second_moment
    )
    new_biases, bias_first_out, bias_second_out = adamw(
        biases, first_sum * factor, bias_first, bias_second
    )
    return (
        block_out,
        input_grad,
        second_sum,
        grad_norm,
        new_weights,
        first_out,
        second_out,
        new_biases,
        bias_first_out,
        bias_second_out,
    )


def solution(mesh):
    in_specs = (
        P(("outer", "inner"), None),
        P(),
        P(("outer", "inner")),
        P(),
        P(("outer", "inner"), None),
        P(("outer", "inner")),
        P(("outer", "inner")),
        P(("outer", "inner")),
        P(),
        P(),
        P(),
    )
    out_specs = (
        P(("outer", "inner"), None),
        P(("outer", "inner"), None),
        P(),
        P(),
        P(("outer", "inner")),
        P(("outer", "inner")),
        P(("outer", "inner")),
        P(),
        P(),
        P(),
    )
    kernels = dict(mesh.shape) == {"outer": 4, "inner": 8}
    return jax.shard_map(
        functools.partial(on_device, kernels=kernels), mesh=mesh, in_specs=in_specs, out_specs=out_specs, check_vma=False
    )
```

```python
import functools
import math

import jax
import jax.numpy as jnp
from jax import lax
from jax.experimental import pallas as pl
from jax.experimental.pallas import tpu as pltpu
from jax.sharding import PartitionSpec as P

D = 1152
H = 16
HD = 72
FF = 4608
FRAMES = 16
STEP = 8


NORM_EPS = 1e-06
LEARN_RATE = 0.02
BETA_FIRST = 0.5
BETA_SECOND = 0.55
ADAM_EPS = 1e-08
WEIGHT_DECAY = 0.01
CLIP_NORM = 1.0
BLOCK_UNITS = 4 * D + 2 * FF


MESH = pl.DeviceIdType.MESH
UNITS = 648
GROUPS8 = 81
QUART = 20
FIRST = 8
SECOND = QUART - FIRST
MAIN = 80
TAIL = 1
DEPTH = (4, 4, 3)
BASE = (0, 4, 8)


def flip(z, d):
    if d == 0:
        return z
    if d == 1:
        return z + 1 - 2 * (z % 2)
    if d == 2:
        return z + 2 - 4 * (z // 2)
    return 3 - z


class Place:
    def __init__(self):
        self.o = lax.axis_index("outer")
        self.i = lax.axis_index("inner")
        self.x, self.c = self.o // 2, self.o % 2
        self.z, self.y = self.i // 2, self.i % 2
        self.xo, self.co, self.yo = 1 - self.x, 1 - self.c, 1 - self.y

    def dev(self, dx=0, dc=0, dz=0, dy=0):
        x = self.xo if dx else self.x
        c = self.co if dc else self.c
        y = self.yo if dy else self.y
        return (x * 2 + c, flip(self.z, dz) * 2 + y)

    def greet(self):
        peers = [
            self.dev(dx, dc, 0, dy) for dx in (0, 1) for dc in (0, 1) for dy in (0, 1)
        ][1:]
        peers += [self.dev(dz=1), self.dev(dz=2), self.dev(dz=3)]
        barrier = pltpu.get_barrier_semaphore()
        for peer in peers:
            pl.semaphore_signal(barrier, inc=1, device_id=peer, device_id_type=MESH)
        pl.semaphore_wait(barrier, len(peers))


class Copies:
    def __init__(self, send_sems, recv_sems):
        self.send_sems, self.recv_sems = send_sems, recv_sems
        self.count = 0
        self.sent = []

    def slot(self):
        self.count += 1
        return self.count - 1

    def make(self, slot, src, dst, device):
        return pltpu.make_async_remote_copy(
            src_ref=src, dst_ref=dst, send_sem=self.send_sems.at[slot],
            recv_sem=self.recv_sems.at[slot], device_id=device, device_id_type=MESH,
        )

    def send(self, slot, src, dst, device, cond=None):
        def go():
            self.make(slot, src, dst, device).start()
        if cond is None:
            go()
        else:
            pl.when(cond)(go)
        self.sent.append((slot, src, dst, device, cond))

    def wait_recv(self, slot, dst, device, cond=None):
        def go():
            self.make(slot, dst, dst, device).wait_recv()
        if cond is None:
            go()
        else:
            pl.when(cond)(go)

    def wait_send(self, wanted):
        for entry in self.sent:
            if entry[0] == wanted:
                slot, src, dst, device, cond = entry

                def go():
                    self.make(slot, src, dst, device).wait_send()
                if cond is None:
                    go()
                else:
                    pl.when(cond)(go)
        self.sent = [entry for entry in self.sent if entry[0] != wanted]

    def drain(self):
        for slot, src, dst, device, cond in self.sent:
            def go(slot=slot, src=src, dst=dst, device=device):
                self.make(slot, src, dst, device).wait_send()
            if cond is None:
                go()
            else:
                pl.when(cond)(go)
        self.sent = []


def ok(zb, p):
    return None if DEPTH[p] == 4 else zb < DEPTH[p]


def both(a, b):
    if a is None:
        return b
    if b is None:
        return a
    return jnp.logical_and(a, b)


GATHER_COPIES = 3 * (3 + 5 + 4 * 4 + 8) + 7


def gather_stages(me, cp, shard, full, local_sems):
    def part(p, zb, yb, x, c, first=0, n=QUART):
        return full.at[p, zb, yb, pl.ds((2 * QUART * x + QUART * c + first), n)]

    def own_of(p):
        return both(me.o == p, ok(me.z, p))

    quarter = (2 * QUART * me.x + QUART * me.c)
    own_tail = pltpu.make_async_copy(
        shard.at[pl.ds(MAIN, TAIL)], full.at[me.o, me.z, me.y, pl.ds(MAIN, TAIL)], local_sems.at[0]
    )
    own_tail.start()

    def local_quarter(p):
        return pltpu.make_async_copy(
            shard.at[pl.ds(quarter, QUART)], part(p, me.z, me.y, me.x, me.c), local_sems.at[1]
        )

    slots = {}

    def s0(p):
        @pl.when(own_of(p))
        def _():
            local_quarter(p).start()
        for dx, dc in ((1, 0), (0, 1), (1, 1)):
            s = slots["s0", p, dx, dc] = cp.slot()
            x = me.xo if dx else me.x
            c = me.co if dc else me.c
            cp.send(
                s, shard.at[pl.ds((2 * QUART * x + QUART * c), QUART)],
                part(p, me.z, me.y, x, c), me.dev(dx=dx, dc=dc), own_of(p),
            )

    def s0_wait(p):
        @pl.when(own_of(p))
        def _():
            local_quarter(p).wait()
        ox, oc = p // 2, p % 2
        for dx, dc in ((1, 0), (0, 1), (1, 1)):
            x = me.xo if dx else me.x
            c = me.co if dc else me.c
            cond = both(jnp.logical_and(x == ox, c == oc), ok(me.z, p))
            cp.wait_recv(
                slots["s0", p, dx, dc], part(p, me.z, me.y, me.x, me.c), me.dev(dx=dx, dc=dc), cond
            )

    def spread(p, d):
        zb = place(d)
        mine = part(p, zb, me.y, me.x, me.c)
        s = slots["y1", p, d] = cp.slot()
        cp.send(s, mine, mine, me.dev(dy=1), ok(zb, p))
        s = slots["x1", p, d] = cp.slot()
        cp.send(s, mine, mine, me.dev(dx=1), ok(zb, p))

    def place(e):
        return (me.z, flip(me.z, 1), 2 - me.z // 2, 3 - 3 * (me.z // 2))[e]

    inner = (me.z + 1) // 2 == 1
    outer = jnp.logical_not(inner)

    def pass_on(p, zb, name, device, cond):
        view = part(p, zb, me.y, me.x, me.c)
        s = slots[name, p] = cp.slot()
        cp.send(s, view, view, device, both(cond, ok(zb, p)))

    def arrive(p, e, name, device, cond):
        zb = place(e)
        view = part(p, zb, me.y, me.x, me.c)
        cp.wait_recv(slots[name, p], view, device, both(cond, ok(zb, p)))

    def s1(p):
        s0_wait(p)
        pass_on(p, me.z, "own to 1", me.dev(dz=1), None)
        pass_on(p, me.z, "own to 3", me.dev(dz=3), inner)
        spread(p, 0)

    def s2(p):
        arrive(p, 1, "own to 1", me.dev(dz=1), None)
        pass_on(p, place(1), "1 to 3", me.dev(dz=3), inner)
        spread(p, 1)
        arrive(p, 2, "own to 3", me.dev(dz=3), inner)
        pass_on(p, place(2), "near to 1", me.dev(dz=1), inner)
        arrive(p, 2, "near to 1", me.dev(dz=1), outer)
        spread(p, 2)
        arrive(p, 3, "1 to 3", me.dev(dz=3), inner)
        pass_on(p, place(3), "far to 1", me.dev(dz=1), inner)
        arrive(p, 3, "far to 1", me.dev(dz=1), outer)
        spread(p, 3)

    def s3(p, entries=(0, 1, 2, 3)):
        for d in entries:
            zb = place(d)
            cp.wait_recv(
                slots["y1", p, d], part(p, zb, me.yo, me.x, me.c), me.dev(dy=1), ok(zb, p)
            )
            s = slots["x2", p, d] = cp.slot()
            out = part(p, zb, me.yo, me.x, me.c, 0, FIRST)
            cp.send(s, out, out, me.dev(dx=1), ok(zb, p))
            cp.wait_recv(
                slots["x1", p, d], part(p, zb, me.y, me.xo, me.c), me.dev(dx=1), ok(zb, p)
            )
            s = slots["y2", p, d] = cp.slot()
            out = part(p, zb, me.y, me.xo, me.c, FIRST, SECOND)
            cp.send(s, out, out, me.dev(dy=1), ok(zb, p))

    def lane(p, zb, x, c):
        return full.at[p, zb, :, pl.ds((2 * QUART * x + QUART * c), QUART)]

    def s4(p):
        for d in (0, 1, 2, 3):
            zb = place(d)
            cp.wait_recv(
                slots["x2", p, d], part(p, zb, me.yo, me.xo, me.c, 0, FIRST), me.dev(dx=1),
                ok(zb, p),
            )
            cp.wait_recv(
                slots["y2", p, d], part(p, zb, me.yo, me.xo, me.c, FIRST, SECOND), me.dev(dy=1),
                ok(zb, p),
            )
            for h in (0, 1):
                s = slots["c", p, d, h] = cp.slot()
                cp.send(s, lane(p, zb, h, me.c), lane(p, zb, h, me.c), me.dev(dc=1), ok(zb, p))

    def s5(p):
        for d in (0, 1, 2, 3):
            zb = place(d)
            for h in (0, 1):
                cp.wait_recv(
                    slots["c", p, d, h], lane(p, zb, h, me.co), me.dev(dc=1), ok(zb, p)
                )

    tails = pl.ds(MAIN, TAIL)

    def t1():
        own_tail.wait()
        block = full.at[me.o, me.z, me.y, tails]
        for d in (1, 2, 3):
            s = slots["tz", d] = cp.slot()
            cp.send(s, block, block, me.dev(dz=d))

    def t2():
        for d in (1, 2, 3):
            zb = flip(me.z, d)
            cp.wait_recv(slots["tz", d], full.at[me.o, zb, me.y, tails], me.dev(dz=d))
        s = slots["ty"] = cp.slot()
        block = full.at[me.o, :, me.y, tails]
        cp.send(s, block, block, me.dev(dy=1))

    def t3():
        cp.wait_recv(slots["ty"], full.at[me.o, :, me.yo, tails], me.dev(dy=1))
        s = slots["tx"] = cp.slot()
        block = full.at[me.o, :, :, tails]
        cp.send(s, block, block, me.dev(dx=1))

    def t4():
        cp.wait_recv(slots["tx"], full.at[me.xo * 2 + me.c, :, :, tails], me.dev(dx=1))
        for h in (0, 1):
            s = slots["tc", h] = cp.slot()
            block = full.at[h * 2 + me.c, :, :, tails]
            cp.send(s, block, block, me.dev(dc=1))

    def t5():
        for h in (0, 1):
            cp.wait_recv(slots["tc", h], full.at[h * 2 + me.co, :, :, tails], me.dev(dc=1))

    return dict(s0=s0, s1=s1, s2=s2, s3=s3, s4=s4, s5=s5, t1=t1, t2=t2, t3=t3, t4=t4, t5=t5)


SCATTER_COPIES = 3 * (4 * 2 + 4 * 4 + 3 + 3) + 8
RING = 6
ORDER = (3, 2, 1, 0)
f32 = jnp.float32


def guarded(cond, fn):
    if cond is None:
        fn()
    else:
        pl.when(cond)(fn)


def add_rows(dst, srcs, n):
    step = 2 if n % 2 == 0 else 1

    def body(j, carry):
        at = pl.ds(j * step, step)
        total = srcs[0][at].astype(f32)
        for src in srcs[1:]:
            total = total + src[at].astype(f32)
        dst[at] = total.astype(dst.dtype)
        return carry

    lax.fori_loop(0, n // step, body, 0)


def scatter_stages(
    me, cp, partial, out, other, own, stage, rx2, ry2, rx1, ry1, rz, final, tail, tail_in, tail_z,
    local_sems, credit,
):
    slots = {}

    def block(k):
        p, d = 2 - k // 4, ORDER[k % 4]
        zb = flip(me.z, d)
        return p, d, zb, ok(zb, p), k % RING

    def exchange(p):
        for d in ORDER:
            zb = flip(me.z, d)
            for h in (0, 1):
                s = slots["c", p, d, h] = cp.slot()
                view = pl.ds(2 * QUART * h + QUART * me.co, QUART)
                cp.send(
                    s, partial.at[p, zb, :, view], other.at[p, zb, :, h], me.dev(dc=1), ok(zb, p)
                )

    def loads(k):
        p, d, zb, cond, slot = block(k)
        copies = []
        for h in (0, 1):
            view = pl.ds(2 * QUART * h + QUART * me.c, QUART)
            copies.append(
                pltpu.make_async_copy(
                    partial.at[p, zb, :, view], own.at[slot, :, h], local_sems.at[h]
                )
            )
            copies.append(
                pltpu.make_async_copy(other.at[p, zb, :, h], stage.at[h], local_sems.at[2 + h])
            )
        return copies

    def prefetch(k):
        p, d, zb, cond, slot = block(k)
        if k >= RING:
            old = block(k - RING)
            for name in ("x2", "y2", "x1", "y1", "z"):
                if (name, old[0], old[1]) in slots:
                    cp.wait_send(slots[name, old[0], old[1]])
        for h in (0, 1):
            cp.wait_recv(slots["c", p, d, h], other.at[p, zb, :, h], me.dev(dc=1), cond)

        def go():
            for copy in loads(k):
                copy.start()

        guarded(cond, go)

    def fold(k):
        p, d, zb, cond, slot = block(k)

        def go():
            for copy in loads(k):
                copy.wait()

            def body(q, carry):
                y, h = q // 2, q % 2
                add_rows(own.at[slot, y, h], [own.at[slot, y, h], stage.at[h, y]], QUART)
                return carry

            lax.fori_loop(0, 4, body, 0)

        guarded(cond, go)
        if k >= RING:
            pl.semaphore_wait(credit.at[0], 1)
            pl.semaphore_wait(credit.at[1], 1)
        far = own.at[slot, me.yo, me.xo]
        s = slots["x2", p, d] = cp.slot()
        cp.send(s, far.at[pl.ds(0, FIRST)], rx2.at[slot], me.dev(dx=1), cond)
        s = slots["y2", p, d] = cp.slot()
        cp.send(s, far.at[pl.ds(FIRST, SECOND)], ry2.at[slot], me.dev(dy=1), cond)

    def second(k):
        p, d, zb, cond, slot = block(k)
        cp.wait_recv(slots["x2", p, d], rx2.at[slot], me.dev(dx=1), cond)
        view = own.at[slot, me.yo, me.x, pl.ds(0, FIRST)]
        guarded(cond, lambda: add_rows(view, [view, rx2.at[slot]], FIRST))
        s = slots["y1", p, d] = cp.slot()
        cp.send(s, own.at[slot, me.yo, me.x], ry1.at[slot], me.dev(dy=1), cond)
        cp.wait_recv(slots["y2", p, d], ry2.at[slot], me.dev(dy=1), cond)
        view2 = own.at[slot, me.y, me.xo, pl.ds(FIRST, SECOND)]
        guarded(cond, lambda: add_rows(view2, [view2, ry2.at[slot]], SECOND))
        s = slots["x1", p, d] = cp.slot()
        cp.send(s, own.at[slot, me.y, me.xo], rx1.at[slot], me.dev(dx=1), cond)

    def third(k):
        p, d, zb, cond, slot = block(k)
        cp.wait_recv(slots["y1", p, d], ry1.at[slot], me.dev(dy=1), cond)
        cp.wait_recv(slots["x1", p, d], rx1.at[slot], me.dev(dx=1), cond)
        view = own.at[slot, me.y, me.x]
        guarded(cond, lambda: add_rows(view, [view, ry1.at[slot], rx1.at[slot]], QUART))
        if k + RING < 12:
            pl.semaphore_signal(
                credit.at[0], inc=1, device_id=me.dev(dx=1), device_id_type=MESH
            )
            pl.semaphore_signal(
                credit.at[1], inc=1, device_id=me.dev(dy=1), device_id_type=MESH
            )
        if d:
            s = slots["z", p, d] = cp.slot()
            cp.send(s, view, rz.at[p, d - 1], me.dev(dz=d), cond)

    def quarter(x, c):
        return out.at[pl.ds(2 * QUART * x + QUART * c, QUART)]

    def settle(p):
        mine = ok(me.z, p)
        for d in (1, 2, 3):
            cp.wait_recv(slots["z", p, d], rz.at[p, d - 1], me.dev(dz=d), mine)
        view = own.at[(4 * (2 - p) + 3) % RING, me.y, me.x]
        guarded(
            mine,
            lambda: add_rows(final.at[p], [view, rz.at[p, 0], rz.at[p, 1], rz.at[p, 2]], QUART),
        )
        ox, oc = p // 2, p % 2
        for dx, dc in ((1, 0), (0, 1), (1, 1)):
            x = me.xo if dx else me.x
            c = me.co if dc else me.c
            s = slots["f", p, dx, dc] = cp.slot()
            cond = both(jnp.logical_and(x == ox, c == oc), mine)
            cp.send(s, final.at[p], quarter(me.x, me.c), me.dev(dx=dx, dc=dc), cond)

        @pl.when(both(me.o == p, mine))
        def _():
            pltpu.make_async_copy(final.at[p], quarter(me.x, me.c), local_sems.at[4]).start()

    def finish(p):
        mine = both(me.o == p, ok(me.z, p))
        for dx, dc in ((1, 0), (0, 1), (1, 1)):
            x = me.xo if dx else me.x
            c = me.co if dc else me.c
            cp.wait_recv(slots["f", p, dx, dc], quarter(x, c), me.dev(dx=dx, dc=dc), mine)

        @pl.when(mine)
        def _():
            pltpu.make_async_copy(final.at[p], quarter(me.x, me.c), local_sems.at[4]).wait()

    def tail_load():
        return pltpu.make_async_copy(
            partial.at[:, :, :, pl.ds(MAIN, TAIL)], tail, local_sems.at[5]
        )

    def tail_add(o, zb, yb, srcs):
        add_rows(tail.at[o, zb, yb], [tail.at[o, zb, yb]] + srcs, TAIL)

    def t0():
        tail_load().start()

    def t1():
        tail_load().wait()
        for h in (0, 1):
            s = slots["tc", h] = cp.slot()
            cp.send(s, tail.at[2 * h + me.co], tail_in.at[h], me.dev(dc=1))

    def t2():
        for h in (0, 1):
            cp.wait_recv(slots["tc", h], tail_in.at[h], me.dev(dc=1))

            def body(q, carry):
                tail_add(2 * h + me.c, q // 2, q % 2, [tail_in.at[h, q // 2, q % 2]])
                return carry
            lax.fori_loop(0, 8, body, 0)
        s = slots["tx"] = cp.slot()
        cp.send(s, tail.at[me.xo * 2 + me.c], tail_in.at[2], me.dev(dx=1))

    def t3():
        cp.wait_recv(slots["tx"], tail_in.at[2], me.dev(dx=1))

        def body(q, carry):
            tail_add(me.o, q // 2, q % 2, [tail_in.at[2, q // 2, q % 2]])
            return carry
        lax.fori_loop(0, 8, body, 0)
        s = slots["ty"] = cp.slot()
        cp.send(s, tail.at[me.o, :, me.yo], tail_in.at[3, :, 0], me.dev(dy=1))

    def t4():
        cp.wait_recv(slots["ty"], tail_in.at[3, :, 0], me.dev(dy=1))

        def body(q, carry):
            tail_add(me.o, q, me.y, [tail_in.at[3, q, 0]])
            return carry
        lax.fori_loop(0, 4, body, 0)
        for d in (1, 2, 3):
            s = slots["tz", d] = cp.slot()
            cp.send(s, tail.at[me.o, flip(me.z, d), me.y], tail_z.at[d - 1], me.dev(dz=d))

    def t5():
        for d in (1, 2, 3):
            cp.wait_recv(slots["tz", d], tail_z.at[d - 1], me.dev(dz=d))
        tail_add(me.o, me.z, me.y, [tail_z.at[0], tail_z.at[1], tail_z.at[2]])
        copy = pltpu.make_async_copy(
            tail.at[me.o, me.z, me.y], out.at[pl.ds(MAIN, TAIL)], local_sems.at[5]
        )
        copy.start()
        copy.wait()

    return dict(
        exchange=exchange, prefetch=prefetch, fold=fold, second=second, third=third,
        settle=settle, finish=finish, tails=(t0, t1, t2, t3, t4, t5),
    )


def scatter_scratch():
    bf = jnp.bfloat16
    return [
        pltpu.VMEM((RING, 2, 2, QUART, 8, D), bf),
        pltpu.VMEM((2, 2, QUART, 8, D), bf),
        pltpu.VMEM((RING, FIRST, 8, D), bf),
        pltpu.VMEM((RING, SECOND, 8, D), bf),
        pltpu.VMEM((RING, QUART, 8, D), bf),
        pltpu.VMEM((RING, QUART, 8, D), bf),
        pltpu.VMEM((3, 3, QUART, 8, D), bf),
        pltpu.VMEM((3, QUART, 8, D), bf),
        pltpu.VMEM((4, 4, 2, TAIL, 8, D), bf),
        pltpu.VMEM((4, 4, 2, TAIL, 8, D), bf),
        pltpu.VMEM((3, TAIL, 8, D), bf),
        pltpu.SemaphoreType.DMA((6,)),
        pltpu.SemaphoreType.REGULAR((2,)),
    ]


bf16 = jnp.bfloat16
MATS = D // 8
AT_PROJ = 3 * MATS
AT_UP = 4 * MATS
AT_DOWN = 8 * MATS
ROOT = math.sqrt(2.0 / math.pi)
CUBIC = 0.044715


def nn_dot(left, right):
    return lax.dot_general(left, right, (((1,), (0,)), ((), ())), preferred_element_type=f32)


def nt_dot(left, right):
    return lax.dot_general(left, right, (((1,), (1,)), ((), ())), preferred_element_type=f32)


def tn_dot(left, right):
    return lax.dot_general(left, right, (((0,), (0,)), ((), ())), preferred_element_type=f32)


def square(ref):
    return ref[...].reshape(D, D)


def norm_rows(values):
    centered = values - jnp.mean(values, axis=-1, keepdims=True)
    inverse = lax.rsqrt(jnp.mean(centered * centered, axis=-1, keepdims=True) + NORM_EPS)
    return centered * inverse, inverse


def norm_rows_back(grad, normed, inverse):
    return inverse * (
        grad
        - jnp.mean(grad, axis=-1, keepdims=True)
        - normed * jnp.mean(grad * normed, axis=-1, keepdims=True)
    )


def frames_of(c):
    return pl.ds(pl.multiple_of(c * FRAMES, FRAMES), FRAMES)


def over_columns(count, body):
    ways = math.gcd(count, 3)

    def step(run, carry):
        for n in range(ways):
            c = ways * run + n
            body(c, frames_of(c), pl.ds(c, 1))
        return carry

    lax.fori_loop(0, count // ways, step, 0)


def split_rows(src, spread, put, ways):
    units = src.shape[0] * 8
    rows = units // ways
    for q in range(9):
        lanes = slice(128 * q, 128 * q + 128)
        spread[q, pl.ds(0, units)] = src[:, :, lanes].astype(f32).reshape(units, 128)
        for w in range(ways):
            part = spread[q, pl.ds(w, rows, stride=ways), :]
            put(w, lanes, part.reshape(rows // 8, 8, 128).astype(bf16))


def head_window(h):
    first = min(HD * h // 128, 7) * 128
    lane = lax.broadcasted_iota(jnp.int32, (1, 256), 1) + first
    mask = jnp.logical_and(lane >= HD * h, lane < HD * h + HD)
    return slice(first, first + 256), jnp.where(mask, 1.0, 0.0).astype(bf16)


def same_column():
    row = lax.broadcasted_iota(jnp.int32, (128, 128), 0)
    col = lax.broadcasted_iota(jnp.int32, (128, 128), 1)
    return lax.shift_right_logical(row, 4) == lax.shift_right_logical(col, 4)


SCORE_SCALE = 1.0 / math.sqrt(HD)


def head_probabilities(masked_queries, keys, inside):
    scores = jnp.where(inside, nt_dot(masked_queries, keys) * SCORE_SCALE, -1e30)
    grown = jnp.exp(scores - jnp.max(scores, axis=-1, keepdims=True))
    return grown / jnp.sum(grown, axis=-1, keepdims=True)


SUM_COPIES = 6
SUM_SLOTS = 10


def sum_stages(me, cp, mine, buf):
    slots = {}

    def send(name, src, dst, device):
        slots[name] = cp.slot()
        cp.send(slots[name], src, dst, device)

    def m1():
        send("c", mine, buf.at[0], me.dev(dc=1))

    def m2():
        cp.wait_recv(slots["c"], buf.at[0], me.dev(dc=1))
        buf[1] = mine[...] + buf[0]
        send("x", buf.at[1], buf.at[2], me.dev(dx=1))

    def m3():
        cp.wait_recv(slots["x"], buf.at[2], me.dev(dx=1))
        buf[3] = buf[1] + buf[2]
        send("y", buf.at[3], buf.at[4], me.dev(dy=1))

    def m4():
        cp.wait_recv(slots["y"], buf.at[4], me.dev(dy=1))
        buf[5] = buf[3] + buf[4]
        buf[6 + me.z] = buf[5]
        for d in (1, 2, 3):
            send(d, buf.at[5], buf.at[6 + me.z], me.dev(dz=d))

    def total():
        for d in (1, 2, 3):
            cp.wait_recv(slots[d], buf.at[6 + flip(me.z, d)], me.dev(dz=d))
        return (buf[6] + buf[7]) + (buf[8] + buf[9])

    return m1, m2, m3, m4, total


CUBE_COPIES = 10
CUBE_SLOTS = 12
CUBE = tuple((dx, dc, dy) for dx in (0, 1) for dc in (0, 1) for dy in (0, 1))


def cube_stages(me, cp, mine, buf):
    slots = {}

    def at(dx, dc, dy):
        x = me.xo if dx else me.x
        c = me.co if dc else me.c
        y = me.yo if dy else me.y
        return buf.at[4 * x + 2 * c + y]

    def m1():
        for way in CUBE[1:]:
            slots[way] = cp.slot()
            cp.send(slots[way], mine, at(0, 0, 0), me.dev(way[0], way[1], 0, way[2]))
        at(0, 0, 0)[...] = mine[...]

    def m2():
        for way in CUBE[1:]:
            cp.wait_recv(slots[way], at(*way), me.dev(way[0], way[1], 0, way[2]))
        total = buf[0]
        for n in range(1, 8):
            total = total + buf[n]
        there = buf.at[8 + me.z]
        there[...] = total
        for d in (1, 2, 3):
            slots[d] = cp.slot()
            cp.send(slots[d], there, there, me.dev(dz=d))

    def total():
        for d in (1, 2, 3):
            cp.wait_recv(slots[d], buf.at[8 + flip(me.z, d)], me.dev(dz=d))
        return (buf[8] + buf[9]) + (buf[10] + buf[11])

    return m1, m2, total


def forward_body(
    weights, tokens, upstream, mods, b_qkv, b_proj, b_up, b_down,
    block_out, natural, input_att, proj_out, attended, branch, input_mlp, active_out, slope_out,
    grad_out, grad_gate, grads, held, spread, acc, hid, proj, active, slope, woven,
    copy_sems, ready,
):
    columns = mods.shape[1]

    lines = held.reshape(8 * MATS, 8, D)

    def fetch(first, groups, slot):
        return pltpu.make_async_copy(
            weights.at[pl.ds(first, groups)], lines.at[pl.ds(slot * MATS, groups)], copy_sems.at[0]
        )

    def whole(mat, slot):
        return pltpu.make_async_copy(
            weights.at[pl.ds(mat * MATS, MATS)], held.at[slot], copy_sems.at[2 + slot]
        )

    def save(mat, slot):
        return pltpu.make_async_copy(held.at[slot], natural.at[mat], copy_sems.at[10 + mat])

    def keep(src, dst, n):
        return pltpu.make_async_copy(src, dst, copy_sems.at[17 + n])

    def unweave(ways, source, slot0):
        def step(j, carry):
            def put(w, lanes, block):
                held[slot0 + w, pl.ds(j * 16, 16), :, lanes] = block

            groups = 16 * ways
            src = lines.at[pl.ds(source * MATS + j * groups, groups)]
            split_rows(src, spread, put, ways)
            return carry

        lax.fori_loop(0, 9, step, 0)

    def first_norm(c, rows, at):
        normed, _ = norm_rows(tokens[rows].astype(f32))
        input_att[rows] = (normed * (1.0 + mods[1, at]) + mods[0, at]).astype(bf16)

    over_columns(columns, first_norm)
    ready("qkv")
    fetch(0, 3 * MATS, 4).start()
    whole(3, 3).start()
    fetch(0, 3 * MATS, 4).wait()
    unweave(3, 4, 0)
    for p in range(3):
        save(p, p).start()

    for p in range(3):
        proj[p] = (nn_dot(input_att[...], square(held.at[p])) + b_qkv[pl.ds(p, 1)]).astype(bf16)
        ready("project", p)
    keep(proj, proj_out, 0).start()

    inside = same_column()

    def attend(g, carry):
        rows = pl.ds(pl.multiple_of(g * 128, 128), 128)
        acc[pl.ds(0, 128)] = jnp.zeros((128, D), f32)
        for h in range(H):
            window, mask = head_window(h)
            probs = head_probabilities(proj[0, rows, window] * mask, proj[1, rows, window], inside)
            acc[pl.ds(0, 128), window] += nn_dot(probs.astype(bf16), proj[2, rows, window] * mask)
        attended[rows] = acc[pl.ds(0, 128)].astype(bf16)
        return carry

    for g in range(columns * FRAMES // 128):
        lax.fori_loop(g, g + 1, attend, 0)
        ready("attend", g)
    ready("proj")
    whole(3, 3).wait()
    branch[...] = nn_dot(attended[...], square(held.at[3])) + b_proj[...]
    for p in range(3):
        save(p, p).wait()

    def second_norm(c, rows, at):
        middle = tokens[rows].astype(f32) + mods[2, at] * branch[rows]
        normed, _ = norm_rows(middle)
        input_mlp[rows] = (normed * (1.0 + mods[4, at]) + mods[3, at]).astype(bf16)
        grad_block = jnp.where(mods[6, at] > 0.5, upstream[rows].astype(f32), 0.0)
        grad_out[rows] = (grad_block * mods[5, at]).astype(bf16)

    over_columns(columns, second_norm)
    ready("up")
    fetch(AT_UP, 4 * MATS, 0).start()
    fetch(AT_UP, 4 * MATS, 0).wait()
    unweave(4, 0, 4)
    for b in range(4):
        save(3 + b, 4 + b).start()

    def raise_(b, carry):
        hid[...] = nn_dot(input_mlp[...], square(held.at[4 + b])) + b_up[pl.ds(b, 1)]

        def gelu(c, rows, at):
            v = hid[rows]
            sq = v * v
            t = jnp.tanh(ROOT * (v + CUBIC * sq * v))
            half = 0.5 * (1.0 + t)
            active[b, rows] = (v * half).astype(bf16)
            rise = half + (0.5 * ROOT) * v * (1.0 - t * t) * (1.0 + 3.0 * CUBIC * sq)
            for q in range(9):
                slope[b, q, rows] = rise[:, 128 * q : 128 * q + 128]

        over_columns(columns, gelu)
        return carry

    for b in range(4):
        lax.fori_loop(b, b + 1, raise_, 0)
        ready("raise", b)
    keep(active, active_out, 1).start()
    keep(slope, slope_out, 2).start()
    whole(8, 0).start()

    def stash(b, r):
        return pltpu.make_async_copy(
            woven.at[pl.ds(48 * r, 48)], grads.at[pl.ds(AT_DOWN + b * MATS + 48 * r, 48)],
            copy_sems.at[20 + r],
        )

    for b in range(4):
        for r in range(3):
            part = tn_dot(active[b, :, 384 * r : 384 * r + 384], grad_out[...])
            if b:
                stash(b - 1, r).wait()
            woven[pl.ds(48 * r, 48)] = part.reshape(48, 8, D).astype(bf16)
            stash(b, r).start()
        ready("outer", b)
    acc[...] = jnp.broadcast_to(b_down[...], acc.shape)
    whole(8, 0).wait()
    acc[...] += nn_dot(active[0], square(held.at[0]))
    ready("down")
    for b in range(1, 4):
        whole(8 + b, b).start()
    for b in range(1, 4):
        whole(8 + b, b).wait()
        acc[...] += nn_dot(active[b], square(held.at[b]))

    def last(c, rows, at):
        x = tokens[rows].astype(f32)
        middle = x + mods[2, at] * branch[rows]
        video = mods[6, at] > 0.5
        outcome = acc[rows]
        block_out[rows] = jnp.where(video, middle + mods[5, at] * outcome, x)
        grad_block = jnp.where(video, upstream[rows].astype(f32), 0.0)
        grad_gate[at] = jnp.sum(grad_block * outcome, axis=0, keepdims=True)

    over_columns(columns, last)
    for b in range(4):
        save(3 + b, 4 + b).wait()
    keep(proj, proj_out, 0).wait()
    keep(active, active_out, 1).wait()
    keep(slope, slope_out, 2).wait()
    for r in range(3):
        stash(3, r).wait()


def forward_kernel(*refs):
    forward_body(*refs, lambda name, step=0: None)


def gather_forward_kernel(
    flat_shard, selector, chosen, base, tokens, upstream, b_qkv, b_proj, b_up, b_down,
    full, mods, shard, *refs,
):
    refs, (partial, sums, send_sems, recv_sems, local_sems) = refs[:-5], refs[-5:]
    lines = refs[-3].reshape(4 * 9 * tokens.shape[0], 128)
    arrival = pltpu.make_async_copy(
        flat_shard, lines.at[pl.ds(0, 9 * UNITS)], local_sems.at[1]
    )
    arrival.start()
    me = Place()
    cp = Copies(send_sems, recv_sems)
    me.greet()
    arrival.wait()

    def regroup(j, carry):
        for q in range(9):
            part = lines[pl.ds(72 * j + q, 8, stride=9), :]
            shard[j, :, 128 * q : 128 * q + 128] = part.astype(bf16)
        return carry

    lax.fori_loop(0, GROUPS8, regroup, 0)
    partial[...] = nn_dot(selector[...], shard[...].reshape(UNITS, D))
    st = gather_stages(me, cp, shard, full, local_sems)
    s0, s1, s2, s3, s4, s5 = (st["s%d" % n] for n in range(6))
    t1, t2, t3, t4, t5 = (st["t%d" % n] for n in range(1, 6))
    m1, m2, m3, m4, total = sum_stages(me, cp, partial, sums)
    s0(0)
    m1()
    s0(1)
    s0(2)
    s1(0)
    m2()
    s1(1)
    m3()
    t1()
    s2(0)
    m4()
    t2()
    s1(2)
    s3(0)
    t3()
    s2(1)
    t4()
    table = exact(chosen[...], total(), (((1,), (0,)), ((), ()))) + base[...]
    columns = mods.shape[1]
    for n in range(7):
        mods[n] = table[n * columns : (n + 1) * columns]

    def ready(name, step=0):
        if name == "qkv":
            s4(0)
            t5()
            s5(0)
        elif name == "project":
            s3(1, (step,))
        elif name == "attend":
            if step == 0:
                s3(1, (3,))
            elif step == 1:
                s2(2)
            else:
                s4(1)
        elif name == "up":
            s5(1)
        elif name == "raise":
            s3(2, (step,))
        elif name == "down":
            s4(2)
            s5(2)

    forward_body(
        full.reshape(4 * 4 * 2 * GROUPS8, 8, D), tokens, upstream, mods, b_qkv, b_proj, b_up,
        b_down, *refs, ready,
    )
    cp.drain()


def forward_shapes(rows, columns):
    shape = jax.ShapeDtypeStruct
    return [
        shape((rows, D), f32),
        shape((7, MATS, 8, D), bf16),
        shape((rows, D), bf16),
        shape((3, rows, D), bf16),
        shape((rows, D), bf16),
        shape((rows, D), f32),
        shape((rows, D), bf16),
        shape((4, rows, D), bf16),
        shape((4, 9, rows, 128), f32),
        shape((rows, D), bf16),
        shape((columns, D), f32),
        shape((32 * UNITS // 8, 8, D), bf16),
    ]


VMEM_SPEC = pl.BlockSpec(memory_space=pltpu.VMEM)
HBM_SPEC = pl.BlockSpec(memory_space=pl.ANY)
FORWARD_SPECS = [
    VMEM_SPEC, HBM_SPEC, VMEM_SPEC, HBM_SPEC, VMEM_SPEC, VMEM_SPEC, VMEM_SPEC, HBM_SPEC, HBM_SPEC,
    VMEM_SPEC, VMEM_SPEC, HBM_SPEC,
]


def forward_scratch(rows):
    return [
        pltpu.VMEM((8, MATS, 8, D), bf16),
        pltpu.VMEM((9, 512, 128), f32),
        pltpu.VMEM((rows, D), f32),
        pltpu.VMEM((rows, D), f32),
        pltpu.VMEM((3, rows, D), bf16),
        pltpu.VMEM((4, rows, D), bf16),
        pltpu.VMEM((4, 9, rows, 128), f32),
        pltpu.VMEM((MATS, 8, D), bf16),
        pltpu.SemaphoreType.DMA((23,)),
    ]


def forward(weights, tokens, upstream, mods, b_qkv, b_proj, b_up, b_down):
    rows = tokens.shape[0]
    return pl.pallas_call(
        forward_kernel,
        out_shape=forward_shapes(rows, mods.shape[1]),
        in_specs=[HBM_SPEC] + [VMEM_SPEC] * 7,
        out_specs=FORWARD_SPECS,
        scratch_shapes=forward_scratch(rows),
        compiler_params=pltpu.CompilerParams(vmem_limit_bytes=62 * 2**20),
        name="block_forward",
    )(weights, tokens, upstream, mods, b_qkv, b_proj, b_up, b_down)


def gather_forward(
    flat_shard, selector, chosen, base, tokens, upstream, b_qkv, b_proj, b_up, b_down
):
    rows = tokens.shape[0]
    columns = rows // FRAMES
    copies = GATHER_COPIES + SUM_COPIES
    return pl.pallas_call(
        gather_forward_kernel,
        out_shape=[
            jax.ShapeDtypeStruct((4, 4, 2, GROUPS8, 8, D), bf16),
            jax.ShapeDtypeStruct((7, columns, D), f32),
            jax.ShapeDtypeStruct((GROUPS8, 8, D), bf16),
        ]
        + forward_shapes(rows, columns),
        in_specs=[HBM_SPEC] + [VMEM_SPEC] * 9,
        out_specs=[HBM_SPEC, VMEM_SPEC, VMEM_SPEC] + FORWARD_SPECS,
        scratch_shapes=forward_scratch(rows)
        + [
            pltpu.VMEM((selector.shape[0], D), f32),
            pltpu.VMEM((SUM_SLOTS, selector.shape[0], D), f32),
            pltpu.SemaphoreType.DMA((copies,)),
            pltpu.SemaphoreType.DMA((copies,)),
            pltpu.SemaphoreType.DMA((2,)),
        ],
        compiler_params=pltpu.CompilerParams(
            collective_id=0, has_side_effects=True, vmem_limit_bytes=63 * 2**20
        ),
        name="gather_forward",
    )(flat_shard, selector, chosen, base, tokens, upstream, b_qkv, b_proj, b_up, b_down)


UP_RUNS = ((0, 256), (256, 256), (512, 256), (768, 256), (1024, 128))
QKV_RUNS = ((0, 384), (384, 384), (768, 384))


def backward_body(
    weights, natural, slope, tokens, upstream, mods, input_att, proj, attended, branch,
    input_mlp, grad_out,
    grads, input_grad, grad_mods, bias_sums,
    held, woven, spread, grad_hidden, grad_branch, grad_att, acc, copy_sems, tick,
):
    columns = mods.shape[1]
    row_count = columns * FRAMES

    def fetch(first, slot):
        return pltpu.make_async_copy(natural.at[first], held.at[slot], copy_sems.at[slot])

    def flat_mat(first, slot):
        return pltpu.make_async_copy(
            weights.at[pl.ds(first, MATS)], held.at[slot], copy_sems.at[slot]
        )

    def stream(b, slot):
        at = pl.ds(pl.multiple_of(slot * row_count, row_count), row_count)
        return (
            flat_mat(AT_DOWN + b * MATS, slot),
            pltpu.make_async_copy(slope.at[b], spread.at[:, at], copy_sems.at[4 + slot]),
        )

    def store(first, offset, groups, n):
        return pltpu.make_async_copy(
            woven.at[pl.ds(offset, groups)], grads.at[pl.ds(first, groups)], copy_sems.at[6 + n]
        )

    bias_sums[...] = jnp.zeros_like(bias_sums)

    def add_bias(row, values):
        bias_sums[pl.ds(row, 1)] += jnp.sum(values.astype(f32), axis=0, keepdims=True)

    def outer(first, left, right):
        for r in range(3):
            part = tn_dot(left[:, 384 * r : 384 * r + 384], right[...])
            woven[pl.ds(48 * r, 48)] = part.reshape(48, 8, D).astype(bf16)
            store(first + 48 * r, 48 * r, 48, r).start()

    for copy in stream(0, 0):
        copy.start()

    def down(b, carry):
        slot = lax.rem(b, 2)
        for copy in stream(b, slot):
            copy.wait()

        @pl.when(b < 3)
        def _():
            for copy in stream(b + 1, 1 - slot):
                copy.start()

        acc[...] = nt_dot(grad_out[...], square(held.at[slot]))

        def through(c, rows, at):
            there = pl.ds(pl.multiple_of(slot * row_count + c * FRAMES, FRAMES), FRAMES)
            rise = jnp.concatenate([spread[q, there] for q in range(9)], axis=1)
            grad = (acc[rows] * rise).astype(bf16)
            grad_hidden[b, rows] = grad
            add_bias(5 + b, grad)

        over_columns(columns, through)
        return carry

    tick("begin")
    for b in range(4):
        lax.fori_loop(b, b + 1, down, 0)
        tick("down", b)
    fetch(3, 0).start()

    def down_bias(c, rows, at):
        add_bias(4, grad_out[rows])

    over_columns(columns, down_bias)

    def weave(first, ways, left, right, runs, name):
        before = None
        for k, (start, count) in enumerate(runs):
            for w in range(ways):
                part = tn_dot(left[:, start : start + count], right[w])
                for q in range(9):
                    spread[q, pl.ds(w, count, stride=ways), :] = part[:, 128 * q : 128 * q + 128]
            if before is not None:
                before.wait()

            def pack(j, carry):
                for q in range(9):
                    lines = spread[q, pl.ds(pl.multiple_of(j * 128, 128), 128), :]
                    woven[pl.ds(j * 16, 16), :, 128 * q : 128 * q + 128] = lines.reshape(
                        16, 8, 128
                    ).astype(bf16)
                return carry

            groups = count * ways // 8
            lax.fori_loop(0, groups // 16, pack, 0)
            before = store(first + start * ways // 8, 0, groups, 0)
            before.start()
            tick(name, k)
        before.wait()

    weave(AT_UP, 4, input_mlp, grad_hidden, UP_RUNS, "up run")
    tick("up")
    acc[...] = jnp.zeros_like(acc)
    for b in range(4):
        fetch(3 + b, b % 2).wait()
        if b < 3:
            fetch(4 + b, 1 - b % 2).start()
        acc[...] += nt_dot(grad_hidden[b], square(held.at[b % 2]))
        tick("up input", b)
    flat_mat(AT_PROJ, 0).start()

    def second_norm_back(c, rows, at):
        br = branch[rows]
        gate = mods[2, at]
        normed, inverse = norm_rows(tokens[rows].astype(f32) + gate * br)
        grad = acc[rows]
        grad_mods[3, at] = jnp.sum(grad, axis=0, keepdims=True)
        grad_mods[4, at] = jnp.sum(grad * normed, axis=0, keepdims=True)
        grad_block = jnp.where(mods[6, at] > 0.5, upstream[rows].astype(f32), 0.0)
        grad_middle = grad_block + norm_rows_back(grad * (1.0 + mods[4, at]), normed, inverse)
        input_grad[rows] = grad_middle
        grad_mods[2, at] = jnp.sum(grad_middle * br, axis=0, keepdims=True)
        grad = (grad_middle * gate).astype(bf16)
        grad_branch[rows] = grad
        add_bias(3, grad)

    over_columns(columns, second_norm_back)
    tick("norm")
    outer(AT_PROJ, attended, grad_branch)
    flat_mat(AT_PROJ, 0).wait()
    grad_att[...] = nt_dot(grad_branch[...], square(held.at[0])).astype(bf16)
    fetch(0, 0).start()
    for r in range(3):
        store(AT_PROJ + 48 * r, 48 * r, 48, r).wait()
    tick("proj")
    inside = same_column()

    def attend_back(g, carry):
        rows = pl.ds(pl.multiple_of(g * 128, 128), 128)
        for p in range(3):
            acc[pl.ds(p * 128, 128)] = jnp.zeros((128, D), f32)
        for h in range(H):
            window, mask = head_window(h)
            queries = proj[0, rows, window] * mask
            keys = proj[1, rows, window]
            grad = grad_att[rows, window] * mask
            probs = head_probabilities(queries, keys, inside)
            grad_probs = nt_dot(grad, proj[2, rows, window])
            mean = jnp.sum(grad_probs * probs, axis=-1, keepdims=True)
            grad_scores = (probs * (grad_probs - mean)).astype(bf16)
            acc[pl.ds(0, 128), window] += nn_dot(grad_scores, keys * mask)
            acc[pl.ds(128, 128), window] += tn_dot(grad_scores, queries)
            acc[pl.ds(256, 128), window] += tn_dot(probs.astype(bf16), grad)
        for p in range(3):
            scale = SCORE_SCALE if p < 2 else 1.0
            grad = (acc[pl.ds(p * 128, 128)] * scale).astype(bf16)
            grad_hidden[p, rows] = grad
            add_bias(p, grad)
        return carry

    for g in range(row_count // 128):
        lax.fori_loop(g, g + 1, attend_back, 0)
        tick("attend", g)
    weave(0, 3, input_att, grad_hidden, QKV_RUNS, "qkv run")
    tick("qkv")
    acc[...] = jnp.zeros_like(acc)
    for p in range(3):
        fetch(p, p % 2).wait()
        if p < 2:
            fetch(p + 1, 1 - p % 2).start()
        acc[...] += nt_dot(grad_hidden[p], square(held.at[p % 2]))
        tick("qkv input", p)

    def first_norm_back(c, rows, at):
        normed, inverse = norm_rows(tokens[rows].astype(f32))
        grad = acc[rows]
        grad_mods[0, at] = jnp.sum(grad, axis=0, keepdims=True)
        grad_mods[1, at] = jnp.sum(grad * normed, axis=0, keepdims=True)
        grad_states = input_grad[rows] + norm_rows_back(
            grad * (1.0 + mods[1, at]), normed, inverse
        )
        up_rows = upstream[rows].astype(f32)
        input_grad[rows] = jnp.where(mods[6, at] > 0.5, grad_states, up_rows)

    over_columns(columns, first_norm_back)
    tick("end")


def backward_kernel(given, *refs):
    backward_body(*refs, lambda name, step=0: None)


def backward_scatter_kernel(*refs):
    (
        given, weights, natural, slope, tokens, upstream, mods, input_att, proj, attended, branch,
        input_mlp, grad_out, grad_gate, member,
        out, grads, other, input_grad, total_small,
        grad_mods, bias_sums, held, woven, spread, grad_hidden, grad_branch, grad_att, acc, copy_sems,
        own, stage, rx2, ry2, rx1, ry1, rz, final, tail, tail_in, tail_z, local_sems, credit,
        small, sums, send_sems, recv_sems,
    ) = refs
    me = Place()
    cp = Copies(send_sems, recv_sems)
    me.greet()
    st = scatter_stages(
        me, cp, grads, out, other, own, stage, rx2, ry2, rx1, ry1, rz, final, tail, tail_in,
        tail_z, local_sems, credit,
    )
    t0, t1, t2, t3, t4, t5 = st["tails"]
    m1, m2, m3, m4, total = sum_stages(me, cp, small, sums)
    groups = member.shape[0]

    def run(steps):
        acts = dict(
            E=st["exchange"], P=st["prefetch"], A=st["fold"], B=st["second"], C=st["third"],
            S=st["settle"],
        )
        for step in steps.split():
            acts[step[0]](int(step[1:]))

    turns = {
        ("begin", 0): "E2 P0",
        ("down", 1): "A0 P1",
        ("down", 3): "A1 P2 B0",
        ("up run", 1): "A2 P3 B1 C0",
        ("up run", 4): "A3 B2 C1",
        ("up", 0): "E1 P4",
        ("up input", 1): "A4 P5 B3 C2",
        ("norm", 0): "A5 P6 B4 C3",
        ("proj", 0): "S2",
        ("attend", 0): "A6 P7 B5 C4",
        ("attend", 1): "A7 B6 C5",
        ("qkv", 0): "E0 P8",
        ("qkv input", 0): "A8 P9",
        ("attend", 2): "B7 C6",
        ("qkv input", 2): "A9 P10 B8 C7",
    }

    def tick(name, step=0):
        run(turns.get((name, step), ""))
        if (name, step) == ("qkv", 0):
            t0()
        if (name, step) == ("qkv input", 0):
            t1()
        if (name, step) == ("qkv input", 2):
            t2()
        if name == "end":
            for n in range(6):
                plane = grad_mods[n] if n < 5 else grad_gate[...]
                small[pl.ds(n * groups, groups)] = exact(
                    member[...], plane, (((1,), (0,)), ((), ()))
                )
            small[pl.ds(6 * groups, 9)] = bias_sums[pl.ds(0, 9)]
            small[pl.ds(6 * groups + 9, small.shape[0] - 6 * groups - 9)] = jnp.zeros(
                (small.shape[0] - 6 * groups - 9, D), f32
            )
            m1()
            run("A10 P11 B9 C8")
            t3()
            m2()
            run("A11 B10 C9 S1")
            t4()
            m3()
            t5()
            m4()
            run("B11 C10 C11 S0")
            total_small[...] = total()
            for p in (2, 1, 0):
                st["finish"](p)
            cp.drain()

    backward_body(
        weights, natural, slope, tokens, upstream, mods, input_att, proj, attended, branch,
        input_mlp, grad_out,
        grads.reshape(4 * 4 * 2 * GROUPS8, 8, D), input_grad, grad_mods, bias_sums,
        held, woven, spread, grad_hidden, grad_branch, grad_att, acc, copy_sems,
        tick,
    )


def backward_shapes(rows, columns):
    shape = jax.ShapeDtypeStruct
    return [
        shape((rows, D), f32),
        shape((5, columns, D), f32),
        shape((16, D), f32),
    ]


def backward_scratch(rows):
    return [
        pltpu.VMEM((2, MATS, 8, D), bf16),
        pltpu.VMEM((MATS, 8, D), bf16),
        pltpu.VMEM((9, D, 128), f32),
        pltpu.VMEM((4, rows, D), bf16),
        pltpu.VMEM((rows, D), bf16),
        pltpu.VMEM((rows, D), bf16),
        pltpu.VMEM((rows, D), f32),
        pltpu.SemaphoreType.DMA((9,)),
    ]


def backward(*operands):
    rows, columns = operands[4].shape[0], operands[6].shape[1]
    return pl.pallas_call(
        backward_kernel,
        out_shape=[jax.ShapeDtypeStruct((32 * UNITS // 8, 8, D), bf16)]
        + backward_shapes(rows, columns),
        in_specs=[HBM_SPEC] * 4 + [VMEM_SPEC] * 9,
        out_specs=[HBM_SPEC] + [VMEM_SPEC] * 3,
        input_output_aliases={0: 0},
        scratch_shapes=backward_scratch(rows),
        compiler_params=pltpu.CompilerParams(vmem_limit_bytes=62 * 2**20),
        name="block_backward",
    )(*operands)


def backward_scatter(operands, grad_gate, member):
    rows, columns = operands[4].shape[0], operands[6].shape[1]
    small = small_rows(member.shape[0])
    copies = SCATTER_COPIES + SUM_COPIES
    shape = jax.ShapeDtypeStruct
    input_grad, grad_mods, bias_sums = backward_shapes(rows, columns)
    return pl.pallas_call(
        backward_scatter_kernel,
        out_shape=[
            shape((GROUPS8, 8, D), bf16),
            shape((4, 4, 2, GROUPS8, 8, D), bf16),
            shape((3, 4, 2, 2, QUART, 8, D), bf16),
            input_grad,
            shape((small, D), f32),
        ],
        in_specs=[HBM_SPEC] * 4 + [VMEM_SPEC] * 11,
        out_specs=[HBM_SPEC] * 3 + [VMEM_SPEC] * 2,
        input_output_aliases={0: 1},
        scratch_shapes=[
            pltpu.VMEM(grad_mods.shape, f32),
            pltpu.VMEM(bias_sums.shape, f32),
        ]
        + backward_scratch(rows)
        + scatter_scratch()
        + [
            pltpu.VMEM((small, D), f32),
            pltpu.VMEM((SUM_SLOTS, small, D), f32),
            pltpu.SemaphoreType.DMA((copies,)),
            pltpu.SemaphoreType.DMA((copies,)),
        ],
        compiler_params=pltpu.CompilerParams(
            collective_id=1, has_side_effects=True, vmem_limit_bytes=63 * 2**20
        ),
        name="backward_scatter",
    )(*operands, grad_gate, member)


def small_rows(groups):
    return -(-(6 * groups + 9) // 8) * 8


def adamw_rows(value, grad, first, second):
    first_new = BETA_FIRST * first + (1.0 - BETA_FIRST) * grad
    second_new = BETA_SECOND * second + (1.0 - BETA_SECOND) * grad * grad
    first_hat = first_new / (1.0 - BETA_FIRST**STEP)
    second_hat = second_new / (1.0 - BETA_SECOND**STEP)
    step = first_hat / (jnp.sqrt(second_hat) + ADAM_EPS) + WEIGHT_DECAY * value
    return value - LEARN_RATE * step, first_new, second_new


def norm_kernel(
    shard_sum, low, small, selector, parts_t, row_of, in_ada, cond,
    cond_grad, norm_out, flat, bias_flat,
    ada, mine, own_cond, sums, cond_sums, send_sems, recv_sems,
):
    groups = cond.shape[0]
    me = Place()
    cp = Copies(send_sems, recv_sems)
    me.greet()
    m1, m2, total = cube_stages(me, cp, mine, sums)
    n1, n2, cond_total = cube_stages(me, cp, own_cond, cond_sums)
    dims = (((1,), (0,)), ((), ()))
    parts = small[pl.ds(0, 6 * groups)]
    ada[...] = exact(selector[...], parts, dims)

    def spread_group(j, square):
        rows = pl.ds(pl.multiple_of(j * 8, 8), 8)
        grad = jnp.where(in_ada[rows] > 0.5, ada[rows], shard_sum[j].astype(f32))
        for q in range(9):
            flat[pl.ds(72 * j + q, 8, stride=9), :] = grad[:, 128 * q : 128 * q + 128]
        return square + grad * grad

    square = lax.fori_loop(0, GROUPS8, spread_group, jnp.zeros((8, D), f32))
    lanes = square[:, :128]
    for q in range(1, 9):
        lanes = lanes + square[:, 128 * q : 128 * q + 128]
    mine[...] = lanes
    m1()
    products = exact(parts, low[...].reshape(UNITS, D).astype(f32), (((1,), (1,)), ((), ())))
    products = products * parts_t[...]
    folded = products[:groups]
    for n in range(1, 6):
        folded = folded + products[n * groups : (n + 1) * groups]
    lane = lax.broadcasted_iota(jnp.int32, (UNITS, 128), 1)
    own_cond[...] = jnp.zeros_like(own_cond)
    for q in range(9):
        hit = jnp.where(row_of[...] == lane + 128 * q, 1.0, 0.0)
        own_cond[pl.ds(0, groups), 128 * q : 128 * q + 128] = exact(folded, hit, dims)
    n1()
    m2()
    bias_rows = [small[pl.ds(6 * groups + n, 1)] for n in (0, 2, 3, 5, 6, 7, 8, 4)]
    for n in range(6):
        bias_rows.append(jnp.sum(small[pl.ds(n * groups, groups)], axis=0, keepdims=True))
    for t, line in enumerate(bias_rows):
        for q in range(9):
            bias_flat[pl.ds(9 * t + q, 1)] = line[:, 128 * q : 128 * q + 128]
    bias_square = jnp.sum(bias_flat[...] * bias_flat[...], axis=0, keepdims=True)
    n2()
    squares = jnp.sum(total(), axis=0, keepdims=True) + bias_square
    norm_out[...] = jnp.sqrt(jnp.sum(squares, axis=1, keepdims=True))
    summed = cond_total()
    c = cond[...]
    gate = 1.0 / (1.0 + jnp.exp(-c))
    cond_grad[...] = summed[:groups] * (gate * (1.0 + c * (1.0 - gate)))
    cp.drain()


def norm_exchange(*operands):
    cond = operands[7]
    shape = jax.ShapeDtypeStruct
    payload = 8 * (cond.shape[0] // 8 + 1)
    return pl.pallas_call(
        norm_kernel,
        out_shape=[
            shape(cond.shape, f32), shape((1, 1), f32), shape((9 * UNITS, 128), f32),
            shape((BIAS_LINES, 128), f32),
        ],
        in_specs=[VMEM_SPEC] * len(operands),
        out_specs=[VMEM_SPEC] * 4,
        scratch_shapes=[
            pltpu.VMEM((UNITS, D), f32),
            pltpu.VMEM((8, 128), f32),
            pltpu.VMEM((payload, D), f32),
            pltpu.VMEM((CUBE_SLOTS, 8, 128), f32),
            pltpu.VMEM((CUBE_SLOTS, payload, D), f32),
            pltpu.SemaphoreType.DMA((2 * CUBE_COPIES,)),
            pltpu.SemaphoreType.DMA((2 * CUBE_COPIES,)),
        ],
        compiler_params=pltpu.CompilerParams(
            collective_id=2, has_side_effects=True, vmem_limit_bytes=40 * 2**20
        ),
        name="norm_exchange",
    )(*operands)


BIAS_LINES = 126


def adamw_kernel(
    norm, flat, weights, first, second, bias_flat, biases, bias_first, bias_second, block_in,
    grad_in,
    new_weights, first_out, second_out, new_biases, bias_first_out, bias_second_out, block_out,
    grad_out,
    sems,
):
    passed = (
        pltpu.make_async_copy(block_in, block_out, sems.at[0]),
        pltpu.make_async_copy(grad_in, grad_out, sems.at[1]),
    )
    factor = jnp.minimum(1.0, CLIP_NORM / (norm[...] + 1e-06))
    step = pl.program_id(0)

    @pl.when(step == 0)
    def _():
        for copy in passed:
            copy.start()
        new_biases[...], bias_first_out[...], bias_second_out[...] = adamw_rows(
            biases[...], bias_flat[...] * factor, bias_first[...], bias_second[...]
        )

    def update(j, carry):
        at = pl.ds(pl.multiple_of(j * 72, 8), 72)
        new_weights[at], first_out[at], second_out[at] = adamw_rows(
            weights[at], flat[at] * factor, first[at], second[at]
        )
        return carry

    lax.fori_loop(0, 9, update, 0)

    @pl.when(step == pl.num_programs(0) - 1)
    def _():
        for copy in passed:
            copy.wait()


def adamw_update(norm, flat, state, bias_flat, bias_state, block_in, grad_in):
    shape = jax.ShapeDtypeStruct
    run = pl.BlockSpec((648, 128), lambda j: (j, 0))
    bias = pl.BlockSpec((BIAS_LINES, 128), lambda j: (0, 0))
    like = [shape(flat.shape, f32)] * 3 + [shape((BIAS_LINES, 128), f32)] * 3
    return pl.pallas_call(
        adamw_kernel,
        out_shape=like + [shape(block_in.shape, f32), shape(grad_in.shape, f32)],
        grid=(flat.shape[0] // 648,),
        in_specs=[pl.BlockSpec((1, 1), lambda j: (0, 0))]
        + [run] * 4
        + [bias] * 4
        + [HBM_SPEC] * 2,
        out_specs=[run] * 3 + [bias] * 3 + [HBM_SPEC] * 2,
        scratch_shapes=[pltpu.SemaphoreType.DMA((2,))],
        compiler_params=pltpu.CompilerParams(vmem_limit_bytes=40 * 2**20),
        name="adamw",
    )(norm, flat, *state, bias_flat, *bias_state, block_in, grad_in)


def gather_blocks(shard_low):
    whole = lax.all_gather(shard_low, ("outer", "inner"), axis=0, tiled=True)
    return whole.reshape(-1, 8, D)


def scatter_blocks(grads, units):
    axes = ("outer", "inner")
    whole = grads.reshape(-1, D)[: lax.axis_size(axes) * units].astype(f32)
    return lax.psum_scatter(whole, axes, scatter_dimension=0, tiled=True)


def split_bias(vector):
    widths = [D, D, D, FF, D, 6 * D]
    pieces = []
    offset = 0
    for span_width in widths:
        pieces.append(lax.slice_in_dim(vector, offset, offset + span_width))
        offset = offset + span_width
    return pieces


def exact(left, right, dims):
    return lax.dot_general(
        left, right, dims, precision=lax.Precision.HIGHEST, preferred_element_type=jnp.float32
    )


def ada_selector(soft_cond, first_unit, units):
    groups = soft_cond.shape[0]
    spread = jnp.repeat(soft_cond.astype(jnp.float32), 6, axis=1)
    spread = jnp.pad(spread, ((0, 0), (units, units)))
    start = jnp.clip(first_unit - BLOCK_UNITS + units, 0, 6 * D + units)
    local = lax.dynamic_slice(spread, (jnp.int32(0), start), (groups, units))
    unit = first_unit - BLOCK_UNITS + jnp.arange(units, dtype=jnp.int32)
    part = (unit[:, None] % 6 == jnp.arange(6, dtype=jnp.int32)[None, :]) & (unit[:, None] >= 0)
    part = part.astype(jnp.float32)
    selector = local.T[:, :, None] * part[:, None, :]
    return selector.reshape(units, groups * 6), part


def adamw(parameter, gradient, first_state, second_state):
    first_new = BETA_FIRST * first_state + (1.0 - BETA_FIRST) * gradient
    second_new = BETA_SECOND * second_state + (1.0 - BETA_SECOND) * gradient * gradient
    first_hat = first_new / (1.0 - BETA_FIRST**STEP)
    second_hat = second_new / (1.0 - BETA_SECOND**STEP)
    updated = parameter - LEARN_RATE * (
        first_hat / (jnp.sqrt(second_hat) + ADAM_EPS) + WEIGHT_DECAY * parameter
    )
    return (updated, first_new, second_new)


def with_kernels(
    tokens, conditioning, output_grad, state, bias_state, first_unit, selector, ada_part,
    membership, video_plane, b_ada, bias_args,
):
    columns, groups = membership.shape
    units = UNITS
    eye = jnp.eye(6, dtype=f32)
    chosen = membership[None, :, None, :] * eye[:, None, :, None]
    chosen = jnp.pad(chosen.reshape(6 * columns, 6 * groups), ((0, columns), (0, 0)))
    base = jnp.repeat(b_ada.reshape(6, D), columns, axis=0)
    base = jnp.concatenate([base, video_plane])
    by_part = selector.reshape(units, groups, 6).transpose(0, 2, 1).reshape(units, 6 * groups)
    state = [part.reshape(9 * units, 128) for part in state]
    (
        flat, mods, shard_low, block_out, natural, input_att, proj, attended, branch, input_mlp, _,
        slope, grad_out, grad_gate, grads,
    ) = gather_forward(
        state[0], by_part.T.astype(bf16), chosen, base, tokens, output_grad, *bias_args
    )
    flat = flat.reshape(-1, 8, D)
    shard_sum, _, _, input_grad, small = backward_scatter(
        (
            grads.reshape(4, 4, 2, GROUPS8, 8, D), flat, natural, slope, tokens, output_grad, mods,
            input_att, proj, attended, branch, input_mlp, grad_out,
        ),
        grad_gate, membership.T,
    )
    unit = first_unit - BLOCK_UNITS + jnp.arange(units, dtype=jnp.int32)
    row_of = jnp.where(unit >= 0, unit // 6, -1)[:, None]
    parts_t = jnp.repeat(ada_part.T, groups, axis=0)
    in_ada = (unit >= 0).astype(f32)[:, None]
    cond_grad, norm, flat_grad, bias_flat = norm_exchange(
        shard_sum, shard_low, small, by_part, parts_t, row_of, in_ada, conditioning
    )
    *updated, block_out, input_grad = adamw_update(
        norm, flat_grad, state, bias_flat, [part.reshape(-1, 128) for part in bias_state],
        block_out, input_grad,
    )
    return (block_out, input_grad, cond_grad, norm[0, 0], *[part.reshape(-1) for part in updated])


def on_device(
    tokens,
    conditioning,
    column_sample,
    is_image,
    output_grad,
    weights,
    first_moment,
    second_moment,
    biases,
    bias_first,
    bias_second,
    kernels,
):
    columns = column_sample.shape[0]
    groups = conditioning.shape[0]
    units = weights.shape[0] // D
    axes = ("outer", "inner")
    first_unit = lax.axis_index(axes).astype(jnp.int32) * units
    b_query, b_value, b_proj, b_up, b_down, b_ada = split_bias(biases)
    soft_cond = jax.nn.silu(conditioning).astype(bf16)
    selector, ada_part = ada_selector(soft_cond, first_unit, units)
    membership = (column_sample[:, None] == jnp.arange(groups, dtype=jnp.int32)[None, :]).astype(
        f32
    )
    video_cols = exact(membership, 1.0 - is_image.astype(f32)[:, None], (((1,), (0,)), ((), ())))
    b_qkv = jnp.stack([b_query, jnp.zeros((D,), f32), b_value])
    bias_args = (b_qkv, b_proj[None], b_up.reshape(4, D), b_down[None])
    video_plane = jnp.broadcast_to(video_cols, (columns, D))
    if kernels:
        return with_kernels(
            tokens, conditioning, output_grad, (weights, first_moment, second_moment),
            (biases, bias_first, bias_second), first_unit, selector, ada_part, membership,
            video_plane, b_ada, bias_args,
        )
    shard_low = weights.reshape(units, D).astype(bf16)
    flat = gather_blocks(shard_low)
    mods_all = lax.psum(tn_dot(selector.astype(bf16), shard_low), axes)
    mods_all = mods_all.reshape(groups, 6 * D) + b_ada
    mods = jnp.take(mods_all, column_sample, axis=0).reshape(columns, 6, D).transpose(1, 0, 2)
    mods = jnp.concatenate([mods, video_plane[None]])
    (
        block_out, natural, input_att, proj, attended, branch, input_mlp, _, slope, grad_out,
        grad_gate, grads,
    ) = forward(flat, tokens, output_grad, mods, *bias_args)
    grads, input_grad, grad_mods, bias_sums = backward(
        grads, flat, natural, slope, tokens, output_grad, mods, input_att, proj, attended, branch,
        input_mlp, grad_out,
    )
    grad_mods = jnp.concatenate([grad_mods, grad_gate[None]])
    mods_local = exact(membership, grad_mods, (((0,), (1,)), ((), ())))
    bias_sums, grad_mods_all = lax.psum((bias_sums, mods_local.transpose(1, 0, 2)), axes)
    block_shard = scatter_blocks(grads, units)
    grad_mods_all = grad_mods_all.transpose(1, 0, 2).reshape(groups, 6 * D)
    bias_head = jnp.concatenate([bias_sums[:1], bias_sums[2:4], bias_sums[5:9], bias_sums[4:5]])
    first_sum = jnp.concatenate([bias_head.reshape(-1), jnp.sum(grad_mods_all, axis=0)])
    mods_parts = grad_mods_all.reshape(groups * 6, D)
    ada_shard = exact(selector, mods_parts, (((1,), (0,)), ((), ())))
    unit = first_unit + jnp.arange(units, dtype=jnp.int32)
    grad_units = jnp.where(unit[:, None] >= BLOCK_UNITS, ada_shard, block_shard)
    products = exact(shard_low.astype(jnp.float32), mods_parts, (((1,), (1,)), ((), ())))
    products = jnp.sum(products.reshape(units, groups, 6) * ada_part[:, None, :], axis=2)
    spread = jnp.zeros((groups, 6 * D + 2 * units), jnp.float32)
    start = jnp.clip(first_unit - BLOCK_UNITS + units, 0, 6 * D + units)
    spread = lax.dynamic_update_slice(spread, products.T, (jnp.int32(0), start))
    grad_soft = jnp.sum(spread[:, units : units + 6 * D].reshape(groups, D, 6), axis=2)
    square_sum = jnp.sum(grad_units * grad_units)
    square_sum, grad_soft = lax.psum((square_sum, grad_soft), axes)
    silu_out, silu_back = jax.vjp(jax.nn.silu, conditioning)
    second_sum = silu_back(grad_soft)[0]
    grad_shard = grad_units.reshape(-1)
    grad_norm = jnp.sqrt(square_sum + jnp.sum(first_sum * first_sum))
    factor = jnp.minimum(1.0, CLIP_NORM / (grad_norm + 1e-06))
    new_weights, first_out, second_out = adamw(
        weights, grad_shard * factor, first_moment, second_moment
    )
    new_biases, bias_first_out, bias_second_out = adamw(
        biases, first_sum * factor, bias_first, bias_second
    )
    return (
        block_out,
        input_grad,
        second_sum,
        grad_norm,
        new_weights,
        first_out,
        second_out,
        new_biases,
        bias_first_out,
        bias_second_out,
    )


def solution(mesh):
    in_specs = (
        P(("outer", "inner"), None),
        P(),
        P(("outer", "inner")),
        P(),
        P(("outer", "inner"), None),
        P(("outer", "inner")),
        P(("outer", "inner")),
        P(("outer", "inner")),
        P(),
        P(),
        P(),
    )
    out_specs = (
        P(("outer", "inner"), None),
        P(("outer", "inner"), None),
        P(),
        P(),
        P(("outer", "inner")),
        P(("outer", "inner")),
        P(("outer", "inner")),
        P(),
        P(),
        P(),
    )
    kernels = dict(mesh.shape) == {"outer": 4, "inner": 8}
    return jax.shard_map(
        functools.partial(on_device, kernels=kernels), mesh=mesh, in_specs=in_specs, out_specs=out_specs, check_vma=False
    )
```

```python
import functools
import math

import jax
import jax.numpy as jnp
from jax import lax
from jax.experimental import pallas as pl
from jax.experimental.pallas import tpu as pltpu
from jax.sharding import PartitionSpec as P

D = 1152
H = 16
HD = 72
FF = 4608
FRAMES = 16
STEP = 8


NORM_EPS = 1e-06
LEARN_RATE = 0.02
BETA_FIRST = 0.5
BETA_SECOND = 0.55
ADAM_EPS = 1e-08
WEIGHT_DECAY = 0.01
CLIP_NORM = 1.0
BLOCK_UNITS = 4 * D + 2 * FF


MESH = pl.DeviceIdType.MESH
UNITS = 648
GROUPS8 = 81
QUART = 20
FIRST = 8
SECOND = QUART - FIRST
MAIN = 80
TAIL = 1
DEPTH = (4, 4, 3)
BASE = (0, 4, 8)


def flip(z, d):
    if d == 0:
        return z
    if d == 1:
        return z + 1 - 2 * (z % 2)
    if d == 2:
        return z + 2 - 4 * (z // 2)
    return 3 - z


class Place:
    def __init__(self):
        self.o = lax.axis_index("outer")
        self.i = lax.axis_index("inner")
        self.x, self.c = self.o // 2, self.o % 2
        self.z, self.y = self.i // 2, self.i % 2
        self.xo, self.co, self.yo = 1 - self.x, 1 - self.c, 1 - self.y

    def dev(self, dx=0, dc=0, dz=0, dy=0):
        x = self.xo if dx else self.x
        c = self.co if dc else self.c
        y = self.yo if dy else self.y
        return (x * 2 + c, flip(self.z, dz) * 2 + y)

    def greet(self):
        peers = [
            self.dev(dx, dc, 0, dy) for dx in (0, 1) for dc in (0, 1) for dy in (0, 1)
        ][1:]
        peers += [self.dev(dz=1), self.dev(dz=2), self.dev(dz=3)]
        barrier = pltpu.get_barrier_semaphore()
        for peer in peers:
            pl.semaphore_signal(barrier, inc=1, device_id=peer, device_id_type=MESH)
        pl.semaphore_wait(barrier, len(peers))


class Copies:
    def __init__(self, send_sems, recv_sems):
        self.send_sems, self.recv_sems = send_sems, recv_sems
        self.count = 0
        self.sent = []

    def slot(self):
        self.count += 1
        return self.count - 1

    def make(self, slot, src, dst, device):
        return pltpu.make_async_remote_copy(
            src_ref=src, dst_ref=dst, send_sem=self.send_sems.at[slot],
            recv_sem=self.recv_sems.at[slot], device_id=device, device_id_type=MESH,
        )

    def send(self, slot, src, dst, device, cond=None):
        def go():
            self.make(slot, src, dst, device).start()
        if cond is None:
            go()
        else:
            pl.when(cond)(go)
        self.sent.append((slot, src, dst, device, cond))

    def wait_recv(self, slot, dst, device, cond=None):
        def go():
            self.make(slot, dst, dst, device).wait_recv()
        if cond is None:
            go()
        else:
            pl.when(cond)(go)

    def wait_send(self, wanted):
        for entry in self.sent:
            if entry[0] == wanted:
                slot, src, dst, device, cond = entry

                def go():
                    self.make(slot, src, dst, device).wait_send()
                if cond is None:
                    go()
                else:
                    pl.when(cond)(go)
        self.sent = [entry for entry in self.sent if entry[0] != wanted]

    def drain(self):
        for slot, src, dst, device, cond in self.sent:
            def go(slot=slot, src=src, dst=dst, device=device):
                self.make(slot, src, dst, device).wait_send()
            if cond is None:
                go()
            else:
                pl.when(cond)(go)
        self.sent = []


def ok(zb, p):
    return None if DEPTH[p] == 4 else zb < DEPTH[p]


def both(a, b):
    if a is None:
        return b
    if b is None:
        return a
    return jnp.logical_and(a, b)


GATHER_COPIES = 3 * (3 + 5 + 4 * 4 + 8) + 7


def gather_stages(me, cp, shard, full, local_sems):
    def part(p, zb, yb, x, c, first=0, n=QUART):
        return full.at[p, zb, yb, pl.ds((2 * QUART * x + QUART * c + first), n)]

    def own_of(p):
        return both(me.o == p, ok(me.z, p))

    quarter = (2 * QUART * me.x + QUART * me.c)
    own_tail = pltpu.make_async_copy(
        shard.at[pl.ds(MAIN, TAIL)], full.at[me.o, me.z, me.y, pl.ds(MAIN, TAIL)], local_sems.at[0]
    )
    own_tail.start()

    def local_quarter(p):
        return pltpu.make_async_copy(
            shard.at[pl.ds(quarter, QUART)], part(p, me.z, me.y, me.x, me.c), local_sems.at[1]
        )

    slots = {}

    def s0(p):
        @pl.when(own_of(p))
        def _():
            local_quarter(p).start()
        for dx, dc in ((1, 0), (0, 1), (1, 1)):
            s = slots["s0", p, dx, dc] = cp.slot()
            x = me.xo if dx else me.x
            c = me.co if dc else me.c
            cp.send(
                s, shard.at[pl.ds((2 * QUART * x + QUART * c), QUART)],
                part(p, me.z, me.y, x, c), me.dev(dx=dx, dc=dc), own_of(p),
            )

    def s0_wait(p):
        @pl.when(own_of(p))
        def _():
            local_quarter(p).wait()
        ox, oc = p // 2, p % 2
        for dx, dc in ((1, 0), (0, 1), (1, 1)):
            x = me.xo if dx else me.x
            c = me.co if dc else me.c
            cond = both(jnp.logical_and(x == ox, c == oc), ok(me.z, p))
            cp.wait_recv(
                slots["s0", p, dx, dc], part(p, me.z, me.y, me.x, me.c), me.dev(dx=dx, dc=dc), cond
            )

    def spread(p, d):
        zb = place(d)
        mine = part(p, zb, me.y, me.x, me.c)
        s = slots["y1", p, d] = cp.slot()
        cp.send(s, mine, mine, me.dev(dy=1), ok(zb, p))
        s = slots["x1", p, d] = cp.slot()
        cp.send(s, mine, mine, me.dev(dx=1), ok(zb, p))

    def place(e):
        return (me.z, flip(me.z, 1), 2 - me.z // 2, 3 - 3 * (me.z // 2))[e]

    inner = (me.z + 1) // 2 == 1
    outer = jnp.logical_not(inner)

    def pass_on(p, zb, name, device, cond):
        view = part(p, zb, me.y, me.x, me.c)
        s = slots[name, p] = cp.slot()
        cp.send(s, view, view, device, both(cond, ok(zb, p)))

    def arrive(p, e, name, device, cond):
        zb = place(e)
        view = part(p, zb, me.y, me.x, me.c)
        cp.wait_recv(slots[name, p], view, device, both(cond, ok(zb, p)))

    def s1(p):
        s0_wait(p)
        pass_on(p, me.z, "own to 1", me.dev(dz=1), None)
        pass_on(p, me.z, "own to 3", me.dev(dz=3), inner)
        spread(p, 0)

    def s2(p):
        arrive(p, 1, "own to 1", me.dev(dz=1), None)
        pass_on(p, place(1), "1 to 3", me.dev(dz=3), inner)
        spread(p, 1)
        arrive(p, 2, "own to 3", me.dev(dz=3), inner)
        pass_on(p, place(2), "near to 1", me.dev(dz=1), inner)
        arrive(p, 2, "near to 1", me.dev(dz=1), outer)
        spread(p, 2)
        arrive(p, 3, "1 to 3", me.dev(dz=3), inner)
        pass_on(p, place(3), "far to 1", me.dev(dz=1), inner)
        arrive(p, 3, "far to 1", me.dev(dz=1), outer)
        spread(p, 3)

    def s3(p, entries=(0, 1, 2, 3)):
        for d in entries:
            zb = place(d)
            cp.wait_recv(
                slots["y1", p, d], part(p, zb, me.yo, me.x, me.c), me.dev(dy=1), ok(zb, p)
            )
            s = slots["x2", p, d] = cp.slot()
            out = part(p, zb, me.yo, me.x, me.c, 0, FIRST)
            cp.send(s, out, out, me.dev(dx=1), ok(zb, p))
            cp.wait_recv(
                slots["x1", p, d], part(p, zb, me.y, me.xo, me.c), me.dev(dx=1), ok(zb, p)
            )
            s = slots["y2", p, d] = cp.slot()
            out = part(p, zb, me.y, me.xo, me.c, FIRST, SECOND)
            cp.send(s, out, out, me.dev(dy=1), ok(zb, p))

    def lane(p, zb, x, c):
        return full.at[p, zb, :, pl.ds((2 * QUART * x + QUART * c), QUART)]

    def s4(p):
        for d in (0, 1, 2, 3):
            zb = place(d)
            cp.wait_recv(
                slots["x2", p, d], part(p, zb, me.yo, me.xo, me.c, 0, FIRST), me.dev(dx=1),
                ok(zb, p),
            )
            cp.wait_recv(
                slots["y2", p, d], part(p, zb, me.yo, me.xo, me.c, FIRST, SECOND), me.dev(dy=1),
                ok(zb, p),
            )
            for h in (0, 1):
                s = slots["c", p, d, h] = cp.slot()
                cp.send(s, lane(p, zb, h, me.c), lane(p, zb, h, me.c), me.dev(dc=1), ok(zb, p))

    def s5(p):
        for d in (0, 1, 2, 3):
            zb = place(d)
            for h in (0, 1):
                cp.wait_recv(
                    slots["c", p, d, h], lane(p, zb, h, me.co), me.dev(dc=1), ok(zb, p)
                )

    tails = pl.ds(MAIN, TAIL)

    def t1():
        own_tail.wait()
        block = full.at[me.o, me.z, me.y, tails]
        for d in (1, 2, 3):
            s = slots["tz", d] = cp.slot()
            cp.send(s, block, block, me.dev(dz=d))

    def t2():
        for d in (1, 2, 3):
            zb = flip(me.z, d)
            cp.wait_recv(slots["tz", d], full.at[me.o, zb, me.y, tails], me.dev(dz=d))
        s = slots["ty"] = cp.slot()
        block = full.at[me.o, :, me.y, tails]
        cp.send(s, block, block, me.dev(dy=1))

    def t3():
        cp.wait_recv(slots["ty"], full.at[me.o, :, me.yo, tails], me.dev(dy=1))
        s = slots["tx"] = cp.slot()
        block = full.at[me.o, :, :, tails]
        cp.send(s, block, block, me.dev(dx=1))

    def t4():
        cp.wait_recv(slots["tx"], full.at[me.xo * 2 + me.c, :, :, tails], me.dev(dx=1))
        for h in (0, 1):
            s = slots["tc", h] = cp.slot()
            block = full.at[h * 2 + me.c, :, :, tails]
            cp.send(s, block, block, me.dev(dc=1))

    def t5():
        for h in (0, 1):
            cp.wait_recv(slots["tc", h], full.at[h * 2 + me.co, :, :, tails], me.dev(dc=1))

    return dict(s0=s0, s1=s1, s2=s2, s3=s3, s4=s4, s5=s5, t1=t1, t2=t2, t3=t3, t4=t4, t5=t5)


SCATTER_COPIES = 3 * (4 * 2 + 4 * 4 + 3 + 3) + 8
RING = 6
ORDER = (3, 2, 1, 0)
f32 = jnp.float32


def guarded(cond, fn):
    if cond is None:
        fn()
    else:
        pl.when(cond)(fn)


def add_rows(dst, srcs, n):
    step = math.gcd(n, 4)

    def body(j, carry):
        at = pl.ds(j * step, step)
        total = srcs[0][at].astype(f32)
        for src in srcs[1:]:
            total = total + src[at].astype(f32)
        dst[at] = total.astype(dst.dtype)
        return carry

    lax.fori_loop(0, n // step, body, 0)


def scatter_stages(
    me, cp, partial, out, other, own, stage, rx2, ry2, rx1, ry1, rz, final, tail, tail_in, tail_z,
    local_sems, credit,
):
    slots = {}

    def block(k):
        p, d = 2 - k // 4, ORDER[k % 4]
        zb = flip(me.z, d)
        return p, d, zb, ok(zb, p), k % RING

    def exchange(p):
        for d in ORDER:
            zb = flip(me.z, d)
            for h in (0, 1):
                s = slots["c", p, d, h] = cp.slot()
                view = pl.ds(2 * QUART * h + QUART * me.co, QUART)
                cp.send(
                    s, partial.at[p, zb, :, view], other.at[p, zb, :, h], me.dev(dc=1), ok(zb, p)
                )

    def loads(k):
        p, d, zb, cond, slot = block(k)
        copies = []
        for h in (0, 1):
            view = pl.ds(2 * QUART * h + QUART * me.c, QUART)
            copies.append(
                pltpu.make_async_copy(
                    partial.at[p, zb, :, view], own.at[slot, :, h], local_sems.at[h]
                )
            )
            copies.append(
                pltpu.make_async_copy(other.at[p, zb, :, h], stage.at[h], local_sems.at[2 + h])
            )
        return copies

    def prefetch(k):
        p, d, zb, cond, slot = block(k)
        if k >= RING:
            old = block(k - RING)
            for name in ("x2", "y2", "x1", "y1", "z"):
                if (name, old[0], old[1]) in slots:
                    cp.wait_send(slots[name, old[0], old[1]])
        for h in (0, 1):
            cp.wait_recv(slots["c", p, d, h], other.at[p, zb, :, h], me.dev(dc=1), cond)

        def go():
            for copy in loads(k):
                copy.start()

        guarded(cond, go)

    def fold(k):
        p, d, zb, cond, slot = block(k)

        def go():
            for copy in loads(k):
                copy.wait()

            def body(q, carry):
                y, h = q // 2, q % 2
                add_rows(own.at[slot, y, h], [own.at[slot, y, h], stage.at[h, y]], QUART)
                return carry

            lax.fori_loop(0, 4, body, 0)

        guarded(cond, go)
        if k >= RING:
            pl.semaphore_wait(credit.at[0], 1)
            pl.semaphore_wait(credit.at[1], 1)
        far = own.at[slot, me.yo, me.xo]
        s = slots["x2", p, d] = cp.slot()
        cp.send(s, far.at[pl.ds(0, FIRST)], rx2.at[slot], me.dev(dx=1), cond)
        s = slots["y2", p, d] = cp.slot()
        cp.send(s, far.at[pl.ds(FIRST, SECOND)], ry2.at[slot], me.dev(dy=1), cond)

    def second(k):
        p, d, zb, cond, slot = block(k)
        cp.wait_recv(slots["x2", p, d], rx2.at[slot], me.dev(dx=1), cond)
        view = own.at[slot, me.yo, me.x, pl.ds(0, FIRST)]
        guarded(cond, lambda: add_rows(view, [view, rx2.at[slot]], FIRST))
        s = slots["y1", p, d] = cp.slot()
        cp.send(s, own.at[slot, me.yo, me.x], ry1.at[slot], me.dev(dy=1), cond)
        cp.wait_recv(slots["y2", p, d], ry2.at[slot], me.dev(dy=1), cond)
        view2 = own.at[slot, me.y, me.xo, pl.ds(FIRST, SECOND)]
        guarded(cond, lambda: add_rows(view2, [view2, ry2.at[slot]], SECOND))
        s = slots["x1", p, d] = cp.slot()
        cp.send(s, own.at[slot, me.y, me.xo], rx1.at[slot], me.dev(dx=1), cond)

    def third(k):
        p, d, zb, cond, slot = block(k)
        cp.wait_recv(slots["y1", p, d], ry1.at[slot], me.dev(dy=1), cond)
        cp.wait_recv(slots["x1", p, d], rx1.at[slot], me.dev(dx=1), cond)
        view = own.at[slot, me.y, me.x]
        guarded(cond, lambda: add_rows(view, [view, ry1.at[slot], rx1.at[slot]], QUART))
        if k + RING < 12:
            pl.semaphore_signal(
                credit.at[0], inc=1, device_id=me.dev(dx=1), device_id_type=MESH
            )
            pl.semaphore_signal(
                credit.at[1], inc=1, device_id=me.dev(dy=1), device_id_type=MESH
            )
        if d:
            s = slots["z", p, d] = cp.slot()
            cp.send(s, view, rz.at[p, d - 1], me.dev(dz=d), cond)

    def quarter(x, c):
        return out.at[pl.ds(2 * QUART * x + QUART * c, QUART)]

    def settle(p):
        mine = ok(me.z, p)
        for d in (1, 2, 3):
            cp.wait_recv(slots["z", p, d], rz.at[p, d - 1], me.dev(dz=d), mine)
        view = own.at[(4 * (2 - p) + 3) % RING, me.y, me.x]
        guarded(
            mine,
            lambda: add_rows(final.at[p], [view, rz.at[p, 0], rz.at[p, 1], rz.at[p, 2]], QUART),
        )
        ox, oc = p // 2, p % 2
        for dx, dc in ((1, 0), (0, 1), (1, 1)):
            x = me.xo if dx else me.x
            c = me.co if dc else me.c
            s = slots["f", p, dx, dc] = cp.slot()
            cond = both(jnp.logical_and(x == ox, c == oc), mine)
            cp.send(s, final.at[p], quarter(me.x, me.c), me.dev(dx=dx, dc=dc), cond)

        @pl.when(both(me.o == p, mine))
        def _():
            pltpu.make_async_copy(final.at[p], quarter(me.x, me.c), local_sems.at[4]).start()

    def finish(p):
        mine = both(me.o == p, ok(me.z, p))
        for dx, dc in ((1, 0), (0, 1), (1, 1)):
            x = me.xo if dx else me.x
            c = me.co if dc else me.c
            cp.wait_recv(slots["f", p, dx, dc], quarter(x, c), me.dev(dx=dx, dc=dc), mine)

        @pl.when(mine)
        def _():
            pltpu.make_async_copy(final.at[p], quarter(me.x, me.c), local_sems.at[4]).wait()

    def tail_load():
        return pltpu.make_async_copy(
            partial.at[:, :, :, pl.ds(MAIN, TAIL)], tail, local_sems.at[5]
        )

    def tail_add(o, zb, yb, srcs):
        add_rows(tail.at[o, zb, yb], [tail.at[o, zb, yb]] + srcs, TAIL)

    def t0():
        tail_load().start()

    def t1():
        tail_load().wait()
        for h in (0, 1):
            s = slots["tc", h] = cp.slot()
            cp.send(s, tail.at[2 * h + me.co], tail_in.at[h], me.dev(dc=1))

    def t2():
        for h in (0, 1):
            cp.wait_recv(slots["tc", h], tail_in.at[h], me.dev(dc=1))

            def body(q, carry):
                tail_add(2 * h + me.c, q // 2, q % 2, [tail_in.at[h, q // 2, q % 2]])
                return carry
            lax.fori_loop(0, 8, body, 0)
        s = slots["tx"] = cp.slot()
        cp.send(s, tail.at[me.xo * 2 + me.c], tail_in.at[2], me.dev(dx=1))

    def t3():
        cp.wait_recv(slots["tx"], tail_in.at[2], me.dev(dx=1))

        def body(q, carry):
            tail_add(me.o, q // 2, q % 2, [tail_in.at[2, q // 2, q % 2]])
            return carry
        lax.fori_loop(0, 8, body, 0)
        s = slots["ty"] = cp.slot()
        cp.send(s, tail.at[me.o, :, me.yo], tail_in.at[3, :, 0], me.dev(dy=1))

    def t4():
        cp.wait_recv(slots["ty"], tail_in.at[3, :, 0], me.dev(dy=1))

        def body(q, carry):
            tail_add(me.o, q, me.y, [tail_in.at[3, q, 0]])
            return carry
        lax.fori_loop(0, 4, body, 0)
        for d in (1, 2, 3):
            s = slots["tz", d] = cp.slot()
            cp.send(s, tail.at[me.o, flip(me.z, d), me.y], tail_z.at[d - 1], me.dev(dz=d))

    def t5():
        for d in (1, 2, 3):
            cp.wait_recv(slots["tz", d], tail_z.at[d - 1], me.dev(dz=d))
        tail_add(me.o, me.z, me.y, [tail_z.at[0], tail_z.at[1], tail_z.at[2]])
        copy = pltpu.make_async_copy(
            tail.at[me.o, me.z, me.y], out.at[pl.ds(MAIN, TAIL)], local_sems.at[5]
        )
        copy.start()
        copy.wait()

    return dict(
        exchange=exchange, prefetch=prefetch, fold=fold, second=second, third=third,
        settle=settle, finish=finish, tails=(t0, t1, t2, t3, t4, t5),
    )


def scatter_scratch():
    bf = jnp.bfloat16
    return [
        pltpu.VMEM((RING, 2, 2, QUART, 8, D), bf),
        pltpu.VMEM((2, 2, QUART, 8, D), bf),
        pltpu.VMEM((RING, FIRST, 8, D), bf),
        pltpu.VMEM((RING, SECOND, 8, D), bf),
        pltpu.VMEM((RING, QUART, 8, D), bf),
        pltpu.VMEM((RING, QUART, 8, D), bf),
        pltpu.VMEM((3, 3, QUART, 8, D), bf),
        pltpu.VMEM((3, QUART, 8, D), bf),
        pltpu.VMEM((4, 4, 2, TAIL, 8, D), bf),
        pltpu.VMEM((4, 4, 2, TAIL, 8, D), bf),
        pltpu.VMEM((3, TAIL, 8, D), bf),
        pltpu.SemaphoreType.DMA((6,)),
        pltpu.SemaphoreType.REGULAR((2,)),
    ]


bf16 = jnp.bfloat16
MATS = D // 8
AT_PROJ = 3 * MATS
AT_UP = 4 * MATS
AT_DOWN = 8 * MATS
ROOT = math.sqrt(2.0 / math.pi)
CUBIC = 0.044715


def nn_dot(left, right):
    return lax.dot_general(left, right, (((1,), (0,)), ((), ())), preferred_element_type=f32)


def nt_dot(left, right):
    return lax.dot_general(left, right, (((1,), (1,)), ((), ())), preferred_element_type=f32)


def tn_dot(left, right):
    return lax.dot_general(left, right, (((0,), (0,)), ((), ())), preferred_element_type=f32)


def square(ref):
    return ref[...].reshape(D, D)


def norm_rows(values):
    centered = values - jnp.mean(values, axis=-1, keepdims=True)
    inverse = lax.rsqrt(jnp.mean(centered * centered, axis=-1, keepdims=True) + NORM_EPS)
    return centered * inverse, inverse


def norm_rows_back(grad, normed, inverse):
    return inverse * (
        grad
        - jnp.mean(grad, axis=-1, keepdims=True)
        - normed * jnp.mean(grad * normed, axis=-1, keepdims=True)
    )


def frames_of(c):
    return pl.ds(pl.multiple_of(c * FRAMES, FRAMES), FRAMES)


def over_columns(count, body):
    ways = math.gcd(count, 3)

    def step(run, carry):
        for n in range(ways):
            c = ways * run + n
            body(c, frames_of(c), pl.ds(c, 1))
        return carry

    lax.fori_loop(0, count // ways, step, 0)


def split_rows(src, spread, put, ways):
    units = src.shape[0] * 8
    rows = units // ways
    for q in range(9):
        lanes = slice(128 * q, 128 * q + 128)
        spread[q, pl.ds(0, units)] = src[:, :, lanes].astype(f32).reshape(units, 128)
        for w in range(ways):
            part = spread[q, pl.ds(w, rows, stride=ways), :]
            put(w, lanes, part.reshape(rows // 8, 8, 128).astype(bf16))


def head_window(h):
    first = min(HD * h // 128, 7) * 128
    lane = lax.broadcasted_iota(jnp.int32, (1, 256), 1) + first
    mask = jnp.logical_and(lane >= HD * h, lane < HD * h + HD)
    return slice(first, first + 256), jnp.where(mask, 1.0, 0.0).astype(bf16)


def same_column():
    row = lax.broadcasted_iota(jnp.int32, (128, 128), 0)
    col = lax.broadcasted_iota(jnp.int32, (128, 128), 1)
    return lax.shift_right_logical(row, 4) == lax.shift_right_logical(col, 4)


SCORE_SCALE = 1.0 / math.sqrt(HD)


def head_probabilities(masked_queries, keys, inside):
    scores = jnp.where(inside, nt_dot(masked_queries, keys) * SCORE_SCALE, -1e30)
    grown = jnp.exp(scores - jnp.max(scores, axis=-1, keepdims=True))
    return grown / jnp.sum(grown, axis=-1, keepdims=True)


SUM_COPIES = 6
SUM_SLOTS = 10


def sum_stages(me, cp, mine, buf):
    slots = {}

    def send(name, src, dst, device):
        slots[name] = cp.slot()
        cp.send(slots[name], src, dst, device)

    def m1():
        send("c", mine, buf.at[0], me.dev(dc=1))

    def m2():
        cp.wait_recv(slots["c"], buf.at[0], me.dev(dc=1))
        buf[1] = mine[...] + buf[0]
        send("x", buf.at[1], buf.at[2], me.dev(dx=1))

    def m3():
        cp.wait_recv(slots["x"], buf.at[2], me.dev(dx=1))
        buf[3] = buf[1] + buf[2]
        send("y", buf.at[3], buf.at[4], me.dev(dy=1))

    def m4():
        cp.wait_recv(slots["y"], buf.at[4], me.dev(dy=1))
        buf[5] = buf[3] + buf[4]
        buf[6 + me.z] = buf[5]
        for d in (1, 2, 3):
            send(d, buf.at[5], buf.at[6 + me.z], me.dev(dz=d))

    def total():
        for d in (1, 2, 3):
            cp.wait_recv(slots[d], buf.at[6 + flip(me.z, d)], me.dev(dz=d))
        return (buf[6] + buf[7]) + (buf[8] + buf[9])

    return m1, m2, m3, m4, total


CUBE_COPIES = 10
CUBE_SLOTS = 12
CUBE = tuple((dx, dc, dy) for dx in (0, 1) for dc in (0, 1) for dy in (0, 1))


def cube_stages(me, cp, mine, buf):
    slots = {}

    def at(dx, dc, dy):
        x = me.xo if dx else me.x
        c = me.co if dc else me.c
        y = me.yo if dy else me.y
        return buf.at[4 * x + 2 * c + y]

    def m1():
        for way in CUBE[1:]:
            slots[way] = cp.slot()
            cp.send(slots[way], mine, at(0, 0, 0), me.dev(way[0], way[1], 0, way[2]))
        at(0, 0, 0)[...] = mine[...]

    def m2():
        for way in CUBE[1:]:
            cp.wait_recv(slots[way], at(*way), me.dev(way[0], way[1], 0, way[2]))
        total = buf[0]
        for n in range(1, 8):
            total = total + buf[n]
        there = buf.at[8 + me.z]
        there[...] = total
        for d in (1, 2, 3):
            slots[d] = cp.slot()
            cp.send(slots[d], there, there, me.dev(dz=d))

    def total():
        for d in (1, 2, 3):
            cp.wait_recv(slots[d], buf.at[8 + flip(me.z, d)], me.dev(dz=d))
        return (buf[8] + buf[9]) + (buf[10] + buf[11])

    return m1, m2, total


def forward_body(
    weights, tokens, upstream, mods, b_qkv, b_proj, b_up, b_down,
    block_out, natural, input_att, proj_out, attended, branch, input_mlp, active_out, slope_out,
    grad_out, grad_gate, grads, held, spread, acc, hid, proj, active, slope, woven,
    copy_sems, ready,
):
    columns = mods.shape[1]

    lines = held.reshape(8 * MATS, 8, D)

    def fetch(first, groups, slot):
        return pltpu.make_async_copy(
            weights.at[pl.ds(first, groups)], lines.at[pl.ds(slot * MATS, groups)], copy_sems.at[0]
        )

    def whole(mat, slot):
        return pltpu.make_async_copy(
            weights.at[pl.ds(mat * MATS, MATS)], held.at[slot], copy_sems.at[2 + slot]
        )

    def save(mat, slot):
        return pltpu.make_async_copy(held.at[slot], natural.at[mat], copy_sems.at[10 + mat])

    def keep(src, dst, n):
        return pltpu.make_async_copy(src, dst, copy_sems.at[17 + n])

    def unweave(ways, source, slot0):
        def step(j, carry):
            def put(w, lanes, block):
                held[slot0 + w, pl.ds(j * 16, 16), :, lanes] = block

            groups = 16 * ways
            src = lines.at[pl.ds(source * MATS + j * groups, groups)]
            split_rows(src, spread, put, ways)
            return carry

        lax.fori_loop(0, 9, step, 0)

    def first_norm(c, rows, at):
        normed, _ = norm_rows(tokens[rows].astype(f32))
        input_att[rows] = (normed * (1.0 + mods[1, at]) + mods[0, at]).astype(bf16)

    over_columns(columns, first_norm)
    ready("qkv")
    fetch(0, 3 * MATS, 4).start()
    whole(3, 3).start()
    fetch(0, 3 * MATS, 4).wait()
    unweave(3, 4, 0)
    for p in range(3):
        save(p, p).start()

    for p in range(3):
        proj[p] = (nn_dot(input_att[...], square(held.at[p])) + b_qkv[pl.ds(p, 1)]).astype(bf16)
        ready("project", p)
    keep(proj, proj_out, 0).start()

    inside = same_column()

    def attend(g, carry):
        rows = pl.ds(pl.multiple_of(g * 128, 128), 128)
        acc[pl.ds(0, 128)] = jnp.zeros((128, D), f32)
        for h in range(H):
            window, mask = head_window(h)
            probs = head_probabilities(proj[0, rows, window] * mask, proj[1, rows, window], inside)
            acc[pl.ds(0, 128), window] += nn_dot(probs.astype(bf16), proj[2, rows, window] * mask)
        attended[rows] = acc[pl.ds(0, 128)].astype(bf16)
        return carry

    for g in range(columns * FRAMES // 128):
        lax.fori_loop(g, g + 1, attend, 0)
        ready("attend", g)
    ready("proj")
    whole(3, 3).wait()
    branch[...] = nn_dot(attended[...], square(held.at[3])) + b_proj[...]
    for p in range(3):
        save(p, p).wait()

    def second_norm(c, rows, at):
        middle = tokens[rows].astype(f32) + mods[2, at] * branch[rows]
        normed, _ = norm_rows(middle)
        input_mlp[rows] = (normed * (1.0 + mods[4, at]) + mods[3, at]).astype(bf16)
        grad_block = jnp.where(mods[6, at] > 0.5, upstream[rows].astype(f32), 0.0)
        grad_out[rows] = (grad_block * mods[5, at]).astype(bf16)

    over_columns(columns, second_norm)
    ready("up")
    fetch(AT_UP, 4 * MATS, 0).start()
    fetch(AT_UP, 4 * MATS, 0).wait()
    unweave(4, 0, 4)
    for b in range(4):
        save(3 + b, 4 + b).start()

    def raise_(b, carry):
        hid[...] = nn_dot(input_mlp[...], square(held.at[4 + b])) + b_up[pl.ds(b, 1)]

        def gelu(c, rows, at):
            v = hid[rows]
            sq = v * v
            t = jnp.tanh(ROOT * (v + CUBIC * sq * v))
            half = 0.5 * (1.0 + t)
            active[b, rows] = (v * half).astype(bf16)
            rise = half + (0.5 * ROOT) * v * (1.0 - t * t) * (1.0 + 3.0 * CUBIC * sq)
            for q in range(9):
                slope[b, q, rows] = rise[:, 128 * q : 128 * q + 128]

        over_columns(columns, gelu)
        return carry

    for b in range(4):
        lax.fori_loop(b, b + 1, raise_, 0)
        ready("raise", b)
    keep(active, active_out, 1).start()
    keep(slope, slope_out, 2).start()
    whole(8, 0).start()

    def stash(b, r):
        return pltpu.make_async_copy(
            woven.at[pl.ds(48 * r, 48)], grads.at[pl.ds(AT_DOWN + b * MATS + 48 * r, 48)],
            copy_sems.at[20 + r],
        )

    for b in range(4):
        for r in range(3):
            part = tn_dot(active[b, :, 384 * r : 384 * r + 384], grad_out[...])
            if b:
                stash(b - 1, r).wait()
            woven[pl.ds(48 * r, 48)] = part.reshape(48, 8, D).astype(bf16)
            stash(b, r).start()
        ready("outer", b)
    acc[...] = jnp.broadcast_to(b_down[...], acc.shape)
    whole(8, 0).wait()
    acc[...] += nn_dot(active[0], square(held.at[0]))
    ready("down")
    for b in range(1, 4):
        whole(8 + b, b).start()
    for b in range(1, 4):
        whole(8 + b, b).wait()
        acc[...] += nn_dot(active[b], square(held.at[b]))

    def last(c, rows, at):
        x = tokens[rows].astype(f32)
        middle = x + mods[2, at] * branch[rows]
        video = mods[6, at] > 0.5
        outcome = acc[rows]
        block_out[rows] = jnp.where(video, middle + mods[5, at] * outcome, x)
        grad_block = jnp.where(video, upstream[rows].astype(f32), 0.0)
        grad_gate[at] = jnp.sum(grad_block * outcome, axis=0, keepdims=True)

    over_columns(columns, last)
    for b in range(4):
        save(3 + b, 4 + b).wait()
    keep(proj, proj_out, 0).wait()
    keep(active, active_out, 1).wait()
    keep(slope, slope_out, 2).wait()
    for r in range(3):
        stash(3, r).wait()


def forward_kernel(*refs):
    forward_body(*refs, lambda name, step=0: None)


def gather_forward_kernel(
    flat_shard, selector, chosen, base, tokens, upstream, b_qkv, b_proj, b_up, b_down,
    full, mods, shard, *refs,
):
    refs, (partial, sums, send_sems, recv_sems, local_sems) = refs[:-5], refs[-5:]
    lines = refs[-3].reshape(4 * 9 * tokens.shape[0], 128)
    arrival = pltpu.make_async_copy(
        flat_shard, lines.at[pl.ds(0, 9 * UNITS)], local_sems.at[1]
    )
    arrival.start()
    me = Place()
    cp = Copies(send_sems, recv_sems)
    me.greet()
    arrival.wait()

    def regroup(run, carry):
        for j in range(3):
            for q in range(9):
                part = lines[pl.ds(216 * run + 72 * j + q, 8, stride=9), :]
                shard[3 * run + j, :, 128 * q : 128 * q + 128] = part.astype(bf16)
        return carry

    lax.fori_loop(0, GROUPS8 // 3, regroup, 0)
    partial[...] = nn_dot(selector[...], shard[...].reshape(UNITS, D))
    st = gather_stages(me, cp, shard, full, local_sems)
    s0, s1, s2, s3, s4, s5 = (st["s%d" % n] for n in range(6))
    t1, t2, t3, t4, t5 = (st["t%d" % n] for n in range(1, 6))
    m1, m2, m3, m4, total = sum_stages(me, cp, partial, sums)
    s0(0)
    m1()
    s0(1)
    s0(2)
    s1(0)
    m2()
    s1(1)
    m3()
    t1()
    s2(0)
    m4()
    t2()
    s1(2)
    s3(0)
    t3()
    s2(1)
    t4()
    table = picked(chosen[...], total()) + base[...]
    columns = mods.shape[1]
    for n in range(7):
        mods[n] = table[n * columns : (n + 1) * columns]

    def ready(name, step=0):
        if name == "qkv":
            s4(0)
            t5()
            s5(0)
        elif name == "project":
            s3(1, (step,))
        elif name == "attend":
            if step == 0:
                s3(1, (3,))
            elif step == 1:
                s2(2)
            else:
                s4(1)
        elif name == "up":
            s5(1)
        elif name == "raise":
            s3(2, (step,))
        elif name == "down":
            s4(2)
            s5(2)

    forward_body(
        full.reshape(4 * 4 * 2 * GROUPS8, 8, D), tokens, upstream, mods, b_qkv, b_proj, b_up,
        b_down, *refs, ready,
    )
    cp.drain()


def forward_shapes(rows, columns):
    shape = jax.ShapeDtypeStruct
    return [
        shape((rows, D), f32),
        shape((7, MATS, 8, D), bf16),
        shape((rows, D), bf16),
        shape((3, rows, D), bf16),
        shape((rows, D), bf16),
        shape((rows, D), f32),
        shape((rows, D), bf16),
        shape((4, rows, D), bf16),
        shape((4, 9, rows, 128), f32),
        shape((rows, D), bf16),
        shape((columns, D), f32),
        shape((32 * UNITS // 8, 8, D), bf16),
    ]


VMEM_SPEC = pl.BlockSpec(memory_space=pltpu.VMEM)
HBM_SPEC = pl.BlockSpec(memory_space=pl.ANY)
FORWARD_SPECS = [
    VMEM_SPEC, HBM_SPEC, VMEM_SPEC, HBM_SPEC, VMEM_SPEC, VMEM_SPEC, VMEM_SPEC, HBM_SPEC, HBM_SPEC,
    VMEM_SPEC, VMEM_SPEC, HBM_SPEC,
]


def forward_scratch(rows):
    return [
        pltpu.VMEM((8, MATS, 8, D), bf16),
        pltpu.VMEM((9, 512, 128), f32),
        pltpu.VMEM((rows, D), f32),
        pltpu.VMEM((rows, D), f32),
        pltpu.VMEM((3, rows, D), bf16),
        pltpu.VMEM((4, rows, D), bf16),
        pltpu.VMEM((4, 9, rows, 128), f32),
        pltpu.VMEM((MATS, 8, D), bf16),
        pltpu.SemaphoreType.DMA((23,)),
    ]


def forward(weights, tokens, upstream, mods, b_qkv, b_proj, b_up, b_down):
    rows = tokens.shape[0]
    return pl.pallas_call(
        forward_kernel,
        out_shape=forward_shapes(rows, mods.shape[1]),
        in_specs=[HBM_SPEC] + [VMEM_SPEC] * 7,
        out_specs=FORWARD_SPECS,
        scratch_shapes=forward_scratch(rows),
        compiler_params=pltpu.CompilerParams(vmem_limit_bytes=62 * 2**20),
        name="block_forward",
    )(weights, tokens, upstream, mods, b_qkv, b_proj, b_up, b_down)


def gather_forward(
    flat_shard, selector, chosen, base, tokens, upstream, b_qkv, b_proj, b_up, b_down
):
    rows = tokens.shape[0]
    columns = rows // FRAMES
    copies = GATHER_COPIES + SUM_COPIES
    return pl.pallas_call(
        gather_forward_kernel,
        out_shape=[
            jax.ShapeDtypeStruct((4, 4, 2, GROUPS8, 8, D), bf16),
            jax.ShapeDtypeStruct((7, columns, D), f32),
            jax.ShapeDtypeStruct((GROUPS8, 8, D), bf16),
        ]
        + forward_shapes(rows, columns),
        in_specs=[HBM_SPEC] + [VMEM_SPEC] * 9,
        out_specs=[HBM_SPEC, VMEM_SPEC, VMEM_SPEC] + FORWARD_SPECS,
        scratch_shapes=forward_scratch(rows)
        + [
            pltpu.VMEM((selector.shape[0], D), f32),
            pltpu.VMEM((SUM_SLOTS, selector.shape[0], D), f32),
            pltpu.SemaphoreType.DMA((copies,)),
            pltpu.SemaphoreType.DMA((copies,)),
            pltpu.SemaphoreType.DMA((2,)),
        ],
        compiler_params=pltpu.CompilerParams(
            collective_id=0, has_side_effects=True, vmem_limit_bytes=63 * 2**20
        ),
        name="gather_forward",
    )(flat_shard, selector, chosen, base, tokens, upstream, b_qkv, b_proj, b_up, b_down)


UP_RUNS = ((0, 256), (256, 256), (512, 256), (768, 256), (1024, 128))
QKV_RUNS = ((0, 384), (384, 384), (768, 384))


def backward_body(
    weights, natural, slope, tokens, upstream, mods, input_att, proj, attended, branch,
    input_mlp, grad_out,
    grads, input_grad, grad_mods, bias_sums,
    held, woven, spread, grad_hidden, grad_branch, grad_att, acc, copy_sems, tick,
):
    columns = mods.shape[1]
    row_count = columns * FRAMES

    def fetch(first, slot):
        return pltpu.make_async_copy(natural.at[first], held.at[slot], copy_sems.at[slot])

    def flat_mat(first, slot):
        return pltpu.make_async_copy(
            weights.at[pl.ds(first, MATS)], held.at[slot], copy_sems.at[slot]
        )

    def stream(b, slot):
        at = pl.ds(pl.multiple_of(slot * row_count, row_count), row_count)
        return (
            flat_mat(AT_DOWN + b * MATS, slot),
            pltpu.make_async_copy(slope.at[b], spread.at[:, at], copy_sems.at[4 + slot]),
        )

    def store(first, offset, groups, n):
        return pltpu.make_async_copy(
            woven.at[pl.ds(offset, groups)], grads.at[pl.ds(first, groups)], copy_sems.at[6 + n]
        )

    bias_sums[...] = jnp.zeros_like(bias_sums)

    def add_bias(row, values):
        bias_sums[pl.ds(row, 1)] += jnp.sum(values.astype(f32), axis=0, keepdims=True)

    def outer(first, left, right):
        for r in range(3):
            part = tn_dot(left[:, 384 * r : 384 * r + 384], right[...])
            woven[pl.ds(48 * r, 48)] = part.reshape(48, 8, D).astype(bf16)
            store(first + 48 * r, 48 * r, 48, r).start()

    for copy in stream(0, 0):
        copy.start()

    def down(b, carry):
        slot = lax.rem(b, 2)
        for copy in stream(b, slot):
            copy.wait()

        @pl.when(b < 3)
        def _():
            for copy in stream(b + 1, 1 - slot):
                copy.start()

        acc[...] = nt_dot(grad_out[...], square(held.at[slot]))

        def through(c, rows, at):
            there = pl.ds(pl.multiple_of(slot * row_count + c * FRAMES, FRAMES), FRAMES)
            rise = jnp.concatenate([spread[q, there] for q in range(9)], axis=1)
            grad = (acc[rows] * rise).astype(bf16)
            grad_hidden[b, rows] = grad
            add_bias(5 + b, grad)

        over_columns(columns, through)
        return carry

    tick("begin")
    for b in range(4):
        lax.fori_loop(b, b + 1, down, 0)
        tick("down", b)
    fetch(3, 0).start()

    def down_bias(c, rows, at):
        add_bias(4, grad_out[rows])

    over_columns(columns, down_bias)

    def weave(first, ways, left, right, runs, name):
        before = None
        for k, (start, count) in enumerate(runs):
            for w in range(ways):
                part = tn_dot(left[:, start : start + count], right[w])
                for q in range(9):
                    spread[q, pl.ds(w, count, stride=ways), :] = part[:, 128 * q : 128 * q + 128]
            if before is not None:
                before.wait()

            def pack(j, carry):
                for q in range(9):
                    lines = spread[q, pl.ds(pl.multiple_of(j * 128, 128), 128), :]
                    woven[pl.ds(j * 16, 16), :, 128 * q : 128 * q + 128] = lines.reshape(
                        16, 8, 128
                    ).astype(bf16)
                return carry

            groups = count * ways // 8
            lax.fori_loop(0, groups // 16, pack, 0)
            before = store(first + start * ways // 8, 0, groups, 0)
            before.start()
            tick(name, k)
        before.wait()

    weave(AT_UP, 4, input_mlp, grad_hidden, UP_RUNS, "up run")
    tick("up")
    acc[...] = jnp.zeros_like(acc)
    for b in range(4):
        fetch(3 + b, b % 2).wait()
        if b < 3:
            fetch(4 + b, 1 - b % 2).start()
        acc[...] += nt_dot(grad_hidden[b], square(held.at[b % 2]))
        tick("up input", b)
    flat_mat(AT_PROJ, 0).start()

    def second_norm_back(c, rows, at):
        br = branch[rows]
        gate = mods[2, at]
        normed, inverse = norm_rows(tokens[rows].astype(f32) + gate * br)
        grad = acc[rows]
        grad_mods[3, at] = jnp.sum(grad, axis=0, keepdims=True)
        grad_mods[4, at] = jnp.sum(grad * normed, axis=0, keepdims=True)
        grad_block = jnp.where(mods[6, at] > 0.5, upstream[rows].astype(f32), 0.0)
        grad_middle = grad_block + norm_rows_back(grad * (1.0 + mods[4, at]), normed, inverse)
        input_grad[rows] = grad_middle
        grad_mods[2, at] = jnp.sum(grad_middle * br, axis=0, keepdims=True)
        grad = (grad_middle * gate).astype(bf16)
        grad_branch[rows] = grad
        add_bias(3, grad)

    over_columns(columns, second_norm_back)
    tick("norm")
    outer(AT_PROJ, attended, grad_branch)
    flat_mat(AT_PROJ, 0).wait()
    grad_att[...] = nt_dot(grad_branch[...], square(held.at[0])).astype(bf16)
    fetch(0, 0).start()
    for r in range(3):
        store(AT_PROJ + 48 * r, 48 * r, 48, r).wait()
    tick("proj")
    inside = same_column()

    def attend_back(g, carry):
        rows = pl.ds(pl.multiple_of(g * 128, 128), 128)
        for p in range(3):
            acc[pl.ds(p * 128, 128)] = jnp.zeros((128, D), f32)
        for h in range(H):
            window, mask = head_window(h)
            queries = proj[0, rows, window] * mask
            keys = proj[1, rows, window]
            grad = grad_att[rows, window] * mask
            probs = head_probabilities(queries, keys, inside)
            grad_probs = nt_dot(grad, proj[2, rows, window])
            mean = jnp.sum(grad_probs * probs, axis=-1, keepdims=True)
            grad_scores = (probs * (grad_probs - mean)).astype(bf16)
            acc[pl.ds(0, 128), window] += nn_dot(grad_scores, keys * mask)
            acc[pl.ds(128, 128), window] += tn_dot(grad_scores, queries)
            acc[pl.ds(256, 128), window] += tn_dot(probs.astype(bf16), grad)
        for p in range(3):
            scale = SCORE_SCALE if p < 2 else 1.0
            grad = (acc[pl.ds(p * 128, 128)] * scale).astype(bf16)
            grad_hidden[p, rows] = grad
            add_bias(p, grad)
        return carry

    for g in range(row_count // 128):
        lax.fori_loop(g, g + 1, attend_back, 0)
        tick("attend", g)
    weave(0, 3, input_att, grad_hidden, QKV_RUNS, "qkv run")
    tick("qkv")
    acc[...] = jnp.zeros_like(acc)
    for p in range(3):
        fetch(p, p % 2).wait()
        if p < 2:
            fetch(p + 1, 1 - p % 2).start()
        acc[...] += nt_dot(grad_hidden[p], square(held.at[p % 2]))
        tick("qkv input", p)

    def first_norm_back(c, rows, at):
        normed, inverse = norm_rows(tokens[rows].astype(f32))
        grad = acc[rows]
        grad_mods[0, at] = jnp.sum(grad, axis=0, keepdims=True)
        grad_mods[1, at] = jnp.sum(grad * normed, axis=0, keepdims=True)
        grad_states = input_grad[rows] + norm_rows_back(
            grad * (1.0 + mods[1, at]), normed, inverse
        )
        up_rows = upstream[rows].astype(f32)
        input_grad[rows] = jnp.where(mods[6, at] > 0.5, grad_states, up_rows)

    over_columns(columns, first_norm_back)
    tick("end")


def backward_kernel(given, *refs):
    backward_body(*refs, lambda name, step=0: None)


def backward_scatter_kernel(*refs):
    (
        given, weights, natural, slope, tokens, upstream, mods, input_att, proj, attended, branch,
        input_mlp, grad_out, grad_gate, member,
        out, grads, other, input_grad, total_small,
        grad_mods, bias_sums, held, woven, spread, grad_hidden, grad_branch, grad_att, acc, copy_sems,
        own, stage, rx2, ry2, rx1, ry1, rz, final, tail, tail_in, tail_z, local_sems, credit,
        small, sums, send_sems, recv_sems,
    ) = refs
    me = Place()
    cp = Copies(send_sems, recv_sems)
    me.greet()
    st = scatter_stages(
        me, cp, grads, out, other, own, stage, rx2, ry2, rx1, ry1, rz, final, tail, tail_in,
        tail_z, local_sems, credit,
    )
    t0, t1, t2, t3, t4, t5 = st["tails"]
    m1, m2, m3, m4, total = sum_stages(me, cp, small, sums)
    groups = member.shape[0]

    def run(steps):
        acts = dict(
            E=st["exchange"], P=st["prefetch"], A=st["fold"], B=st["second"], C=st["third"],
            S=st["settle"],
        )
        for step in steps.split():
            acts[step[0]](int(step[1:]))

    turns = {
        ("begin", 0): "E2 P0",
        ("down", 1): "A0 P1",
        ("down", 3): "A1 P2 B0",
        ("up run", 1): "A2 P3 B1 C0",
        ("up run", 4): "A3 B2 C1",
        ("up", 0): "E1 P4",
        ("up input", 1): "A4 P5 B3 C2",
        ("norm", 0): "A5 P6 B4 C3",
        ("proj", 0): "S2",
        ("attend", 0): "A6 P7 B5 C4",
        ("attend", 1): "A7 B6 C5",
        ("qkv", 0): "E0 P8",
        ("qkv input", 0): "A8 P9",
        ("attend", 2): "B7 C6",
        ("qkv input", 2): "A9 P10 B8 C7",
    }

    def tick(name, step=0):
        run(turns.get((name, step), ""))
        if (name, step) == ("qkv", 0):
            t0()
        if (name, step) == ("qkv input", 0):
            t1()
        if (name, step) == ("qkv input", 2):
            t2()
        if name == "end":
            for n in range(6):
                plane = grad_mods[n] if n < 5 else grad_gate[...]
                small[pl.ds(n * groups, groups)] = picked(member[...], plane)
            small[pl.ds(6 * groups, 9)] = bias_sums[pl.ds(0, 9)]
            small[pl.ds(6 * groups + 9, small.shape[0] - 6 * groups - 9)] = jnp.zeros(
                (small.shape[0] - 6 * groups - 9, D), f32
            )
            m1()
            run("A10 P11 B9 C8")
            t3()
            m2()
            run("A11 B10 C9 S1")
            t4()
            m3()
            t5()
            m4()
            run("B11 C10 C11 S0")
            total_small[...] = total()
            for p in (2, 1, 0):
                st["finish"](p)
            cp.drain()

    backward_body(
        weights, natural, slope, tokens, upstream, mods, input_att, proj, attended, branch,
        input_mlp, grad_out,
        grads.reshape(4 * 4 * 2 * GROUPS8, 8, D), input_grad, grad_mods, bias_sums,
        held, woven, spread, grad_hidden, grad_branch, grad_att, acc, copy_sems,
        tick,
    )


def backward_shapes(rows, columns):
    shape = jax.ShapeDtypeStruct
    return [
        shape((rows, D), f32),
        shape((5, columns, D), f32),
        shape((16, D), f32),
    ]


def backward_scratch(rows):
    return [
        pltpu.VMEM((2, MATS, 8, D), bf16),
        pltpu.VMEM((MATS, 8, D), bf16),
        pltpu.VMEM((9, D, 128), f32),
        pltpu.VMEM((4, rows, D), bf16),
        pltpu.VMEM((rows, D), bf16),
        pltpu.VMEM((rows, D), bf16),
        pltpu.VMEM((rows, D), f32),
        pltpu.SemaphoreType.DMA((9,)),
    ]


def backward(*operands):
    rows, columns = operands[4].shape[0], operands[6].shape[1]
    return pl.pallas_call(
        backward_kernel,
        out_shape=[jax.ShapeDtypeStruct((32 * UNITS // 8, 8, D), bf16)]
        + backward_shapes(rows, columns),
        in_specs=[HBM_SPEC] * 4 + [VMEM_SPEC] * 9,
        out_specs=[HBM_SPEC] + [VMEM_SPEC] * 3,
        input_output_aliases={0: 0},
        scratch_shapes=backward_scratch(rows),
        compiler_params=pltpu.CompilerParams(vmem_limit_bytes=62 * 2**20),
        name="block_backward",
    )(*operands)


def backward_scatter(operands, grad_gate, member):
    rows, columns = operands[4].shape[0], operands[6].shape[1]
    small = small_rows(member.shape[0])
    copies = SCATTER_COPIES + SUM_COPIES
    shape = jax.ShapeDtypeStruct
    input_grad, grad_mods, bias_sums = backward_shapes(rows, columns)
    return pl.pallas_call(
        backward_scatter_kernel,
        out_shape=[
            shape((GROUPS8, 8, D), bf16),
            shape((4, 4, 2, GROUPS8, 8, D), bf16),
            shape((3, 4, 2, 2, QUART, 8, D), bf16),
            input_grad,
            shape((small, D), f32),
        ],
        in_specs=[HBM_SPEC] * 4 + [VMEM_SPEC] * 11,
        out_specs=[HBM_SPEC] * 3 + [VMEM_SPEC] * 2,
        input_output_aliases={0: 1},
        scratch_shapes=[
            pltpu.VMEM(grad_mods.shape, f32),
            pltpu.VMEM(bias_sums.shape, f32),
        ]
        + backward_scratch(rows)
        + scatter_scratch()
        + [
            pltpu.VMEM((small, D), f32),
            pltpu.VMEM((SUM_SLOTS, small, D), f32),
            pltpu.SemaphoreType.DMA((copies,)),
            pltpu.SemaphoreType.DMA((copies,)),
        ],
        compiler_params=pltpu.CompilerParams(
            collective_id=1, has_side_effects=True, vmem_limit_bytes=63 * 2**20
        ),
        name="backward_scatter",
    )(*operands, grad_gate, member)


def small_rows(groups):
    return -(-(6 * groups + 9) // 8) * 8


def adamw_rows(value, grad, first, second):
    first_new = BETA_FIRST * first + (1.0 - BETA_FIRST) * grad
    second_new = BETA_SECOND * second + (1.0 - BETA_SECOND) * grad * grad
    first_hat = first_new * (1.0 / (1.0 - BETA_FIRST**STEP))
    second_hat = second_new * (1.0 / (1.0 - BETA_SECOND**STEP))
    step = first_hat / (jnp.sqrt(second_hat) + ADAM_EPS) + WEIGHT_DECAY * value
    return value - LEARN_RATE * step, first_new, second_new


def norm_kernel(
    shard_sum, low, small, selector, parts_t, row_of, in_ada, cond,
    cond_grad, norm_out, flat, bias_flat,
    ada, mine, own_cond, sums, cond_sums, send_sems, recv_sems,
):
    groups = cond.shape[0]
    me = Place()
    cp = Copies(send_sems, recv_sems)
    me.greet()
    m1, m2, total = cube_stages(me, cp, mine, sums)
    n1, n2, cond_total = cube_stages(me, cp, own_cond, cond_sums)
    parts = small[pl.ds(0, 6 * groups)]
    ada[...] = picked(selector[...], parts)

    def spread_group(run, square):
        for n in range(3):
            j = 3 * run + n
            rows = pl.ds(pl.multiple_of(j * 8, 8), 8)
            grad = jnp.where(in_ada[rows] > 0.5, ada[rows], shard_sum[j].astype(f32))
            for q in range(9):
                flat[pl.ds(72 * j + q, 8, stride=9), :] = grad[:, 128 * q : 128 * q + 128]
            square = square + grad * grad
        return square

    square = lax.fori_loop(0, GROUPS8 // 3, spread_group, jnp.zeros((8, D), f32))
    lanes = square[:, :128]
    for q in range(1, 9):
        lanes = lanes + square[:, 128 * q : 128 * q + 128]
    mine[...] = lanes
    m1()
    rows = 6 * groups
    products = nt_dot(jnp.concatenate(three_parts(parts), axis=0), low[...].reshape(UNITS, D))
    products = products[:rows] + products[rows : 2 * rows] + products[2 * rows :]
    products = products * parts_t[...]
    folded = products[:groups]
    for n in range(1, 6):
        folded = folded + products[n * groups : (n + 1) * groups]
    lane = lax.broadcasted_iota(jnp.int32, (UNITS, 128), 1)
    own_cond[...] = jnp.zeros_like(own_cond)
    folded = jnp.concatenate(three_parts(folded), axis=0)
    for q in range(9):
        hit = jnp.where(row_of[...] == lane + 128 * q, 1.0, 0.0).astype(bf16)
        there = nn_dot(folded, hit)
        there = there[:groups] + there[groups : 2 * groups] + there[2 * groups :]
        own_cond[pl.ds(0, groups), 128 * q : 128 * q + 128] = there
    n1()
    m2()
    bias_rows = [small[pl.ds(6 * groups + n, 1)] for n in (0, 2, 3, 5, 6, 7, 8, 4)]
    for n in range(6):
        bias_rows.append(jnp.sum(small[pl.ds(n * groups, groups)], axis=0, keepdims=True))
    for t, line in enumerate(bias_rows):
        for q in range(9):
            bias_flat[pl.ds(9 * t + q, 1)] = line[:, 128 * q : 128 * q + 128]
    bias_square = jnp.sum(bias_flat[...] * bias_flat[...], axis=0, keepdims=True)
    n2()
    squares = jnp.sum(total(), axis=0, keepdims=True) + bias_square
    norm_out[...] = jnp.sqrt(jnp.sum(squares, axis=1, keepdims=True))
    summed = cond_total()
    c = cond[...]
    gate = 1.0 / (1.0 + jnp.exp(-c))
    cond_grad[...] = summed[:groups] * (gate * (1.0 + c * (1.0 - gate)))
    cp.drain()


def norm_exchange(*operands):
    cond = operands[7]
    shape = jax.ShapeDtypeStruct
    payload = 8 * (cond.shape[0] // 8 + 1)
    return pl.pallas_call(
        norm_kernel,
        out_shape=[
            shape(cond.shape, f32), shape((1, 1), f32), shape((9 * UNITS, 128), f32),
            shape((BIAS_LINES, 128), f32),
        ],
        in_specs=[VMEM_SPEC] * len(operands),
        out_specs=[VMEM_SPEC] * 4,
        scratch_shapes=[
            pltpu.VMEM((UNITS, D), f32),
            pltpu.VMEM((8, 128), f32),
            pltpu.VMEM((payload, D), f32),
            pltpu.VMEM((CUBE_SLOTS, 8, 128), f32),
            pltpu.VMEM((CUBE_SLOTS, payload, D), f32),
            pltpu.SemaphoreType.DMA((2 * CUBE_COPIES,)),
            pltpu.SemaphoreType.DMA((2 * CUBE_COPIES,)),
        ],
        compiler_params=pltpu.CompilerParams(
            collective_id=2, has_side_effects=True, vmem_limit_bytes=24 * 2**20
        ),
        name="norm_exchange",
    )(*operands)


BIAS_LINES = 126


def adamw_kernel(
    norm, flat, weights, first, second, bias_flat, biases, bias_first, bias_second, block_in,
    grad_in,
    new_weights, first_out, second_out, new_biases, bias_first_out, bias_second_out, block_out,
    grad_out,
    stage, sems,
):
    passed = (
        pltpu.make_async_copy(block_in, block_out, sems.at[0]),
        pltpu.make_async_copy(grad_in, grad_out, sems.at[1]),
    )
    for copy in passed:
        copy.start()
    factor = jnp.minimum(1.0, CLIP_NORM / (norm[...] + 1e-06))
    results = (new_weights, first_out, second_out)
    run = 648
    count = flat.shape[0] // run

    def away(n, j):
        at = pl.ds(j * run, run)
        return pltpu.make_async_copy(stage.at[n, at], results[n].at[at], sems.at[2 + n])

    for j in range(count):

        def update(i, carry):
            at = pl.ds(pl.multiple_of(j * run + i * 216, 8), 216)
            stage[0, at], stage[1, at], stage[2, at] = adamw_rows(
                weights[at], flat[at] * factor, first[at], second[at]
            )
            return carry

        lax.fori_loop(0, run // 216, update, 0)
        for n in range(3):
            if j:
                away(n, j - 1).wait()
            away(n, j).start()
    new_biases[...], bias_first_out[...], bias_second_out[...] = adamw_rows(
        biases[...], bias_flat[...] * factor, bias_first[...], bias_second[...]
    )
    for n in range(3):
        away(n, count - 1).wait()
    for copy in passed:
        copy.wait()


def adamw_update(norm, flat, state, bias_flat, bias_state, block_in, grad_in):
    shape = jax.ShapeDtypeStruct
    like = [shape(flat.shape, f32)] * 3 + [shape((BIAS_LINES, 128), f32)] * 3
    return pl.pallas_call(
        adamw_kernel,
        out_shape=like + [shape(block_in.shape, f32), shape(grad_in.shape, f32)],
        in_specs=[VMEM_SPEC] * 11,
        out_specs=[HBM_SPEC] * 3 + [VMEM_SPEC] * 3 + [HBM_SPEC] * 2,
        scratch_shapes=[pltpu.VMEM((3, *flat.shape), f32), pltpu.SemaphoreType.DMA((5,))],
        compiler_params=pltpu.CompilerParams(vmem_limit_bytes=40 * 2**20),
        name="adamw",
    )(norm, flat, *state, bias_flat, *bias_state, block_in, grad_in)


def gather_blocks(shard_low):
    whole = lax.all_gather(shard_low, ("outer", "inner"), axis=0, tiled=True)
    return whole.reshape(-1, 8, D)


def scatter_blocks(grads, units):
    axes = ("outer", "inner")
    whole = grads.reshape(-1, D)[: lax.axis_size(axes) * units].astype(f32)
    return lax.psum_scatter(whole, axes, scatter_dimension=0, tiled=True)


def split_bias(vector):
    widths = [D, D, D, FF, D, 6 * D]
    pieces = []
    offset = 0
    for span_width in widths:
        pieces.append(lax.slice_in_dim(vector, offset, offset + span_width))
        offset = offset + span_width
    return pieces


def exact(left, right, dims):
    return lax.dot_general(
        left, right, dims, precision=lax.Precision.HIGHEST, preferred_element_type=jnp.float32
    )


def three_parts(values):
    high = values.astype(bf16)
    rest = values - high.astype(f32)
    middle = rest.astype(bf16)
    low_part = (rest - middle.astype(f32)).astype(bf16)
    return high, middle, low_part


def picked(choice, values):
    high, middle, low_part = three_parts(values)
    choice = choice.astype(bf16)
    return nn_dot(
        jnp.concatenate([choice] * 3, axis=1), jnp.concatenate([high, middle, low_part], axis=0)
    )


def ada_selector(soft_cond, first_unit, units):
    groups = soft_cond.shape[0]
    spread = jnp.repeat(soft_cond.astype(jnp.float32), 6, axis=1)
    spread = jnp.pad(spread, ((0, 0), (units, units)))
    start = jnp.clip(first_unit - BLOCK_UNITS + units, 0, 6 * D + units)
    local = lax.dynamic_slice(spread, (jnp.int32(0), start), (groups, units))
    unit = first_unit - BLOCK_UNITS + jnp.arange(units, dtype=jnp.int32)
    part = (unit[:, None] % 6 == jnp.arange(6, dtype=jnp.int32)[None, :]) & (unit[:, None] >= 0)
    part = part.astype(jnp.float32)
    selector = local.T[:, :, None] * part[:, None, :]
    return selector.reshape(units, groups * 6), part


def adamw(parameter, gradient, first_state, second_state):
    first_new = BETA_FIRST * first_state + (1.0 - BETA_FIRST) * gradient
    second_new = BETA_SECOND * second_state + (1.0 - BETA_SECOND) * gradient * gradient
    first_hat = first_new / (1.0 - BETA_FIRST**STEP)
    second_hat = second_new / (1.0 - BETA_SECOND**STEP)
    updated = parameter - LEARN_RATE * (
        first_hat / (jnp.sqrt(second_hat) + ADAM_EPS) + WEIGHT_DECAY * parameter
    )
    return (updated, first_new, second_new)


def with_kernels(
    tokens, conditioning, output_grad, state, bias_state, first_unit, selector, ada_part,
    membership, video_plane, b_ada, bias_args,
):
    columns, groups = membership.shape
    units = UNITS
    eye = jnp.eye(6, dtype=f32)
    chosen = membership[None, :, None, :] * eye[:, None, :, None]
    chosen = jnp.pad(chosen.reshape(6 * columns, 6 * groups), ((0, columns), (0, 0)))
    base = jnp.repeat(b_ada.reshape(6, D), columns, axis=0)
    base = jnp.concatenate([base, video_plane])
    by_part = selector.reshape(units, groups, 6).transpose(0, 2, 1).reshape(units, 6 * groups)
    state = [part.reshape(9 * units, 128) for part in state]
    (
        flat, mods, shard_low, block_out, natural, input_att, proj, attended, branch, input_mlp, _,
        slope, grad_out, grad_gate, grads,
    ) = gather_forward(
        state[0], by_part.T.astype(bf16), chosen, base, tokens, output_grad, *bias_args
    )
    flat = flat.reshape(-1, 8, D)
    shard_sum, _, _, input_grad, small = backward_scatter(
        (
            grads.reshape(4, 4, 2, GROUPS8, 8, D), flat, natural, slope, tokens, output_grad, mods,
            input_att, proj, attended, branch, input_mlp, grad_out,
        ),
        grad_gate, membership.T,
    )
    unit = first_unit - BLOCK_UNITS + jnp.arange(units, dtype=jnp.int32)
    row_of = jnp.where(unit >= 0, unit // 6, -1)[:, None]
    parts_t = jnp.repeat(ada_part.T, groups, axis=0)
    in_ada = (unit >= 0).astype(f32)[:, None]
    cond_grad, norm, flat_grad, bias_flat = norm_exchange(
        shard_sum, shard_low, small, by_part, parts_t, row_of, in_ada, conditioning
    )
    *updated, block_out, input_grad = adamw_update(
        norm, flat_grad, state, bias_flat, [part.reshape(-1, 128) for part in bias_state],
        block_out, input_grad,
    )
    return (block_out, input_grad, cond_grad, norm[0, 0], *[part.reshape(-1) for part in updated])


def on_device(
    tokens,
    conditioning,
    column_sample,
    is_image,
    output_grad,
    weights,
    first_moment,
    second_moment,
    biases,
    bias_first,
    bias_second,
    kernels,
):
    columns = column_sample.shape[0]
    groups = conditioning.shape[0]
    units = weights.shape[0] // D
    axes = ("outer", "inner")
    first_unit = lax.axis_index(axes).astype(jnp.int32) * units
    b_query, b_value, b_proj, b_up, b_down, b_ada = split_bias(biases)
    soft_cond = jax.nn.silu(conditioning).astype(bf16)
    selector, ada_part = ada_selector(soft_cond, first_unit, units)
    membership = (column_sample[:, None] == jnp.arange(groups, dtype=jnp.int32)[None, :]).astype(
        f32
    )
    video_cols = exact(membership, 1.0 - is_image.astype(f32)[:, None], (((1,), (0,)), ((), ())))
    b_qkv = jnp.stack([b_query, jnp.zeros((D,), f32), b_value])
    bias_args = (b_qkv, b_proj[None], b_up.reshape(4, D), b_down[None])
    video_plane = jnp.broadcast_to(video_cols, (columns, D))
    if kernels:
        return with_kernels(
            tokens, conditioning, output_grad, (weights, first_moment, second_moment),
            (biases, bias_first, bias_second), first_unit, selector, ada_part, membership,
            video_plane, b_ada, bias_args,
        )
    shard_low = weights.reshape(units, D).astype(bf16)
    flat = gather_blocks(shard_low)
    mods_all = lax.psum(tn_dot(selector.astype(bf16), shard_low), axes)
    mods_all = mods_all.reshape(groups, 6 * D) + b_ada
    mods = jnp.take(mods_all, column_sample, axis=0).reshape(columns, 6, D).transpose(1, 0, 2)
    mods = jnp.concatenate([mods, video_plane[None]])
    (
        block_out, natural, input_att, proj, attended, branch, input_mlp, _, slope, grad_out,
        grad_gate, grads,
    ) = forward(flat, tokens, output_grad, mods, *bias_args)
    grads, input_grad, grad_mods, bias_sums = backward(
        grads, flat, natural, slope, tokens, output_grad, mods, input_att, proj, attended, branch,
        input_mlp, grad_out,
    )
    grad_mods = jnp.concatenate([grad_mods, grad_gate[None]])
    mods_local = exact(membership, grad_mods, (((0,), (1,)), ((), ())))
    bias_sums, grad_mods_all = lax.psum((bias_sums, mods_local.transpose(1, 0, 2)), axes)
    block_shard = scatter_blocks(grads, units)
    grad_mods_all = grad_mods_all.transpose(1, 0, 2).reshape(groups, 6 * D)
    bias_head = jnp.concatenate([bias_sums[:1], bias_sums[2:4], bias_sums[5:9], bias_sums[4:5]])
    first_sum = jnp.concatenate([bias_head.reshape(-1), jnp.sum(grad_mods_all, axis=0)])
    mods_parts = grad_mods_all.reshape(groups * 6, D)
    ada_shard = exact(selector, mods_parts, (((1,), (0,)), ((), ())))
    unit = first_unit + jnp.arange(units, dtype=jnp.int32)
    grad_units = jnp.where(unit[:, None] >= BLOCK_UNITS, ada_shard, block_shard)
    products = exact(shard_low.astype(jnp.float32), mods_parts, (((1,), (1,)), ((), ())))
    products = jnp.sum(products.reshape(units, groups, 6) * ada_part[:, None, :], axis=2)
    spread = jnp.zeros((groups, 6 * D + 2 * units), jnp.float32)
    start = jnp.clip(first_unit - BLOCK_UNITS + units, 0, 6 * D + units)
    spread = lax.dynamic_update_slice(spread, products.T, (jnp.int32(0), start))
    grad_soft = jnp.sum(spread[:, units : units + 6 * D].reshape(groups, D, 6), axis=2)
    square_sum = jnp.sum(grad_units * grad_units)
    square_sum, grad_soft = lax.psum((square_sum, grad_soft), axes)
    silu_out, silu_back = jax.vjp(jax.nn.silu, conditioning)
    second_sum = silu_back(grad_soft)[0]
    grad_shard = grad_units.reshape(-1)
    grad_norm = jnp.sqrt(square_sum + jnp.sum(first_sum * first_sum))
    factor = jnp.minimum(1.0, CLIP_NORM / (grad_norm + 1e-06))
    new_weights, first_out, second_out = adamw(
        weights, grad_shard * factor, first_moment, second_moment
    )
    new_biases, bias_first_out, bias_second_out = adamw(
        biases, first_sum * factor, bias_first, bias_second
    )
    return (
        block_out,
        input_grad,
        second_sum,
        grad_norm,
        new_weights,
        first_out,
        second_out,
        new_biases,
        bias_first_out,
        bias_second_out,
    )


def solution(mesh):
    in_specs = (
        P(("outer", "inner"), None),
        P(),
        P(("outer", "inner")),
        P(),
        P(("outer", "inner"), None),
        P(("outer", "inner")),
        P(("outer", "inner")),
        P(("outer", "inner")),
        P(),
        P(),
        P(),
    )
    out_specs = (
        P(("outer", "inner"), None),
        P(("outer", "inner"), None),
        P(),
        P(),
        P(("outer", "inner")),
        P(("outer", "inner")),
        P(("outer", "inner")),
        P(),
        P(),
        P(),
    )
    kernels = dict(mesh.shape) == {"outer": 4, "inner": 8}
    return jax.shard_map(
        functools.partial(on_device, kernels=kernels), mesh=mesh, in_specs=in_specs, out_specs=out_specs, check_vma=False
    )
```

```python
import functools
import math

import jax
import jax.numpy as jnp
from jax import lax
from jax.experimental import pallas as pl
from jax.experimental.pallas import tpu as pltpu
from jax.sharding import PartitionSpec as P

D = 1152
H = 16
HD = 72
FF = 4608
FRAMES = 16
STEP = 8


NORM_EPS = 1e-06
LEARN_RATE = 0.02
BETA_FIRST = 0.5
BETA_SECOND = 0.55
ADAM_EPS = 1e-08
WEIGHT_DECAY = 0.01
CLIP_NORM = 1.0
BLOCK_UNITS = 4 * D + 2 * FF


MESH = pl.DeviceIdType.MESH
UNITS = 648
GROUPS8 = 81
QUART = 20
FIRST = 8
SECOND = QUART - FIRST
MAIN = 80
TAIL = 1
DEPTH = (4, 4, 3)
BASE = (0, 4, 8)


def flip(z, d):
    if d == 0:
        return z
    if d == 1:
        return z + 1 - 2 * (z % 2)
    if d == 2:
        return z + 2 - 4 * (z // 2)
    return 3 - z


class Place:
    def __init__(self):
        self.o = lax.axis_index("outer")
        self.i = lax.axis_index("inner")
        self.x, self.c = self.o // 2, self.o % 2
        self.z, self.y = self.i // 2, self.i % 2
        self.xo, self.co, self.yo = 1 - self.x, 1 - self.c, 1 - self.y

    def dev(self, dx=0, dc=0, dz=0, dy=0):
        x = self.xo if dx else self.x
        c = self.co if dc else self.c
        y = self.yo if dy else self.y
        return (x * 2 + c, flip(self.z, dz) * 2 + y)

    def greet(self):
        peers = [
            self.dev(dx, dc, 0, dy) for dx in (0, 1) for dc in (0, 1) for dy in (0, 1)
        ][1:]
        peers += [self.dev(dz=1), self.dev(dz=2), self.dev(dz=3)]
        barrier = pltpu.get_barrier_semaphore()
        for peer in peers:
            pl.semaphore_signal(barrier, inc=1, device_id=peer, device_id_type=MESH)
        pl.semaphore_wait(barrier, len(peers))


class Copies:
    def __init__(self, send_sems, recv_sems):
        self.send_sems, self.recv_sems = send_sems, recv_sems
        self.count = 0
        self.sent = []

    def slot(self):
        self.count += 1
        return self.count - 1

    def make(self, slot, src, dst, device):
        return pltpu.make_async_remote_copy(
            src_ref=src, dst_ref=dst, send_sem=self.send_sems.at[slot],
            recv_sem=self.recv_sems.at[slot], device_id=device, device_id_type=MESH,
        )

    def send(self, slot, src, dst, device, cond=None):
        def go():
            self.make(slot, src, dst, device).start()
        if cond is None:
            go()
        else:
            pl.when(cond)(go)
        self.sent.append((slot, src, dst, device, cond))

    def wait_recv(self, slot, dst, device, cond=None):
        def go():
            self.make(slot, dst, dst, device).wait_recv()
        if cond is None:
            go()
        else:
            pl.when(cond)(go)

    def wait_send(self, wanted):
        for entry in self.sent:
            if entry[0] == wanted:
                slot, src, dst, device, cond = entry

                def go():
                    self.make(slot, src, dst, device).wait_send()
                if cond is None:
                    go()
                else:
                    pl.when(cond)(go)
        self.sent = [entry for entry in self.sent if entry[0] != wanted]

    def drain(self):
        for slot, src, dst, device, cond in self.sent:
            def go(slot=slot, src=src, dst=dst, device=device):
                self.make(slot, src, dst, device).wait_send()
            if cond is None:
                go()
            else:
                pl.when(cond)(go)
        self.sent = []


def ok(zb, p):
    return None if DEPTH[p] == 4 else zb < DEPTH[p]


def both(a, b):
    if a is None:
        return b
    if b is None:
        return a
    return jnp.logical_and(a, b)


GATHER_COPIES = 3 * (3 + 5 + 4 * 4 + 8) + 7


def gather_stages(me, cp, shard, full, local_sems):
    def part(p, zb, yb, x, c, first=0, n=QUART):
        return full.at[p, zb, yb, pl.ds((2 * QUART * x + QUART * c + first), n)]

    def own_of(p):
        return both(me.o == p, ok(me.z, p))

    quarter = (2 * QUART * me.x + QUART * me.c)
    own_tail = pltpu.make_async_copy(
        shard.at[pl.ds(MAIN, TAIL)], full.at[me.o, me.z, me.y, pl.ds(MAIN, TAIL)], local_sems.at[0]
    )
    own_tail.start()

    def local_quarter(p):
        return pltpu.make_async_copy(
            shard.at[pl.ds(quarter, QUART)], part(p, me.z, me.y, me.x, me.c), local_sems.at[1]
        )

    slots = {}

    def s0(p):
        @pl.when(own_of(p))
        def _():
            local_quarter(p).start()
        for dx, dc in ((1, 0), (0, 1), (1, 1)):
            s = slots["s0", p, dx, dc] = cp.slot()
            x = me.xo if dx else me.x
            c = me.co if dc else me.c
            cp.send(
                s, shard.at[pl.ds((2 * QUART * x + QUART * c), QUART)],
                part(p, me.z, me.y, x, c), me.dev(dx=dx, dc=dc), own_of(p),
            )

    def s0_wait(p):
        @pl.when(own_of(p))
        def _():
            local_quarter(p).wait()
        ox, oc = p // 2, p % 2
        for dx, dc in ((1, 0), (0, 1), (1, 1)):
            x = me.xo if dx else me.x
            c = me.co if dc else me.c
            cond = both(jnp.logical_and(x == ox, c == oc), ok(me.z, p))
            cp.wait_recv(
                slots["s0", p, dx, dc], part(p, me.z, me.y, me.x, me.c), me.dev(dx=dx, dc=dc), cond
            )

    def spread(p, d):
        zb = place(d)
        mine = part(p, zb, me.y, me.x, me.c)
        s = slots["y1", p, d] = cp.slot()
        cp.send(s, mine, mine, me.dev(dy=1), ok(zb, p))
        s = slots["x1", p, d] = cp.slot()
        cp.send(s, mine, mine, me.dev(dx=1), ok(zb, p))

    def place(e):
        return (me.z, flip(me.z, 1), 2 - me.z // 2, 3 - 3 * (me.z // 2))[e]

    inner = (me.z + 1) // 2 == 1
    outer = jnp.logical_not(inner)

    def pass_on(p, zb, name, device, cond):
        view = part(p, zb, me.y, me.x, me.c)
        s = slots[name, p] = cp.slot()
        cp.send(s, view, view, device, both(cond, ok(zb, p)))

    def arrive(p, e, name, device, cond):
        zb = place(e)
        view = part(p, zb, me.y, me.x, me.c)
        cp.wait_recv(slots[name, p], view, device, both(cond, ok(zb, p)))

    def s1(p):
        s0_wait(p)
        pass_on(p, me.z, "own to 1", me.dev(dz=1), None)
        pass_on(p, me.z, "own to 3", me.dev(dz=3), inner)
        spread(p, 0)

    def s2(p):
        arrive(p, 1, "own to 1", me.dev(dz=1), None)
        pass_on(p, place(1), "1 to 3", me.dev(dz=3), inner)
        spread(p, 1)
        arrive(p, 2, "own to 3", me.dev(dz=3), inner)
        pass_on(p, place(2), "near to 1", me.dev(dz=1), inner)
        arrive(p, 2, "near to 1", me.dev(dz=1), outer)
        spread(p, 2)
        arrive(p, 3, "1 to 3", me.dev(dz=3), inner)
        pass_on(p, place(3), "far to 1", me.dev(dz=1), inner)
        arrive(p, 3, "far to 1", me.dev(dz=1), outer)
        spread(p, 3)

    def s3(p, entries=(0, 1, 2, 3)):
        for d in entries:
            zb = place(d)
            cp.wait_recv(
                slots["y1", p, d], part(p, zb, me.yo, me.x, me.c), me.dev(dy=1), ok(zb, p)
            )
            s = slots["x2", p, d] = cp.slot()
            out = part(p, zb, me.yo, me.x, me.c, 0, FIRST)
            cp.send(s, out, out, me.dev(dx=1), ok(zb, p))
            cp.wait_recv(
                slots["x1", p, d], part(p, zb, me.y, me.xo, me.c), me.dev(dx=1), ok(zb, p)
            )
            s = slots["y2", p, d] = cp.slot()
            out = part(p, zb, me.y, me.xo, me.c, FIRST, SECOND)
            cp.send(s, out, out, me.dev(dy=1), ok(zb, p))

    def lane(p, zb, x, c):
        return full.at[p, zb, :, pl.ds((2 * QUART * x + QUART * c), QUART)]

    def s4(p):
        for d in (0, 1, 2, 3):
            zb = place(d)
            cp.wait_recv(
                slots["x2", p, d], part(p, zb, me.yo, me.xo, me.c, 0, FIRST), me.dev(dx=1),
                ok(zb, p),
            )
            cp.wait_recv(
                slots["y2", p, d], part(p, zb, me.yo, me.xo, me.c, FIRST, SECOND), me.dev(dy=1),
                ok(zb, p),
            )
            for h in (0, 1):
                s = slots["c", p, d, h] = cp.slot()
                cp.send(s, lane(p, zb, h, me.c), lane(p, zb, h, me.c), me.dev(dc=1), ok(zb, p))

    def s5(p):
        for d in (0, 1, 2, 3):
            zb = place(d)
            for h in (0, 1):
                cp.wait_recv(
                    slots["c", p, d, h], lane(p, zb, h, me.co), me.dev(dc=1), ok(zb, p)
                )

    tails = pl.ds(MAIN, TAIL)

    def t1():
        own_tail.wait()
        block = full.at[me.o, me.z, me.y, tails]
        for d in (1, 2, 3):
            s = slots["tz", d] = cp.slot()
            cp.send(s, block, block, me.dev(dz=d))

    def t2():
        for d in (1, 2, 3):
            zb = flip(me.z, d)
            cp.wait_recv(slots["tz", d], full.at[me.o, zb, me.y, tails], me.dev(dz=d))
        s = slots["ty"] = cp.slot()
        block = full.at[me.o, :, me.y, tails]
        cp.send(s, block, block, me.dev(dy=1))

    def t3():
        cp.wait_recv(slots["ty"], full.at[me.o, :, me.yo, tails], me.dev(dy=1))
        s = slots["tx"] = cp.slot()
        block = full.at[me.o, :, :, tails]
        cp.send(s, block, block, me.dev(dx=1))

    def t4():
        cp.wait_recv(slots["tx"], full.at[me.xo * 2 + me.c, :, :, tails], me.dev(dx=1))
        for h in (0, 1):
            s = slots["tc", h] = cp.slot()
            block = full.at[h * 2 + me.c, :, :, tails]
            cp.send(s, block, block, me.dev(dc=1))

    def t5():
        for h in (0, 1):
            cp.wait_recv(slots["tc", h], full.at[h * 2 + me.co, :, :, tails], me.dev(dc=1))

    return dict(s0=s0, s1=s1, s2=s2, s3=s3, s4=s4, s5=s5, t1=t1, t2=t2, t3=t3, t4=t4, t5=t5)


SCATTER_COPIES = 3 * (4 * 2 + 4 * 4 + 3 + 3) + 8
RING = 6
ORDER = (3, 2, 1, 0)
f32 = jnp.float32


def guarded(cond, fn):
    if cond is None:
        fn()
    else:
        pl.when(cond)(fn)


def add_rows(dst, srcs, n):
    step = math.gcd(n, 4)

    def body(j, carry):
        at = pl.ds(j * step, step)
        total = srcs[0][at].astype(f32)
        for src in srcs[1:]:
            total = total + src[at].astype(f32)
        dst[at] = total.astype(dst.dtype)
        return carry

    lax.fori_loop(0, n // step, body, 0)


def scatter_stages(
    me, cp, partial, out, other, own, stage, rx2, ry2, rx1, ry1, rz, final, tail, tail_in, tail_z,
    local_sems, credit,
):
    slots = {}

    def block(k):
        p, d = 2 - k // 4, ORDER[k % 4]
        zb = flip(me.z, d)
        return p, d, zb, ok(zb, p), k % RING

    def exchange(p):
        for d in ORDER:
            zb = flip(me.z, d)
            for h in (0, 1):
                s = slots["c", p, d, h] = cp.slot()
                view = pl.ds(2 * QUART * h + QUART * me.co, QUART)
                cp.send(
                    s, partial.at[p, zb, :, view], other.at[p, zb, :, h], me.dev(dc=1), ok(zb, p)
                )

    def loads(k):
        p, d, zb, cond, slot = block(k)
        copies = []
        for h in (0, 1):
            view = pl.ds(2 * QUART * h + QUART * me.c, QUART)
            copies.append(
                pltpu.make_async_copy(
                    partial.at[p, zb, :, view], own.at[slot, :, h], local_sems.at[h]
                )
            )
            copies.append(
                pltpu.make_async_copy(other.at[p, zb, :, h], stage.at[h], local_sems.at[2 + h])
            )
        return copies

    def prefetch(k):
        p, d, zb, cond, slot = block(k)
        if k >= RING:
            old = block(k - RING)
            for name in ("x2", "y2", "x1", "y1", "z"):
                if (name, old[0], old[1]) in slots:
                    cp.wait_send(slots[name, old[0], old[1]])
        for h in (0, 1):
            cp.wait_recv(slots["c", p, d, h], other.at[p, zb, :, h], me.dev(dc=1), cond)

        def go():
            for copy in loads(k):
                copy.start()

        guarded(cond, go)

    def fold(k):
        p, d, zb, cond, slot = block(k)

        def go():
            for copy in loads(k):
                copy.wait()

            def body(q, carry):
                y, h = q // 2, q % 2
                add_rows(own.at[slot, y, h], [own.at[slot, y, h], stage.at[h, y]], QUART)
                return carry

            lax.fori_loop(0, 4, body, 0)

        guarded(cond, go)
        if k >= RING:
            pl.semaphore_wait(credit.at[0], 1)
            pl.semaphore_wait(credit.at[1], 1)
        far = own.at[slot, me.yo, me.xo]
        s = slots["x2", p, d] = cp.slot()
        cp.send(s, far.at[pl.ds(0, FIRST)], rx2.at[slot], me.dev(dx=1), cond)
        s = slots["y2", p, d] = cp.slot()
        cp.send(s, far.at[pl.ds(FIRST, SECOND)], ry2.at[slot], me.dev(dy=1), cond)

    def second(k):
        p, d, zb, cond, slot = block(k)
        cp.wait_recv(slots["x2", p, d], rx2.at[slot], me.dev(dx=1), cond)
        view = own.at[slot, me.yo, me.x, pl.ds(0, FIRST)]
        guarded(cond, lambda: add_rows(view, [view, rx2.at[slot]], FIRST))
        s = slots["y1", p, d] = cp.slot()
        cp.send(s, own.at[slot, me.yo, me.x], ry1.at[slot], me.dev(dy=1), cond)
        cp.wait_recv(slots["y2", p, d], ry2.at[slot], me.dev(dy=1), cond)
        view2 = own.at[slot, me.y, me.xo, pl.ds(FIRST, SECOND)]
        guarded(cond, lambda: add_rows(view2, [view2, ry2.at[slot]], SECOND))
        s = slots["x1", p, d] = cp.slot()
        cp.send(s, own.at[slot, me.y, me.xo], rx1.at[slot], me.dev(dx=1), cond)

    def third(k):
        p, d, zb, cond, slot = block(k)
        cp.wait_recv(slots["y1", p, d], ry1.at[slot], me.dev(dy=1), cond)
        cp.wait_recv(slots["x1", p, d], rx1.at[slot], me.dev(dx=1), cond)
        view = own.at[slot, me.y, me.x]
        guarded(cond, lambda: add_rows(view, [view, ry1.at[slot], rx1.at[slot]], QUART))
        if k + RING < 12:
            pl.semaphore_signal(
                credit.at[0], inc=1, device_id=me.dev(dx=1), device_id_type=MESH
            )
            pl.semaphore_signal(
                credit.at[1], inc=1, device_id=me.dev(dy=1), device_id_type=MESH
            )
        if d:
            s = slots["z", p, d] = cp.slot()
            cp.send(s, view, rz.at[p, d - 1], me.dev(dz=d), cond)

    def quarter(x, c):
        return out.at[pl.ds(2 * QUART * x + QUART * c, QUART)]

    def settle(p):
        mine = ok(me.z, p)
        for d in (1, 2, 3):
            cp.wait_recv(slots["z", p, d], rz.at[p, d - 1], me.dev(dz=d), mine)
        view = own.at[(4 * (2 - p) + 3) % RING, me.y, me.x]
        guarded(
            mine,
            lambda: add_rows(final.at[p], [view, rz.at[p, 0], rz.at[p, 1], rz.at[p, 2]], QUART),
        )
        ox, oc = p // 2, p % 2
        for dx, dc in ((1, 0), (0, 1), (1, 1)):
            x = me.xo if dx else me.x
            c = me.co if dc else me.c
            s = slots["f", p, dx, dc] = cp.slot()
            cond = both(jnp.logical_and(x == ox, c == oc), mine)
            cp.send(s, final.at[p], quarter(me.x, me.c), me.dev(dx=dx, dc=dc), cond)

        @pl.when(both(me.o == p, mine))
        def _():
            pltpu.make_async_copy(final.at[p], quarter(me.x, me.c), local_sems.at[4]).start()

    def finish(p):
        mine = both(me.o == p, ok(me.z, p))
        for dx, dc in ((1, 0), (0, 1), (1, 1)):
            x = me.xo if dx else me.x
            c = me.co if dc else me.c
            cp.wait_recv(slots["f", p, dx, dc], quarter(x, c), me.dev(dx=dx, dc=dc), mine)

        @pl.when(mine)
        def _():
            pltpu.make_async_copy(final.at[p], quarter(me.x, me.c), local_sems.at[4]).wait()

    def tail_load():
        return pltpu.make_async_copy(
            partial.at[:, :, :, pl.ds(MAIN, TAIL)], tail, local_sems.at[5]
        )

    def tail_add(o, zb, yb, srcs):
        add_rows(tail.at[o, zb, yb], [tail.at[o, zb, yb]] + srcs, TAIL)

    def t0():
        tail_load().start()

    def t1():
        tail_load().wait()
        for h in (0, 1):
            s = slots["tc", h] = cp.slot()
            cp.send(s, tail.at[2 * h + me.co], tail_in.at[h], me.dev(dc=1))

    def t2():
        for h in (0, 1):
            cp.wait_recv(slots["tc", h], tail_in.at[h], me.dev(dc=1))

            def body(q, carry):
                tail_add(2 * h + me.c, q // 2, q % 2, [tail_in.at[h, q // 2, q % 2]])
                return carry
            lax.fori_loop(0, 8, body, 0)
        s = slots["tx"] = cp.slot()
        cp.send(s, tail.at[me.xo * 2 + me.c], tail_in.at[2], me.dev(dx=1))

    def t3():
        cp.wait_recv(slots["tx"], tail_in.at[2], me.dev(dx=1))

        def body(q, carry):
            tail_add(me.o, q // 2, q % 2, [tail_in.at[2, q // 2, q % 2]])
            return carry
        lax.fori_loop(0, 8, body, 0)
        s = slots["ty"] = cp.slot()
        cp.send(s, tail.at[me.o, :, me.yo], tail_in.at[3, :, 0], me.dev(dy=1))

    def t4():
        cp.wait_recv(slots["ty"], tail_in.at[3, :, 0], me.dev(dy=1))

        def body(q, carry):
            tail_add(me.o, q, me.y, [tail_in.at[3, q, 0]])
            return carry
        lax.fori_loop(0, 4, body, 0)
        for d in (1, 2, 3):
            s = slots["tz", d] = cp.slot()
            cp.send(s, tail.at[me.o, flip(me.z, d), me.y], tail_z.at[d - 1], me.dev(dz=d))

    def t5():
        for d in (1, 2, 3):
            cp.wait_recv(slots["tz", d], tail_z.at[d - 1], me.dev(dz=d))
        tail_add(me.o, me.z, me.y, [tail_z.at[0], tail_z.at[1], tail_z.at[2]])
        copy = pltpu.make_async_copy(
            tail.at[me.o, me.z, me.y], out.at[pl.ds(MAIN, TAIL)], local_sems.at[5]
        )
        copy.start()
        copy.wait()

    return dict(
        exchange=exchange, prefetch=prefetch, fold=fold, second=second, third=third,
        settle=settle, finish=finish, tails=(t0, t1, t2, t3, t4, t5),
    )


def scatter_scratch():
    bf = jnp.bfloat16
    return [
        pltpu.VMEM((RING, 2, 2, QUART, 8, D), bf),
        pltpu.VMEM((2, 2, QUART, 8, D), bf),
        pltpu.VMEM((RING, FIRST, 8, D), bf),
        pltpu.VMEM((RING, SECOND, 8, D), bf),
        pltpu.VMEM((RING, QUART, 8, D), bf),
        pltpu.VMEM((RING, QUART, 8, D), bf),
        pltpu.VMEM((3, 3, QUART, 8, D), bf),
        pltpu.VMEM((3, QUART, 8, D), bf),
        pltpu.VMEM((4, 4, 2, TAIL, 8, D), bf),
        pltpu.VMEM((4, 4, 2, TAIL, 8, D), bf),
        pltpu.VMEM((3, TAIL, 8, D), bf),
        pltpu.SemaphoreType.DMA((6,)),
        pltpu.SemaphoreType.REGULAR((2,)),
    ]


bf16 = jnp.bfloat16
MATS = D // 8
AT_PROJ = 3 * MATS
AT_UP = 4 * MATS
AT_DOWN = 8 * MATS
ROOT = math.sqrt(2.0 / math.pi)
CUBIC = 0.044715


def nn_dot(left, right):
    return lax.dot_general(left, right, (((1,), (0,)), ((), ())), preferred_element_type=f32)


def nt_dot(left, right):
    return lax.dot_general(left, right, (((1,), (1,)), ((), ())), preferred_element_type=f32)


def tn_dot(left, right):
    return lax.dot_general(left, right, (((0,), (0,)), ((), ())), preferred_element_type=f32)


def square(ref):
    return ref[...].reshape(D, D)


def norm_rows(values):
    centered = values - jnp.mean(values, axis=-1, keepdims=True)
    inverse = lax.rsqrt(jnp.mean(centered * centered, axis=-1, keepdims=True) + NORM_EPS)
    return centered * inverse, inverse


def norm_rows_back(grad, normed, inverse):
    return inverse * (
        grad
        - jnp.mean(grad, axis=-1, keepdims=True)
        - normed * jnp.mean(grad * normed, axis=-1, keepdims=True)
    )


def frames_of(c):
    return pl.ds(pl.multiple_of(c * FRAMES, FRAMES), FRAMES)


def over_columns(count, body):
    ways = math.gcd(count, 3)

    def step(run, carry):
        for n in range(ways):
            c = ways * run + n
            body(c, frames_of(c), pl.ds(c, 1))
        return carry

    lax.fori_loop(0, count // ways, step, 0)


def split_rows(src, spread, put, ways):
    units = src.shape[0] * 8
    rows = units // ways
    for q in range(9):
        lanes = slice(128 * q, 128 * q + 128)
        spread[q, pl.ds(0, units)] = src[:, :, lanes].astype(f32).reshape(units, 128)
        for w in range(ways):
            part = spread[q, pl.ds(w, rows, stride=ways), :]
            put(w, lanes, part.reshape(rows // 8, 8, 128).astype(bf16))


def head_window(h):
    first = min(HD * h // 128, 7) * 128
    lane = lax.broadcasted_iota(jnp.int32, (1, 256), 1) + first
    mask = jnp.logical_and(lane >= HD * h, lane < HD * h + HD)
    return slice(first, first + 256), jnp.where(mask, 1.0, 0.0).astype(bf16)


def same_column():
    row = lax.broadcasted_iota(jnp.int32, (128, 128), 0)
    col = lax.broadcasted_iota(jnp.int32, (128, 128), 1)
    return lax.shift_right_logical(row, 4) == lax.shift_right_logical(col, 4)


SCORE_SCALE = 1.0 / math.sqrt(HD)


def head_probabilities(masked_queries, keys, inside):
    scores = jnp.where(inside, nt_dot(masked_queries, keys) * SCORE_SCALE, -1e30)
    grown = jnp.exp(scores - jnp.max(scores, axis=-1, keepdims=True))
    return grown / jnp.sum(grown, axis=-1, keepdims=True)


SUM_COPIES = 6
SUM_SLOTS = 10


def sum_stages(me, cp, mine, buf):
    slots = {}

    def send(name, src, dst, device):
        slots[name] = cp.slot()
        cp.send(slots[name], src, dst, device)

    def m1():
        send("c", mine, buf.at[0], me.dev(dc=1))

    def m2():
        cp.wait_recv(slots["c"], buf.at[0], me.dev(dc=1))
        buf[1] = mine[...] + buf[0]
        send("x", buf.at[1], buf.at[2], me.dev(dx=1))

    def m3():
        cp.wait_recv(slots["x"], buf.at[2], me.dev(dx=1))
        buf[3] = buf[1] + buf[2]
        send("y", buf.at[3], buf.at[4], me.dev(dy=1))

    def m4():
        cp.wait_recv(slots["y"], buf.at[4], me.dev(dy=1))
        buf[5] = buf[3] + buf[4]
        buf[6 + me.z] = buf[5]
        for d in (1, 2, 3):
            send(d, buf.at[5], buf.at[6 + me.z], me.dev(dz=d))

    def total():
        for d in (1, 2, 3):
            cp.wait_recv(slots[d], buf.at[6 + flip(me.z, d)], me.dev(dz=d))
        return (buf[6] + buf[7]) + (buf[8] + buf[9])

    return m1, m2, m3, m4, total


CUBE_COPIES = 10
CUBE_SLOTS = 12
CUBE = tuple((dx, dc, dy) for dx in (0, 1) for dc in (0, 1) for dy in (0, 1))


def cube_stages(me, cp, mine, buf):
    slots = {}

    def at(dx, dc, dy):
        x = me.xo if dx else me.x
        c = me.co if dc else me.c
        y = me.yo if dy else me.y
        return buf.at[4 * x + 2 * c + y]

    def m1():
        for way in CUBE[1:]:
            slots[way] = cp.slot()
            cp.send(slots[way], mine, at(0, 0, 0), me.dev(way[0], way[1], 0, way[2]))
        at(0, 0, 0)[...] = mine[...]

    def m2():
        for way in CUBE[1:]:
            cp.wait_recv(slots[way], at(*way), me.dev(way[0], way[1], 0, way[2]))
        total = buf[0]
        for n in range(1, 8):
            total = total + buf[n]
        there = buf.at[8 + me.z]
        there[...] = total
        for d in (1, 2, 3):
            slots[d] = cp.slot()
            cp.send(slots[d], there, there, me.dev(dz=d))

    def total():
        for d in (1, 2, 3):
            cp.wait_recv(slots[d], buf.at[8 + flip(me.z, d)], me.dev(dz=d))
        return (buf[8] + buf[9]) + (buf[10] + buf[11])

    return m1, m2, total


def forward_body(
    weights, tokens, upstream, mods, b_qkv, b_proj, b_up, b_down,
    block_out, natural, input_att, proj_out, attended, branch, input_mlp, active_out, slope_out,
    grad_out, grad_gate, grads, held, spread, acc, hid, proj, active, slope, woven,
    copy_sems, ready,
):
    columns = mods.shape[1]

    lines = held.reshape(8 * MATS, 8, D)

    def fetch(first, groups, slot):
        return pltpu.make_async_copy(
            weights.at[pl.ds(first, groups)], lines.at[pl.ds(slot * MATS, groups)], copy_sems.at[0]
        )

    def whole(mat, slot):
        return pltpu.make_async_copy(
            weights.at[pl.ds(mat * MATS, MATS)], held.at[slot], copy_sems.at[2 + slot]
        )

    def save(mat, slot):
        return pltpu.make_async_copy(held.at[slot], natural.at[mat], copy_sems.at[10 + mat])

    def keep(src, dst, n):
        return pltpu.make_async_copy(src, dst, copy_sems.at[17 + n])

    def unweave(ways, source, slot0):
        def step(j, carry):
            def put(w, lanes, block):
                held[slot0 + w, pl.ds(j * 16, 16), :, lanes] = block

            groups = 16 * ways
            src = lines.at[pl.ds(source * MATS + j * groups, groups)]
            split_rows(src, spread, put, ways)
            return carry

        lax.fori_loop(0, 9, step, 0)

    def first_norm(c, rows, at):
        normed, _ = norm_rows(tokens[rows].astype(f32))
        input_att[rows] = (normed * (1.0 + mods[1, at]) + mods[0, at]).astype(bf16)

    over_columns(columns, first_norm)
    ready("qkv")
    fetch(0, 3 * MATS, 4).start()
    whole(3, 3).start()
    fetch(0, 3 * MATS, 4).wait()
    unweave(3, 4, 0)
    for p in range(3):
        save(p, p).start()

    for p in range(3):
        proj[p] = (nn_dot(input_att[...], square(held.at[p])) + b_qkv[pl.ds(p, 1)]).astype(bf16)
        ready("project", p)
    keep(proj, proj_out, 0).start()

    inside = same_column()

    def attend(g, carry):
        rows = pl.ds(pl.multiple_of(g * 128, 128), 128)
        acc[pl.ds(0, 128)] = jnp.zeros((128, D), f32)
        for h in range(H):
            window, mask = head_window(h)
            probs = head_probabilities(proj[0, rows, window] * mask, proj[1, rows, window], inside)
            acc[pl.ds(0, 128), window] += nn_dot(probs.astype(bf16), proj[2, rows, window] * mask)
        attended[rows] = acc[pl.ds(0, 128)].astype(bf16)
        return carry

    for g in range(columns * FRAMES // 128):
        lax.fori_loop(g, g + 1, attend, 0)
        ready("attend", g)
    ready("proj")
    whole(3, 3).wait()
    branch[...] = nn_dot(attended[...], square(held.at[3])) + b_proj[...]
    for p in range(3):
        save(p, p).wait()

    def second_norm(c, rows, at):
        middle = tokens[rows].astype(f32) + mods[2, at] * branch[rows]
        normed, _ = norm_rows(middle)
        input_mlp[rows] = (normed * (1.0 + mods[4, at]) + mods[3, at]).astype(bf16)
        grad_block = jnp.where(mods[6, at] > 0.5, upstream[rows].astype(f32), 0.0)
        grad_out[rows] = (grad_block * mods[5, at]).astype(bf16)

    over_columns(columns, second_norm)
    ready("up")
    fetch(AT_UP, 4 * MATS, 0).start()
    fetch(AT_UP, 4 * MATS, 0).wait()
    unweave(4, 0, 4)
    for b in range(4):
        save(3 + b, 4 + b).start()

    def raise_(b, carry):
        hid[...] = nn_dot(input_mlp[...], square(held.at[4 + b])) + b_up[pl.ds(b, 1)]

        def gelu(c, rows, at):
            v = hid[rows]
            sq = v * v
            t = jnp.tanh(ROOT * (v + CUBIC * sq * v))
            half = 0.5 * (1.0 + t)
            active[b, rows] = (v * half).astype(bf16)
            rise = half + (0.5 * ROOT) * v * (1.0 - t * t) * (1.0 + 3.0 * CUBIC * sq)
            for q in range(9):
                slope[b, q, rows] = rise[:, 128 * q : 128 * q + 128]

        over_columns(columns, gelu)
        return carry

    for b in range(4):
        lax.fori_loop(b, b + 1, raise_, 0)
        ready("raise", b)
    keep(active, active_out, 1).start()
    keep(slope, slope_out, 2).start()
    whole(8, 0).start()

    def stash(b, r):
        return pltpu.make_async_copy(
            woven.at[pl.ds(48 * r, 48)], grads.at[pl.ds(AT_DOWN + b * MATS + 48 * r, 48)],
            copy_sems.at[20 + r],
        )

    for b in range(4):
        for r in range(3):
            part = tn_dot(active[b, :, 384 * r : 384 * r + 384], grad_out[...])
            if b:
                stash(b - 1, r).wait()
            woven[pl.ds(48 * r, 48)] = part.reshape(48, 8, D).astype(bf16)
            stash(b, r).start()
        ready("outer", b)
    acc[...] = jnp.broadcast_to(b_down[...], acc.shape)
    whole(8, 0).wait()
    acc[...] += nn_dot(active[0], square(held.at[0]))
    ready("down")
    for b in range(1, 4):
        whole(8 + b, b).start()
    for b in range(1, 4):
        whole(8 + b, b).wait()
        acc[...] += nn_dot(active[b], square(held.at[b]))

    def last(c, rows, at):
        x = tokens[rows].astype(f32)
        middle = x + mods[2, at] * branch[rows]
        video = mods[6, at] > 0.5
        outcome = acc[rows]
        block_out[rows] = jnp.where(video, middle + mods[5, at] * outcome, x)
        grad_block = jnp.where(video, upstream[rows].astype(f32), 0.0)
        grad_gate[at] = jnp.sum(grad_block * outcome, axis=0, keepdims=True)

    over_columns(columns, last)
    for b in range(4):
        save(3 + b, 4 + b).wait()
    keep(proj, proj_out, 0).wait()
    keep(active, active_out, 1).wait()
    keep(slope, slope_out, 2).wait()
    for r in range(3):
        stash(3, r).wait()


def forward_kernel(*refs):
    forward_body(*refs, lambda name, step=0: None)


def gather_forward_kernel(
    flat_shard, selector, chosen, base, tokens, upstream, b_qkv, b_proj, b_up, b_down,
    full, mods, shard, *refs,
):
    refs, (partial, sums, send_sems, recv_sems, local_sems) = refs[:-5], refs[-5:]
    lines = refs[-3].reshape(4 * 9 * tokens.shape[0], 128)
    arrival = pltpu.make_async_copy(
        flat_shard, lines.at[pl.ds(0, 9 * UNITS)], local_sems.at[1]
    )
    arrival.start()
    me = Place()
    cp = Copies(send_sems, recv_sems)
    me.greet()
    arrival.wait()

    def regroup(run, carry):
        for j in range(3):
            for q in range(9):
                part = lines[pl.ds(216 * run + 72 * j + q, 8, stride=9), :]
                shard[3 * run + j, :, 128 * q : 128 * q + 128] = part.astype(bf16)
        return carry

    lax.fori_loop(0, GROUPS8 // 3, regroup, 0)
    partial[...] = nn_dot(selector[...], shard[...].reshape(UNITS, D))
    st = gather_stages(me, cp, shard, full, local_sems)
    s0, s1, s2, s3, s4, s5 = (st["s%d" % n] for n in range(6))
    t1, t2, t3, t4, t5 = (st["t%d" % n] for n in range(1, 6))
    m1, m2, m3, m4, total = sum_stages(me, cp, partial, sums)
    s0(0)
    m1()
    s0(1)
    s0(2)
    s1(0)
    m2()
    s1(1)
    m3()
    t1()
    s2(0)
    m4()
    t2()
    s1(2)
    s3(0)
    t3()
    s2(1)
    t4()
    table = picked(chosen[...], total()) + base[...]
    columns = mods.shape[1]
    for n in range(7):
        mods[n] = table[n * columns : (n + 1) * columns]

    def ready(name, step=0):
        if name == "qkv":
            s4(0)
            t5()
            s5(0)
        elif name == "project":
            s3(1, (step,))
        elif name == "attend":
            if step == 0:
                s3(1, (3,))
            elif step == 1:
                s2(2)
            else:
                s4(1)
        elif name == "up":
            s5(1)
        elif name == "raise":
            s3(2, (step,))
        elif name == "down":
            s4(2)
            s5(2)

    forward_body(
        full.reshape(4 * 4 * 2 * GROUPS8, 8, D), tokens, upstream, mods, b_qkv, b_proj, b_up,
        b_down, *refs, ready,
    )
    cp.drain()


def forward_shapes(rows, columns):
    shape = jax.ShapeDtypeStruct
    return [
        shape((rows, D), f32),
        shape((7, MATS, 8, D), bf16),
        shape((rows, D), bf16),
        shape((3, rows, D), bf16),
        shape((rows, D), bf16),
        shape((rows, D), f32),
        shape((rows, D), bf16),
        shape((4, rows, D), bf16),
        shape((4, 9, rows, 128), f32),
        shape((rows, D), bf16),
        shape((columns, D), f32),
        shape((32 * UNITS // 8, 8, D), bf16),
    ]


VMEM_SPEC = pl.BlockSpec(memory_space=pltpu.VMEM)
HBM_SPEC = pl.BlockSpec(memory_space=pl.ANY)
FORWARD_SPECS = [
    VMEM_SPEC, HBM_SPEC, VMEM_SPEC, HBM_SPEC, VMEM_SPEC, VMEM_SPEC, VMEM_SPEC, HBM_SPEC, HBM_SPEC,
    VMEM_SPEC, VMEM_SPEC, HBM_SPEC,
]


def forward_scratch(rows):
    return [
        pltpu.VMEM((8, MATS, 8, D), bf16),
        pltpu.VMEM((9, 512, 128), f32),
        pltpu.VMEM((rows, D), f32),
        pltpu.VMEM((rows, D), f32),
        pltpu.VMEM((3, rows, D), bf16),
        pltpu.VMEM((4, rows, D), bf16),
        pltpu.VMEM((4, 9, rows, 128), f32),
        pltpu.VMEM((MATS, 8, D), bf16),
        pltpu.SemaphoreType.DMA((23,)),
    ]


def forward(weights, tokens, upstream, mods, b_qkv, b_proj, b_up, b_down):
    rows = tokens.shape[0]
    return pl.pallas_call(
        forward_kernel,
        out_shape=forward_shapes(rows, mods.shape[1]),
        in_specs=[HBM_SPEC] + [VMEM_SPEC] * 7,
        out_specs=FORWARD_SPECS,
        scratch_shapes=forward_scratch(rows),
        compiler_params=pltpu.CompilerParams(vmem_limit_bytes=62 * 2**20),
        name="block_forward",
    )(weights, tokens, upstream, mods, b_qkv, b_proj, b_up, b_down)


def gather_forward(
    flat_shard, selector, chosen, base, tokens, upstream, b_qkv, b_proj, b_up, b_down
):
    rows = tokens.shape[0]
    columns = rows // FRAMES
    copies = GATHER_COPIES + SUM_COPIES
    return pl.pallas_call(
        gather_forward_kernel,
        out_shape=[
            jax.ShapeDtypeStruct((4, 4, 2, GROUPS8, 8, D), bf16),
            jax.ShapeDtypeStruct((7, columns, D), f32),
            jax.ShapeDtypeStruct((GROUPS8, 8, D), bf16),
        ]
        + forward_shapes(rows, columns),
        in_specs=[HBM_SPEC] + [VMEM_SPEC] * 9,
        out_specs=[HBM_SPEC, VMEM_SPEC, VMEM_SPEC] + FORWARD_SPECS,
        scratch_shapes=forward_scratch(rows)
        + [
            pltpu.VMEM((selector.shape[0], D), f32),
            pltpu.VMEM((SUM_SLOTS, selector.shape[0], D), f32),
            pltpu.SemaphoreType.DMA((copies,)),
            pltpu.SemaphoreType.DMA((copies,)),
            pltpu.SemaphoreType.DMA((2,)),
        ],
        compiler_params=pltpu.CompilerParams(
            collective_id=0, has_side_effects=True, vmem_limit_bytes=63 * 2**20
        ),
        name="gather_forward",
    )(flat_shard, selector, chosen, base, tokens, upstream, b_qkv, b_proj, b_up, b_down)


UP_RUNS = ((0, 256), (256, 256), (512, 256), (768, 256), (1024, 128))
QKV_RUNS = ((0, 384), (384, 384), (768, 384))


def backward_body(
    weights, natural, slope, tokens, upstream, mods, input_att, proj, attended, branch,
    input_mlp, grad_out,
    grads, input_grad, grad_mods, bias_sums,
    held, woven, spread, grad_hidden, grad_branch, grad_att, acc, copy_sems, tick,
):
    columns = mods.shape[1]
    row_count = columns * FRAMES

    def fetch(first, slot):
        return pltpu.make_async_copy(natural.at[first], held.at[slot], copy_sems.at[slot])

    def flat_mat(first, slot):
        return pltpu.make_async_copy(
            weights.at[pl.ds(first, MATS)], held.at[slot], copy_sems.at[slot]
        )

    def stream(b, slot):
        at = pl.ds(pl.multiple_of(slot * row_count, row_count), row_count)
        return (
            flat_mat(AT_DOWN + b * MATS, slot),
            pltpu.make_async_copy(slope.at[b], spread.at[:, at], copy_sems.at[4 + slot]),
        )

    def store(first, offset, groups, n):
        return pltpu.make_async_copy(
            woven.at[pl.ds(offset, groups)], grads.at[pl.ds(first, groups)], copy_sems.at[6 + n]
        )

    bias_sums[...] = jnp.zeros_like(bias_sums)

    def add_bias(row, values):
        bias_sums[pl.ds(row, 1)] += jnp.sum(values.astype(f32), axis=0, keepdims=True)

    def outer(first, left, right):
        for r in range(3):
            part = tn_dot(left[:, 384 * r : 384 * r + 384], right[...])
            woven[pl.ds(48 * r, 48)] = part.reshape(48, 8, D).astype(bf16)
            store(first + 48 * r, 48 * r, 48, r).start()

    for copy in stream(0, 0):
        copy.start()

    def down(b, carry):
        slot = lax.rem(b, 2)
        for copy in stream(b, slot):
            copy.wait()

        @pl.when(b < 3)
        def _():
            for copy in stream(b + 1, 1 - slot):
                copy.start()

        acc[...] = nt_dot(grad_out[...], square(held.at[slot]))

        def through(c, rows, at):
            there = pl.ds(pl.multiple_of(slot * row_count + c * FRAMES, FRAMES), FRAMES)
            rise = jnp.concatenate([spread[q, there] for q in range(9)], axis=1)
            grad = (acc[rows] * rise).astype(bf16)
            grad_hidden[b, rows] = grad
            add_bias(5 + b, grad)

        over_columns(columns, through)
        return carry

    tick("begin")
    for b in range(4):
        lax.fori_loop(b, b + 1, down, 0)
        tick("down", b)
    fetch(3, 0).start()

    def down_bias(c, rows, at):
        add_bias(4, grad_out[rows])

    over_columns(columns, down_bias)

    def weave(first, ways, left, right, runs, name):
        before = None
        for k, (start, count) in enumerate(runs):
            for w in range(ways):
                part = tn_dot(left[:, start : start + count], right[w])
                for q in range(9):
                    spread[q, pl.ds(w, count, stride=ways), :] = part[:, 128 * q : 128 * q + 128]
            if before is not None:
                before.wait()

            def pack(j, carry):
                for q in range(9):
                    lines = spread[q, pl.ds(pl.multiple_of(j * 128, 128), 128), :]
                    woven[pl.ds(j * 16, 16), :, 128 * q : 128 * q + 128] = lines.reshape(
                        16, 8, 128
                    ).astype(bf16)
                return carry

            groups = count * ways // 8
            lax.fori_loop(0, groups // 16, pack, 0)
            before = store(first + start * ways // 8, 0, groups, 0)
            before.start()
            tick(name, k)
        before.wait()

    weave(AT_UP, 4, input_mlp, grad_hidden, UP_RUNS, "up run")
    tick("up")
    acc[...] = jnp.zeros_like(acc)
    for b in range(4):
        fetch(3 + b, b % 2).wait()
        if b < 3:
            fetch(4 + b, 1 - b % 2).start()
        acc[...] += nt_dot(grad_hidden[b], square(held.at[b % 2]))
        tick("up input", b)
    flat_mat(AT_PROJ, 0).start()

    def second_norm_back(c, rows, at):
        br = branch[rows]
        gate = mods[2, at]
        normed, inverse = norm_rows(tokens[rows].astype(f32) + gate * br)
        grad = acc[rows]
        grad_mods[3, at] = jnp.sum(grad, axis=0, keepdims=True)
        grad_mods[4, at] = jnp.sum(grad * normed, axis=0, keepdims=True)
        grad_block = jnp.where(mods[6, at] > 0.5, upstream[rows].astype(f32), 0.0)
        grad_middle = grad_block + norm_rows_back(grad * (1.0 + mods[4, at]), normed, inverse)
        input_grad[rows] = grad_middle
        grad_mods[2, at] = jnp.sum(grad_middle * br, axis=0, keepdims=True)
        grad = (grad_middle * gate).astype(bf16)
        grad_branch[rows] = grad
        add_bias(3, grad)

    over_columns(columns, second_norm_back)
    tick("norm")
    outer(AT_PROJ, attended, grad_branch)
    flat_mat(AT_PROJ, 0).wait()
    grad_att[...] = nt_dot(grad_branch[...], square(held.at[0])).astype(bf16)
    fetch(0, 0).start()
    for r in range(3):
        store(AT_PROJ + 48 * r, 48 * r, 48, r).wait()
    tick("proj")
    inside = same_column()

    def attend_back(g, carry):
        rows = pl.ds(pl.multiple_of(g * 128, 128), 128)
        for p in range(3):
            acc[pl.ds(p * 128, 128)] = jnp.zeros((128, D), f32)
        for h in range(H):
            window, mask = head_window(h)
            queries = proj[0, rows, window] * mask
            keys = proj[1, rows, window]
            grad = grad_att[rows, window] * mask
            probs = head_probabilities(queries, keys, inside)
            grad_probs = nt_dot(grad, proj[2, rows, window])
            mean = jnp.sum(grad_probs * probs, axis=-1, keepdims=True)
            grad_scores = (probs * (grad_probs - mean)).astype(bf16)
            acc[pl.ds(0, 128), window] += nn_dot(grad_scores, keys * mask)
            acc[pl.ds(128, 128), window] += tn_dot(grad_scores, queries)
            acc[pl.ds(256, 128), window] += tn_dot(probs.astype(bf16), grad)
        for p in range(3):
            scale = SCORE_SCALE if p < 2 else 1.0
            grad = (acc[pl.ds(p * 128, 128)] * scale).astype(bf16)
            grad_hidden[p, rows] = grad
            add_bias(p, grad)
        return carry

    for g in range(row_count // 128):
        lax.fori_loop(g, g + 1, attend_back, 0)
        tick("attend", g)
    weave(0, 3, input_att, grad_hidden, QKV_RUNS, "qkv run")
    tick("qkv")
    acc[...] = jnp.zeros_like(acc)
    for p in range(3):
        fetch(p, p % 2).wait()
        if p < 2:
            fetch(p + 1, 1 - p % 2).start()
        acc[...] += nt_dot(grad_hidden[p], square(held.at[p % 2]))
        tick("qkv input", p)

    def first_norm_back(c, rows, at):
        normed, inverse = norm_rows(tokens[rows].astype(f32))
        grad = acc[rows]
        grad_mods[0, at] = jnp.sum(grad, axis=0, keepdims=True)
        grad_mods[1, at] = jnp.sum(grad * normed, axis=0, keepdims=True)
        grad_states = input_grad[rows] + norm_rows_back(
            grad * (1.0 + mods[1, at]), normed, inverse
        )
        up_rows = upstream[rows].astype(f32)
        input_grad[rows] = jnp.where(mods[6, at] > 0.5, grad_states, up_rows)

    over_columns(columns, first_norm_back)
    tick("end")


def backward_kernel(given, *refs):
    backward_body(*refs, lambda name, step=0: None)


def backward_scatter_kernel(*refs):
    (
        given, weights, natural, slope, tokens, upstream, mods, input_att, proj, attended, branch,
        input_mlp, grad_out, grad_gate, member,
        out, grads, other, input_grad, total_small,
        grad_mods, bias_sums, held, woven, spread, grad_hidden, grad_branch, grad_att, acc, copy_sems,
        own, stage, rx2, ry2, rx1, ry1, rz, final, tail, tail_in, tail_z, local_sems, credit,
        small, sums, send_sems, recv_sems,
    ) = refs
    me = Place()
    cp = Copies(send_sems, recv_sems)
    me.greet()
    st = scatter_stages(
        me, cp, grads, out, other, own, stage, rx2, ry2, rx1, ry1, rz, final, tail, tail_in,
        tail_z, local_sems, credit,
    )
    t0, t1, t2, t3, t4, t5 = st["tails"]
    m1, m2, m3, m4, total = sum_stages(me, cp, small, sums)
    groups = member.shape[0]

    def run(steps):
        acts = dict(
            E=st["exchange"], P=st["prefetch"], A=st["fold"], B=st["second"], C=st["third"],
            S=st["settle"],
        )
        for step in steps.split():
            acts[step[0]](int(step[1:]))

    turns = {
        ("begin", 0): "E2 P0",
        ("down", 0): "A0 P1",
        ("down", 2): "A1 P2 B0",
        ("up run", 0): "A2 P3 B1 C0",
        ("up run", 3): "A3 B2 C1",
        ("up", 0): "E1 P4",
        ("up input", 0): "A4 P5 B3 C2",
        ("norm", 0): "A5 P6 B4 C3",
        ("proj", 0): "S2",
        ("attend", 0): "A6 P7 B5 C4",
        ("attend", 1): "A7 B6 C5",
        ("attend", 2): "B7 C6",
        ("qkv", 0): "E0 P8",
        ("qkv input", 0): "A8 P9",
        ("qkv input", 2): "A10 P11 B9 C8",
        ("qkv input", 1): "A9 P10 B8 C7",
    }

    def tick(name, step=0):
        run(turns.get((name, step), ""))
        if (name, step) == ("qkv", 0):
            t0()
        if (name, step) == ("qkv input", 0):
            t1()
        if (name, step) == ("qkv input", 2):
            t2()
        if name == "end":
            for n in range(6):
                plane = grad_mods[n] if n < 5 else grad_gate[...]
                small[pl.ds(n * groups, groups)] = picked(member[...], plane)
            small[pl.ds(6 * groups, 9)] = bias_sums[pl.ds(0, 9)]
            small[pl.ds(6 * groups + 9, small.shape[0] - 6 * groups - 9)] = jnp.zeros(
                (small.shape[0] - 6 * groups - 9, D), f32
            )
            m1()
            run("A11 B10 C9 S1")
            t3()
            m2()
            run("B11 C10 C11 S0")
            t4()
            m3()
            t5()
            m4()
            run("")
            total_small[...] = total()
            for p in (2, 1, 0):
                st["finish"](p)
            cp.drain()

    backward_body(
        weights, natural, slope, tokens, upstream, mods, input_att, proj, attended, branch,
        input_mlp, grad_out,
        grads.reshape(4 * 4 * 2 * GROUPS8, 8, D), input_grad, grad_mods, bias_sums,
        held, woven, spread, grad_hidden, grad_branch, grad_att, acc, copy_sems,
        tick,
    )


def backward_shapes(rows, columns):
    shape = jax.ShapeDtypeStruct
    return [
        shape((rows, D), f32),
        shape((5, columns, D), f32),
        shape((16, D), f32),
    ]


def backward_scratch(rows):
    return [
        pltpu.VMEM((2, MATS, 8, D), bf16),
        pltpu.VMEM((MATS, 8, D), bf16),
        pltpu.VMEM((9, D, 128), f32),
        pltpu.VMEM((4, rows, D), bf16),
        pltpu.VMEM((rows, D), bf16),
        pltpu.VMEM((rows, D), bf16),
        pltpu.VMEM((rows, D), f32),
        pltpu.SemaphoreType.DMA((9,)),
    ]


def backward(*operands):
    rows, columns = operands[4].shape[0], operands[6].shape[1]
    return pl.pallas_call(
        backward_kernel,
        out_shape=[jax.ShapeDtypeStruct((32 * UNITS // 8, 8, D), bf16)]
        + backward_shapes(rows, columns),
        in_specs=[HBM_SPEC] * 4 + [VMEM_SPEC] * 9,
        out_specs=[HBM_SPEC] + [VMEM_SPEC] * 3,
        input_output_aliases={0: 0},
        scratch_shapes=backward_scratch(rows),
        compiler_params=pltpu.CompilerParams(vmem_limit_bytes=62 * 2**20),
        name="block_backward",
    )(*operands)


def backward_scatter(operands, grad_gate, member):
    rows, columns = operands[4].shape[0], operands[6].shape[1]
    small = small_rows(member.shape[0])
    copies = SCATTER_COPIES + SUM_COPIES
    shape = jax.ShapeDtypeStruct
    input_grad, grad_mods, bias_sums = backward_shapes(rows, columns)
    return pl.pallas_call(
        backward_scatter_kernel,
        out_shape=[
            shape((GROUPS8, 8, D), bf16),
            shape((4, 4, 2, GROUPS8, 8, D), bf16),
            shape((3, 4, 2, 2, QUART, 8, D), bf16),
            input_grad,
            shape((small, D), f32),
        ],
        in_specs=[HBM_SPEC] * 4 + [VMEM_SPEC] * 11,
        out_specs=[HBM_SPEC] * 3 + [VMEM_SPEC] * 2,
        input_output_aliases={0: 1},
        scratch_shapes=[
            pltpu.VMEM(grad_mods.shape, f32),
            pltpu.VMEM(bias_sums.shape, f32),
        ]
        + backward_scratch(rows)
        + scatter_scratch()
        + [
            pltpu.VMEM((small, D), f32),
            pltpu.VMEM((SUM_SLOTS, small, D), f32),
            pltpu.SemaphoreType.DMA((copies,)),
            pltpu.SemaphoreType.DMA((copies,)),
        ],
        compiler_params=pltpu.CompilerParams(
            collective_id=1, has_side_effects=True, vmem_limit_bytes=63 * 2**20
        ),
        name="backward_scatter",
    )(*operands, grad_gate, member)


def small_rows(groups):
    return -(-(6 * groups + 9) // 8) * 8


def adamw_rows(value, grad, first, second):
    first_new = BETA_FIRST * first + (1.0 - BETA_FIRST) * grad
    second_new = BETA_SECOND * second + (1.0 - BETA_SECOND) * grad * grad
    first_hat = first_new * (1.0 / (1.0 - BETA_FIRST**STEP))
    second_hat = second_new * (1.0 / (1.0 - BETA_SECOND**STEP))
    step = first_hat / (jnp.sqrt(second_hat) + ADAM_EPS) + WEIGHT_DECAY * value
    return value - LEARN_RATE * step, first_new, second_new


def norm_kernel(
    shard_sum, low, small, selector, parts_t, row_of, in_ada, cond,
    cond_grad, norm_out, flat, bias_flat,
    ada, mine, own_cond, sums, cond_sums, send_sems, recv_sems,
):
    groups = cond.shape[0]
    me = Place()
    cp = Copies(send_sems, recv_sems)
    me.greet()
    m1, m2, total = cube_stages(me, cp, mine, sums)
    n1, n2, cond_total = cube_stages(me, cp, own_cond, cond_sums)
    parts = small[pl.ds(0, 6 * groups)]
    ada[...] = picked(selector[...], parts)

    def spread_group(run, square):
        for n in range(3):
            j = 3 * run + n
            rows = pl.ds(pl.multiple_of(j * 8, 8), 8)
            grad = jnp.where(in_ada[rows] > 0.5, ada[rows], shard_sum[j].astype(f32))
            for q in range(9):
                flat[pl.ds(72 * j + q, 8, stride=9), :] = grad[:, 128 * q : 128 * q + 128]
            square = square + grad * grad
        return square

    square = lax.fori_loop(0, GROUPS8 // 3, spread_group, jnp.zeros((8, D), f32))
    lanes = square[:, :128]
    for q in range(1, 9):
        lanes = lanes + square[:, 128 * q : 128 * q + 128]
    mine[...] = lanes
    m1()
    rows = 6 * groups
    products = nt_dot(jnp.concatenate(three_parts(parts), axis=0), low[...].reshape(UNITS, D))
    products = products[:rows] + products[rows : 2 * rows] + products[2 * rows :]
    products = products * parts_t[...]
    folded = products[:groups]
    for n in range(1, 6):
        folded = folded + products[n * groups : (n + 1) * groups]
    lane = lax.broadcasted_iota(jnp.int32, (UNITS, 128), 1)
    own_cond[...] = jnp.zeros_like(own_cond)
    folded = jnp.concatenate(three_parts(folded), axis=0)
    for q in range(9):
        hit = jnp.where(row_of[...] == lane + 128 * q, 1.0, 0.0).astype(bf16)
        there = nn_dot(folded, hit)
        there = there[:groups] + there[groups : 2 * groups] + there[2 * groups :]
        own_cond[pl.ds(0, groups), 128 * q : 128 * q + 128] = there
    n1()
    m2()
    bias_rows = [small[pl.ds(6 * groups + n, 1)] for n in (0, 2, 3, 5, 6, 7, 8, 4)]
    for n in range(6):
        bias_rows.append(jnp.sum(small[pl.ds(n * groups, groups)], axis=0, keepdims=True))
    for t, line in enumerate(bias_rows):
        for q in range(9):
            bias_flat[pl.ds(9 * t + q, 1)] = line[:, 128 * q : 128 * q + 128]
    bias_square = jnp.sum(bias_flat[...] * bias_flat[...], axis=0, keepdims=True)
    n2()
    squares = jnp.sum(total(), axis=0, keepdims=True) + bias_square
    norm_out[...] = jnp.sqrt(jnp.sum(squares, axis=1, keepdims=True))
    summed = cond_total()
    c = cond[...]
    gate = 1.0 / (1.0 + jnp.exp(-c))
    cond_grad[...] = summed[:groups] * (gate * (1.0 + c * (1.0 - gate)))
    cp.drain()


def norm_exchange(*operands):
    cond = operands[7]
    shape = jax.ShapeDtypeStruct
    payload = 8 * (cond.shape[0] // 8 + 1)
    return pl.pallas_call(
        norm_kernel,
        out_shape=[
            shape(cond.shape, f32), shape((1, 1), f32), shape((9 * UNITS, 128), f32),
            shape((BIAS_LINES, 128), f32),
        ],
        in_specs=[VMEM_SPEC] * len(operands),
        out_specs=[VMEM_SPEC] * 4,
        scratch_shapes=[
            pltpu.VMEM((UNITS, D), f32),
            pltpu.VMEM((8, 128), f32),
            pltpu.VMEM((payload, D), f32),
            pltpu.VMEM((CUBE_SLOTS, 8, 128), f32),
            pltpu.VMEM((CUBE_SLOTS, payload, D), f32),
            pltpu.SemaphoreType.DMA((2 * CUBE_COPIES,)),
            pltpu.SemaphoreType.DMA((2 * CUBE_COPIES,)),
        ],
        compiler_params=pltpu.CompilerParams(
            collective_id=2, has_side_effects=True, vmem_limit_bytes=24 * 2**20
        ),
        name="norm_exchange",
    )(*operands)


BIAS_LINES = 126


def adamw_kernel(
    norm, flat, weights, first, second, bias_flat, biases, bias_first, bias_second, block_in,
    grad_in,
    new_weights, first_out, second_out, new_biases, bias_first_out, bias_second_out, block_out,
    grad_out,
    stage, sems,
):
    passed = (
        pltpu.make_async_copy(block_in, block_out, sems.at[0]),
        pltpu.make_async_copy(grad_in, grad_out, sems.at[1]),
    )
    for copy in passed:
        copy.start()
    factor = jnp.minimum(1.0, CLIP_NORM / (norm[...] + 1e-06))
    results = (new_weights, first_out, second_out)
    run = 648
    count = flat.shape[0] // run

    def away(n, j):
        at = pl.ds(j * run, run)
        return pltpu.make_async_copy(stage.at[n, at], results[n].at[at], sems.at[2 + n])

    for j in range(count):

        def update(i, carry):
            at = pl.ds(pl.multiple_of(j * run + i * 216, 8), 216)
            stage[0, at], stage[1, at], stage[2, at] = adamw_rows(
                weights[at], flat[at] * factor, first[at], second[at]
            )
            return carry

        lax.fori_loop(0, run // 216, update, 0)
        for n in range(3):
            if j:
                away(n, j - 1).wait()
            away(n, j).start()
    new_biases[...], bias_first_out[...], bias_second_out[...] = adamw_rows(
        biases[...], bias_flat[...] * factor, bias_first[...], bias_second[...]
    )
    for n in range(3):
        away(n, count - 1).wait()
    for copy in passed:
        copy.wait()


def adamw_update(norm, flat, state, bias_flat, bias_state, block_in, grad_in):
    shape = jax.ShapeDtypeStruct
    like = [shape(flat.shape, f32)] * 3 + [shape((BIAS_LINES, 128), f32)] * 3
    return pl.pallas_call(
        adamw_kernel,
        out_shape=like + [shape(block_in.shape, f32), shape(grad_in.shape, f32)],
        in_specs=[VMEM_SPEC] * 11,
        out_specs=[HBM_SPEC] * 3 + [VMEM_SPEC] * 3 + [HBM_SPEC] * 2,
        scratch_shapes=[pltpu.VMEM((3, *flat.shape), f32), pltpu.SemaphoreType.DMA((5,))],
        compiler_params=pltpu.CompilerParams(vmem_limit_bytes=40 * 2**20),
        name="adamw",
    )(norm, flat, *state, bias_flat, *bias_state, block_in, grad_in)


def gather_blocks(shard_low):
    whole = lax.all_gather(shard_low, ("outer", "inner"), axis=0, tiled=True)
    return whole.reshape(-1, 8, D)


def scatter_blocks(grads, units):
    axes = ("outer", "inner")
    whole = grads.reshape(-1, D)[: lax.axis_size(axes) * units].astype(f32)
    return lax.psum_scatter(whole, axes, scatter_dimension=0, tiled=True)


def split_bias(vector):
    widths = [D, D, D, FF, D, 6 * D]
    pieces = []
    offset = 0
    for span_width in widths:
        pieces.append(lax.slice_in_dim(vector, offset, offset + span_width))
        offset = offset + span_width
    return pieces


def exact(left, right, dims):
    return lax.dot_general(
        left, right, dims, precision=lax.Precision.HIGHEST, preferred_element_type=jnp.float32
    )


def three_parts(values):
    high = values.astype(bf16)
    rest = values - high.astype(f32)
    middle = rest.astype(bf16)
    low_part = (rest - middle.astype(f32)).astype(bf16)
    return high, middle, low_part


def picked(choice, values):
    high, middle, low_part = three_parts(values)
    choice = choice.astype(bf16)
    return nn_dot(
        jnp.concatenate([choice] * 3, axis=1), jnp.concatenate([high, middle, low_part], axis=0)
    )


def ada_selector(soft_cond, first_unit, units):
    groups = soft_cond.shape[0]
    spread = jnp.repeat(soft_cond.astype(jnp.float32), 6, axis=1)
    spread = jnp.pad(spread, ((0, 0), (units, units)))
    start = jnp.clip(first_unit - BLOCK_UNITS + units, 0, 6 * D + units)
    local = lax.dynamic_slice(spread, (jnp.int32(0), start), (groups, units))
    unit = first_unit - BLOCK_UNITS + jnp.arange(units, dtype=jnp.int32)
    part = (unit[:, None] % 6 == jnp.arange(6, dtype=jnp.int32)[None, :]) & (unit[:, None] >= 0)
    part = part.astype(jnp.float32)
    selector = local.T[:, :, None] * part[:, None, :]
    return selector.reshape(units, groups * 6), part


def adamw(parameter, gradient, first_state, second_state):
    first_new = BETA_FIRST * first_state + (1.0 - BETA_FIRST) * gradient
    second_new = BETA_SECOND * second_state + (1.0 - BETA_SECOND) * gradient * gradient
    first_hat = first_new / (1.0 - BETA_FIRST**STEP)
    second_hat = second_new / (1.0 - BETA_SECOND**STEP)
    updated = parameter - LEARN_RATE * (
        first_hat / (jnp.sqrt(second_hat) + ADAM_EPS) + WEIGHT_DECAY * parameter
    )
    return (updated, first_new, second_new)


def with_kernels(
    tokens, conditioning, output_grad, state, bias_state, first_unit, selector, ada_part,
    membership, video_plane, b_ada, bias_args,
):
    columns, groups = membership.shape
    units = UNITS
    eye = jnp.eye(6, dtype=f32)
    chosen = membership[None, :, None, :] * eye[:, None, :, None]
    chosen = jnp.pad(chosen.reshape(6 * columns, 6 * groups), ((0, columns), (0, 0)))
    base = jnp.repeat(b_ada.reshape(6, D), columns, axis=0)
    base = jnp.concatenate([base, video_plane])
    by_part = selector.reshape(units, groups, 6).transpose(0, 2, 1).reshape(units, 6 * groups)
    state = [part.reshape(9 * units, 128) for part in state]
    (
        flat, mods, shard_low, block_out, natural, input_att, proj, attended, branch, input_mlp, _,
        slope, grad_out, grad_gate, grads,
    ) = gather_forward(
        state[0], by_part.T.astype(bf16), chosen, base, tokens, output_grad, *bias_args
    )
    flat = flat.reshape(-1, 8, D)
    shard_sum, _, _, input_grad, small = backward_scatter(
        (
            grads.reshape(4, 4, 2, GROUPS8, 8, D), flat, natural, slope, tokens, output_grad, mods,
            input_att, proj, attended, branch, input_mlp, grad_out,
        ),
        grad_gate, membership.T,
    )
    unit = first_unit - BLOCK_UNITS + jnp.arange(units, dtype=jnp.int32)
    row_of = jnp.where(unit >= 0, unit // 6, -1)[:, None]
    parts_t = jnp.repeat(ada_part.T, groups, axis=0)
    in_ada = (unit >= 0).astype(f32)[:, None]
    cond_grad, norm, flat_grad, bias_flat = norm_exchange(
        shard_sum, shard_low, small, by_part, parts_t, row_of, in_ada, conditioning
    )
    *updated, block_out, input_grad = adamw_update(
        norm, flat_grad, state, bias_flat, [part.reshape(-1, 128) for part in bias_state],
        block_out, input_grad,
    )
    return (block_out, input_grad, cond_grad, norm[0, 0], *[part.reshape(-1) for part in updated])


def on_device(
    tokens,
    conditioning,
    column_sample,
    is_image,
    output_grad,
    weights,
    first_moment,
    second_moment,
    biases,
    bias_first,
    bias_second,
    kernels,
):
    columns = column_sample.shape[0]
    groups = conditioning.shape[0]
    units = weights.shape[0] // D
    axes = ("outer", "inner")
    first_unit = lax.axis_index(axes).astype(jnp.int32) * units
    b_query, b_value, b_proj, b_up, b_down, b_ada = split_bias(biases)
    soft_cond = jax.nn.silu(conditioning).astype(bf16)
    selector, ada_part = ada_selector(soft_cond, first_unit, units)
    membership = (column_sample[:, None] == jnp.arange(groups, dtype=jnp.int32)[None, :]).astype(
        f32
    )
    video_cols = exact(membership, 1.0 - is_image.astype(f32)[:, None], (((1,), (0,)), ((), ())))
    b_qkv = jnp.stack([b_query, jnp.zeros((D,), f32), b_value])
    bias_args = (b_qkv, b_proj[None], b_up.reshape(4, D), b_down[None])
    video_plane = jnp.broadcast_to(video_cols, (columns, D))
    if kernels:
        return with_kernels(
            tokens, conditioning, output_grad, (weights, first_moment, second_moment),
            (biases, bias_first, bias_second), first_unit, selector, ada_part, membership,
            video_plane, b_ada, bias_args,
        )
    shard_low = weights.reshape(units, D).astype(bf16)
    flat = gather_blocks(shard_low)
    mods_all = lax.psum(tn_dot(selector.astype(bf16), shard_low), axes)
    mods_all = mods_all.reshape(groups, 6 * D) + b_ada
    mods = jnp.take(mods_all, column_sample, axis=0).reshape(columns, 6, D).transpose(1, 0, 2)
    mods = jnp.concatenate([mods, video_plane[None]])
    (
        block_out, natural, input_att, proj, attended, branch, input_mlp, _, slope, grad_out,
        grad_gate, grads,
    ) = forward(flat, tokens, output_grad, mods, *bias_args)
    grads, input_grad, grad_mods, bias_sums = backward(
        grads, flat, natural, slope, tokens, output_grad, mods, input_att, proj, attended, branch,
        input_mlp, grad_out,
    )
    grad_mods = jnp.concatenate([grad_mods, grad_gate[None]])
    mods_local = exact(membership, grad_mods, (((0,), (1,)), ((), ())))
    bias_sums, grad_mods_all = lax.psum((bias_sums, mods_local.transpose(1, 0, 2)), axes)
    block_shard = scatter_blocks(grads, units)
    grad_mods_all = grad_mods_all.transpose(1, 0, 2).reshape(groups, 6 * D)
    bias_head = jnp.concatenate([bias_sums[:1], bias_sums[2:4], bias_sums[5:9], bias_sums[4:5]])
    first_sum = jnp.concatenate([bias_head.reshape(-1), jnp.sum(grad_mods_all, axis=0)])
    mods_parts = grad_mods_all.reshape(groups * 6, D)
    ada_shard = exact(selector, mods_parts, (((1,), (0,)), ((), ())))
    unit = first_unit + jnp.arange(units, dtype=jnp.int32)
    grad_units = jnp.where(unit[:, None] >= BLOCK_UNITS, ada_shard, block_shard)
    products = exact(shard_low.astype(jnp.float32), mods_parts, (((1,), (1,)), ((), ())))
    products = jnp.sum(products.reshape(units, groups, 6) * ada_part[:, None, :], axis=2)
    spread = jnp.zeros((groups, 6 * D + 2 * units), jnp.float32)
    start = jnp.clip(first_unit - BLOCK_UNITS + units, 0, 6 * D + units)
    spread = lax.dynamic_update_slice(spread, products.T, (jnp.int32(0), start))
    grad_soft = jnp.sum(spread[:, units : units + 6 * D].reshape(groups, D, 6), axis=2)
    square_sum = jnp.sum(grad_units * grad_units)
    square_sum, grad_soft = lax.psum((square_sum, grad_soft), axes)
    silu_out, silu_back = jax.vjp(jax.nn.silu, conditioning)
    second_sum = silu_back(grad_soft)[0]
    grad_shard = grad_units.reshape(-1)
    grad_norm = jnp.sqrt(square_sum + jnp.sum(first_sum * first_sum))
    factor = jnp.minimum(1.0, CLIP_NORM / (grad_norm + 1e-06))
    new_weights, first_out, second_out = adamw(
        weights, grad_shard * factor, first_moment, second_moment
    )
    new_biases, bias_first_out, bias_second_out = adamw(
        biases, first_sum * factor, bias_first, bias_second
    )
    return (
        block_out,
        input_grad,
        second_sum,
        grad_norm,
        new_weights,
        first_out,
        second_out,
        new_biases,
        bias_first_out,
        bias_second_out,
    )


def solution(mesh):
    in_specs = (
        P(("outer", "inner"), None),
        P(),
        P(("outer", "inner")),
        P(),
        P(("outer", "inner"), None),
        P(("outer", "inner")),
        P(("outer", "inner")),
        P(("outer", "inner")),
        P(),
        P(),
        P(),
    )
    out_specs = (
        P(("outer", "inner"), None),
        P(("outer", "inner"), None),
        P(),
        P(),
        P(("outer", "inner")),
        P(("outer", "inner")),
        P(("outer", "inner")),
        P(),
        P(),
        P(),
    )
    kernels = dict(mesh.shape) == {"outer": 4, "inner": 8}
    return jax.shard_map(
        functools.partial(on_device, kernels=kernels), mesh=mesh, in_specs=in_specs, out_specs=out_specs, check_vma=False
    )
```

```python
import functools
import math

import jax
import jax.numpy as jnp
from jax import lax
from jax.experimental import pallas as pl
from jax.experimental.pallas import tpu as pltpu
from jax.sharding import PartitionSpec as P

D = 1152
H = 16
HD = 72
FF = 4608
FRAMES = 16
STEP = 8


NORM_EPS = 1e-06
LEARN_RATE = 0.02
BETA_FIRST = 0.5
BETA_SECOND = 0.55
ADAM_EPS = 1e-08
WEIGHT_DECAY = 0.01
CLIP_NORM = 1.0
BLOCK_UNITS = 4 * D + 2 * FF


MESH = pl.DeviceIdType.MESH
UNITS = 648
GROUPS8 = 81
QUART = 20
FIRST = 8
SECOND = QUART - FIRST
MAIN = 80
TAIL = 1
DEPTH = (4, 4, 3)
BASE = (0, 4, 8)


def flip(z, d):
    if d == 0:
        return z
    if d == 1:
        return z + 1 - 2 * (z % 2)
    if d == 2:
        return z + 2 - 4 * (z // 2)
    return 3 - z


class Place:
    def __init__(self):
        self.o = lax.axis_index("outer")
        self.i = lax.axis_index("inner")
        self.x, self.c = self.o // 2, self.o % 2
        self.z, self.y = self.i // 2, self.i % 2
        self.xo, self.co, self.yo = 1 - self.x, 1 - self.c, 1 - self.y

    def dev(self, dx=0, dc=0, dz=0, dy=0):
        x = self.xo if dx else self.x
        c = self.co if dc else self.c
        y = self.yo if dy else self.y
        return (x * 2 + c, flip(self.z, dz) * 2 + y)

    def greet(self):
        peers = [
            self.dev(dx, dc, 0, dy) for dx in (0, 1) for dc in (0, 1) for dy in (0, 1)
        ][1:]
        peers += [self.dev(dz=1), self.dev(dz=2), self.dev(dz=3)]
        barrier = pltpu.get_barrier_semaphore()
        for peer in peers:
            pl.semaphore_signal(barrier, inc=1, device_id=peer, device_id_type=MESH)
        pl.semaphore_wait(barrier, len(peers))


class Copies:
    def __init__(self, send_sems, recv_sems):
        self.send_sems, self.recv_sems = send_sems, recv_sems
        self.count = 0
        self.sent = []

    def slot(self):
        self.count += 1
        return self.count - 1

    def make(self, slot, src, dst, device):
        return pltpu.make_async_remote_copy(
            src_ref=src, dst_ref=dst, send_sem=self.send_sems.at[slot],
            recv_sem=self.recv_sems.at[slot], device_id=device, device_id_type=MESH,
        )

    def send(self, slot, src, dst, device, cond=None):
        def go():
            self.make(slot, src, dst, device).start()
        if cond is None:
            go()
        else:
            pl.when(cond)(go)
        self.sent.append((slot, src, dst, device, cond))

    def wait_recv(self, slot, dst, device, cond=None):
        def go():
            self.make(slot, dst, dst, device).wait_recv()
        if cond is None:
            go()
        else:
            pl.when(cond)(go)

    def wait_send(self, wanted):
        for entry in self.sent:
            if entry[0] == wanted:
                slot, src, dst, device, cond = entry

                def go():
                    self.make(slot, src, dst, device).wait_send()
                if cond is None:
                    go()
                else:
                    pl.when(cond)(go)
        self.sent = [entry for entry in self.sent if entry[0] != wanted]

    def drain(self):
        for slot, src, dst, device, cond in self.sent:
            def go(slot=slot, src=src, dst=dst, device=device):
                self.make(slot, src, dst, device).wait_send()
            if cond is None:
                go()
            else:
                pl.when(cond)(go)
        self.sent = []


def ok(zb, p):
    return None if DEPTH[p] == 4 else zb < DEPTH[p]


def both(a, b):
    if a is None:
        return b
    if b is None:
        return a
    return jnp.logical_and(a, b)


GATHER_COPIES = 3 * (3 + 5 + 4 * 4 + 8) + 7


def gather_stages(me, cp, shard, full, local_sems):
    def part(p, zb, yb, x, c, first=0, n=QUART):
        return full.at[p, zb, yb, pl.ds((2 * QUART * x + QUART * c + first), n)]

    def own_of(p):
        return both(me.o == p, ok(me.z, p))

    quarter = (2 * QUART * me.x + QUART * me.c)
    own_tail = pltpu.make_async_copy(
        shard.at[pl.ds(MAIN, TAIL)], full.at[me.o, me.z, me.y, pl.ds(MAIN, TAIL)], local_sems.at[0]
    )
    own_tail.start()

    def local_quarter(p):
        return pltpu.make_async_copy(
            shard.at[pl.ds(quarter, QUART)], part(p, me.z, me.y, me.x, me.c), local_sems.at[1]
        )

    slots = {}

    def s0(p):
        @pl.when(own_of(p))
        def _():
            local_quarter(p).start()
        for dx, dc in ((1, 0), (0, 1), (1, 1)):
            s = slots["s0", p, dx, dc] = cp.slot()
            x = me.xo if dx else me.x
            c = me.co if dc else me.c
            cp.send(
                s, shard.at[pl.ds((2 * QUART * x + QUART * c), QUART)],
                part(p, me.z, me.y, x, c), me.dev(dx=dx, dc=dc), own_of(p),
            )

    def s0_wait(p):
        @pl.when(own_of(p))
        def _():
            local_quarter(p).wait()
        ox, oc = p // 2, p % 2
        for dx, dc in ((1, 0), (0, 1), (1, 1)):
            x = me.xo if dx else me.x
            c = me.co if dc else me.c
            cond = both(jnp.logical_and(x == ox, c == oc), ok(me.z, p))
            cp.wait_recv(
                slots["s0", p, dx, dc], part(p, me.z, me.y, me.x, me.c), me.dev(dx=dx, dc=dc), cond
            )

    def spread(p, d):
        zb = place(d)
        mine = part(p, zb, me.y, me.x, me.c)
        s = slots["y1", p, d] = cp.slot()
        cp.send(s, mine, mine, me.dev(dy=1), ok(zb, p))
        s = slots["x1", p, d] = cp.slot()
        cp.send(s, mine, mine, me.dev(dx=1), ok(zb, p))

    def place(e):
        return (me.z, flip(me.z, 1), 2 - me.z // 2, 3 - 3 * (me.z // 2))[e]

    inner = (me.z + 1) // 2 == 1
    outer = jnp.logical_not(inner)

    def pass_on(p, zb, name, device, cond):
        view = part(p, zb, me.y, me.x, me.c)
        s = slots[name, p] = cp.slot()
        cp.send(s, view, view, device, both(cond, ok(zb, p)))

    def arrive(p, e, name, device, cond):
        zb = place(e)
        view = part(p, zb, me.y, me.x, me.c)
        cp.wait_recv(slots[name, p], view, device, both(cond, ok(zb, p)))

    def s1(p):
        s0_wait(p)
        pass_on(p, me.z, "own to 1", me.dev(dz=1), None)
        pass_on(p, me.z, "own to 3", me.dev(dz=3), inner)
        spread(p, 0)

    def s2(p):
        arrive(p, 1, "own to 1", me.dev(dz=1), None)
        pass_on(p, place(1), "1 to 3", me.dev(dz=3), inner)
        spread(p, 1)
        arrive(p, 2, "own to 3", me.dev(dz=3), inner)
        pass_on(p, place(2), "near to 1", me.dev(dz=1), inner)
        arrive(p, 2, "near to 1", me.dev(dz=1), outer)
        spread(p, 2)
        arrive(p, 3, "1 to 3", me.dev(dz=3), inner)
        pass_on(p, place(3), "far to 1", me.dev(dz=1), inner)
        arrive(p, 3, "far to 1", me.dev(dz=1), outer)
        spread(p, 3)

    def s3(p, entries=(0, 1, 2, 3)):
        for d in entries:
            zb = place(d)
            cp.wait_recv(
                slots["y1", p, d], part(p, zb, me.yo, me.x, me.c), me.dev(dy=1), ok(zb, p)
            )
            s = slots["x2", p, d] = cp.slot()
            out = part(p, zb, me.yo, me.x, me.c, 0, FIRST)
            cp.send(s, out, out, me.dev(dx=1), ok(zb, p))
            cp.wait_recv(
                slots["x1", p, d], part(p, zb, me.y, me.xo, me.c), me.dev(dx=1), ok(zb, p)
            )
            s = slots["y2", p, d] = cp.slot()
            out = part(p, zb, me.y, me.xo, me.c, FIRST, SECOND)
            cp.send(s, out, out, me.dev(dy=1), ok(zb, p))

    def lane(p, zb, x, c):
        return full.at[p, zb, :, pl.ds((2 * QUART * x + QUART * c), QUART)]

    def s4(p):
        for d in (0, 1, 2, 3):
            zb = place(d)
            cp.wait_recv(
                slots["x2", p, d], part(p, zb, me.yo, me.xo, me.c, 0, FIRST), me.dev(dx=1),
                ok(zb, p),
            )
            cp.wait_recv(
                slots["y2", p, d], part(p, zb, me.yo, me.xo, me.c, FIRST, SECOND), me.dev(dy=1),
                ok(zb, p),
            )
            for h in (0, 1):
                s = slots["c", p, d, h] = cp.slot()
                cp.send(s, lane(p, zb, h, me.c), lane(p, zb, h, me.c), me.dev(dc=1), ok(zb, p))

    def s5(p):
        for d in (0, 1, 2, 3):
            zb = place(d)
            for h in (0, 1):
                cp.wait_recv(
                    slots["c", p, d, h], lane(p, zb, h, me.co), me.dev(dc=1), ok(zb, p)
                )

    tails = pl.ds(MAIN, TAIL)

    def t1():
        own_tail.wait()
        block = full.at[me.o, me.z, me.y, tails]
        for d in (1, 2, 3):
            s = slots["tz", d] = cp.slot()
            cp.send(s, block, block, me.dev(dz=d))

    def t2():
        for d in (1, 2, 3):
            zb = flip(me.z, d)
            cp.wait_recv(slots["tz", d], full.at[me.o, zb, me.y, tails], me.dev(dz=d))
        s = slots["ty"] = cp.slot()
        block = full.at[me.o, :, me.y, tails]
        cp.send(s, block, block, me.dev(dy=1))

    def t3():
        cp.wait_recv(slots["ty"], full.at[me.o, :, me.yo, tails], me.dev(dy=1))
        s = slots["tx"] = cp.slot()
        block = full.at[me.o, :, :, tails]
        cp.send(s, block, block, me.dev(dx=1))

    def t4():
        cp.wait_recv(slots["tx"], full.at[me.xo * 2 + me.c, :, :, tails], me.dev(dx=1))
        for h in (0, 1):
            s = slots["tc", h] = cp.slot()
            block = full.at[h * 2 + me.c, :, :, tails]
            cp.send(s, block, block, me.dev(dc=1))

    def t5():
        for h in (0, 1):
            cp.wait_recv(slots["tc", h], full.at[h * 2 + me.co, :, :, tails], me.dev(dc=1))

    return dict(s0=s0, s1=s1, s2=s2, s3=s3, s4=s4, s5=s5, t1=t1, t2=t2, t3=t3, t4=t4, t5=t5)


SCATTER_COPIES = 3 * (4 * 2 + 4 * 4 + 3 + 3) + 8
RING = 6
ORDER = (3, 2, 1, 0)
f32 = jnp.float32


def guarded(cond, fn):
    if cond is None:
        fn()
    else:
        pl.when(cond)(fn)


def add_rows(dst, srcs, n):
    step = math.gcd(n, 4)

    def body(j, carry):
        at = pl.ds(j * step, step)
        total = srcs[0][at].astype(f32)
        for src in srcs[1:]:
            total = total + src[at].astype(f32)
        dst[at] = total.astype(dst.dtype)
        return carry

    lax.fori_loop(0, n // step, body, 0)


def scatter_stages(
    me, cp, partial, out, other, own, stage, rx2, ry2, rx1, ry1, rz, final, tail, tail_in, tail_z,
    local_sems, credit,
):
    slots = {}

    def block(k):
        p, d = 2 - k // 4, ORDER[k % 4]
        zb = flip(me.z, d)
        return p, d, zb, ok(zb, p), k % RING

    def exchange(p):
        for d in ORDER:
            zb = flip(me.z, d)
            for h in (0, 1):
                s = slots["c", p, d, h] = cp.slot()
                view = pl.ds(2 * QUART * h + QUART * me.co, QUART)
                cp.send(
                    s, partial.at[p, zb, :, view], other.at[p, zb, :, h], me.dev(dc=1), ok(zb, p)
                )

    def loads(k):
        p, d, zb, cond, slot = block(k)
        copies = []
        for h in (0, 1):
            view = pl.ds(2 * QUART * h + QUART * me.c, QUART)
            copies.append(
                pltpu.make_async_copy(
                    partial.at[p, zb, :, view], own.at[slot, :, h], local_sems.at[h]
                )
            )
            copies.append(
                pltpu.make_async_copy(other.at[p, zb, :, h], stage.at[h], local_sems.at[2 + h])
            )
        return copies

    def prefetch(k):
        p, d, zb, cond, slot = block(k)
        if k >= RING:
            old = block(k - RING)
            for name in ("x2", "y2", "x1", "y1", "z"):
                if (name, old[0], old[1]) in slots:
                    cp.wait_send(slots[name, old[0], old[1]])
        for h in (0, 1):
            cp.wait_recv(slots["c", p, d, h], other.at[p, zb, :, h], me.dev(dc=1), cond)

        def go():
            for copy in loads(k):
                copy.start()

        guarded(cond, go)

    def fold(k):
        p, d, zb, cond, slot = block(k)

        def go():
            for copy in loads(k):
                copy.wait()

            def body(q, carry):
                y, h = q // 2, q % 2
                add_rows(own.at[slot, y, h], [own.at[slot, y, h], stage.at[h, y]], QUART)
                return carry

            lax.fori_loop(0, 4, body, 0)

        guarded(cond, go)
        if k >= RING:
            pl.semaphore_wait(credit.at[0], 1)
            pl.semaphore_wait(credit.at[1], 1)
        far = own.at[slot, me.yo, me.xo]
        s = slots["x2", p, d] = cp.slot()
        cp.send(s, far.at[pl.ds(0, FIRST)], rx2.at[slot], me.dev(dx=1), cond)
        s = slots["y2", p, d] = cp.slot()
        cp.send(s, far.at[pl.ds(FIRST, SECOND)], ry2.at[slot], me.dev(dy=1), cond)

    def second(k):
        p, d, zb, cond, slot = block(k)
        cp.wait_recv(slots["x2", p, d], rx2.at[slot], me.dev(dx=1), cond)
        view = own.at[slot, me.yo, me.x, pl.ds(0, FIRST)]
        guarded(cond, lambda: add_rows(view, [view, rx2.at[slot]], FIRST))
        s = slots["y1", p, d] = cp.slot()
        cp.send(s, own.at[slot, me.yo, me.x], ry1.at[slot], me.dev(dy=1), cond)
        cp.wait_recv(slots["y2", p, d], ry2.at[slot], me.dev(dy=1), cond)
        view2 = own.at[slot, me.y, me.xo, pl.ds(FIRST, SECOND)]
        guarded(cond, lambda: add_rows(view2, [view2, ry2.at[slot]], SECOND))
        s = slots["x1", p, d] = cp.slot()
        cp.send(s, own.at[slot, me.y, me.xo], rx1.at[slot], me.dev(dx=1), cond)

    def third(k):
        p, d, zb, cond, slot = block(k)
        cp.wait_recv(slots["y1", p, d], ry1.at[slot], me.dev(dy=1), cond)
        cp.wait_recv(slots["x1", p, d], rx1.at[slot], me.dev(dx=1), cond)
        view = own.at[slot, me.y, me.x]
        guarded(cond, lambda: add_rows(view, [view, ry1.at[slot], rx1.at[slot]], QUART))
        if k + RING < 12:
            pl.semaphore_signal(
                credit.at[0], inc=1, device_id=me.dev(dx=1), device_id_type=MESH
            )
            pl.semaphore_signal(
                credit.at[1], inc=1, device_id=me.dev(dy=1), device_id_type=MESH
            )
        if d:
            s = slots["z", p, d] = cp.slot()
            cp.send(s, view, rz.at[p, d - 1], me.dev(dz=d), cond)

    def quarter(x, c):
        return out.at[pl.ds(2 * QUART * x + QUART * c, QUART)]

    def settle(p):
        mine = ok(me.z, p)
        for d in (1, 2, 3):
            cp.wait_recv(slots["z", p, d], rz.at[p, d - 1], me.dev(dz=d), mine)
        view = own.at[(4 * (2 - p) + 3) % RING, me.y, me.x]
        guarded(
            mine,
            lambda: add_rows(final.at[p], [view, rz.at[p, 0], rz.at[p, 1], rz.at[p, 2]], QUART),
        )
        ox, oc = p // 2, p % 2
        for dx, dc in ((1, 0), (0, 1), (1, 1)):
            x = me.xo if dx else me.x
            c = me.co if dc else me.c
            s = slots["f", p, dx, dc] = cp.slot()
            cond = both(jnp.logical_and(x == ox, c == oc), mine)
            cp.send(s, final.at[p], quarter(me.x, me.c), me.dev(dx=dx, dc=dc), cond)

        @pl.when(both(me.o == p, mine))
        def _():
            pltpu.make_async_copy(final.at[p], quarter(me.x, me.c), local_sems.at[4]).start()

    def finish(p):
        mine = both(me.o == p, ok(me.z, p))
        for dx, dc in ((1, 0), (0, 1), (1, 1)):
            x = me.xo if dx else me.x
            c = me.co if dc else me.c
            cp.wait_recv(slots["f", p, dx, dc], quarter(x, c), me.dev(dx=dx, dc=dc), mine)

        @pl.when(mine)
        def _():
            pltpu.make_async_copy(final.at[p], quarter(me.x, me.c), local_sems.at[4]).wait()

    def tail_load():
        return pltpu.make_async_copy(
            partial.at[:, :, :, pl.ds(MAIN, TAIL)], tail, local_sems.at[5]
        )

    def tail_add(o, zb, yb, srcs):
        add_rows(tail.at[o, zb, yb], [tail.at[o, zb, yb]] + srcs, TAIL)

    def t0():
        tail_load().start()

    def t1():
        tail_load().wait()
        for h in (0, 1):
            s = slots["tc", h] = cp.slot()
            cp.send(s, tail.at[2 * h + me.co], tail_in.at[h], me.dev(dc=1))

    def t2():
        for h in (0, 1):
            cp.wait_recv(slots["tc", h], tail_in.at[h], me.dev(dc=1))

            def body(q, carry):
                tail_add(2 * h + me.c, q // 2, q % 2, [tail_in.at[h, q // 2, q % 2]])
                return carry
            lax.fori_loop(0, 8, body, 0)
        s = slots["tx"] = cp.slot()
        cp.send(s, tail.at[me.xo * 2 + me.c], tail_in.at[2], me.dev(dx=1))

    def t3():
        cp.wait_recv(slots["tx"], tail_in.at[2], me.dev(dx=1))

        def body(q, carry):
            tail_add(me.o, q // 2, q % 2, [tail_in.at[2, q // 2, q % 2]])
            return carry
        lax.fori_loop(0, 8, body, 0)
        s = slots["ty"] = cp.slot()
        cp.send(s, tail.at[me.o, :, me.yo], tail_in.at[3, :, 0], me.dev(dy=1))

    def t4():
        cp.wait_recv(slots["ty"], tail_in.at[3, :, 0], me.dev(dy=1))

        def body(q, carry):
            tail_add(me.o, q, me.y, [tail_in.at[3, q, 0]])
            return carry
        lax.fori_loop(0, 4, body, 0)
        for d in (1, 2, 3):
            s = slots["tz", d] = cp.slot()
            cp.send(s, tail.at[me.o, flip(me.z, d), me.y], tail_z.at[d - 1], me.dev(dz=d))

    def t5():
        for d in (1, 2, 3):
            cp.wait_recv(slots["tz", d], tail_z.at[d - 1], me.dev(dz=d))
        tail_add(me.o, me.z, me.y, [tail_z.at[0], tail_z.at[1], tail_z.at[2]])
        copy = pltpu.make_async_copy(
            tail.at[me.o, me.z, me.y], out.at[pl.ds(MAIN, TAIL)], local_sems.at[5]
        )
        copy.start()
        copy.wait()

    return dict(
        exchange=exchange, prefetch=prefetch, fold=fold, second=second, third=third,
        settle=settle, finish=finish, tails=(t0, t1, t2, t3, t4, t5),
    )


def scatter_scratch():
    bf = jnp.bfloat16
    return [
        pltpu.VMEM((RING, 2, 2, QUART, 8, D), bf),
        pltpu.VMEM((2, 2, QUART, 8, D), bf),
        pltpu.VMEM((RING, FIRST, 8, D), bf),
        pltpu.VMEM((RING, SECOND, 8, D), bf),
        pltpu.VMEM((RING, QUART, 8, D), bf),
        pltpu.VMEM((RING, QUART, 8, D), bf),
        pltpu.VMEM((3, 3, QUART, 8, D), bf),
        pltpu.VMEM((3, QUART, 8, D), bf),
        pltpu.VMEM((4, 4, 2, TAIL, 8, D), bf),
        pltpu.VMEM((4, 4, 2, TAIL, 8, D), bf),
        pltpu.VMEM((3, TAIL, 8, D), bf),
        pltpu.SemaphoreType.DMA((6,)),
        pltpu.SemaphoreType.REGULAR((2,)),
    ]


bf16 = jnp.bfloat16
MATS = D // 8
AT_PROJ = 3 * MATS
AT_UP = 4 * MATS
AT_DOWN = 8 * MATS
ROOT = math.sqrt(2.0 / math.pi)
CUBIC = 0.044715


def nn_dot(left, right):
    return lax.dot_general(left, right, (((1,), (0,)), ((), ())), preferred_element_type=f32)


def nt_dot(left, right):
    return lax.dot_general(left, right, (((1,), (1,)), ((), ())), preferred_element_type=f32)


def tn_dot(left, right):
    return lax.dot_general(left, right, (((0,), (0,)), ((), ())), preferred_element_type=f32)


def square(ref):
    return ref[...].reshape(D, D)


def norm_rows(values):
    centered = values - jnp.mean(values, axis=-1, keepdims=True)
    inverse = lax.rsqrt(jnp.mean(centered * centered, axis=-1, keepdims=True) + NORM_EPS)
    return centered * inverse, inverse


def norm_rows_back(grad, normed, inverse):
    return inverse * (
        grad
        - jnp.mean(grad, axis=-1, keepdims=True)
        - normed * jnp.mean(grad * normed, axis=-1, keepdims=True)
    )


def frames_of(c):
    return pl.ds(pl.multiple_of(c * FRAMES, FRAMES), FRAMES)


def over_columns(count, body):
    ways = math.gcd(count, 3)

    def step(run, carry):
        for n in range(ways):
            c = ways * run + n
            body(c, frames_of(c), pl.ds(c, 1))
        return carry

    lax.fori_loop(0, count // ways, step, 0)


def split_rows(src, spread, put, ways):
    units = src.shape[0] * 8
    rows = units // ways
    for q in range(9):
        lanes = slice(128 * q, 128 * q + 128)
        spread[q, pl.ds(0, units)] = src[:, :, lanes].astype(f32).reshape(units, 128)
        for w in range(ways):
            part = spread[q, pl.ds(w, rows, stride=ways), :]
            put(w, lanes, part.reshape(rows // 8, 8, 128).astype(bf16))


def head_window(h):
    first = min(HD * h // 128, 7) * 128
    lane = lax.broadcasted_iota(jnp.int32, (1, 256), 1) + first
    mask = jnp.logical_and(lane >= HD * h, lane < HD * h + HD)
    return slice(first, first + 256), jnp.where(mask, 1.0, 0.0).astype(bf16)


def same_column():
    row = lax.broadcasted_iota(jnp.int32, (128, 128), 0)
    col = lax.broadcasted_iota(jnp.int32, (128, 128), 1)
    return lax.shift_right_logical(row, 4) == lax.shift_right_logical(col, 4)


SCORE_SCALE = 1.0 / math.sqrt(HD)


def head_probabilities(masked_queries, keys, inside):
    scores = jnp.where(inside, nt_dot(masked_queries, keys) * SCORE_SCALE, -1e30)
    grown = jnp.exp(scores - jnp.max(scores, axis=-1, keepdims=True))
    return grown / jnp.sum(grown, axis=-1, keepdims=True)


SUM_COPIES = 6
SUM_SLOTS = 10


def sum_stages(me, cp, mine, buf):
    slots = {}

    def send(name, src, dst, device):
        slots[name] = cp.slot()
        cp.send(slots[name], src, dst, device)

    def m1():
        send("c", mine, buf.at[0], me.dev(dc=1))

    def m2():
        cp.wait_recv(slots["c"], buf.at[0], me.dev(dc=1))
        buf[1] = mine[...] + buf[0]
        send("x", buf.at[1], buf.at[2], me.dev(dx=1))

    def m3():
        cp.wait_recv(slots["x"], buf.at[2], me.dev(dx=1))
        buf[3] = buf[1] + buf[2]
        send("y", buf.at[3], buf.at[4], me.dev(dy=1))

    def m4():
        cp.wait_recv(slots["y"], buf.at[4], me.dev(dy=1))
        buf[5] = buf[3] + buf[4]
        buf[6 + me.z] = buf[5]
        for d in (1, 2, 3):
            send(d, buf.at[5], buf.at[6 + me.z], me.dev(dz=d))

    def total():
        for d in (1, 2, 3):
            cp.wait_recv(slots[d], buf.at[6 + flip(me.z, d)], me.dev(dz=d))
        return (buf[6] + buf[7]) + (buf[8] + buf[9])

    return m1, m2, m3, m4, total


CUBE_COPIES = 10
CUBE_SLOTS = 12
CUBE = tuple((dx, dc, dy) for dx in (0, 1) for dc in (0, 1) for dy in (0, 1))


def cube_stages(me, cp, mine, buf):
    slots = {}

    def at(dx, dc, dy):
        x = me.xo if dx else me.x
        c = me.co if dc else me.c
        y = me.yo if dy else me.y
        return buf.at[4 * x + 2 * c + y]

    def m1():
        for way in CUBE[1:]:
            slots[way] = cp.slot()
            cp.send(slots[way], mine, at(0, 0, 0), me.dev(way[0], way[1], 0, way[2]))
        at(0, 0, 0)[...] = mine[...]

    def m2():
        for way in CUBE[1:]:
            cp.wait_recv(slots[way], at(*way), me.dev(way[0], way[1], 0, way[2]))
        total = buf[0]
        for n in range(1, 8):
            total = total + buf[n]
        there = buf.at[8 + me.z]
        there[...] = total
        for d in (1, 2, 3):
            slots[d] = cp.slot()
            cp.send(slots[d], there, there, me.dev(dz=d))

    def total():
        for d in (1, 2, 3):
            cp.wait_recv(slots[d], buf.at[8 + flip(me.z, d)], me.dev(dz=d))
        return (buf[8] + buf[9]) + (buf[10] + buf[11])

    return m1, m2, total


def forward_body(
    weights, tokens, upstream, mods, b_qkv, b_proj, b_up, b_down,
    block_out, natural, input_att, proj_out, attended, branch, input_mlp, active_out, slope_out,
    grad_out, grad_gate, grads, held, spread, acc, hid, proj, active, slope, woven,
    copy_sems, ready,
):
    columns = mods.shape[1]

    lines = held.reshape(8 * MATS, 8, D)

    def fetch(first, groups, slot):
        return pltpu.make_async_copy(
            weights.at[pl.ds(first, groups)], lines.at[pl.ds(slot * MATS, groups)], copy_sems.at[0]
        )

    def whole(mat, slot):
        return pltpu.make_async_copy(
            weights.at[pl.ds(mat * MATS, MATS)], held.at[slot], copy_sems.at[2 + slot]
        )

    def save(mat, slot):
        return pltpu.make_async_copy(held.at[slot], natural.at[mat], copy_sems.at[10 + mat])

    def keep(src, dst, n):
        return pltpu.make_async_copy(src, dst, copy_sems.at[17 + n])

    def unweave(ways, source, slot0):
        def step(j, carry):
            def put(w, lanes, block):
                held[slot0 + w, pl.ds(j * 16, 16), :, lanes] = block

            groups = 16 * ways
            src = lines.at[pl.ds(source * MATS + j * groups, groups)]
            split_rows(src, spread, put, ways)
            return carry

        lax.fori_loop(0, 9, step, 0)

    def first_norm(c, rows, at):
        normed, _ = norm_rows(tokens[rows].astype(f32))
        input_att[rows] = (normed * (1.0 + mods[1, at]) + mods[0, at]).astype(bf16)

    over_columns(columns, first_norm)
    ready("qkv")
    fetch(0, 3 * MATS, 4).start()
    whole(3, 3).start()
    fetch(0, 3 * MATS, 4).wait()
    unweave(3, 4, 0)
    for p in range(3):
        save(p, p).start()

    for p in range(3):
        proj[p] = (nn_dot(input_att[...], square(held.at[p])) + b_qkv[pl.ds(p, 1)]).astype(bf16)
        ready("project", p)
    keep(proj, proj_out, 0).start()

    inside = same_column()

    def attend(g, carry):
        rows = pl.ds(pl.multiple_of(g * 128, 128), 128)
        acc[pl.ds(0, 128)] = jnp.zeros((128, D), f32)
        for h in range(H):
            window, mask = head_window(h)
            probs = head_probabilities(proj[0, rows, window] * mask, proj[1, rows, window], inside)
            acc[pl.ds(0, 128), window] += nn_dot(probs.astype(bf16), proj[2, rows, window] * mask)
        attended[rows] = acc[pl.ds(0, 128)].astype(bf16)
        return carry

    for g in range(columns * FRAMES // 128):
        lax.fori_loop(g, g + 1, attend, 0)
        ready("attend", g)
    ready("proj")
    whole(3, 3).wait()
    branch[...] = nn_dot(attended[...], square(held.at[3])) + b_proj[...]
    for p in range(3):
        save(p, p).wait()

    def second_norm(c, rows, at):
        middle = tokens[rows].astype(f32) + mods[2, at] * branch[rows]
        normed, _ = norm_rows(middle)
        input_mlp[rows] = (normed * (1.0 + mods[4, at]) + mods[3, at]).astype(bf16)
        grad_block = jnp.where(mods[6, at] > 0.5, upstream[rows].astype(f32), 0.0)
        grad_out[rows] = (grad_block * mods[5, at]).astype(bf16)

    over_columns(columns, second_norm)
    ready("up")
    fetch(AT_UP, 4 * MATS, 0).start()
    fetch(AT_UP, 4 * MATS, 0).wait()
    unweave(4, 0, 4)
    for b in range(4):
        save(3 + b, 4 + b).start()

    def raise_(b, carry):
        hid[...] = nn_dot(input_mlp[...], square(held.at[4 + b])) + b_up[pl.ds(b, 1)]

        def gelu(c, rows, at):
            v = hid[rows]
            sq = v * v
            t = jnp.tanh(ROOT * (v + CUBIC * sq * v))
            half = 0.5 * (1.0 + t)
            active[b, rows] = (v * half).astype(bf16)
            rise = half + (0.5 * ROOT) * v * (1.0 - t * t) * (1.0 + 3.0 * CUBIC * sq)
            for q in range(9):
                slope[b, q, rows] = rise[:, 128 * q : 128 * q + 128]

        over_columns(columns, gelu)
        return carry

    for b in range(4):
        lax.fori_loop(b, b + 1, raise_, 0)
        ready("raise", b)
    keep(active, active_out, 1).start()
    keep(slope, slope_out, 2).start()
    whole(8, 0).start()

    def stash(b, r):
        return pltpu.make_async_copy(
            woven.at[pl.ds(48 * r, 48)], grads.at[pl.ds(AT_DOWN + b * MATS + 48 * r, 48)],
            copy_sems.at[20 + r],
        )

    for b in range(4):
        for r in range(3):
            part = tn_dot(active[b, :, 384 * r : 384 * r + 384], grad_out[...])
            if b:
                stash(b - 1, r).wait()
            woven[pl.ds(48 * r, 48)] = part.reshape(48, 8, D).astype(bf16)
            stash(b, r).start()
        ready("outer", b)
    acc[...] = jnp.broadcast_to(b_down[...], acc.shape)
    whole(8, 0).wait()
    acc[...] += nn_dot(active[0], square(held.at[0]))
    ready("down")
    for b in range(1, 4):
        whole(8 + b, b).start()
    for b in range(1, 4):
        whole(8 + b, b).wait()
        acc[...] += nn_dot(active[b], square(held.at[b]))

    def last(c, rows, at):
        x = tokens[rows].astype(f32)
        middle = x + mods[2, at] * branch[rows]
        video = mods[6, at] > 0.5
        outcome = acc[rows]
        block_out[rows] = jnp.where(video, middle + mods[5, at] * outcome, x)
        grad_block = jnp.where(video, upstream[rows].astype(f32), 0.0)
        grad_gate[at] = jnp.sum(grad_block * outcome, axis=0, keepdims=True)

    over_columns(columns, last)
    for b in range(4):
        save(3 + b, 4 + b).wait()
    keep(proj, proj_out, 0).wait()
    keep(active, active_out, 1).wait()
    keep(slope, slope_out, 2).wait()
    for r in range(3):
        stash(3, r).wait()


def forward_kernel(*refs):
    forward_body(*refs, lambda name, step=0: None)


def gather_forward_kernel(
    flat_shard, selector, chosen, base, tokens, upstream, b_qkv, b_proj, b_up, b_down,
    full, mods, shard, *refs,
):
    refs, (partial, sums, send_sems, recv_sems, local_sems) = refs[:-5], refs[-5:]
    lines = refs[-3].reshape(4 * 9 * tokens.shape[0], 128)
    arrival = pltpu.make_async_copy(
        flat_shard, lines.at[pl.ds(0, 9 * UNITS)], local_sems.at[1]
    )
    arrival.start()
    me = Place()
    cp = Copies(send_sems, recv_sems)
    me.greet()
    arrival.wait()

    def regroup(run, carry):
        for j in range(3):
            for q in range(9):
                part = lines[pl.ds(216 * run + 72 * j + q, 8, stride=9), :]
                shard[3 * run + j, :, 128 * q : 128 * q + 128] = part.astype(bf16)
        return carry

    lax.fori_loop(0, GROUPS8 // 3, regroup, 0)
    partial[...] = nn_dot(selector[...], shard[...].reshape(UNITS, D))
    st = gather_stages(me, cp, shard, full, local_sems)
    s0, s1, s2, s3, s4, s5 = (st["s%d" % n] for n in range(6))
    t1, t2, t3, t4, t5 = (st["t%d" % n] for n in range(1, 6))
    m1, m2, m3, m4, total = sum_stages(me, cp, partial, sums)
    s0(0)
    m1()
    s0(1)
    s0(2)
    s1(0)
    m2()
    s1(1)
    m3()
    t1()
    s2(0)
    m4()
    t2()
    s1(2)
    s3(0)
    t3()
    s2(1)
    t4()
    table = picked(chosen[...], total()) + base[...]
    columns = mods.shape[1]
    for n in range(7):
        mods[n] = table[n * columns : (n + 1) * columns]

    def ready(name, step=0):
        if name == "qkv":
            s4(0)
            t5()
            s5(0)
        elif name == "project":
            s3(1, (step,))
        elif name == "attend":
            if step == 0:
                s3(1, (3,))
            elif step == 1:
                s2(2)
            else:
                s4(1)
        elif name == "up":
            s5(1)
        elif name == "raise":
            s3(2, (step,))
        elif name == "down":
            s4(2)
            s5(2)

    forward_body(
        full.reshape(4 * 4 * 2 * GROUPS8, 8, D), tokens, upstream, mods, b_qkv, b_proj, b_up,
        b_down, *refs, ready,
    )
    cp.drain()


def forward_shapes(rows, columns):
    shape = jax.ShapeDtypeStruct
    return [
        shape((rows, D), f32),
        shape((7, MATS, 8, D), bf16),
        shape((rows, D), bf16),
        shape((3, rows, D), bf16),
        shape((rows, D), bf16),
        shape((rows, D), f32),
        shape((rows, D), bf16),
        shape((4, rows, D), bf16),
        shape((4, 9, rows, 128), f32),
        shape((rows, D), bf16),
        shape((columns, D), f32),
        shape((32 * UNITS // 8, 8, D), bf16),
    ]


VMEM_SPEC = pl.BlockSpec(memory_space=pltpu.VMEM)
HBM_SPEC = pl.BlockSpec(memory_space=pl.ANY)
FORWARD_SPECS = [
    VMEM_SPEC, HBM_SPEC, VMEM_SPEC, HBM_SPEC, VMEM_SPEC, VMEM_SPEC, VMEM_SPEC, HBM_SPEC, HBM_SPEC,
    VMEM_SPEC, VMEM_SPEC, HBM_SPEC,
]


def forward_scratch(rows):
    return [
        pltpu.VMEM((8, MATS, 8, D), bf16),
        pltpu.VMEM((9, 512, 128), f32),
        pltpu.VMEM((rows, D), f32),
        pltpu.VMEM((rows, D), f32),
        pltpu.VMEM((3, rows, D), bf16),
        pltpu.VMEM((4, rows, D), bf16),
        pltpu.VMEM((4, 9, rows, 128), f32),
        pltpu.VMEM((MATS, 8, D), bf16),
        pltpu.SemaphoreType.DMA((23,)),
    ]


def forward(weights, tokens, upstream, mods, b_qkv, b_proj, b_up, b_down):
    rows = tokens.shape[0]
    return pl.pallas_call(
        forward_kernel,
        out_shape=forward_shapes(rows, mods.shape[1]),
        in_specs=[HBM_SPEC] + [VMEM_SPEC] * 7,
        out_specs=FORWARD_SPECS,
        scratch_shapes=forward_scratch(rows),
        compiler_params=pltpu.CompilerParams(vmem_limit_bytes=62 * 2**20),
        name="block_forward",
    )(weights, tokens, upstream, mods, b_qkv, b_proj, b_up, b_down)


def gather_forward(
    flat_shard, selector, chosen, base, tokens, upstream, b_qkv, b_proj, b_up, b_down
):
    rows = tokens.shape[0]
    columns = rows // FRAMES
    copies = GATHER_COPIES + SUM_COPIES
    return pl.pallas_call(
        gather_forward_kernel,
        out_shape=[
            jax.ShapeDtypeStruct((4, 4, 2, GROUPS8, 8, D), bf16),
            jax.ShapeDtypeStruct((7, columns, D), f32),
            jax.ShapeDtypeStruct((GROUPS8, 8, D), bf16),
        ]
        + forward_shapes(rows, columns),
        in_specs=[HBM_SPEC] + [VMEM_SPEC] * 9,
        out_specs=[HBM_SPEC, VMEM_SPEC, VMEM_SPEC] + FORWARD_SPECS,
        scratch_shapes=forward_scratch(rows)
        + [
            pltpu.VMEM((selector.shape[0], D), f32),
            pltpu.VMEM((SUM_SLOTS, selector.shape[0], D), f32),
            pltpu.SemaphoreType.DMA((copies,)),
            pltpu.SemaphoreType.DMA((copies,)),
            pltpu.SemaphoreType.DMA((2,)),
        ],
        compiler_params=pltpu.CompilerParams(
            collective_id=0, has_side_effects=True, vmem_limit_bytes=63 * 2**20
        ),
        name="gather_forward",
    )(flat_shard, selector, chosen, base, tokens, upstream, b_qkv, b_proj, b_up, b_down)


UP_RUNS = ((0, 256), (256, 256), (512, 256), (768, 256), (1024, 128))
QKV_RUNS = ((0, 384), (384, 384), (768, 384))


def backward_body(
    weights, natural, slope, tokens, upstream, mods, input_att, proj, attended, branch,
    input_mlp, grad_out,
    grads, input_grad, grad_mods, bias_sums,
    held, woven, spread, grad_hidden, grad_branch, grad_att, acc, copy_sems, tick,
):
    columns = mods.shape[1]
    row_count = columns * FRAMES

    def fetch(first, slot):
        return pltpu.make_async_copy(natural.at[first], held.at[slot], copy_sems.at[slot])

    def flat_mat(first, slot):
        return pltpu.make_async_copy(
            weights.at[pl.ds(first, MATS)], held.at[slot], copy_sems.at[slot]
        )

    def stream(b, slot):
        at = pl.ds(pl.multiple_of(slot * row_count, row_count), row_count)
        return (
            flat_mat(AT_DOWN + b * MATS, slot),
            pltpu.make_async_copy(slope.at[b], spread.at[:, at], copy_sems.at[4 + slot]),
        )

    def store(first, offset, groups, n):
        return pltpu.make_async_copy(
            woven.at[pl.ds(offset, groups)], grads.at[pl.ds(first, groups)], copy_sems.at[6 + n]
        )

    bias_sums[...] = jnp.zeros_like(bias_sums)

    def add_bias(row, values):
        bias_sums[pl.ds(row, 1)] += jnp.sum(values.astype(f32), axis=0, keepdims=True)

    def outer(first, left, right):
        for r in range(3):
            part = tn_dot(left[:, 384 * r : 384 * r + 384], right[...])
            woven[pl.ds(48 * r, 48)] = part.reshape(48, 8, D).astype(bf16)
            store(first + 48 * r, 48 * r, 48, r).start()

    for copy in stream(0, 0):
        copy.start()

    def down(b, carry):
        slot = lax.rem(b, 2)
        for copy in stream(b, slot):
            copy.wait()

        @pl.when(b < 3)
        def _():
            for copy in stream(b + 1, 1 - slot):
                copy.start()

        acc[...] = nt_dot(grad_out[...], square(held.at[slot]))

        def through(c, rows, at):
            there = pl.ds(pl.multiple_of(slot * row_count + c * FRAMES, FRAMES), FRAMES)
            rise = jnp.concatenate([spread[q, there] for q in range(9)], axis=1)
            grad = (acc[rows] * rise).astype(bf16)
            grad_hidden[b, rows] = grad
            add_bias(5 + b, grad)

        over_columns(columns, through)
        return carry

    tick("begin")
    for b in range(4):
        lax.fori_loop(b, b + 1, down, 0)
        tick("down", b)
    fetch(3, 0).start()

    def down_bias(c, rows, at):
        add_bias(4, grad_out[rows])

    over_columns(columns, down_bias)

    def weave(first, ways, left, right, runs, name):
        before = None
        for k, (start, count) in enumerate(runs):
            for w in range(ways):
                part = tn_dot(left[:, start : start + count], right[w])
                for q in range(9):
                    spread[q, pl.ds(w, count, stride=ways), :] = part[:, 128 * q : 128 * q + 128]
            if before is not None:
                before.wait()

            def pack(j, carry):
                for q in range(9):
                    lines = spread[q, pl.ds(pl.multiple_of(j * 128, 128), 128), :]
                    woven[pl.ds(j * 16, 16), :, 128 * q : 128 * q + 128] = lines.reshape(
                        16, 8, 128
                    ).astype(bf16)
                return carry

            groups = count * ways // 8
            lax.fori_loop(0, groups // 16, pack, 0)
            before = store(first + start * ways // 8, 0, groups, 0)
            before.start()
            tick(name, k)
        before.wait()

    weave(AT_UP, 4, input_mlp, grad_hidden, UP_RUNS, "up run")
    tick("up")
    acc[...] = jnp.zeros_like(acc)
    for b in range(4):
        fetch(3 + b, b % 2).wait()
        if b < 3:
            fetch(4 + b, 1 - b % 2).start()
        acc[...] += nt_dot(grad_hidden[b], square(held.at[b % 2]))
        tick("up input", b)
    flat_mat(AT_PROJ, 0).start()

    def second_norm_back(c, rows, at):
        br = branch[rows]
        gate = mods[2, at]
        normed, inverse = norm_rows(tokens[rows].astype(f32) + gate * br)
        grad = acc[rows]
        grad_mods[3, at] = jnp.sum(grad, axis=0, keepdims=True)
        grad_mods[4, at] = jnp.sum(grad * normed, axis=0, keepdims=True)
        grad_block = jnp.where(mods[6, at] > 0.5, upstream[rows].astype(f32), 0.0)
        grad_middle = grad_block + norm_rows_back(grad * (1.0 + mods[4, at]), normed, inverse)
        input_grad[rows] = grad_middle
        grad_mods[2, at] = jnp.sum(grad_middle * br, axis=0, keepdims=True)
        grad = (grad_middle * gate).astype(bf16)
        grad_branch[rows] = grad
        add_bias(3, grad)

    over_columns(columns, second_norm_back)
    tick("norm")
    outer(AT_PROJ, attended, grad_branch)
    flat_mat(AT_PROJ, 0).wait()
    grad_att[...] = nt_dot(grad_branch[...], square(held.at[0])).astype(bf16)
    fetch(0, 0).start()
    for r in range(3):
        store(AT_PROJ + 48 * r, 48 * r, 48, r).wait()
    tick("proj")
    inside = same_column()

    def attend_back(g, carry):
        rows = pl.ds(pl.multiple_of(g * 128, 128), 128)
        for p in range(3):
            acc[pl.ds(p * 128, 128)] = jnp.zeros((128, D), f32)
        for h in range(H):
            window, mask = head_window(h)
            queries = proj[0, rows, window] * mask
            keys = proj[1, rows, window]
            grad = grad_att[rows, window] * mask
            probs = head_probabilities(queries, keys, inside)
            grad_probs = nt_dot(grad, proj[2, rows, window])
            mean = jnp.sum(grad_probs * probs, axis=-1, keepdims=True)
            grad_scores = (probs * (grad_probs - mean)).astype(bf16)
            acc[pl.ds(0, 128), window] += nn_dot(grad_scores, keys * mask)
            acc[pl.ds(128, 128), window] += tn_dot(grad_scores, queries)
            acc[pl.ds(256, 128), window] += tn_dot(probs.astype(bf16), grad)
        for p in range(3):
            scale = SCORE_SCALE if p < 2 else 1.0
            grad = (acc[pl.ds(p * 128, 128)] * scale).astype(bf16)
            grad_hidden[p, rows] = grad
            add_bias(p, grad)
        return carry

    for g in range(row_count // 128):
        lax.fori_loop(g, g + 1, attend_back, 0)
        tick("attend", g)
    weave(0, 3, input_att, grad_hidden, QKV_RUNS, "qkv run")
    tick("qkv")
    acc[...] = jnp.zeros_like(acc)
    for p in range(3):
        fetch(p, p % 2).wait()
        if p < 2:
            fetch(p + 1, 1 - p % 2).start()
        acc[...] += nt_dot(grad_hidden[p], square(held.at[p % 2]))
        tick("qkv input", p)

    def first_norm_back(c, rows, at):
        normed, inverse = norm_rows(tokens[rows].astype(f32))
        grad = acc[rows]
        grad_mods[0, at] = jnp.sum(grad, axis=0, keepdims=True)
        grad_mods[1, at] = jnp.sum(grad * normed, axis=0, keepdims=True)
        grad_states = input_grad[rows] + norm_rows_back(
            grad * (1.0 + mods[1, at]), normed, inverse
        )
        up_rows = upstream[rows].astype(f32)
        input_grad[rows] = jnp.where(mods[6, at] > 0.5, grad_states, up_rows)

    over_columns(columns, first_norm_back)
    tick("end")


def backward_kernel(given, *refs):
    backward_body(*refs, lambda name, step=0: None)


def backward_scatter_kernel(*refs):
    (
        given, weights, natural, slope, tokens, upstream, mods, input_att, proj, attended, branch,
        input_mlp, grad_out, grad_gate, member,
        out, grads, other, input_grad, total_small,
        grad_mods, bias_sums, held, woven, spread, grad_hidden, grad_branch, grad_att, acc, copy_sems,
        own, stage, rx2, ry2, rx1, ry1, rz, final, tail, tail_in, tail_z, local_sems, credit,
        small, sums, send_sems, recv_sems,
    ) = refs
    me = Place()
    cp = Copies(send_sems, recv_sems)
    me.greet()
    st = scatter_stages(
        me, cp, grads, out, other, own, stage, rx2, ry2, rx1, ry1, rz, final, tail, tail_in,
        tail_z, local_sems, credit,
    )
    t0, t1, t2, t3, t4, t5 = st["tails"]
    m1, m2, m3, m4, total = sum_stages(me, cp, small, sums)
    groups = member.shape[0]

    def run(steps):
        acts = dict(
            E=st["exchange"], P=st["prefetch"], A=st["fold"], B=st["second"], C=st["third"],
            S=st["settle"],
        )
        for step in steps.split():
            acts[step[0]](int(step[1:]))

    turns = {
        ("begin", 0): "E2 P0",
        ("down", 0): "A0 P1",
        ("down", 2): "A1 P2 B0",
        ("up run", 0): "A2 P3 B1 C0",
        ("up run", 3): "A3 B2 C1",
        ("up", 0): "E1 P4",
        ("up input", 0): "A4 P5 B3 C2",
        ("norm", 0): "A5 P6 B4 C3",
        ("proj", 0): "S2",
        ("attend", 0): "A6 P7 B5 C4",
        ("attend", 1): "A7 B6 C5",
        ("attend", 2): "B7 C6",
        ("qkv", 0): "E0 P8",
        ("qkv input", 0): "A8 P9",
        ("qkv input", 2): "A10 P11 B9 C8",
        ("qkv input", 1): "A9 P10 B8 C7",
    }

    def tick(name, step=0):
        run(turns.get((name, step), ""))
        if (name, step) == ("qkv", 0):
            t0()
        if (name, step) == ("qkv input", 0):
            t1()
        if (name, step) == ("qkv input", 2):
            t2()
        if name == "end":
            for n in range(6):
                plane = grad_mods[n] if n < 5 else grad_gate[...]
                small[pl.ds(n * groups, groups)] = picked(member[...], plane)
            small[pl.ds(6 * groups, 9)] = bias_sums[pl.ds(0, 9)]
            small[pl.ds(6 * groups + 9, small.shape[0] - 6 * groups - 9)] = jnp.zeros(
                (small.shape[0] - 6 * groups - 9, D), f32
            )
            m1()
            run("A11 B10 C9 S1")
            t3()
            m2()
            run("B11 C10 C11 S0")
            t4()
            m3()
            t5()
            m4()
            run("")
            total_small[...] = total()
            for p in (2, 1, 0):
                st["finish"](p)
            cp.drain()

    backward_body(
        weights, natural, slope, tokens, upstream, mods, input_att, proj, attended, branch,
        input_mlp, grad_out,
        grads.reshape(4 * 4 * 2 * GROUPS8, 8, D), input_grad, grad_mods, bias_sums,
        held, woven, spread, grad_hidden, grad_branch, grad_att, acc, copy_sems,
        tick,
    )


def backward_shapes(rows, columns):
    shape = jax.ShapeDtypeStruct
    return [
        shape((rows, D), f32),
        shape((5, columns, D), f32),
        shape((16, D), f32),
    ]


def backward_scratch(rows):
    return [
        pltpu.VMEM((2, MATS, 8, D), bf16),
        pltpu.VMEM((MATS, 8, D), bf16),
        pltpu.VMEM((9, D, 128), f32),
        pltpu.VMEM((4, rows, D), bf16),
        pltpu.VMEM((rows, D), bf16),
        pltpu.VMEM((rows, D), bf16),
        pltpu.VMEM((rows, D), f32),
        pltpu.SemaphoreType.DMA((9,)),
    ]


def backward(*operands):
    rows, columns = operands[4].shape[0], operands[6].shape[1]
    return pl.pallas_call(
        backward_kernel,
        out_shape=[jax.ShapeDtypeStruct((32 * UNITS // 8, 8, D), bf16)]
        + backward_shapes(rows, columns),
        in_specs=[HBM_SPEC] * 4 + [VMEM_SPEC] * 9,
        out_specs=[HBM_SPEC] + [VMEM_SPEC] * 3,
        input_output_aliases={0: 0},
        scratch_shapes=backward_scratch(rows),
        compiler_params=pltpu.CompilerParams(vmem_limit_bytes=62 * 2**20),
        name="block_backward",
    )(*operands)


def backward_scatter(operands, grad_gate, member):
    rows, columns = operands[4].shape[0], operands[6].shape[1]
    small = small_rows(member.shape[0])
    copies = SCATTER_COPIES + SUM_COPIES
    shape = jax.ShapeDtypeStruct
    input_grad, grad_mods, bias_sums = backward_shapes(rows, columns)
    return pl.pallas_call(
        backward_scatter_kernel,
        out_shape=[
            shape((GROUPS8, 8, D), bf16),
            shape((4, 4, 2, GROUPS8, 8, D), bf16),
            shape((3, 4, 2, 2, QUART, 8, D), bf16),
            input_grad,
            shape((small, D), f32),
        ],
        in_specs=[HBM_SPEC] * 4 + [VMEM_SPEC] * 11,
        out_specs=[HBM_SPEC] * 3 + [VMEM_SPEC] * 2,
        input_output_aliases={0: 1},
        scratch_shapes=[
            pltpu.VMEM(grad_mods.shape, f32),
            pltpu.VMEM(bias_sums.shape, f32),
        ]
        + backward_scratch(rows)
        + scatter_scratch()
        + [
            pltpu.VMEM((small, D), f32),
            pltpu.VMEM((SUM_SLOTS, small, D), f32),
            pltpu.SemaphoreType.DMA((copies,)),
            pltpu.SemaphoreType.DMA((copies,)),
        ],
        compiler_params=pltpu.CompilerParams(
            collective_id=1, has_side_effects=True, vmem_limit_bytes=63 * 2**20
        ),
        name="backward_scatter",
    )(*operands, grad_gate, member)


def small_rows(groups):
    return -(-(6 * groups + 9) // 8) * 8


def adamw_rows(value, grad, first, second):
    first_new = BETA_FIRST * first + (1.0 - BETA_FIRST) * grad
    second_new = BETA_SECOND * second + (1.0 - BETA_SECOND) * grad * grad
    first_hat = first_new * (1.0 / (1.0 - BETA_FIRST**STEP))
    second_hat = second_new * (1.0 / (1.0 - BETA_SECOND**STEP))
    step = first_hat / (jnp.sqrt(second_hat) + ADAM_EPS) + WEIGHT_DECAY * value
    return value - LEARN_RATE * step, first_new, second_new


def norm_kernel(
    shard_sum, low, small, selector, parts_t, row_of, in_ada, cond,
    cond_grad, norm_out, flat, bias_flat,
    ada, mine, own_cond, sums, cond_sums, send_sems, recv_sems,
):
    groups = cond.shape[0]
    me = Place()
    cp = Copies(send_sems, recv_sems)
    me.greet()
    m1, m2, total = cube_stages(me, cp, mine, sums)
    n1, n2, cond_total = cube_stages(me, cp, own_cond, cond_sums)
    parts = small[pl.ds(0, 6 * groups)]
    ada[...] = picked(selector[...], parts)

    def spread_group(run, square):
        for n in range(3):
            j = 3 * run + n
            rows = pl.ds(pl.multiple_of(j * 8, 8), 8)
            grad = jnp.where(in_ada[rows] > 0.5, ada[rows], shard_sum[j].astype(f32))
            for q in range(9):
                flat[pl.ds(72 * j + q, 8, stride=9), :] = grad[:, 128 * q : 128 * q + 128]
            square = square + grad * grad
        return square

    square = lax.fori_loop(0, GROUPS8 // 3, spread_group, jnp.zeros((8, D), f32))
    lanes = square[:, :128]
    for q in range(1, 9):
        lanes = lanes + square[:, 128 * q : 128 * q + 128]
    mine[...] = lanes
    m1()
    rows = 6 * groups
    products = nt_dot(jnp.concatenate(three_parts(parts), axis=0), low[...].reshape(UNITS, D))
    products = products[:rows] + products[rows : 2 * rows] + products[2 * rows :]
    products = products * parts_t[...]
    folded = products[:groups]
    for n in range(1, 6):
        folded = folded + products[n * groups : (n + 1) * groups]
    lane = lax.broadcasted_iota(jnp.int32, (UNITS, 128), 1)
    own_cond[...] = jnp.zeros_like(own_cond)
    folded = jnp.concatenate(three_parts(folded), axis=0)
    for q in range(9):
        hit = jnp.where(row_of[...] == lane + 128 * q, 1.0, 0.0).astype(bf16)
        there = nn_dot(folded, hit)
        there = there[:groups] + there[groups : 2 * groups] + there[2 * groups :]
        own_cond[pl.ds(0, groups), 128 * q : 128 * q + 128] = there
    n1()
    m2()
    bias_rows = [small[pl.ds(6 * groups + n, 1)] for n in (0, 2, 3, 5, 6, 7, 8, 4)]
    for n in range(6):
        bias_rows.append(jnp.sum(small[pl.ds(n * groups, groups)], axis=0, keepdims=True))
    for t, line in enumerate(bias_rows):
        for q in range(9):
            bias_flat[pl.ds(9 * t + q, 1)] = line[:, 128 * q : 128 * q + 128]
    bias_square = jnp.sum(bias_flat[...] * bias_flat[...], axis=0, keepdims=True)
    n2()
    squares = jnp.sum(total(), axis=0, keepdims=True) + bias_square
    norm_out[...] = jnp.sqrt(jnp.sum(squares, axis=1, keepdims=True))
    summed = cond_total()
    c = cond[...]
    gate = 1.0 / (1.0 + jnp.exp(-c))
    cond_grad[...] = summed[:groups] * (gate * (1.0 + c * (1.0 - gate)))
    cp.drain()


def norm_exchange(*operands):
    cond = operands[7]
    shape = jax.ShapeDtypeStruct
    payload = 8 * (cond.shape[0] // 8 + 1)
    return pl.pallas_call(
        norm_kernel,
        out_shape=[
            shape(cond.shape, f32), shape((1, 1), f32), shape((9 * UNITS, 128), f32),
            shape((BIAS_LINES, 128), f32),
        ],
        in_specs=[VMEM_SPEC] * len(operands),
        out_specs=[VMEM_SPEC] * 4,
        scratch_shapes=[
            pltpu.VMEM((UNITS, D), f32),
            pltpu.VMEM((8, 128), f32),
            pltpu.VMEM((payload, D), f32),
            pltpu.VMEM((CUBE_SLOTS, 8, 128), f32),
            pltpu.VMEM((CUBE_SLOTS, payload, D), f32),
            pltpu.SemaphoreType.DMA((2 * CUBE_COPIES,)),
            pltpu.SemaphoreType.DMA((2 * CUBE_COPIES,)),
        ],
        compiler_params=pltpu.CompilerParams(
            collective_id=2, has_side_effects=True, vmem_limit_bytes=24 * 2**20
        ),
        name="norm_exchange",
    )(*operands)


BIAS_LINES = 126


def adamw_kernel(
    norm, flat, weights, first, second, bias_flat, biases, bias_first, bias_second, block_in,
    grad_in,
    new_weights, first_out, second_out, new_biases, bias_first_out, bias_second_out, block_out,
    grad_out,
    stage, sems,
):
    passed = (
        pltpu.make_async_copy(block_in, block_out, sems.at[0]),
        pltpu.make_async_copy(grad_in, grad_out, sems.at[1]),
    )
    for copy in passed:
        copy.start()
    factor = jnp.minimum(1.0, CLIP_NORM / (norm[...] + 1e-06))
    results = (new_weights, first_out, second_out)
    run = 648
    count = flat.shape[0] // run

    def away(n, j):
        at = pl.ds(j * run, run)
        return pltpu.make_async_copy(stage.at[n, at], results[n].at[at], sems.at[2 + 3 * j + n])

    for j in range(count):

        def update(i, carry):
            at = pl.ds(pl.multiple_of(j * run + i * 216, 8), 216)
            stage[0, at], stage[1, at], stage[2, at] = adamw_rows(
                weights[at], flat[at] * factor, first[at], second[at]
            )
            return carry

        lax.fori_loop(0, run // 216, update, 0)
        for n in range(3):
            away(n, j).start()
    new_biases[...], bias_first_out[...], bias_second_out[...] = adamw_rows(
        biases[...], bias_flat[...] * factor, bias_first[...], bias_second[...]
    )
    for j in range(count):
        for n in range(3):
            away(n, j).wait()
    for copy in passed:
        copy.wait()


def adamw_update(norm, flat, state, bias_flat, bias_state, block_in, grad_in):
    shape = jax.ShapeDtypeStruct
    like = [shape(flat.shape, f32)] * 3 + [shape((BIAS_LINES, 128), f32)] * 3
    return pl.pallas_call(
        adamw_kernel,
        out_shape=like + [shape(block_in.shape, f32), shape(grad_in.shape, f32)],
        in_specs=[VMEM_SPEC] * 11,
        out_specs=[HBM_SPEC] * 3 + [VMEM_SPEC] * 3 + [HBM_SPEC] * 2,
        scratch_shapes=[pltpu.VMEM((3, *flat.shape), f32), pltpu.SemaphoreType.DMA((29,))],
        compiler_params=pltpu.CompilerParams(vmem_limit_bytes=40 * 2**20),
        name="adamw",
    )(norm, flat, *state, bias_flat, *bias_state, block_in, grad_in)


def gather_blocks(shard_low):
    whole = lax.all_gather(shard_low, ("outer", "inner"), axis=0, tiled=True)
    return whole.reshape(-1, 8, D)


def scatter_blocks(grads, units):
    axes = ("outer", "inner")
    whole = grads.reshape(-1, D)[: lax.axis_size(axes) * units].astype(f32)
    return lax.psum_scatter(whole, axes, scatter_dimension=0, tiled=True)


def split_bias(vector):
    widths = [D, D, D, FF, D, 6 * D]
    pieces = []
    offset = 0
    for span_width in widths:
        pieces.append(lax.slice_in_dim(vector, offset, offset + span_width))
        offset = offset + span_width
    return pieces


def exact(left, right, dims):
    return lax.dot_general(
        left, right, dims, precision=lax.Precision.HIGHEST, preferred_element_type=jnp.float32
    )


def three_parts(values):
    high = values.astype(bf16)
    rest = values - high.astype(f32)
    middle = rest.astype(bf16)
    low_part = (rest - middle.astype(f32)).astype(bf16)
    return high, middle, low_part


def picked(choice, values):
    high, middle, low_part = three_parts(values)
    choice = choice.astype(bf16)
    return nn_dot(
        jnp.concatenate([choice] * 3, axis=1), jnp.concatenate([high, middle, low_part], axis=0)
    )


def ada_selector(soft_cond, first_unit, units):
    groups = soft_cond.shape[0]
    spread = jnp.repeat(soft_cond.astype(jnp.float32), 6, axis=1)
    spread = jnp.pad(spread, ((0, 0), (units, units)))
    start = jnp.clip(first_unit - BLOCK_UNITS + units, 0, 6 * D + units)
    local = lax.dynamic_slice(spread, (jnp.int32(0), start), (groups, units))
    unit = first_unit - BLOCK_UNITS + jnp.arange(units, dtype=jnp.int32)
    part = (unit[:, None] % 6 == jnp.arange(6, dtype=jnp.int32)[None, :]) & (unit[:, None] >= 0)
    part = part.astype(jnp.float32)
    selector = local.T[:, :, None] * part[:, None, :]
    return selector.reshape(units, groups * 6), part


def adamw(parameter, gradient, first_state, second_state):
    first_new = BETA_FIRST * first_state + (1.0 - BETA_FIRST) * gradient
    second_new = BETA_SECOND * second_state + (1.0 - BETA_SECOND) * gradient * gradient
    first_hat = first_new / (1.0 - BETA_FIRST**STEP)
    second_hat = second_new / (1.0 - BETA_SECOND**STEP)
    updated = parameter - LEARN_RATE * (
        first_hat / (jnp.sqrt(second_hat) + ADAM_EPS) + WEIGHT_DECAY * parameter
    )
    return (updated, first_new, second_new)


def with_kernels(
    tokens, conditioning, output_grad, state, bias_state, first_unit, selector, ada_part,
    membership, video_plane, b_ada, bias_args,
):
    columns, groups = membership.shape
    units = UNITS
    eye = jnp.eye(6, dtype=f32)
    chosen = membership[None, :, None, :] * eye[:, None, :, None]
    chosen = jnp.pad(chosen.reshape(6 * columns, 6 * groups), ((0, columns), (0, 0)))
    base = jnp.repeat(b_ada.reshape(6, D), columns, axis=0)
    base = jnp.concatenate([base, video_plane])
    by_part = selector.reshape(units, groups, 6).transpose(0, 2, 1).reshape(units, 6 * groups)
    state = [part.reshape(9 * units, 128) for part in state]
    (
        flat, mods, shard_low, block_out, natural, input_att, proj, attended, branch, input_mlp, _,
        slope, grad_out, grad_gate, grads,
    ) = gather_forward(
        state[0], by_part.T.astype(bf16), chosen, base, tokens, output_grad, *bias_args
    )
    flat = flat.reshape(-1, 8, D)
    shard_sum, _, _, input_grad, small = backward_scatter(
        (
            grads.reshape(4, 4, 2, GROUPS8, 8, D), flat, natural, slope, tokens, output_grad, mods,
            input_att, proj, attended, branch, input_mlp, grad_out,
        ),
        grad_gate, membership.T,
    )
    unit = first_unit - BLOCK_UNITS + jnp.arange(units, dtype=jnp.int32)
    row_of = jnp.where(unit >= 0, unit // 6, -1)[:, None]
    parts_t = jnp.repeat(ada_part.T, groups, axis=0)
    in_ada = (unit >= 0).astype(f32)[:, None]
    cond_grad, norm, flat_grad, bias_flat = norm_exchange(
        shard_sum, shard_low, small, by_part, parts_t, row_of, in_ada, conditioning
    )
    *updated, block_out, input_grad = adamw_update(
        norm, flat_grad, state, bias_flat, [part.reshape(-1, 128) for part in bias_state],
        block_out, input_grad,
    )
    return (block_out, input_grad, cond_grad, norm[0, 0], *[part.reshape(-1) for part in updated])


def on_device(
    tokens,
    conditioning,
    column_sample,
    is_image,
    output_grad,
    weights,
    first_moment,
    second_moment,
    biases,
    bias_first,
    bias_second,
    kernels,
):
    columns = column_sample.shape[0]
    groups = conditioning.shape[0]
    units = weights.shape[0] // D
    axes = ("outer", "inner")
    first_unit = lax.axis_index(axes).astype(jnp.int32) * units
    b_query, b_value, b_proj, b_up, b_down, b_ada = split_bias(biases)
    soft_cond = jax.nn.silu(conditioning).astype(bf16)
    selector, ada_part = ada_selector(soft_cond, first_unit, units)
    membership = (column_sample[:, None] == jnp.arange(groups, dtype=jnp.int32)[None, :]).astype(
        f32
    )
    video_cols = exact(membership, 1.0 - is_image.astype(f32)[:, None], (((1,), (0,)), ((), ())))
    b_qkv = jnp.stack([b_query, jnp.zeros((D,), f32), b_value])
    bias_args = (b_qkv, b_proj[None], b_up.reshape(4, D), b_down[None])
    video_plane = jnp.broadcast_to(video_cols, (columns, D))
    if kernels:
        return with_kernels(
            tokens, conditioning, output_grad, (weights, first_moment, second_moment),
            (biases, bias_first, bias_second), first_unit, selector, ada_part, membership,
            video_plane, b_ada, bias_args,
        )
    shard_low = weights.reshape(units, D).astype(bf16)
    flat = gather_blocks(shard_low)
    mods_all = lax.psum(tn_dot(selector.astype(bf16), shard_low), axes)
    mods_all = mods_all.reshape(groups, 6 * D) + b_ada
    mods = jnp.take(mods_all, column_sample, axis=0).reshape(columns, 6, D).transpose(1, 0, 2)
    mods = jnp.concatenate([mods, video_plane[None]])
    (
        block_out, natural, input_att, proj, attended, branch, input_mlp, _, slope, grad_out,
        grad_gate, grads,
    ) = forward(flat, tokens, output_grad, mods, *bias_args)
    grads, input_grad, grad_mods, bias_sums = backward(
        grads, flat, natural, slope, tokens, output_grad, mods, input_att, proj, attended, branch,
        input_mlp, grad_out,
    )
    grad_mods = jnp.concatenate([grad_mods, grad_gate[None]])
    mods_local = exact(membership, grad_mods, (((0,), (1,)), ((), ())))
    bias_sums, grad_mods_all = lax.psum((bias_sums, mods_local.transpose(1, 0, 2)), axes)
    block_shard = scatter_blocks(grads, units)
    grad_mods_all = grad_mods_all.transpose(1, 0, 2).reshape(groups, 6 * D)
    bias_head = jnp.concatenate([bias_sums[:1], bias_sums[2:4], bias_sums[5:9], bias_sums[4:5]])
    first_sum = jnp.concatenate([bias_head.reshape(-1), jnp.sum(grad_mods_all, axis=0)])
    mods_parts = grad_mods_all.reshape(groups * 6, D)
    ada_shard = exact(selector, mods_parts, (((1,), (0,)), ((), ())))
    unit = first_unit + jnp.arange(units, dtype=jnp.int32)
    grad_units = jnp.where(unit[:, None] >= BLOCK_UNITS, ada_shard, block_shard)
    products = exact(shard_low.astype(jnp.float32), mods_parts, (((1,), (1,)), ((), ())))
    products = jnp.sum(products.reshape(units, groups, 6) * ada_part[:, None, :], axis=2)
    spread = jnp.zeros((groups, 6 * D + 2 * units), jnp.float32)
    start = jnp.clip(first_unit - BLOCK_UNITS + units, 0, 6 * D + units)
    spread = lax.dynamic_update_slice(spread, products.T, (jnp.int32(0), start))
    grad_soft = jnp.sum(spread[:, units : units + 6 * D].reshape(groups, D, 6), axis=2)
    square_sum = jnp.sum(grad_units * grad_units)
    square_sum, grad_soft = lax.psum((square_sum, grad_soft), axes)
    silu_out, silu_back = jax.vjp(jax.nn.silu, conditioning)
    second_sum = silu_back(grad_soft)[0]
    grad_shard = grad_units.reshape(-1)
    grad_norm = jnp.sqrt(square_sum + jnp.sum(first_sum * first_sum))
    factor = jnp.minimum(1.0, CLIP_NORM / (grad_norm + 1e-06))
    new_weights, first_out, second_out = adamw(
        weights, grad_shard * factor, first_moment, second_moment
    )
    new_biases, bias_first_out, bias_second_out = adamw(
        biases, first_sum * factor, bias_first, bias_second
    )
    return (
        block_out,
        input_grad,
        second_sum,
        grad_norm,
        new_weights,
        first_out,
        second_out,
        new_biases,
        bias_first_out,
        bias_second_out,
    )


def solution(mesh):
    in_specs = (
        P(("outer", "inner"), None),
        P(),
        P(("outer", "inner")),
        P(),
        P(("outer", "inner"), None),
        P(("outer", "inner")),
        P(("outer", "inner")),
        P(("outer", "inner")),
        P(),
        P(),
        P(),
    )
    out_specs = (
        P(("outer", "inner"), None),
        P(("outer", "inner"), None),
        P(),
        P(),
        P(("outer", "inner")),
        P(("outer", "inner")),
        P(("outer", "inner")),
        P(),
        P(),
        P(),
    )
    kernels = dict(mesh.shape) == {"outer": 4, "inner": 8}
    return jax.shard_map(
        functools.partial(on_device, kernels=kernels), mesh=mesh, in_specs=in_specs, out_specs=out_specs, check_vma=False
    )
```
